256 devices in a mesh: dp: 32 (over z_hi, y, core), seq: 8 (over z_lo, x).
Axes of the slice: x: 4, y: 4, z: 8 (z_hi: 4, z_lo: 2; z = z_hi * 2 + z_lo), core: 2. Of those that a mesh axis runs over, the one named last changes fastest.
Arguments:
- seq_in: bfloat16 [32, 2048, 768], P('dp', 'seq'), may hold values from -40 to 40
- bases: int32 [32, 131072], P('dp', 'seq'), may hold values from 0 to 3
- conv_weight: bfloat16 [3072, 768], P('dp'), may hold values from -0.109375 to 0.109375
- dna_weight: bfloat16 [512, 768], P('dp'), may hold values from -0.5 to 0.5
- qkv_weight: bfloat16 [768, 1536], P('dp'), may hold values from -12 to 12
- out_weight: bfloat16 [512, 768], P('dp'), may hold values from -0.25 to 0.25
- cotangent: bfloat16 [32, 1024, 768], P('dp', 'seq'), may hold values from -6 to 6
Outputs:
- seq_grad: bfloat16 [32, 2048, 768], P('dp', 'seq')
- conv_grad: float32 [3072, 768], P('dp')
- dna_grad: float32 [512, 768], P('dp')
- qkv_grad: float32 [768, 1536], P('dp')
- out_grad: float32 [512, 768], P('dp')
The draws below stay inside these ranges and needn't reach their ends.
All inputs are finite; a program needn't handle non-finite values.
Results may differ from the reference program's by a relative error of at most 0.02.
Values may be sent and summed in bfloat16 or wider, within the bound.
A program may use at most 128 MiB of HBM per device.

```python
import math
import jax
import jax.numpy as jnp
from jax import lax

CIN = 768
D = 768
H = 4
DH = 128
BIN = 128
SAMPLES = 32
LEN = 1024
N_SEQ = 8


def draw_seq_in(key, part):
    key = jax.random.fold_in(key, 11)
    first_key, second_key, third_key = jax.random.split(key, 3)
    full_shape = (SAMPLES, 2 * LEN, CIN)
    values = jnp.clip(jax.random.normal(first_key, full_shape, jnp.float32), -4.0, 4.0)
    row_scale = jnp.exp(jax.random.uniform(second_key, (SAMPLES, 2 * LEN, 1), jnp.float32, 0.0, math.log(10.0)))
    column_scale = jnp.exp(jax.random.uniform(third_key, (1, 1, CIN), jnp.float32, 0.0, math.log(10.0)))
    return (0.1 * values * row_scale * column_scale).astype(jnp.bfloat16)


def draw_qkv_weight(key, part):
    key = jax.random.fold_in(key, 23)
    first_key, second_key, third_key = jax.random.split(key, 3)
    width = H * DH
    query_part = jnp.clip(jax.random.normal(first_key, (D, width), jnp.float32), -6.0, 6.0) / math.sqrt(D)
    key_part = jnp.clip(jax.random.normal(second_key, (D, width), jnp.float32), -6.0, 6.0) / math.sqrt(D)
    value_part = jnp.clip(jax.random.normal(third_key, (D, width), jnp.float32), -6.0, 6.0) / math.sqrt(D)
    return jnp.concatenate([query_part, key_part, value_part], axis=1).astype(jnp.bfloat16)


def place_ends(entries, key, smallest, largest):
    spot = [jax.random.randint(jax.random.fold_in(key, axis), (), 0, length) for axis, length in enumerate(entries.shape)]
    longest = entries.shape.index(max(entries.shape))
    neighbour = spot[:longest] + [(spot[longest] + 1) % entries.shape[longest]] + spot[longest + 1:]
    return entries.at[tuple(spot)].set(smallest).at[tuple(neighbour)].set(largest)


def block_scale(stream_key, shape, pieces, low, largest):
    def one(axis_at, blocks):
        heights = jax.random.uniform(jax.random.fold_in(jax.random.fold_in(stream_key, 6), axis_at), (blocks,), jnp.float32, low / len(pieces), largest / len(pieces))
        return jnp.repeat(jnp.exp(heights), shape[axis_at] // blocks).reshape((-1,) + (1,) * (len(shape) - axis_at - 1))

    factor_of = one(*pieces[0])
    for cut in pieces[1:]:
        factor_of = factor_of * one(*cut)
    return factor_of


def normal_values(own_key, extent, scale, most, shards=(), held_as=jnp.bfloat16):
    array = scale * jax.random.normal(own_key, extent, jnp.float32)
    if shards:
        array = array * block_scale(own_key, extent, shards, -0.22, 0.18)
    return jnp.clip(array, -most, most).astype(held_as)


def setup_inputs(seed: int = 0) -> dict:
    arg_keys = jax.random.split(jax.random.key(seed), 8)
    return {
        "seq_in": draw_seq_in(jax.random.fold_in(arg_keys[7], 71), 0),
        "bases": place_ends(jax.random.randint(arg_keys[1], (SAMPLES, LEN * BIN), 0, 4), jax.random.fold_in(arg_keys[1], 1), 0, 3).astype(jnp.int32),
        "conv_weight": normal_values(arg_keys[2], (4 * CIN, D), (4 * CIN) ** -0.5, 0.109375, ((0, 32),)),
        "dna_weight": normal_values(arg_keys[3], (4 * BIN, D), BIN ** -0.5, 0.5, ((0, 32),)),
        "qkv_weight": draw_qkv_weight(jax.random.fold_in(arg_keys[7], 71), 0),
        "out_weight": normal_values(arg_keys[5], (H * DH, D), (H * DH) ** -0.5, 0.25, ((0, 32),)),
        "cotangent": normal_values(arg_keys[6], (SAMPLES, LEN, D), 1.0, 6.0, ((0, 32), (1, 8))),
    }


epsilon = 1e-06

def unfold_rows(padded, length, channels):
    first_pair = padded[:2 * length].reshape(length, 2 * channels)
    second_pair = padded[2:].reshape(length, 2 * channels)
    return jnp.concatenate([first_pair, second_pair], axis=1)

def shard_partial(left_rows, right_rows):
    block_rows = left_rows.shape[0] // N_SEQ
    left_parts = left_rows.astype(jnp.float32).reshape(N_SEQ, block_rows, left_rows.shape[1])
    right_parts = right_rows.astype(jnp.float32).reshape(N_SEQ, block_rows, right_rows.shape[1])
    partial_sums = jnp.einsum('stl,str->slr', left_parts, right_parts)
    rounded = lax.optimization_barrier(partial_sums.astype(jnp.bfloat16))
    return lax.optimization_barrier(jnp.sum(rounded.astype(jnp.float32), axis=0))

def sample_step(rows_in, letters_row, upstream, conv_weight, dna_weight, qkv_weight, out_weight):
    length = upstream.shape[0]
    channels = rows_in.shape[1]
    padded = jnp.pad(rows_in, ((1, 1), (0, 0)))
    unfolded = unfold_rows(padded, length, channels)
    letters = letters_row.reshape(length, BIN, 1)
    onehot = (letters == jnp.arange(4, dtype=jnp.int32)).astype(jnp.bfloat16).reshape(length, 4 * BIN)
    pre_act = jnp.dot(unfolded, conv_weight, preferred_element_type=jnp.float32) + jnp.dot(onehot, dna_weight, preferred_element_type=jnp.float32)
    feature = jax.nn.gelu(pre_act).astype(jnp.bfloat16)
    feat_wide = feature.astype(jnp.float32)
    inverse = lax.rsqrt(lax.optimization_barrier(jnp.mean(feat_wide * feat_wide, axis=1, keepdims=True)) + epsilon)
    unit_rows = feat_wide * inverse
    normed = unit_rows.astype(jnp.bfloat16)
    projected = jnp.dot(normed, qkv_weight, preferred_element_type=jnp.float32).astype(jnp.bfloat16)
    width = H * DH
    scaling = 1.0 / math.sqrt(DH)
    queries = projected[:, :width]
    keys_all = projected[:, width:2 * width]
    values_all = projected[:, 2 * width:]
    d_attend = jnp.dot(upstream, out_weight.T, preferred_element_type=jnp.float32).astype(jnp.bfloat16)
    attended = []
    query_grads = []
    key_grads = []
    value_grads = []
    for head_index in range(H):
        columns = slice(head_index * DH, (head_index + 1) * DH)
        query_head = queries[:, columns]
        key_head = keys_all[:, columns]
        value_head = values_all[:, columns]
        scores = jnp.dot(query_head, key_head.T, preferred_element_type=jnp.float32) * scaling
        highest = lax.optimization_barrier(jnp.max(scores, axis=1, keepdims=True))
        powers = jnp.exp(scores - highest)
        probs = powers / lax.optimization_barrier(jnp.sum(powers, axis=1, keepdims=True))
        probs_low = probs.astype(jnp.bfloat16)
        attended.append(jnp.dot(probs_low, value_head, preferred_element_type=jnp.float32).astype(jnp.bfloat16))
        d_probs = jnp.dot(d_attend[:, columns], value_head.T, preferred_element_type=jnp.float32)
        inner = lax.optimization_barrier(jnp.sum(probs * d_probs, axis=1, keepdims=True))
        d_scores = (probs * (d_probs - inner) * scaling).astype(jnp.bfloat16)
        query_grads.append(jnp.dot(d_scores, key_head, preferred_element_type=jnp.float32))
        key_grads.append(jnp.dot(d_scores.T, query_head, preferred_element_type=jnp.float32))
        value_grads.append(jnp.dot(probs_low.T, d_attend[:, columns], preferred_element_type=jnp.float32))
    d_projected = jnp.concatenate(query_grads + key_grads + value_grads, axis=1).astype(jnp.bfloat16)
    attend_all = jnp.concatenate(attended, axis=1)
    d_normed = jnp.dot(d_projected, qkv_weight.T, preferred_element_type=jnp.float32)
    d_feature = upstream.astype(jnp.float32) + inverse * (d_normed - unit_rows * lax.optimization_barrier(jnp.mean(d_normed * unit_rows, axis=1, keepdims=True)))
    d_pre = jax.vjp(jax.nn.gelu, pre_act)[1](d_feature)[0].astype(jnp.bfloat16)
    d_unfolded = jnp.dot(d_pre, conv_weight.T, preferred_element_type=jnp.float32)
    lower_taps = d_unfolded[:, :2 * channels].reshape(2 * length, channels)
    upper_taps = d_unfolded[:, 2 * channels:].reshape(2 * length, channels)
    d_padded = jnp.pad(lower_taps, ((0, 2), (0, 0))) + jnp.pad(upper_taps, ((2, 0), (0, 0)))
    d_rows = d_padded[1:-1].astype(jnp.bfloat16)
    grads = (shard_partial(unfolded, d_pre), shard_partial(onehot, d_pre), shard_partial(normed, d_projected), shard_partial(attend_all, upstream))
    return (d_rows, grads)

def reference(seq_in, bases, conv_weight, dna_weight, qkv_weight, out_weight, cotangent):

    def advance(running, inputs):
        rows_in, letters_row, upstream = inputs
        d_rows, grads = sample_step(rows_in, letters_row, upstream, conv_weight, dna_weight, qkv_weight, out_weight)
        return (tuple((old_sum + gradient for old_sum, gradient in zip(running, grads))), d_rows)
    initial = (jnp.zeros(conv_weight.shape, jnp.float32), jnp.zeros(dna_weight.shape, jnp.float32), jnp.zeros(qkv_weight.shape, jnp.float32), jnp.zeros(out_weight.shape, jnp.float32))
    totals, seq_grad = lax.scan(advance, initial, (seq_in, bases, cotangent))
    return (seq_grad, totals[0], totals[1], totals[2], totals[3])
```

```python
import math

import jax
import jax.numpy as jnp
from jax import lax
from jax.experimental import pallas as pl
from jax.experimental.pallas import tpu as pltpu
from jax.sharding import PartitionSpec as P

H = 4
BIN = 128
BF16 = jnp.bfloat16
F32 = jnp.float32
MESH = pl.DeviceIdType.MESH
epsilon = 1e-06

SIZES = {"zh": 4, "y": 4, "c": 2, "zl": 2, "x": 4}
PEERS = [(a, k) for a in ("zh", "y", "x") for k in (1, 2, 3)] + [("zl", 1), ("c", 1)]


def here():
    dp = lax.axis_index("dp")
    sq = lax.axis_index("seq")
    return {"zh": dp // 8, "y": lax.rem(dp // 2, 4), "c": lax.rem(dp, 2), "zl": sq // 4, "x": lax.rem(sq, 4)}


def moved(at, **steps):
    to = dict(at)
    for axis, step in steps.items():
        to[axis] = lax.rem(at[axis] + step, SIZES[axis])
    return to


def device(at):
    return (at["zh"] * 8 + at["y"] * 2 + at["c"], at["zl"] * 4 + at["x"])


def meet(devices):
    barrier = pltpu.get_barrier_semaphore()
    for one in devices:
        pl.semaphore_signal(barrier, inc=1, device_id=one, device_id_type=MESH)
    pl.semaphore_wait(barrier, len(devices))


class Sender:
    def __init__(self, send_sems, recv_sems):
        self.send_sems, self.recv_sems, self.used, self.copies = send_sems, recv_sems, 0, []

    def __call__(self, src, dst, to):
        copy = pltpu.make_async_remote_copy(
            src_ref=src,
            dst_ref=dst,
            send_sem=self.send_sems.at[self.used],
            recv_sem=self.recv_sems.at[self.used],
            device_id=to,
            device_id_type=MESH,
        )
        copy.start()
        self.used += 1
        self.copies.append(copy)
        return copy

    def finish(self):
        for copy in self.copies:
            copy.wait_send()


def arrive(copies):
    for copy in copies:
        copy.wait_recv()


def rows16(index, base=0):
    return pl.ds(pl.multiple_of(index * 16 + base, 16), 16)


def half_columns(index):
    return pl.ds(pl.multiple_of(index * 384, 128), 384)


def gather_kernel(
    conv_s, do_s, qkv_s, rows_in, conv_g, do_g, qkv_g, before, after, send_sems, recv_sems, local_sems
):
    at = here()
    zh, y, c, zl, x = (at[a] for a in ("zh", "y", "c", "zl", "x"))
    sq = lax.axis_index("seq")
    dp = lax.axis_index("dp")
    behind, ahead = (dp, lax.rem(sq + 7, 8)), (dp, lax.rem(sq + 1, 8))
    meet([device(moved(at, **{a: k})) for a, k in PEERS] + [behind, ahead])
    send = Sender(send_sems, recv_sems)
    quarter = rows16(x)
    part, part_rows = x // 2, rows16(lax.rem(x, 2))
    half, other_half = half_columns(zl), half_columns(1 - zl)
    tail = pl.ds(64, 32)

    locals_ = [
        pltpu.make_async_copy(conv_s.at[quarter], conv_g.at[zh, y, c, quarter], local_sems.at[0]),
        pltpu.make_async_copy(conv_s.at[tail], conv_g.at[zh, y, c, tail], local_sems.at[1]),
        pltpu.make_async_copy(do_s, do_g.at[zh, y, c], local_sems.at[2]),
        pltpu.make_async_copy(
            qkv_s.at[part, part_rows, half], qkv_g.at[part, zh, y, c, part_rows, half], local_sems.at[3]
        ),
    ]
    for copy in locals_:
        copy.start()
    a1, b1, c1, a2, b2, c2, a3, c3 = ([] for _ in range(8))
    for k in (1, 2, 3):
        to = device(moved(at, zh=k))
        a1.append(send(conv_s.at[quarter], conv_g.at[zh, y, c, quarter], to))
    for k in (1, 2, 3):
        to = device(moved(at, zh=k))
        c1.append(
            send(qkv_s.at[part, part_rows, half], qkv_g.at[part, zh, y, c, part_rows, half], to)
        )
    for k in (1, 2, 3):
        to = device(moved(at, zh=k))
        b1.append(send(conv_s.at[tail], conv_g.at[zh, y, c, tail], to))
        b1.append(send(do_s, do_g.at[zh, y, c], to))
    halo = [
        send(rows_in.at[pl.ds(240, 16)], before, ahead),
        send(rows_in.at[pl.ds(0, 16)], after, behind),
    ]
    for copy in locals_:
        copy.wait()
    arrive(a1)
    for k in (1, 2, 3):
        block = conv_g.at[:, y, c, quarter]
        a2.append(send(block, block, device(moved(at, y=k))))
    arrive(c1)
    for k in (1, 2, 3):
        block = qkv_g.at[part, :, y, c, part_rows, half]
        c2.append(send(block, block, device(moved(at, y=k))))
    arrive(b1)
    for k in (1, 2, 3):
        to = device(moved(at, y=k))
        b2.append(
            (
                send(conv_g.at[:, y, c, tail], conv_g.at[:, y, c, tail], to),
                send(do_g.at[:, y, c], do_g.at[:, y, c], to),
            )
        )
    sibling = device(moved(at, c=1))
    core = []

    def pass_on(block):
        core.append(send(block, block, sibling))

    arrive(a2)
    for k in (1, 2, 3):
        block = conv_g.at[:, :, c, quarter]
        a3.append(send(block, block, device(moved(at, x=k))))
    arrive(c2)
    for k in (1, 2, 3):
        block = qkv_g.at[part, :, :, c, part_rows, half]
        c3.append(send(block, block, device(moved(at, x=k))))
    pass_on(conv_g.at[:, :, c, quarter])
    pass_on(conv_g.at[:, y, c, tail])
    pass_on(do_g.at[:, y, c])
    arrive(c3)
    block = qkv_g.at[:, :, :, c, :, half]
    c4 = send(block, block, device(moved(at, zl=1)))
    pass_on(block)
    for k in (1, 2, 3):
        arrive(b2[k - 1])
        from_y = lax.rem(y + 4 - k, 4)
        pass_on(conv_g.at[:, from_y, c, tail])
        pass_on(do_g.at[:, from_y, c])
    for k in (1, 2, 3):
        arrive([a3[k - 1]])
        pass_on(conv_g.at[:, :, c, rows16(lax.rem(x + 4 - k, 4))])
    arrive([c4])
    pass_on(qkv_g.at[:, :, :, c, :, other_half])
    arrive(halo)
    arrive(core)
    send.finish()


def gather_weights(conv_s, do_s, qkv_s, rows_in):
    any_spec = pl.BlockSpec(memory_space=pl.ANY)
    return pl.pallas_call(
        gather_kernel,
        name="gather_weights",
        out_shape=(
            jax.ShapeDtypeStruct((4, 4, 2, 96, 768), BF16),
            jax.ShapeDtypeStruct((4, 4, 2, 32, 768), BF16),
            jax.ShapeDtypeStruct((2, 4, 4, 2, 32, 768), BF16),
            jax.ShapeDtypeStruct((16, 768), BF16),
            jax.ShapeDtypeStruct((16, 768), BF16),
        ),
        in_specs=[any_spec] * 4,
        out_specs=(any_spec,) * 5,
        scratch_shapes=[
            pltpu.SemaphoreType.DMA((48,)),
            pltpu.SemaphoreType.DMA((48,)),
            pltpu.SemaphoreType.DMA((4,)),
        ],
        compiler_params=pltpu.CompilerParams(collective_id=1, has_side_effects=True),
    )(conv_s, do_s, qkv_s, rows_in)


def right_dot(left, right):
    return lax.dot_general(left, right, (((1,), (1,)), ((), ())), preferred_element_type=F32)


def row_dot(left, right):
    return lax.dot_general(left, right, (((0,), (0,)), ((), ())), preferred_element_type=F32)


def attention_kernel(
    mine, back, back_kv, got, got_kv, outgo, outgo_kv, d_kv, send_sems, recv_sems, local_sem
):
    at = here()
    x = at["x"]
    partners = [moved(at, x=k) for k in (1, 2, 3)]
    across = [moved(at, x=k, zl=1) for k in range(4)]
    meet([device(p) for p in partners] + [device(p) for p in across])
    send = Sender(send_sems, recv_sems)
    own = pltpu.make_async_copy(mine.at[x], got.at[x], local_sem.at[0])
    own.start()
    arriving = []
    for p in across:
        arriving.append(send(mine.at[p["x"], :, pl.ds(128, 256)], got_kv.at[x], device(p)))
    for p in partners:
        arriving.append(send(mine.at[p["x"]], got.at[x], device(p)))
    own.wait()
    arrive(arriving)

    scaling = 1.0 / math.sqrt(128)
    keys = jnp.concatenate([got[:, :, 128:256].reshape(512, 128), got_kv[:, :, :128].reshape(512, 128)], axis=0)
    values = jnp.concatenate([got[:, :, 256:384].reshape(512, 128), got_kv[:, :, 128:].reshape(512, 128)], axis=0)
    d_kv[...] = jnp.zeros_like(d_kv)

    def block(index, carry):
        queries = got[index, :, 0:128]
        upward = got[index, :, 384:512]
        scores = right_dot(queries, keys) * scaling
        powers = jnp.exp(scores - jnp.max(scores, axis=1, keepdims=True))
        probs = powers / jnp.sum(powers, axis=1, keepdims=True)
        probs_low = probs.astype(BF16)
        outgo[index, :, 0:128] = jnp.dot(probs_low, values, preferred_element_type=F32).astype(BF16)
        d_probs = right_dot(upward, values)
        inner = jnp.sum(probs * d_probs, axis=1, keepdims=True)
        d_scores = (probs * (d_probs - inner) * scaling).astype(BF16)
        outgo[index, :, 128:256] = jnp.dot(d_scores, keys, preferred_element_type=F32).astype(BF16)
        d_kv[:, 0:128] += row_dot(d_scores, queries)
        d_kv[:, 128:256] += row_dot(probs_low, upward)
        return carry

    lax.fori_loop(0, 4, block, 0)
    outgo[:, :, 256:512] = d_kv[0:512].astype(BF16).reshape(4, 128, 256)
    outgo_kv[...] = d_kv[512:1024].astype(BF16).reshape(4, 128, 256)
    own = pltpu.make_async_copy(outgo.at[x], back.at[x], local_sem.at[0])
    own.start()
    arriving = []
    for p in across:
        arriving.append(send(outgo_kv.at[p["x"]], back_kv.at[x], device(p)))
    for p in partners:
        arriving.append(send(outgo.at[p["x"]], back.at[x], device(p)))
    own.wait()
    arrive(arriving)
    send.finish()


def attention(mine):
    vmem = pl.BlockSpec(memory_space=pltpu.VMEM)
    return pl.pallas_call(
        attention_kernel,
        name="attention",
        out_shape=(
            jax.ShapeDtypeStruct((4, 128, 512), BF16),
            jax.ShapeDtypeStruct((4, 128, 256), BF16),
        ),
        in_specs=[vmem],
        out_specs=(vmem, vmem),
        scratch_shapes=[
            pltpu.VMEM((4, 128, 512), BF16),
            pltpu.VMEM((4, 128, 256), BF16),
            pltpu.VMEM((4, 128, 512), BF16),
            pltpu.VMEM((4, 128, 256), BF16),
            pltpu.VMEM((1024, 256), F32),
            pltpu.SemaphoreType.DMA((16,)),
            pltpu.SemaphoreType.DMA((16,)),
            pltpu.SemaphoreType.DMA((1,)),
        ],
        compiler_params=pltpu.CompilerParams(
            collective_id=2, has_side_effects=True, vmem_limit_bytes=40 * 2**20
        ),
    )(mine)


def reduce_kernel(
    conv_p, do_p, qkv_p,
    conv_o, dna_o, out_o, qkv_o,
    conv_r, do_r, qkv_r, conv_v, do_v, qkv_v,
    ra1, ra2, ra3, ra4, sa1, sa2, sa3,
    rb1, rb2, rb3, rb4, sb1, sb2, sb3,
    rc1, rc2, rc3, rc4, sc1, sc2, sc3,
    final,
    send_sems, recv_sems, local_sems,
):
    at = here()
    zh, y, c, zl, x = (at[a] for a in ("zh", "y", "c", "zl", "x"))
    meet([device(moved(at, **{a: k})) for a, k in PEERS])
    send = Sender(send_sems, recv_sems)
    sibling = device(moved(at, c=1))
    near = device(moved(at, zl=1))
    half, other_half = half_columns(zl), half_columns(1 - zl)
    tail = pl.ds(64, 32)
    locals_ = []

    def local(src, dst):
        copy = pltpu.make_async_copy(src, dst, local_sems.at[len(locals_)])
        copy.start()
        locals_.append(copy)

    local(conv_p.at[:, :, c], conv_v)
    local(qkv_p.at[:, :, :, c], qkv_v)
    local(do_p.at[:, :, c], do_v)

    order = [(1, 2, 3, 0)[i] for i in range(4)]
    xs = {k: lax.rem(x + k, 4) for k in order}
    ys = {k: lax.rem(y + k, 4) for k in order}
    zs = {k: lax.rem(zh + k, 4) for k in order}
    core_a, core_b, core_c = {}, {}, {}
    for k in order:
        core_a[k] = [send(conv_p.at[:, :, 1 - c, rows16(xs[k])], conv_r.at[:, :, rows16(xs[k])], sibling)]
        core_b[k] = [
            send(conv_p.at[:, ys[k], 1 - c, tail], conv_r.at[:, ys[k], tail], sibling),
            send(do_p.at[:, ys[k], 1 - c], do_r.at[:, ys[k]], sibling),
        ]
        if k == 1:
            core_c[1] = [send(qkv_p.at[:, :, :, 1 - c, :, other_half], qkv_r.at[:, :, :, :, other_half], sibling)]
    core_c[0] = [send(qkv_p.at[:, :, :, 1 - c, :, half], qkv_r.at[:, :, :, :, half], sibling)]
    for copy in locals_:
        copy.wait()

    def loop(n, body):
        def step(i, carry):
            body(i)
            return carry

        lax.fori_loop(0, n, step, 0)

    def add(target, *terms):
        total = terms[0].astype(F32)
        for term in terms[1:]:
            total += term.astype(F32)
        return total.astype(target.dtype)

    a1, b1, c1 = {}, {}, {}
    for k in order:
        arrive(core_a[k])
        rows = rows16(xs[k])

        def sum_a(i, rows=rows):
            conv_v[i, :, rows] = add(conv_v, conv_v[i, :, rows], conv_r[i, :, rows])

        loop(4, sum_a)
        if k:
            a1[k] = send(conv_v.at[:, :, rows], ra1.at[k - 1], device(moved(at, x=k)))
        arrive(core_b[k])
        ky = ys[k]

        def sum_b(i, ky=ky):
            conv_v[i, ky, 64:96] = add(conv_v, conv_v[i, ky, 64:96], conv_r[i, ky, 64:96])
            do_v[i, ky] = add(do_v, do_v[i, ky], do_r[i, ky])

        loop(4, sum_b)
        if k:
            to = device(moved(at, y=k))
            b1[k] = [
                send(conv_v.at[:, ky, tail], rb1.at[k - 1, :, pl.ds(0, 32)], to),
                send(do_v.at[:, ky], rb1.at[k - 1, :, pl.ds(32, 32)], to),
            ]
        if k in (1, 0):
            arrive(core_c[k])
            columns = other_half if k else half

            def sum_c(i, columns=columns):
                for part in range(2):
                    qkv_v[part, i, :, :, columns] = add(
                        qkv_v, qkv_v[part, i, :, :, columns], qkv_r[part, i, :, :, columns]
                    )

            loop(4, sum_c)
            if k:
                c1[1] = send(qkv_v.at[:, :, :, :, columns], rc1, near)

    arrive(a1.values())

    def first_a(i):
        sa1[i] = add(sa1, conv_v[i, :, rows16(x)], ra1[0, i], ra1[1, i], ra1[2, i])

    loop(4, first_a)
    a2 = [send(sa1.at[:, ys[k]], ra2.at[k - 1], device(moved(at, y=k))) for k in (1, 2, 3)]
    for k in (1, 2, 3):
        arrive(b1[k])

    def first_b(i):
        sb1[i, 0:32] = add(sb1, conv_v[i, y, 64:96], rb1[0, i, 0:32], rb1[1, i, 0:32], rb1[2, i, 0:32])
        sb1[i, 32:64] = add(sb1, do_v[i, y], rb1[0, i, 32:64], rb1[1, i, 32:64], rb1[2, i, 32:64])

    loop(4, first_b)
    b2 = [send(sb1.at[:, rows16(xs[k])], rb2.at[k - 1], device(moved(at, x=k))) for k in (1, 2, 3)]
    arrive(c1.values())

    def first_c(i):
        for part in range(2):
            sc1[part, i] = add(sc1, qkv_v[part, i, :, :, half], rc1[part, i])

    loop(4, first_c)
    c2 = [
        send(
            sc1.at[xs[k] // 2, :, :, rows16(lax.rem(xs[k], 2))],
            rc2.at[k - 1],
            device(moved(at, x=k)),
        )
        for k in (1, 2, 3)
    ]

    arrive(a2)

    def second_a(i):
        sa2[i] = add(sa2, sa1[i, y], ra2[0, i], ra2[1, i], ra2[2, i])

    loop(4, second_a)
    a3 = [send(sa2.at[zs[k]], ra3.at[k - 1], device(moved(at, zh=k))) for k in (1, 2, 3)]
    arrive(b2)

    def second_b(i):
        sb2[i] = add(sb2, sb1[i, rows16(x)], rb2[0, i], rb2[1, i], rb2[2, i])

    loop(4, second_b)
    b3 = [send(sb2.at[zs[k]], rb3.at[k - 1], device(moved(at, zh=k))) for k in (1, 2, 3)]
    arrive(c2)

    def second_c(i):
        own = sc1[x // 2, i, :, rows16(lax.rem(x, 2))]
        sc2[i] = add(sc2, own, rc2[0, i], rc2[1, i], rc2[2, i])

    loop(4, second_c)
    c3 = [send(sc2.at[:, ys[k]], rc3.at[k - 1], device(moved(at, y=k))) for k in (1, 2, 3)]

    arrive(a3)
    sa3[...] = add(sa3, sa2[zh], ra3[0], ra3[1], ra3[2])
    a4 = send(sa3, ra4, near)
    arrive(b3)
    sb3[...] = add(sb3, sb2[zh], rb3[0], rb3[1], rb3[2])
    b4 = send(sb3, rb4, near)
    arrive(c3)

    def third_c(i):
        sc3[i] = add(sc3, sc2[i, y], rc3[0, i], rc3[1, i], rc3[2, i])

    loop(4, third_c)
    c4 = [send(sc3.at[zs[k]], rc4.at[k - 1], device(moved(at, zh=k))) for k in (1, 2, 3)]

    arrive([a4])
    final[x, 0] = add(final, sa3[...], ra4[...])
    arrive([b4])
    final[x, 1] = add(final, sb3[...], rb4[...])
    share = [
        send(final.at[x, pl.ds(0, 2)], final.at[x, pl.ds(0, 2)], device(moved(at, x=k))) for k in (1, 2, 3)
    ]
    arrive(c4)
    final[x, 2, :, half] = add(final, sc3[zh], rc4[0], rc4[1], rc4[2])
    block = final.at[x, 2, :, half]
    arrive([send(block, block, near)])
    share += [send(final.at[x, 2], final.at[x, 2], device(moved(at, x=k))) for k in (1, 2, 3)]
    arrive(share)
    for q in range(4):
        conv_o[16 * q : 16 * q + 16] = final[q, 0].astype(F32)
    conv_o[64:80] = final[0, 1].astype(F32)
    conv_o[80:96] = final[1, 1].astype(F32)
    dna_o[...] = final[2, 1].astype(F32)
    out_o[...] = final[3, 1].astype(F32)
    qkv_o[0:16, 0:768] = final[0, 2].astype(F32)
    qkv_o[16:24, 0:768] = final[1, 2].astype(F32)[0:8]
    qkv_o[0:16, 768:1536] = final[2, 2].astype(F32)
    qkv_o[16:24, 768:1536] = final[3, 2].astype(F32)[0:8]
    send.finish()


def reduce_gradients(conv_p, do_p, qkv_p):
    any_spec = pl.BlockSpec(memory_space=pl.ANY)
    vmem = pl.BlockSpec(memory_space=pltpu.VMEM)
    shapes = [
        (4, 4, 96, 768), (4, 4, 32, 768), (2, 4, 4, 32, 768), (4, 4, 96, 768), (4, 4, 32, 768), (2, 4, 4, 32, 768),
        (3, 4, 4, 16, 768), (3, 4, 16, 768), (3, 16, 768), (16, 768), (4, 4, 16, 768), (4, 16, 768), (16, 768),
        (3, 4, 64, 768), (3, 4, 16, 768), (3, 16, 768), (16, 768), (4, 64, 768), (4, 16, 768), (16, 768),
        (2, 4, 4, 32, 384), (3, 4, 4, 16, 384), (3, 4, 16, 384), (3, 16, 384),
        (2, 4, 4, 32, 384), (4, 4, 16, 384), (4, 16, 384),
        (4, 3, 16, 768),
    ]
    return pl.pallas_call(
        reduce_kernel,
        name="reduce_gradients",
        out_shape=(
            jax.ShapeDtypeStruct((96, 768), F32),
            jax.ShapeDtypeStruct((16, 768), F32),
            jax.ShapeDtypeStruct((16, 768), F32),
            jax.ShapeDtypeStruct((24, 1536), F32),
        ),
        in_specs=[any_spec] * 3,
        out_specs=(vmem,) * 4,
        scratch_shapes=[pltpu.VMEM(shape, BF16) for shape in shapes]
        + [pltpu.SemaphoreType.DMA((64,)), pltpu.SemaphoreType.DMA((64,)), pltpu.SemaphoreType.DMA((3,))],
        compiler_params=pltpu.CompilerParams(
            collective_id=3, has_side_effects=True, vmem_limit_bytes=48 * 2**20
        ),
    )(conv_p, do_p, qkv_p)


def swap_rims(rim_rows):
    peers = lax.axis_size("seq")
    up = [(i, (i + 1) % peers) for i in range(peers - 1)]
    down = [(j, i) for i, j in up]
    return lax.ppermute(rim_rows[1:], "seq", up), lax.ppermute(rim_rows[:1], "seq", down)


def unfold_rows(padded, length, channels):
    first_pair = padded[: 2 * length].reshape(length, 2 * channels)
    second_pair = padded[2:].reshape(length, 2 * channels)
    return jnp.concatenate([first_pair, second_pair], axis=1)


def spread(columns):
    parts = columns.reshape(columns.shape[0], 32, 24)
    return jnp.pad(parts, ((0, 0), (0, 0), (0, 8))).reshape(columns.shape[0], 1024)


def gathered_in(columns):
    return columns.reshape(columns.shape[0], 32, 32)[:, :, :24].reshape(columns.shape[0], 768)


def per_device(seq_in, bases, conv_weight, dna_weight, qkv_weight, out_weight, cotangent):
    rows_in = seq_in[0]
    upstream = cotangent[0]
    tokens_here = upstream.shape[0]
    channels = rows_in.shape[1]
    place = lax.axis_index("seq")
    qkv_parts = jnp.pad(
        jnp.stack([qkv_weight[:, :768], qkv_weight[:, 768:]]), ((0, 0), (0, 8), (0, 0))
    )
    conv_g, do_g, qkv_g, before, after = gather_weights(
        conv_weight, jnp.concatenate([dna_weight, out_weight], axis=0), qkv_parts, rows_in
    )
    conv_full = conv_g.reshape(3072, 768)
    do_full = do_g.reshape(32, 2, 16, 768)
    dna_full = do_full[:, 0].reshape(512, 768)
    out_full = do_full[:, 1].reshape(512, 768)
    qkv_full = qkv_g.reshape(2, 1024, 768)

    first = jnp.where(place > 0, before[15:16], jnp.zeros_like(before[15:16]))
    last = jnp.where(place < 7, after[0:1], jnp.zeros_like(after[0:1]))
    padded = jnp.concatenate([first, rows_in, last], axis=0)
    unfolded = unfold_rows(padded, tokens_here, channels)
    letters = bases[0].reshape(tokens_here, BIN, 1)
    onehot = (
        (letters == jnp.arange(4, dtype=jnp.int32))
        .astype(BF16)
        .reshape(tokens_here, 4 * BIN)
    )
    pre_act = jnp.dot(unfolded, conv_full, preferred_element_type=F32) + jnp.dot(
        onehot, dna_full, preferred_element_type=F32
    )
    feature = jax.nn.gelu(pre_act).astype(BF16)
    feat_wide = feature.astype(F32)
    inverse = lax.rsqrt(jnp.mean(feat_wide * feat_wide, axis=1, keepdims=True) + epsilon)
    unit_rows = feat_wide * inverse
    normed = unit_rows.astype(BF16)
    normed_wide = spread(normed)
    projected = jnp.concatenate(
        [jnp.dot(normed_wide, qkv_full[i], preferred_element_type=F32).astype(BF16) for i in range(2)], axis=1
    )
    d_attend = right_dot(upstream, out_full).astype(BF16)
    mine = (
        jnp.concatenate([projected, d_attend], axis=1)
        .reshape(tokens_here, 4, H, 128)
        .transpose(2, 0, 1, 3)
        .reshape(H, tokens_here, 512)
    )
    back, back_kv = attention(mine)
    attend_all = back[:, :, :128].transpose(1, 0, 2).reshape(tokens_here, 512)
    d_queries = back[:, :, 128:256].transpose(1, 0, 2).reshape(tokens_here, 512)
    d_keys_values = (
        (back[:, :, 256:].astype(F32) + back_kv.astype(F32))
        .astype(BF16)
        .reshape(H, tokens_here, 2, 128)
        .transpose(1, 2, 0, 3)
        .reshape(tokens_here, 1024)
    )
    d_projected = jnp.concatenate([d_queries, d_keys_values], axis=1)
    d_normed = gathered_in(
        right_dot(d_projected[:, :768], qkv_full[0]) + right_dot(d_projected[:, 768:], qkv_full[1])
    )
    d_feature = upstream.astype(F32) + inverse * (
        d_normed - unit_rows * jnp.mean(d_normed * unit_rows, axis=1, keepdims=True)
    )
    d_pre = jax.vjp(jax.nn.gelu, pre_act)[1](d_feature)[0].astype(BF16)
    d_unfolded = right_dot(d_pre, conv_full)
    lower_taps = d_unfolded[:, : 2 * channels].reshape(2 * tokens_here, channels)
    upper_taps = d_unfolded[:, 2 * channels :].reshape(2 * tokens_here, channels)
    d_padded = jnp.pad(lower_taps, ((0, 2), (0, 0))) + jnp.pad(upper_taps, ((2, 0), (0, 0)))
    from_before, from_after = swap_rims(jnp.stack([d_padded[0], d_padded[-1]]))
    middle_rows = d_padded[1:-1]
    middle_rows = middle_rows.at[0].add(from_before[0]).at[-1].add(from_after[0])
    seq_grad = middle_rows.astype(BF16)[None]

    conv_p = row_dot(unfolded, d_pre).astype(BF16).reshape(4, 4, 2, 96, 768)
    dna_p = row_dot(onehot, d_pre).astype(BF16).reshape(4, 4, 2, 16, 768)
    out_p = row_dot(attend_all, upstream).astype(BF16).reshape(4, 4, 2, 16, 768)
    do_p = jnp.concatenate([dna_p, out_p], axis=3)
    qkv_p = jnp.stack(
        [row_dot(normed_wide, d_projected[:, 768 * i : 768 * i + 768]).astype(BF16) for i in range(2)]
    ).reshape(2, 4, 4, 2, 32, 768)
    conv_grad, dna_grad, out_grad, qkv_grad = reduce_gradients(conv_p, do_p, qkv_p)
    return (seq_grad, conv_grad, dna_grad, qkv_grad, out_grad)


def solution(mesh):
    in_specs = (
        P("dp", "seq", None),
        P("dp", "seq"),
        P("dp", None),
        P("dp", None),
        P("dp", None),
        P("dp", None),
        P("dp", "seq", None),
    )
    out_specs = (P("dp", "seq", None), P("dp", None), P("dp", None), P("dp", None), P("dp", None))
    return jax.shard_map(
        per_device, mesh=mesh, in_specs=in_specs, out_specs=out_specs, check_vma=False
    )
```

```python
import math

import jax
import jax.numpy as jnp
from jax import lax
from jax.experimental import pallas as pl
from jax.experimental.pallas import tpu as pltpu
from jax.sharding import PartitionSpec as P

H = 4
BIN = 128
BF16 = jnp.bfloat16
F32 = jnp.float32
MESH = pl.DeviceIdType.MESH
epsilon = 1e-06

SIZES = {"zh": 4, "y": 4, "c": 2, "zl": 2, "x": 4}
PEERS = [(a, k) for a in ("zh", "y", "x") for k in (1, 2, 3)] + [("zl", 1), ("c", 1)]


def here():
    dp = lax.axis_index("dp")
    sq = lax.axis_index("seq")
    return {"zh": dp // 8, "y": lax.rem(dp // 2, 4), "c": lax.rem(dp, 2), "zl": sq // 4, "x": lax.rem(sq, 4)}


def moved(at, **steps):
    to = dict(at)
    for axis, step in steps.items():
        to[axis] = lax.rem(at[axis] + step, SIZES[axis])
    return to


def device(at):
    return (at["zh"] * 8 + at["y"] * 2 + at["c"], at["zl"] * 4 + at["x"])


def meet(devices):
    barrier = pltpu.get_barrier_semaphore()
    for one in devices:
        pl.semaphore_signal(barrier, inc=1, device_id=one, device_id_type=MESH)
    pl.semaphore_wait(barrier, len(devices))


class Sender:
    def __init__(self, send_sems, recv_sems):
        self.send_sems, self.recv_sems, self.used, self.copies = send_sems, recv_sems, 0, []

    def __call__(self, src, dst, to):
        copy = pltpu.make_async_remote_copy(
            src_ref=src,
            dst_ref=dst,
            send_sem=self.send_sems.at[self.used],
            recv_sem=self.recv_sems.at[self.used],
            device_id=to,
            device_id_type=MESH,
        )
        copy.start()
        self.used += 1
        self.copies.append(copy)
        return copy

    def finish(self):
        for copy in self.copies:
            copy.wait_send()


def arrive(copies):
    for copy in copies:
        copy.wait_recv()


def rows16(index, base=0):
    return pl.ds(pl.multiple_of(index * 16 + base, 16), 16)


def half_columns(index):
    return pl.ds(pl.multiple_of(index * 384, 128), 384)


def right_dot(left, right):
    return lax.dot_general(left, right, (((1,), (1,)), ((), ())), preferred_element_type=F32)


def row_dot(left, right):
    return lax.dot_general(left, right, (((0,), (0,)), ((), ())), preferred_element_type=F32)


def dot(left, right):
    return jnp.dot(left, right, preferred_element_type=F32)


def add(target, *terms):
    total = terms[0].astype(F32)
    for term in terms[1:]:
        total += term.astype(F32)
    return total.astype(target.dtype)


def loop(n, body):
    def step(i, carry):
        body(i)
        return carry

    lax.fori_loop(0, n, step, 0)


class Ring:
    def __init__(self, send, at, axis, region):
        self.send, self.me, self.region = send, at[axis], region
        self.right, self.left = device(moved(at, **{axis: 1})), device(moved(at, **{axis: 3}))

    def at(self, step):
        return lax.rem(self.me + step, 4)

    def go(self, index, part, to):
        return [self.send(ref, ref, to) for ref in self.region(index, part)]

    def start(self):
        self.from_left = self.go(self.me, None, self.right)
        self.from_right = self.go(self.me, None, self.left)

    def left_in(self):
        arrive(self.from_left)
        self.far_left = self.go(self.at(3), 0, self.right)
        return self.region(self.at(3), None)

    def right_in(self):
        arrive(self.from_right)
        self.far_right = self.go(self.at(1), 1, self.left)
        return self.region(self.at(1), None)

    def far_left_in(self):
        arrive(self.far_left)
        return self.region(self.at(2), 0)

    def far_right_in(self):
        arrive(self.far_right)
        return self.region(self.at(2), 1)


def layer_kernel(
    conv_s, do_s, qkv_s, pairs, letters, upstream,
    seq_o, conv_o, dna_o, out_o, qkv_o,
    conv_g, do_g, qkv_g, before, after,
    taps, taps_t, onehot, onehot_t, choose, wide, wide_t, unit, slope, inverse, d_proj, attended, shift,
    mine, got, got_kv, outgo, outgo_kv, back, back_kv, d_kv,
    conv_p, do_p, qkv_p, conv_r, do_r, qkv_r,
    ra1, ra2, ra3, ra4, sa1, sa2, sa3,
    rb1, rb2, rb3, rb4, sb1, sb2, sb3,
    rc1, rc2, rc3, rc4, sc1, sc2, sc3,
    final, rim_out, rim_before, rim_after,
    send_sems, recv_sems,
):
    at = here()
    zh, y, c, zl, x = (at[a] for a in ("zh", "y", "c", "zl", "x"))
    sq = lax.axis_index("seq")
    dp = lax.axis_index("dp")
    behind, ahead = (dp, lax.rem(sq + 7, 8)), (dp, lax.rem(sq + 1, 8))
    sibling = device(moved(at, c=1))
    near = device(moved(at, zl=1))
    partners = [moved(at, x=k) for k in (1, 2, 3)]
    across = [moved(at, x=k, zl=1) for k in range(4)]
    everyone = [device(moved(at, **{a: k})) for a, k in PEERS] + [behind, ahead]
    everyone += [device(p) for p in across[1:]]
    barrier = pltpu.get_barrier_semaphore()
    for one in everyone:
        pl.semaphore_signal(barrier, inc=1, device_id=one, device_id_type=MESH)

    row = lax.broadcasted_iota(jnp.int32, (128, 512), 0)
    column = lax.broadcasted_iota(jnp.int32, (128, 512), 1)
    repeat = (column // 4 == row).astype(F32).astype(BF16)
    repeated = dot(letters[...].astype(F32).astype(BF16), repeat)
    onehot[...] = (repeated == lax.rem(column, 4).astype(F32)).astype(F32).astype(BF16)
    onehot_t[...] = onehot[...].T
    row = lax.broadcasted_iota(jnp.int32, (768, 1024), 0)
    column = lax.broadcasted_iota(jnp.int32, (768, 1024), 1)
    inside = lax.rem(column, 32)
    choose[...] = ((column // 32 * 24 + inside == row) & (inside < 24)).astype(F32).astype(BF16)
    quarter = rows16(x)
    part, part_rows = x // 2, rows16(lax.rem(x, 2))
    half, other_half = half_columns(zl), half_columns(1 - zl)
    tail = pl.ds(64, 32)
    conv_g[zh, y, c, quarter] = conv_s[quarter]
    conv_g[zh, y, c, 64:96] = conv_s[64:96]
    do_g[zh, y, c] = do_s[...]
    qkv_g[part, zh, y, c, part_rows, half] = qkv_s[part, part_rows, half]
    pl.semaphore_wait(barrier, len(everyone))

    send = Sender(send_sems, recv_sems)
    a1, b1, c1, a2, c2 = ([] for _ in range(5))
    for k in (1, 2, 3):
        block = qkv_g.at[part, zh, y, c, part_rows, half]
        c1.append(send(block, block, device(moved(at, zh=k))))
    for k in (1, 2, 3):
        block = conv_g.at[zh, y, c, quarter]
        a1.append(send(block, block, device(moved(at, zh=k))))
    halo = [
        send(pairs.at[pl.ds(112, 16), pl.ds(768, 768)], before, ahead),
        send(pairs.at[pl.ds(0, 16), pl.ds(0, 768)], after, behind),
    ]
    for k in (1, 2, 3):
        to = device(moved(at, zh=k))
        for block in (conv_g.at[zh, y, c, tail], do_g.at[zh, y, c]):
            b1.append(send(block, block, to))
    arrive(c1)
    for k in (1, 2, 3):
        block = qkv_g.at[part, :, y, c, part_rows, half]
        c2.append(send(block, block, device(moved(at, y=k))))
    arrive(a1)
    for k in (1, 2, 3):
        block = conv_g.at[:, y, c, quarter]
        a2.append(send(block, block, device(moved(at, y=k))))
    arrive(b1)

    def cut(part):
        return pl.ds(0, 4) if part is None else pl.ds(2 * part, 2)

    def region_a(index, part):
        return [conv_g.at[cut(part), :, c, rows16(index)]]

    def region_b(index, part):
        return [conv_g.at[cut(part), index, c, tail], do_g.at[cut(part), index, c]]

    def region_c(index, part, columns=half):
        return [qkv_g.at[index // 2, cut(part), :, c, rows16(lax.rem(index, 2)), columns]]

    core, far = [], []

    def pass_on(refs):
        for ref in refs:
            core.append(send(ref, ref, sibling))

    def pass_far(refs):
        for ref in refs:
            far.append(send(ref, ref, near))

    ring_a = Ring(send, at, "x", region_a)
    ring_b = Ring(send, at, "y", region_b)
    ring_c = Ring(send, at, "x", region_c)
    ring_b.start()
    pass_on(region_b(y, None))
    arrive(c2)
    ring_c.start()
    pass_far(region_c(x, None))
    pass_on(region_c(x, None))
    arrive(a2)
    ring_a.start()
    pass_on(region_a(x, None))

    arrive(halo)
    taps[1] = pairs[:, 0:768]
    taps[2] = pairs[:, 768:1536]
    shift[8:136] = pairs[:, 768:1536].astype(F32)
    shift[0:8] = jnp.where(sq > 0, before[...].astype(F32)[8:16], 0.0)
    taps[0] = shift[7:135].astype(BF16)
    shift[0:128] = pairs[:, 0:768].astype(F32)
    shift[128:136] = jnp.where(sq < 7, after[...].astype(F32)[0:8], 0.0)
    taps[3] = shift[1:129].astype(BF16)

    refs = ring_c.left_in()
    pass_far(refs)
    pass_on(refs)
    refs = ring_c.right_in()
    pass_far(refs)
    pass_on(refs)
    pass_on(ring_b.left_in())
    pass_on(ring_b.right_in())
    refs = ring_c.far_left_in() + ring_c.far_right_in()
    pass_far(refs)
    pass_on(refs)
    pass_on(ring_a.left_in())
    pass_on(ring_a.right_in())
    pass_on(ring_b.far_left_in())
    pass_on(ring_b.far_right_in())
    for k in (0, 3, 1):
        arrive([far[(0, 3, 1).index(k)]])
        pass_on(region_c(lax.rem(x + k, 4), None, other_half))
    for k in (0, 1):
        arrive([far[3 + k]])
        pass_on(region_c(lax.rem(x + 2, 4), k, other_half))
    pass_on(ring_a.far_left_in())
    pass_on(ring_a.far_right_in())

    def transpose_tap(i):
        taps_t[i] = taps[i].T

    loop(4, transpose_tap)
    arrive(core)

    dna_full = do_g[:, :, :, 0:16].reshape(512, 768)
    out_full = do_g[:, :, :, 16:32].reshape(512, 768)
    d_attend = right_dot(upstream[...], out_full).astype(BF16)
    slope[...] = dot(onehot[...], dna_full)

    def one_tap(i):
        slope[...] += dot(taps[i], conv_g[i].reshape(768, 768))

    loop(4, one_tap)
    pre = slope[...]
    bend = jnp.tanh(math.sqrt(2.0 / math.pi) * (pre + 0.044715 * (pre * pre * pre)))
    share = 0.5 * (1.0 + bend)
    feature = (pre * share).astype(BF16).astype(F32)
    slope[...] = share + pre * (0.5 * (1.0 - bend * bend)) * (
        math.sqrt(2.0 / math.pi) * (1.0 + 3.0 * 0.044715 * (pre * pre))
    )
    scale = lax.rsqrt(jnp.mean(feature * feature, axis=1, keepdims=True) + epsilon)
    inverse[...] = scale
    unit[...] = feature * scale
    wide[...] = dot(unit[...].astype(BF16), choose[...]).astype(BF16)
    for i in range(2):
        projected = dot(wide[...], qkv_g[i].reshape(1024, 768)).astype(BF16)
        for piece in range(6):
            kind, head = divmod(6 * i + piece, 4)
            place = (2, 0, 1)[kind] * 128
            mine[head, :, place : place + 128] = projected[:, 128 * piece : 128 * piece + 128]
    for head in range(H):
        mine[head, :, 384:512] = d_attend[:, 128 * head : 128 * head + 128]

    kv, rest = pl.ds(0, 256), pl.ds(256, 256)
    kv_in, rest_in = [], {}
    for p in across:
        kv_in.append(send(mine.at[p["x"], :, kv], got_kv.at[x], device(p)))
    for p in partners:
        kv_in.append(send(mine.at[p["x"], :, kv], got.at[x, :, kv], device(p)))
    for k, p in zip((1, 2, 3), partners):
        rest_in[k] = send(mine.at[p["x"], :, rest], got.at[x, :, rest], device(p))
    got[x] = mine[x]
    wide_t[...] = wide[...].T
    d_kv[...] = jnp.zeros_like(d_kv)
    arrive(kv_in)
    keys = jnp.concatenate([got[:, :, 0:128].reshape(512, 128), got_kv[:, :, 0:128].reshape(512, 128)], axis=0)
    values = jnp.concatenate([got[:, :, 128:256].reshape(512, 128), got_kv[:, :, 128:256].reshape(512, 128)], axis=0)
    scaling = 1.0 / math.sqrt(128)
    home = []
    for k in (0, 1, 3, 2):
        if k:
            arrive([rest_in[k]])
        source = lax.rem(x + 4 - k, 4)
        queries = got[source, :, 256:384]
        upward = got[source, :, 384:512]
        scores = right_dot(queries, keys) * scaling
        powers = jnp.exp(scores - jnp.max(scores, axis=1, keepdims=True))
        probs = powers * (1.0 / jnp.sum(powers, axis=1, keepdims=True))
        probs_low = probs.astype(BF16)
        outgo[source, :, 0:128] = dot(probs_low, values).astype(BF16)
        d_probs = right_dot(upward, values)
        inner = jnp.sum(probs * d_probs, axis=1, keepdims=True)
        d_scores = (probs * (d_probs - inner) * scaling).astype(BF16)
        outgo[source, :, 128:256] = dot(d_scores, keys).astype(BF16)
        if k:
            block = pl.ds(0, 256)
            to = device(moved(at, x=4 - k))
            home.append(send(outgo.at[source, :, block], back.at[x, :, block], to))
        d_kv[:, 0:128] += row_dot(d_scores, queries)
        d_kv[:, 128:256] += row_dot(probs_low, upward)
    outgo_kv[...] = d_kv[512:1024].astype(BF16).reshape(4, 128, 256)
    for p in across:
        home.append(send(outgo_kv.at[p["x"]], back_kv.at[x], device(p)))
    outgo[:, :, 256:512] = d_kv[0:512].astype(BF16).reshape(4, 128, 256)
    for p in partners:
        block = pl.ds(256, 256)
        home.append(send(outgo.at[p["x"], :, block], back.at[x, :, block], device(p)))
    back[x] = outgo[x]
    arrive(home)
    for head in range(H):
        columns = slice(128 * head, 128 * head + 128)
        attended[:, columns] = back[head, :, 0:128]
        d_proj[:, columns] = back[head, :, 128:256]
        for kind in range(2):
            total = back[head, :, 256 + 128 * kind : 384 + 128 * kind].astype(F32) + back_kv[
                head, :, 128 * kind : 128 * kind + 128
            ].astype(F32)
            start = 512 * (kind + 1) + 128 * head
            d_proj[:, start : start + 128] = total.astype(BF16)

    for i in range(2):
        qkv_p[i] = dot(wide_t[...], d_proj[:, 768 * i : 768 * i + 768]).astype(BF16).reshape(4, 4, 2, 32, 768)
    core_c = {}
    for k, columns in ((1, other_half), (0, half)):
        core_c[k] = [send(qkv_p.at[:, :, :, 1 - c, :, columns], qkv_r.at[:, :, :, :, columns], sibling)]
    d_wide = right_dot(d_proj[:, 0:768], qkv_g[0].reshape(1024, 768)) + right_dot(
        d_proj[:, 768:1536], qkv_g[1].reshape(1024, 768)
    )

    def sum_c(columns):
        def one(i):
            for part in range(2):
                qkv_p[part, i, :, c, :, columns] = add(
                    qkv_p, qkv_p[part, i, :, c, :, columns], qkv_r[part, i, :, :, columns]
                )

        loop(4, one)

    arrive(core_c[1])
    sum_c(other_half)
    c1 = [send(qkv_p.at[:, :, :, c, :, other_half], rc1, near)]
    high = d_wide.astype(BF16)
    low = (d_wide - high.astype(F32)).astype(BF16)
    d_normed = right_dot(high, choose[...]) + right_dot(low, choose[...])
    d_feature = upstream[...].astype(F32) + inverse[...] * (
        d_normed - unit[...] * jnp.mean(d_normed * unit[...], axis=1, keepdims=True)
    )
    d_pre = (d_feature * slope[...]).astype(BF16)

    def one_conv(i):
        conv_p[i] = dot(taps_t[i], d_pre).astype(BF16).reshape(4, 2, 96, 768)

    loop(4, one_conv)
    do_p[:, :, :, 0:16] = dot(onehot_t[...], d_pre).astype(BF16).reshape(4, 4, 2, 16, 768)
    do_p[:, :, :, 16:32] = row_dot(attended[...], upstream[...]).astype(BF16).reshape(4, 4, 2, 16, 768)
    order = (1, 2, 3, 0)
    xs = {k: lax.rem(x + k, 4) for k in order}
    ys = {k: lax.rem(y + k, 4) for k in order}
    zs = {k: lax.rem(zh + k, 4) for k in order}
    core_a, core_b = {}, {}
    for k in order:
        core_a[k] = [send(conv_p.at[:, :, 1 - c, rows16(xs[k])], conv_r.at[:, :, rows16(xs[k])], sibling)]
        core_b[k] = [
            send(conv_p.at[:, ys[k], 1 - c, tail], conv_r.at[:, ys[k], tail], sibling),
            send(do_p.at[:, ys[k], 1 - c], do_r.at[:, ys[k]], sibling),
        ]
    arrive(core_c[0])
    sum_c(half)
    a1, b1 = {}, {}
    for k in order:
        arrive(core_a[k])
        rows = rows16(xs[k])

        def sum_a(i, rows=rows):
            conv_p[i, :, c, rows] = add(conv_p, conv_p[i, :, c, rows], conv_r[i, :, rows])

        loop(4, sum_a)
        if k:
            a1[k] = send(conv_p.at[:, :, c, rows], ra1.at[k - 1], device(moved(at, x=k)))
        arrive(core_b[k])
        ky = ys[k]

        def sum_b(i, ky=ky):
            conv_p[i, ky, c, 64:96] = add(conv_p, conv_p[i, ky, c, 64:96], conv_r[i, ky, 64:96])
            do_p[i, ky, c] = add(do_p, do_p[i, ky, c], do_r[i, ky])

        loop(4, sum_b)
        if k:
            to = device(moved(at, y=k))
            b1[k] = [
                send(conv_p.at[:, ky, c, tail], rb1.at[k - 1, :, pl.ds(0, 32)], to),
                send(do_p.at[:, ky, c], rb1.at[k - 1, :, pl.ds(32, 32)], to),
            ]

    arrive(c1)

    def first_c(i):
        for part in range(2):
            sc1[part, i] = add(sc1, qkv_p[part, i, :, c, :, half], rc1[part, i])

    loop(4, first_c)
    c2 = [
        send(sc1.at[xs[k] // 2, :, :, rows16(lax.rem(xs[k], 2))], rc2.at[k - 1], device(moved(at, x=k)))
        for k in (1, 2, 3)
    ]

    def tap_grad(i):
        return right_dot(d_pre, conv_g[i].reshape(768, 768))

    shift[8:136] = tap_grad(3)
    rim_out[0] = shift[128:136]
    rims = [send(rim_out.at[0], rim_before, ahead)]
    inner_rows = tap_grad(0)
    rim_out[1] = inner_rows[0:8]
    rims.append(send(rim_out.at[1], rim_after, behind))
    even = tap_grad(1)
    odd = tap_grad(2)
    arrive(rims)
    shift[0:8] = jnp.where(sq > 0, rim_before[...], 0.0)
    seq_o[:, 0:768] = (even + shift[7:135]).astype(BF16)
    shift[0:128] = inner_rows
    shift[128:136] = jnp.where(sq < 7, rim_after[...], 0.0)
    seq_o[:, 768:1536] = (odd + shift[1:129]).astype(BF16)

    arrive(a1.values())

    def first_a(i):
        sa1[i] = add(sa1, conv_p[i, :, c, rows16(x)], ra1[0, i], ra1[1, i], ra1[2, i])

    loop(4, first_a)
    a2 = [send(sa1.at[:, ys[k]], ra2.at[k - 1], device(moved(at, y=k))) for k in (1, 2, 3)]
    for k in (1, 2, 3):
        arrive(b1[k])

    def first_b(i):
        sb1[i, 0:32] = add(sb1, conv_p[i, y, c, 64:96], rb1[0, i, 0:32], rb1[1, i, 0:32], rb1[2, i, 0:32])
        sb1[i, 32:64] = add(sb1, do_p[i, y, c], rb1[0, i, 32:64], rb1[1, i, 32:64], rb1[2, i, 32:64])

    loop(4, first_b)
    b2 = [send(sb1.at[:, rows16(xs[k])], rb2.at[k - 1], device(moved(at, x=k))) for k in (1, 2, 3)]

    arrive(c2)

    def second_c(i):
        own = sc1[x // 2, i, :, rows16(lax.rem(x, 2))]
        sc2[i] = add(sc2, own, rc2[0, i], rc2[1, i], rc2[2, i])

    loop(4, second_c)
    c3 = [send(sc2.at[:, ys[k]], rc3.at[k - 1], device(moved(at, y=k))) for k in (1, 2, 3)]
    arrive(a2)

    def second_a(i):
        sa2[i] = add(sa2, sa1[i, y], ra2[0, i], ra2[1, i], ra2[2, i])

    loop(4, second_a)
    a3 = [send(sa2.at[zs[k]], ra3.at[k - 1], device(moved(at, zh=k))) for k in (1, 2, 3)]
    arrive(b2)

    def second_b(i):
        sb2[i] = add(sb2, sb1[i, rows16(x)], rb2[0, i], rb2[1, i], rb2[2, i])

    loop(4, second_b)
    b3 = [send(sb2.at[zs[k]], rb3.at[k - 1], device(moved(at, zh=k))) for k in (1, 2, 3)]

    arrive(c3)

    def third_c(i):
        sc3[i] = add(sc3, sc2[i, y], rc3[0, i], rc3[1, i], rc3[2, i])

    loop(4, third_c)
    c4 = [send(sc3.at[zs[k]], rc4.at[k - 1], device(moved(at, zh=k))) for k in (1, 2, 3)]
    arrive(a3)
    sa3[...] = add(sa3, sa2[zh], ra3[0], ra3[1], ra3[2])
    a4 = send(sa3, ra4, near)
    arrive(b3)
    sb3[...] = add(sb3, sb2[zh], rb3[0], rb3[1], rb3[2])
    b4 = send(sb3, rb4, near)

    arrive(c4)
    final[x, 2, :, half] = add(final, sc3[zh], rc4[0], rc4[1], rc4[2])
    block = final.at[x, 2, :, half]
    c5 = send(block, block, near)
    arrive([a4])
    final[x, 0] = add(final, sa3[...], ra4[...])
    arrive([b4])
    final[x, 1] = add(final, sb3[...], rb4[...])
    block = final.at[x, pl.ds(0, 2)]
    spread = [send(block, block, device(moved(at, x=k))) for k in (1, 2, 3)]
    arrive([c5])
    spread += [send(final.at[x, 2], final.at[x, 2], device(moved(at, x=k))) for k in (1, 2, 3)]
    arrive(spread)
    for q in range(4):
        conv_o[16 * q : 16 * q + 16] = final[q, 0].astype(F32)
    conv_o[64:80] = final[0, 1].astype(F32)
    conv_o[80:96] = final[1, 1].astype(F32)
    dna_o[...] = final[2, 1].astype(F32)
    out_o[...] = final[3, 1].astype(F32)
    qkv_o[0:16, 0:768] = final[0, 2].astype(F32)
    qkv_o[16:24, 0:768] = final[1, 2].astype(F32)[0:8]
    qkv_o[0:16, 768:1536] = final[2, 2].astype(F32)
    qkv_o[16:24, 768:1536] = final[3, 2].astype(F32)[0:8]
    send.finish()


def layer(conv_s, do_s, qkv_s, pairs, letters, upstream):
    vmem = pl.BlockSpec(memory_space=pltpu.VMEM)
    low = [
        (4, 4, 2, 96, 768), (4, 4, 2, 32, 768), (2, 4, 4, 2, 32, 768), (16, 768), (16, 768),
        (4, 128, 768), (4, 768, 128), (128, 512), (512, 128), (768, 1024), (128, 1024), (1024, 128),
    ]
    wide = [(128, 768), (128, 768), (128, 1)]
    low_2 = [(128, 1536), (128, 512)]
    wide_2 = [(136, 768)]
    low_3 = [(4, 128, 512), (4, 128, 512), (4, 128, 256), (4, 128, 512), (4, 128, 256), (4, 128, 512), (4, 128, 256)]
    wide_3 = [(1024, 256)]
    low_4 = [
        (4, 4, 2, 96, 768), (4, 4, 2, 32, 768), (2, 4, 4, 2, 32, 768), (4, 4, 96, 768), (4, 4, 32, 768), (2, 4, 4, 32, 768),
        (3, 4, 4, 16, 768), (3, 4, 16, 768), (3, 16, 768), (16, 768), (4, 4, 16, 768), (4, 16, 768), (16, 768),
        (3, 4, 64, 768), (3, 4, 16, 768), (3, 16, 768), (16, 768), (4, 64, 768), (4, 16, 768), (16, 768),
        (2, 4, 4, 32, 384), (3, 4, 4, 16, 384), (3, 4, 16, 384), (3, 16, 384),
        (2, 4, 4, 32, 384), (4, 4, 16, 384), (4, 16, 384),
        (4, 3, 16, 768),
    ]
    wide_4 = [(2, 8, 768), (8, 768), (8, 768)]
    scratch = []
    for shapes, kind in (
        (low, BF16), (wide, F32), (low_2, BF16), (wide_2, F32), (low_3, BF16), (wide_3, F32), (low_4, BF16), (wide_4, F32),
    ):
        scratch += [pltpu.VMEM(shape, kind) for shape in shapes]
    return pl.pallas_call(
        layer_kernel,
        name="layer",
        out_shape=(
            jax.ShapeDtypeStruct((128, 1536), BF16),
            jax.ShapeDtypeStruct((96, 768), F32),
            jax.ShapeDtypeStruct((16, 768), F32),
            jax.ShapeDtypeStruct((16, 768), F32),
            jax.ShapeDtypeStruct((24, 1536), F32),
        ),
        in_specs=[vmem] * 6,
        out_specs=(vmem,) * 5,
        scratch_shapes=scratch + [pltpu.SemaphoreType.DMA((160,)), pltpu.SemaphoreType.DMA((160,))],
        compiler_params=pltpu.CompilerParams(
            collective_id=1, has_side_effects=True, vmem_limit_bytes=60 * 2**20
        ),
    )(conv_s, do_s, qkv_s, pairs, letters, upstream)


def per_device(seq_in, bases, conv_weight, dna_weight, qkv_weight, out_weight, cotangent):
    qkv_parts = jnp.pad(
        jnp.stack([qkv_weight[:, :768], qkv_weight[:, 768:]]), ((0, 0), (0, 8), (0, 0))
    )
    seq_grad, conv_grad, dna_grad, out_grad, qkv_grad = layer(
        conv_weight,
        jnp.concatenate([dna_weight, out_weight], axis=0),
        qkv_parts,
        seq_in[0].reshape(128, 1536),
        bases[0].reshape(128, BIN),
        cotangent[0],
    )
    return (seq_grad.reshape(1, 256, 768), conv_grad, dna_grad, qkv_grad, out_grad)


def solution(mesh):
    in_specs = (
        P("dp", "seq", None),
        P("dp", "seq"),
        P("dp", None),
        P("dp", None),
        P("dp", None),
        P("dp", None),
        P("dp", "seq", None),
    )
    out_specs = (P("dp", "seq", None), P("dp", None), P("dp", None), P("dp", None), P("dp", None))
    return jax.shard_map(
        per_device, mesh=mesh, in_specs=in_specs, out_specs=out_specs, check_vma=False
    )
```

```python
import math

import jax
import jax.numpy as jnp
from jax import lax
from jax.experimental import pallas as pl
from jax.experimental.pallas import tpu as pltpu
from jax.sharding import PartitionSpec as P

H = 4
BIN = 128
BF16 = jnp.bfloat16
F32 = jnp.float32
MESH = pl.DeviceIdType.MESH
epsilon = 1e-06

SIZES = {"zh": 4, "y": 4, "c": 2, "zl": 2, "x": 4}
PEERS = [(a, k) for a in ("zh", "y", "x") for k in (1, 2, 3)] + [("zl", 1), ("c", 1)]


def here():
    dp = lax.axis_index("dp")
    sq = lax.axis_index("seq")
    return {"zh": dp // 8, "y": lax.rem(dp // 2, 4), "c": lax.rem(dp, 2), "zl": sq // 4, "x": lax.rem(sq, 4)}


def moved(at, **steps):
    to = dict(at)
    for axis, step in steps.items():
        to[axis] = lax.rem(at[axis] + step, SIZES[axis])
    return to


def device(at):
    return (at["zh"] * 8 + at["y"] * 2 + at["c"], at["zl"] * 4 + at["x"])


class Sender:
    def __init__(self, send_sems, recv_sems):
        self.send_sems, self.recv_sems, self.used, self.copies = send_sems, recv_sems, 0, []

    def __call__(self, src, dst, to):
        copy = pltpu.make_async_remote_copy(
            src_ref=src,
            dst_ref=dst,
            send_sem=self.send_sems.at[self.used],
            recv_sem=self.recv_sems.at[self.used],
            device_id=to,
            device_id_type=MESH,
        )
        copy.start()
        self.used += 1
        self.copies.append(copy)
        return copy

    def finish(self):
        for copy in self.copies:
            copy.wait_send()


def arrive(copies):
    for copy in copies:
        copy.wait_recv()


def rows16(index, base=0):
    return pl.ds(pl.multiple_of(index * 16 + base, 16), 16)


def half_columns(index):
    return pl.ds(pl.multiple_of(index * 384, 128), 384)


def right_dot(left, right):
    return lax.dot_general(left, right, (((1,), (1,)), ((), ())), preferred_element_type=F32)


def row_dot(left, right):
    return lax.dot_general(left, right, (((0,), (0,)), ((), ())), preferred_element_type=F32)


def dot(left, right):
    return jnp.dot(left, right, preferred_element_type=F32)


def add(target, *terms):
    total = terms[0].astype(F32)
    for term in terms[1:]:
        total += term.astype(F32)
    return total.astype(target.dtype)


def loop(n, body):
    def step(i, carry):
        body(i)
        return carry

    lax.fori_loop(0, n, step, 0)


class Ring:
    def __init__(self, send, at, axis, region):
        self.send, self.me, self.region = send, at[axis], region
        self.right, self.left = device(moved(at, **{axis: 1})), device(moved(at, **{axis: 3}))

    def at(self, step):
        return lax.rem(self.me + step, 4)

    def go(self, index, part, to):
        return [self.send(ref, ref, to) for ref in self.region(index, part)]

    def start(self):
        self.from_left = self.go(self.me, None, self.right)
        self.from_right = self.go(self.me, None, self.left)

    def left_in(self):
        arrive(self.from_left)
        self.far_left = self.go(self.at(3), 0, self.right)

    def right_in(self):
        arrive(self.from_right)
        self.far_right = self.go(self.at(1), 1, self.left)

    def both_in(self):
        self.left_in()
        self.right_in()

    def far_in(self):
        arrive(self.far_left)
        arrive(self.far_right)


def layer_kernel(
    conv_s, dna_s, qkv_s, out_s, rows_in, letters, upstream,
    seq_o, final,
    conv_g, do_g, qkv_g, qkv_pad, before, after,
    taps, taps_t, onehot, onehot_t, choose, wide, wide_t, d_proj, attended,
    mine, got, got_kv, outgo, outgo_kv, back, back_kv,
    conv_p, do_p, qkv_p, conv_r, do_r, qkv_r,
    fa, na, sa1, ra2, sa2, ra3, sa3, ra4,
    fb, nb, sb1, rb2, sb2, rb3, sb3, rb4,
    fcx, ncx, scx1, rcx2, fcy, ncy, scy1, rcy2, sc2, rc3, sc3, rc4,
    slope, unit, inverse, rows_f, d_kv, rim_out, rim_before, rim_after,
    send_sems, recv_sems,
):
    at = here()
    zh, y, c, zl, x = (at[a] for a in ("zh", "y", "c", "zl", "x"))
    sq = lax.axis_index("seq")
    dp = lax.axis_index("dp")
    behind, ahead = (dp, lax.rem(sq + 7, 8)), (dp, lax.rem(sq + 1, 8))
    sibling = device(moved(at, c=1))
    near = device(moved(at, zl=1))
    partners = [moved(at, x=k) for k in (1, 2, 3)]
    across = [moved(at, x=k, zl=1) for k in range(4)]
    everyone = [device(moved(at, **{a: k})) for a, k in PEERS] + [behind, ahead]
    everyone += [device(p) for p in across[1:]]
    barrier = pltpu.get_barrier_semaphore()
    for one in everyone:
        pl.semaphore_signal(barrier, inc=1, device_id=one, device_id_type=MESH)
    xs = [lax.rem(x + k, 4) for k in range(4)]
    ys = [lax.rem(y + k, 4) for k in range(4)]
    zs = [lax.rem(zh + k, 4) for k in range(4)]

    quarter = rows16(x)
    part, part_rows = x // 2, rows16(lax.rem(x, 2))
    tail, first_half, second_half = pl.ds(64, 32), pl.ds(0, 384), pl.ds(384, 384)
    for i in range(2):
        block = qkv_s[:, 768 * i : 768 * i + 768].astype(F32)
        qkv_pad[i] = jnp.concatenate([block, jnp.zeros((8, 768), F32)], axis=0).astype(BF16)
    conv_g[zh, y, c, quarter] = conv_s[quarter]
    conv_g[zh, y, c, 64:96] = conv_s[64:96]
    do_g[zh, y, c, 0:16] = dna_s[...]
    do_g[zh, y, c, 16:32] = out_s[...]
    qkv_g[part, zh, y, c, part_rows, 0:384] = qkv_pad[part, part_rows, 0:384]
    for i in range(2):
        qkv_g[i, zh, y, c, :, 384:768] = qkv_pad[i, :, 384:768]
    row = lax.broadcasted_iota(jnp.int32, (128, 512), 0)
    column = lax.broadcasted_iota(jnp.int32, (128, 512), 1)
    repeat = (column // 4 == row).astype(F32).astype(BF16)
    repeated = dot(letters[...].astype(F32).astype(BF16), repeat)
    onehot[...] = (repeated == lax.rem(column, 4).astype(F32)).astype(F32).astype(BF16)
    pl.semaphore_wait(barrier, len(everyone))

    send = Sender(send_sems, recv_sems)

    def refs_a(height, step, index, part=None):
        rows = pl.ds(0, 4) if part is None else pl.ds(2 * part, 2)
        rows = rows if height is None else height
        return [
            conv_g.at[rows, step, c, rows16(index)],
            qkv_g.at[index // 2, rows, step, c, rows16(lax.rem(index, 2)), first_half],
        ]

    def refs_b(height, step, part=None):
        if part is None:
            return [
                conv_g.at[height, step, c, tail],
                do_g.at[height, step, c],
                qkv_g.at[:, height, step, c, :, second_half],
            ]
        return [
            conv_g.at[height, step, c, pl.ds(64 + 16 * part, 16)],
            do_g.at[height, step, c, pl.ds(16 * part, 16)],
            qkv_g.at[part, height, step, c, :, second_half],
        ]

    core = []

    def pass_on(refs):
        for ref in refs:
            core.append(send(ref, ref, sibling))

    def pass_a(step):
        pass_on([conv_g.at[:, step, c, pl.ds(0, 64)], qkv_g.at[:, :, step, c, :, first_half]])

    def pass_b(height):
        pass_on([conv_g.at[height, :, c, tail], do_g.at[height, :, c], qkv_g.at[:, height, :, c, :, second_half]])

    a1, a2 = [], []
    for k in (1, 3, 2):
        a1 += [send(ref, ref, device(moved(at, zh=k))) for ref in refs_a(zh, y, x)]
    halo = [
        send(rows_in.at[pl.ds(240, 16)], before, ahead),
        send(rows_in.at[pl.ds(0, 16)], after, behind),
    ]
    ring_z = Ring(send, at, "zh", lambda index, part: refs_b(index, y, part))
    rings_y = [Ring(send, at, "y", lambda index, part, v=zs[k]: refs_b(v, index, part)) for k in range(4)]
    rings_x = [Ring(send, at, "x", lambda index, part, v=ys[k]: refs_a(None, v, index, part)) for k in range(4)]
    ring_z.start()
    rings_y[0].start()
    arrive(a1)
    rings_x[0].start()
    for k in (1, 3, 2):
        a2.append([send(ref, ref, device(moved(at, y=k))) for ref in refs_a(None, y, x)])
    ring_z.left_in()
    rings_y[3].start()
    ring_z.right_in()
    rings_y[1].start()
    rings_y[0].both_in()
    rings_x[0].both_in()
    arrive(a2[0])
    rings_x[3].start()
    arrive(a2[1])
    rings_x[1].start()
    ring_z.far_in()
    rings_y[2].start()
    rings_y[3].both_in()
    rings_y[1].both_in()
    arrive(a2[2])
    rings_x[2].start()
    rings_y[0].far_in()
    pass_b(zs[0])
    rings_x[0].far_in()
    pass_a(ys[0])
    rings_x[3].both_in()
    rings_x[1].both_in()
    rings_y[2].both_in()
    rings_x[2].both_in()

    arrive(halo)
    for j in range(6):
        lanes = slice(128 * j, 128 * j + 128)
        rows_f[j, 8:264] = rows_in[:, lanes].astype(F32)
        rows_f[j, 0:8] = jnp.where(sq > 0, before[:, lanes].astype(F32)[8:16], 0.0)
        rows_f[j, 264:272] = jnp.where(sq < 7, after[:, lanes].astype(F32)[0:8], 0.0)
        for i in range(4):
            taps[i, :, lanes] = rows_f[j, pl.ds(7 + i, 128, stride=2)].astype(BF16)

    rings_y[3].far_in()
    pass_b(zs[3])
    rings_y[1].far_in()
    pass_b(zs[1])
    rings_x[3].far_in()
    pass_a(ys[3])
    rings_x[1].far_in()
    pass_a(ys[1])
    rings_y[2].far_in()
    pass_b(zs[2])
    rings_x[2].far_in()
    pass_a(ys[2])

    def transpose_tap(i):
        taps_t[i] = taps[i].T

    loop(4, transpose_tap)
    onehot_t[...] = onehot[...].T
    row = lax.broadcasted_iota(jnp.int32, (768, 1024), 0)
    column = lax.broadcasted_iota(jnp.int32, (768, 1024), 1)
    inside = lax.rem(column, 32)
    choose[...] = ((column // 32 * 24 + inside == row) & (inside < 24)).astype(F32).astype(BF16)
    arrive(core)

    dna_full = do_g[:, :, :, 0:16].reshape(512, 768)
    out_full = do_g[:, :, :, 16:32].reshape(512, 768)
    d_attend = right_dot(upstream[...], out_full).astype(BF16)
    slope[...] = dot(onehot[...], dna_full)

    def one_tap(i):
        slope[...] += dot(taps[i], conv_g[i].reshape(768, 768))

    loop(4, one_tap)
    pre = slope[...]
    bend = jnp.tanh(math.sqrt(2.0 / math.pi) * (pre + 0.044715 * (pre * pre * pre)))
    share = 0.5 * (1.0 + bend)
    feature = (pre * share).astype(BF16).astype(F32)
    slope[...] = share + pre * (0.5 * (1.0 - bend * bend)) * (
        math.sqrt(2.0 / math.pi) * (1.0 + 3.0 * 0.044715 * (pre * pre))
    )
    scale = lax.rsqrt(jnp.mean(feature * feature, axis=1, keepdims=True) + epsilon)
    inverse[...] = scale
    unit[...] = feature * scale
    wide[...] = dot(unit[...].astype(BF16), choose[...]).astype(BF16)
    for i in range(2):
        projected = dot(wide[...], qkv_g[i].reshape(1024, 768)).astype(BF16)
        for piece in range(6):
            kind, head = divmod(6 * i + piece, 4)
            place = (2, 0, 1)[kind] * 128
            mine[head, :, place : place + 128] = projected[:, 128 * piece : 128 * piece + 128]
    for head in range(H):
        mine[head, :, 384:512] = d_attend[:, 128 * head : 128 * head + 128]

    kv, rest = pl.ds(0, 256), pl.ds(256, 256)
    kv_in, rest_in = [], {}
    for p in across:
        kv_in.append(send(mine.at[p["x"], :, kv], got_kv.at[x], device(p)))
    for p in partners:
        kv_in.append(send(mine.at[p["x"], :, kv], got.at[x, :, kv], device(p)))
    for k, p in zip((1, 2, 3), partners):
        rest_in[k] = send(mine.at[p["x"], :, rest], got.at[x, :, rest], device(p))
    got[x] = mine[x]
    wide_t[...] = wide[...].T
    d_kv[...] = jnp.zeros_like(d_kv)
    arrive(kv_in)
    keys = jnp.concatenate([got[:, :, 0:128].reshape(512, 128), got_kv[:, :, 0:128].reshape(512, 128)], axis=0)
    values = jnp.concatenate([got[:, :, 128:256].reshape(512, 128), got_kv[:, :, 128:256].reshape(512, 128)], axis=0)
    scaling = 1.0 / math.sqrt(128)
    home = []
    for k in (0, 1, 3, 2):
        if k:
            arrive([rest_in[k]])
        source = lax.rem(x + 4 - k, 4)
        queries = got[source, :, 256:384]
        upward = got[source, :, 384:512]
        scores = right_dot(queries, keys) * scaling
        powers = jnp.exp(scores - jnp.max(scores, axis=1, keepdims=True))
        probs = powers * (1.0 / jnp.sum(powers, axis=1, keepdims=True))
        probs_low = probs.astype(BF16)
        outgo[source, :, 0:128] = dot(probs_low, values).astype(BF16)
        d_probs = right_dot(upward, values)
        inner = jnp.sum(probs * d_probs, axis=1, keepdims=True)
        d_scores = (probs * (d_probs - inner) * scaling).astype(BF16)
        outgo[source, :, 128:256] = dot(d_scores, keys).astype(BF16)
        if k:
            block = pl.ds(0, 256)
            to = device(moved(at, x=4 - k))
            home.append(send(outgo.at[source, :, block], back.at[x, :, block], to))
        d_kv[:, 0:128] += row_dot(d_scores, queries)
        d_kv[:, 128:256] += row_dot(probs_low, upward)
    outgo_kv[...] = d_kv[512:1024].astype(BF16).reshape(4, 128, 256)
    for p in across:
        home.append(send(outgo_kv.at[p["x"]], back_kv.at[x], device(p)))
    outgo[:, :, 256:512] = d_kv[0:512].astype(BF16).reshape(4, 128, 256)
    for p in partners:
        block = pl.ds(256, 256)
        home.append(send(outgo.at[p["x"], :, block], back.at[x, :, block], device(p)))
    back[x] = outgo[x]
    arrive(home)
    for head in range(H):
        columns = slice(128 * head, 128 * head + 128)
        attended[:, columns] = back[head, :, 0:128]
        d_proj[:, columns] = back[head, :, 128:256]
        for kind in range(2):
            total = back[head, :, 256 + 128 * kind : 384 + 128 * kind].astype(F32) + back_kv[
                head, :, 128 * kind : 128 * kind + 128
            ].astype(F32)
            start = 512 * (kind + 1) + 128 * head
            d_proj[:, start : start + 128] = total.astype(BF16)

    for i in range(2):
        qkv_p[i] = dot(wide_t[...], d_proj[:, 768 * i : 768 * i + 768]).astype(BF16).reshape(4, 4, 2, 32, 768)

    def rows_of(index):
        return index // 2, rows16(lax.rem(index, 2))

    def chunk_cx(index, parity, target):
        part, rows = rows_of(index)
        if parity is None:
            return [target.at[part, :, :, rows, first_half]]
        return [target.at[part, :, :, parity, rows, first_half]]

    def chunk_cy(index, parity, target):
        if parity is None:
            return [target.at[:, :, index, :, second_half]]
        return [target.at[:, :, index, parity, :, second_half]]

    order = (2, 1, 3, 0)
    core_cx, core_cy, core_a, core_b = {}, {}, {}, {}
    for k in order:
        for got_core, chunk, index in ((core_cx, chunk_cx, xs[k]), (core_cy, chunk_cy, ys[k])):
            got_core[k] = [
                send(src, dst, sibling)
                for src, dst in zip(chunk(index, 1 - c, qkv_p), chunk(index, None, qkv_r))
            ]
    d_wide = right_dot(d_proj[:, 0:768], qkv_g[0].reshape(1024, 768)) + right_dot(
        d_proj[:, 768:1536], qkv_g[1].reshape(1024, 768)
    )

    def sum_cx(k):
        arrive(core_cx[k])
        part, rows = rows_of(xs[k])

        def one(i):
            qkv_p[part, i, :, c, rows, 0:384] = add(
                qkv_p, qkv_p[part, i, :, c, rows, 0:384], qkv_r[part, i, :, rows, 0:384]
            )

        loop(4, one)

    def sum_cy(k):
        arrive(core_cy[k])
        index = ys[k]

        def one(i):
            for part in range(2):
                qkv_p[part, i, index, c, :, 384:768] = add(
                    qkv_p, qkv_p[part, i, index, c, :, 384:768], qkv_r[part, i, index, :, 384:768]
                )

        loop(4, one)

    right_x, left_x = device(moved(at, x=1)), device(moved(at, x=3))
    right_y, left_y = device(moved(at, y=1)), device(moved(at, y=3))
    low, high = pl.ds(0, 2), pl.ds(2, 2)
    sum_cx(2)
    far_part, far_rows = rows_of(xs[2])
    far_cx = [
        send(qkv_p.at[far_part, low, :, c, far_rows, first_half], fcx.at[0], right_x),
        send(qkv_p.at[far_part, high, :, c, far_rows, first_half], fcx.at[1], left_x),
    ]
    sum_cy(2)
    far_cy = [
        send(qkv_p.at[0, :, ys[2], c, :, second_half], fcy.at[0], right_y),
        send(qkv_p.at[1, :, ys[2], c, :, second_half], fcy.at[1], left_y),
    ]
    d_high = d_wide.astype(BF16)
    d_low = (d_wide - d_high.astype(F32)).astype(BF16)
    d_normed = right_dot(d_high, choose[...]) + right_dot(d_low, choose[...])
    d_feature = upstream[...].astype(F32) + inverse[...] * (
        d_normed - unit[...] * jnp.mean(d_normed * unit[...], axis=1, keepdims=True)
    )
    d_pre = (d_feature * slope[...]).astype(BF16)

    near_cx, near_cy = [], []
    for side, k in ((0, 1), (1, 3)):
        sum_cx(k)
        arrive([far_cx[side]])
        near_part, near_rows = rows_of(xs[k])

        def join_cx(i, side=side, near_part=near_part, near_rows=near_rows):
            block = qkv_p[near_part, 2 * side + i, :, c, near_rows, 0:384]
            qkv_p[near_part, 2 * side + i, :, c, near_rows, 0:384] = add(qkv_p, block, fcx[side, i])

        loop(2, join_cx)
        to = (right_x, left_x)[side]
        near_cx.append(send(qkv_p.at[near_part, :, :, c, near_rows, first_half], ncx.at[side], to))
        sum_cy(k)
        arrive([far_cy[side]])

        def join_cy(i, side=side, index=ys[k]):
            block = qkv_p[side, i, index, c, :, 384:768]
            qkv_p[side, i, index, c, :, 384:768] = add(qkv_p, block, fcy[side, i])

        loop(4, join_cy)
        to = (right_y, left_y)[side]
        near_cy.append(send(qkv_p.at[:, :, ys[k], c, :, second_half], ncy.at[side], to))

    def one_conv(i):
        conv_p[i] = dot(taps_t[i], d_pre).astype(BF16).reshape(4, 2, 96, 768)

    loop(4, one_conv)
    do_p[:, :, :, 0:16] = dot(onehot_t[...], d_pre).astype(BF16).reshape(4, 4, 2, 16, 768)
    do_p[:, :, :, 16:32] = row_dot(attended[...], upstream[...]).astype(BF16).reshape(4, 4, 2, 16, 768)
    for k in order:
        core_a[k] = [send(conv_p.at[:, :, 1 - c, rows16(xs[k])], conv_r.at[:, :, rows16(xs[k])], sibling)]
        core_b[k] = [
            send(conv_p.at[:, ys[k], 1 - c, tail], conv_r.at[:, ys[k], tail], sibling),
            send(do_p.at[:, ys[k], 1 - c], do_r.at[:, ys[k]], sibling),
        ]

    def sum_a(k):
        arrive(core_a[k])
        rows = rows16(xs[k])

        def one(i):
            conv_p[i, :, c, rows] = add(conv_p, conv_p[i, :, c, rows], conv_r[i, :, rows])

        loop(4, one)

    def sum_b(k):
        arrive(core_b[k])
        index = ys[k]

        def one(i):
            conv_p[i, index, c, 64:96] = add(conv_p, conv_p[i, index, c, 64:96], conv_r[i, index, 64:96])
            do_p[i, index, c] = add(do_p, do_p[i, index, c], do_r[i, index])

        loop(4, one)

    sum_a(2)
    far_a = [
        send(conv_p.at[low, :, c, rows16(xs[2])], fa.at[0], right_x),
        send(conv_p.at[high, :, c, rows16(xs[2])], fa.at[1], left_x),
    ]
    sum_b(2)
    far_b = []
    for side, heights in ((0, low), (1, high)):
        to = (right_y, left_y)[side]
        far_b.append(
            [
                send(conv_p.at[heights, ys[2], c, tail], fb.at[side, :, pl.ds(0, 32)], to),
                send(do_p.at[heights, ys[2], c], fb.at[side, :, pl.ds(32, 32)], to),
            ]
        )
    near_a, near_b = [], []
    for side, k in ((0, 1), (1, 3)):
        sum_a(k)
        sum_b(k)
        arrive([far_a[side]])

        def join_a(i, side=side, rows=rows16(xs[k])):
            block = conv_p[2 * side + i, :, c, rows]
            conv_p[2 * side + i, :, c, rows] = add(conv_p, block, fa[side, i])

        loop(2, join_a)
        to = (right_x, left_x)[side]
        near_a.append(send(conv_p.at[:, :, c, rows16(xs[k])], na.at[side], to))
        arrive(far_b[side])

        def join_b(i, side=side, index=ys[k]):
            i = 2 * side + i
            conv_p[i, index, c, 64:96] = add(conv_p, conv_p[i, index, c, 64:96], fb[side, i - 2 * side, 0:32])
            do_p[i, index, c] = add(do_p, do_p[i, index, c], fb[side, i - 2 * side, 32:64])

        loop(2, join_b)
        to = (right_y, left_y)[side]
        near_b += [
            send(conv_p.at[:, ys[k], c, tail], nb.at[side, :, pl.ds(0, 32)], to),
            send(do_p.at[:, ys[k], c], nb.at[side, :, pl.ds(32, 32)], to),
        ]

    sum_cx(0)
    arrive(near_cx)

    def first_cx(i):
        scx1[i] = add(scx1, qkv_p[part, i, :, c, part_rows, 0:384], ncx[0, i], ncx[1, i])

    loop(4, first_cx)
    cx2 = [send(scx1.at[:, ys[k]], rcx2.at[k - 1], device(moved(at, y=k))) for k in (1, 2, 3)]
    sum_cy(0)
    arrive(near_cy)

    def first_cy(i):
        for part in range(2):
            scy1[part, i] = add(scy1, qkv_p[part, i, y, c, :, 384:768], ncy[0, part, i], ncy[1, part, i])

    loop(4, first_cy)
    cy2 = []
    for k in (1, 2, 3):
        to_part, to_rows = rows_of(xs[k])
        cy2.append(send(scy1.at[to_part, :, to_rows], rcy2.at[k - 1], device(moved(at, x=k))))
    sum_a(0)
    sum_b(0)

    def tap_grad(i):
        return right_dot(d_pre, conv_g[i].reshape(768, 768))

    rows_f[:, 256:272] = jnp.zeros((6, 16, 128), F32)
    for i in range(4):
        terms = tap_grad(i)
        for j in range(6):
            target = pl.ds(7 + i, 128, stride=2)
            block = terms[:, 128 * j : 128 * j + 128]
            rows_f[j, target] = block if i < 2 else rows_f[j, target] + block
    rim_out[0] = rows_f[:, 264:272]
    rim_out[1] = rows_f[:, 0:8]
    rims = [send(rim_out.at[0], rim_before, ahead), send(rim_out.at[1], rim_after, behind)]

    arrive(cx2)
    arrive(cy2)

    def second_c(i):
        sc2[i, :, 0:384] = add(sc2, scx1[i, y], rcx2[0, i], rcx2[1, i], rcx2[2, i])
        sc2[i, :, 384:768] = add(sc2, scy1[part, i, part_rows], rcy2[0, i], rcy2[1, i], rcy2[2, i])

    loop(4, second_c)
    c3 = [send(sc2.at[zs[k]], rc3.at[k - 1], device(moved(at, zh=k))) for k in (1, 2, 3)]

    arrive(near_a)

    def first_a(i):
        sa1[i] = add(sa1, conv_p[i, :, c, rows16(x)], na[0, i], na[1, i])

    loop(4, first_a)
    a2 = [send(sa1.at[:, ys[k]], ra2.at[k - 1], device(moved(at, y=k))) for k in (1, 2, 3)]
    arrive(near_b)

    def first_b(i):
        sb1[i, 0:32] = add(sb1, conv_p[i, y, c, 64:96], nb[0, i, 0:32], nb[1, i, 0:32])
        sb1[i, 32:64] = add(sb1, do_p[i, y, c], nb[0, i, 32:64], nb[1, i, 32:64])

    loop(4, first_b)
    b2 = [send(sb1.at[:, rows16(xs[k])], rb2.at[k - 1], device(moved(at, x=k))) for k in (1, 2, 3)]
    arrive(rims)
    rows_f[:, 8:9] += jnp.where(sq > 0, rim_before[:, 0:1], 0.0)
    rows_f[:, 263:264] += jnp.where(sq < 7, rim_after[:, 7:8], 0.0)
    for j in range(6):
        seq_o[:, 128 * j : 128 * j + 128] = rows_f[j, 8:264].astype(BF16)
    arrive(c3)
    sc3[...] = add(sc3, sc2[zh], rc3[0], rc3[1], rc3[2])
    c4 = send(sc3, rc4, near)
    arrive(a2)

    def second_a(i):
        sa2[i] = add(sa2, sa1[i, y], ra2[0, i], ra2[1, i], ra2[2, i])

    loop(4, second_a)
    a3 = [send(sa2.at[zs[k]], ra3.at[k - 1], device(moved(at, zh=k))) for k in (1, 2, 3)]
    arrive(b2)

    def second_b(i):
        sb2[i] = add(sb2, sb1[i, rows16(x)], rb2[0, i], rb2[1, i], rb2[2, i])

    loop(4, second_b)
    b3 = [send(sb2.at[zs[k]], rb3.at[k - 1], device(moved(at, zh=k))) for k in (1, 2, 3)]
    arrive([c4])
    final[x, 2] = add(final, sc3[...], rc4[...])
    spread = [send(final.at[x, 2], final.at[x, 2], device(moved(at, x=k))) for k in (1, 2, 3)]

    arrive(a3)
    sa3[...] = add(sa3, sa2[zh], ra3[0], ra3[1], ra3[2])
    a4 = send(sa3, ra4, near)
    arrive(b3)
    sb3[...] = add(sb3, sb2[zh], rb3[0], rb3[1], rb3[2])
    b4 = send(sb3, rb4, near)
    arrive([a4])
    final[x, 0] = add(final, sa3[...], ra4[...])
    arrive([b4])
    final[x, 1] = add(final, sb3[...], rb4[...])
    block = final.at[x, pl.ds(0, 2)]
    spread += [send(block, block, device(moved(at, x=k))) for k in (1, 2, 3)]
    arrive(spread)
    send.finish()


def finish_kernel(seq_i, final, seq_o, conv_o, dna_o, qkv_o, out_o):
    seq_o[0] = seq_i[...]
    for q in range(4):
        conv_o[16 * q : 16 * q + 16] = final[q, 0].astype(F32)
    conv_o[64:80] = final[0, 1].astype(F32)
    conv_o[80:96] = final[1, 1].astype(F32)
    dna_o[...] = final[2, 1].astype(F32)
    out_o[...] = final[3, 1].astype(F32)
    qkv_o[0:16, 0:768] = final[0, 2].astype(F32)
    qkv_o[16:24, 0:768] = final[1, 2].astype(F32)[0:8]
    qkv_o[0:16, 768:1536] = final[2, 2].astype(F32)
    qkv_o[16:24, 768:1536] = final[3, 2].astype(F32)[0:8]


def layer(*operands):
    vmem = pl.BlockSpec(memory_space=pltpu.VMEM)
    low = [
        (4, 4, 2, 96, 768), (4, 4, 2, 32, 768), (2, 4, 4, 2, 32, 768), (2, 32, 768), (16, 768), (16, 768),
        (4, 128, 768), (4, 768, 128), (128, 512), (512, 128), (768, 1024), (128, 1024), (1024, 128), (128, 1536), (128, 512),
        (4, 128, 512), (4, 128, 512), (4, 128, 256), (4, 128, 512), (4, 128, 256), (4, 128, 512), (4, 128, 256),
        (4, 4, 2, 96, 768), (4, 4, 2, 32, 768), (2, 4, 4, 2, 32, 768), (4, 4, 96, 768), (4, 4, 32, 768), (2, 4, 4, 32, 768),
        (2, 2, 4, 16, 768), (2, 4, 4, 16, 768), (4, 4, 16, 768), (3, 4, 16, 768), (4, 16, 768), (3, 16, 768), (16, 768), (16, 768),
        (2, 2, 64, 768), (2, 4, 64, 768), (4, 64, 768), (3, 4, 16, 768), (4, 16, 768), (3, 16, 768), (16, 768), (16, 768),
        (2, 2, 4, 16, 384), (2, 4, 4, 16, 384), (4, 4, 16, 384), (3, 4, 16, 384),
        (2, 4, 32, 384), (2, 2, 4, 32, 384), (2, 4, 32, 384), (3, 4, 16, 384),
        (4, 16, 768), (3, 16, 768), (16, 768), (16, 768),
    ]
    wide = [(128, 768), (128, 768), (128, 1), (6, 272, 128), (1024, 256), (2, 6, 8, 128), (6, 8, 128), (6, 8, 128)]
    seq_i, final = pl.pallas_call(
        layer_kernel,
        name="layer",
        out_shape=(jax.ShapeDtypeStruct((256, 768), BF16), jax.ShapeDtypeStruct((4, 3, 16, 768), BF16)),
        in_specs=[vmem] * 7,
        out_specs=(vmem,) * 2,
        scratch_shapes=[pltpu.VMEM(shape, BF16) for shape in low]
        + [pltpu.VMEM(shape, F32) for shape in wide]
        + [pltpu.SemaphoreType.DMA((240,)), pltpu.SemaphoreType.DMA((240,))],
        compiler_params=pltpu.CompilerParams(
            collective_id=1, has_side_effects=True, vmem_limit_bytes=60 * 2**20
        ),
    )(*operands)
    return pl.pallas_call(
        finish_kernel,
        name="finish",
        out_shape=(
            jax.ShapeDtypeStruct((1, 256, 768), BF16),
            jax.ShapeDtypeStruct((96, 768), F32),
            jax.ShapeDtypeStruct((16, 768), F32),
            jax.ShapeDtypeStruct((24, 1536), F32),
            jax.ShapeDtypeStruct((16, 768), F32),
        ),
        in_specs=[vmem] * 2,
        out_specs=(vmem,) * 5,
    )(seq_i, final)


def per_device(seq_in, bases, conv_weight, dna_weight, qkv_weight, out_weight, cotangent):
    return layer(
        conv_weight, dna_weight, qkv_weight, out_weight, seq_in[0], bases[0].reshape(128, BIN), cotangent[0]
    )


def solution(mesh):
    in_specs = (
        P("dp", "seq", None),
        P("dp", "seq"),
        P("dp", None),
        P("dp", None),
        P("dp", None),
        P("dp", None),
        P("dp", "seq", None),
    )
    out_specs = (P("dp", "seq", None), P("dp", None), P("dp", None), P("dp", None), P("dp", None))
    return jax.shard_map(
        per_device, mesh=mesh, in_specs=in_specs, out_specs=out_specs, check_vma=False
    )
```

```python
import math

import jax
import jax.numpy as jnp
from jax import lax
from jax.experimental import pallas as pl
from jax.experimental.pallas import tpu as pltpu
from jax.sharding import PartitionSpec as P

H = 4
BIN = 128
BF16 = jnp.bfloat16
F32 = jnp.float32
MESH = pl.DeviceIdType.MESH
epsilon = 1e-06

SIZES = {"zh": 4, "y": 4, "c": 2, "zl": 2, "x": 4}
PEERS = [(a, k) for a in ("zh", "y", "x") for k in (1, 2, 3)] + [("zl", 1), ("c", 1)]


def here():
    dp = lax.axis_index("dp")
    sq = lax.axis_index("seq")
    return {"zh": dp // 8, "y": lax.rem(dp // 2, 4), "c": lax.rem(dp, 2), "zl": sq // 4, "x": lax.rem(sq, 4)}


def moved(at, **steps):
    to = dict(at)
    for axis, step in steps.items():
        to[axis] = lax.rem(at[axis] + step, SIZES[axis])
    return to


def device(at):
    return (at["zh"] * 8 + at["y"] * 2 + at["c"], at["zl"] * 4 + at["x"])


class Sender:
    def __init__(self, send_sems, recv_sems):
        self.send_sems, self.recv_sems, self.used, self.copies = send_sems, recv_sems, 0, []

    def __call__(self, src, dst, to):
        copy = pltpu.make_async_remote_copy(
            src_ref=src,
            dst_ref=dst,
            send_sem=self.send_sems.at[self.used],
            recv_sem=self.recv_sems.at[self.used],
            device_id=to,
            device_id_type=MESH,
        )
        copy.start()
        self.used += 1
        self.copies.append(copy)
        return copy

    def finish(self):
        for copy in self.copies:
            copy.wait_send()


def arrive(copies):
    for copy in copies:
        copy.wait_recv()


def rows16(index, base=0):
    return pl.ds(pl.multiple_of(index * 16 + base, 16), 16)


def half_columns(index):
    return pl.ds(pl.multiple_of(index * 384, 128) if not isinstance(index, int) else index * 384, 384)


def right_dot(left, right):
    return lax.dot_general(left, right, (((1,), (1,)), ((), ())), preferred_element_type=F32)


def row_dot(left, right):
    return lax.dot_general(left, right, (((0,), (0,)), ((), ())), preferred_element_type=F32)


def dot(left, right):
    return jnp.dot(left, right, preferred_element_type=F32)


def add(target, *terms):
    total = terms[0].astype(F32)
    for term in terms[1:]:
        total += term.astype(F32)
    return total.astype(target.dtype)


def loop(n, body):
    def step(i, carry):
        body(i)
        return carry

    lax.fori_loop(0, n, step, 0)


class Ring:
    def __init__(self, send, at, axis, region):
        self.send, self.me, self.region = send, at[axis], region
        self.right, self.left = device(moved(at, **{axis: 1})), device(moved(at, **{axis: 3}))

    def at(self, step):
        return lax.rem(self.me + step, 4)

    def go(self, index, part, to):
        return [self.send(ref, ref, to) for ref in self.region(index, part)]

    def start(self):
        self.from_left = self.go(self.me, None, self.right)
        self.from_right = self.go(self.me, None, self.left)

    def left_in(self):
        arrive(self.from_left)
        self.far_left = self.go(self.at(3), 0, self.right)

    def right_in(self):
        arrive(self.from_right)
        self.far_right = self.go(self.at(1), 1, self.left)

    def both_in(self):
        self.left_in()
        self.right_in()

    def far_in(self):
        arrive(self.far_left)
        arrive(self.far_right)


def layer_kernel(
    conv_s, dna_s, qkv_s, out_s, rows_in, letters, upstream,
    seq_o, final, final_x, final_y,
    conv_g, do_g, qx_g, qy_g, before, after,
    taps, taps_t, onehot, onehot_t, choose_x, choose_y, wide_x, wide_y, wide_xt, wide_yt, d_proj, attended,
    mine, got, got_kv, outgo, outgo_kv, back, back_kv,
    conv_p, do_p, qx_p, qy_p, conv_r, do_r, qx_r, qy_r,
    fa, na, sa1, ra2, sa2, ra3, sa3, ra4,
    fb, nb, sb1, rb2, sb2, rb3, sb3, rb4,
    fcx, ncx, scx1, rcx2, scx2, rcx3, scx3, rcx4,
    fcy, ncy, scy1, rcy2, scy2, rcy3, scy3, rcy4,
    slope, unit, inverse, rows_f, d_kv, rim_out, rim_before, rim_after,
    send_sems, recv_sems,
):
    at = here()
    zh, y, c, zl, x = (at[a] for a in ("zh", "y", "c", "zl", "x"))
    sq = lax.axis_index("seq")
    dp = lax.axis_index("dp")
    behind, ahead = (dp, lax.rem(sq + 7, 8)), (dp, lax.rem(sq + 1, 8))
    sibling = device(moved(at, c=1))
    near = device(moved(at, zl=1))
    partners = [moved(at, x=k) for k in (1, 2, 3)]
    across = [moved(at, x=k, zl=1) for k in range(4)]
    everyone = [device(moved(at, **{a: k})) for a, k in PEERS] + [behind, ahead]
    everyone += [device(p) for p in across[1:]]
    barrier = pltpu.get_barrier_semaphore()
    for one in everyone:
        pl.semaphore_signal(barrier, inc=1, device_id=one, device_id_type=MESH)
    xs = [lax.rem(x + k, 4) for k in range(4)]
    ys = [lax.rem(y + k, 4) for k in range(4)]
    zs = [lax.rem(zh + k, 4) for k in range(4)]

    quarter = rows16(x)
    tail = pl.ds(64, 32)

    def corner(index):
        return index // 2, half_columns(lax.rem(index, 2))

    part, part_columns = corner(x)
    conv_g[zh, y, c, quarter] = conv_s[quarter]
    conv_g[zh, y, c, 64:96] = conv_s[64:96]
    do_g[zh, y, c, 0:16] = dna_s[...]
    do_g[zh, y, c, 16:32] = out_s[...]
    qx_g[part, zh, y, c, :, part_columns] = qkv_s[0:16, half_columns(x)]
    last_rows = [qkv_s[:, 768 * i : 768 * i + 768].astype(F32)[16:24] for i in range(2)]
    qy_g[zh, y, c] = jnp.concatenate(last_rows, axis=0).astype(BF16)
    row = lax.broadcasted_iota(jnp.int32, (128, 512), 0)
    column = lax.broadcasted_iota(jnp.int32, (128, 512), 1)
    repeat = (column // 4 == row).astype(F32).astype(BF16)
    repeated = dot(letters[...].astype(F32).astype(BF16), repeat)
    onehot[...] = (repeated == lax.rem(column, 4).astype(F32)).astype(F32).astype(BF16)
    pl.semaphore_wait(barrier, len(everyone))

    send = Sender(send_sems, recv_sems)

    def refs_a(height, step, index, part=None):
        rows = pl.ds(0, 4) if part is None else pl.ds(2 * part, 2)
        rows = rows if height is None else height
        return [
            conv_g.at[rows, step, c, rows16(index)],
            qx_g.at[corner(index)[0], rows, step, c, :, corner(index)[1]],
        ]

    def refs_b(height, step, part=None):
        if part is None:
            return [
                conv_g.at[height, step, c, tail],
                do_g.at[height, step, c],
                qy_g.at[height, step, c],
            ]
        return [
            conv_g.at[height, step, c, pl.ds(64 + 16 * part, 16)],
            do_g.at[height, step, c, pl.ds(16 * part, 16)],
            qy_g.at[height, step, c, :, half_columns(part)],
        ]

    core = []

    def pass_on(refs):
        for ref in refs:
            core.append(send(ref, ref, sibling))

    def pass_a(step):
        pass_on([conv_g.at[:, step, c, pl.ds(0, 64)], qx_g.at[:, :, step, c]])

    def pass_b(height):
        pass_on([conv_g.at[height, :, c, tail], do_g.at[height, :, c], qy_g.at[height, :, c]])

    a1 = []
    for k in (1, 3, 2):
        a1 += [send(ref, ref, device(moved(at, zh=k))) for ref in refs_a(zh, y, x)]
    halo = [
        send(rows_in.at[pl.ds(240, 16)], before, ahead),
        send(rows_in.at[pl.ds(0, 16)], after, behind),
    ]
    ring_z = Ring(send, at, "zh", lambda index, part: refs_b(index, y, part))
    rings_y = [Ring(send, at, "y", lambda index, part, v=zs[k]: refs_b(v, index, part)) for k in range(4)]
    rings_x = [Ring(send, at, "x", lambda index, part, v=ys[k]: refs_a(None, v, index, part)) for k in range(4)]
    ring_a = Ring(send, at, "y", lambda index, part: refs_a(None, index, x, part))
    ring_z.start()
    rings_y[0].start()
    arrive(a1)
    rings_x[0].start()
    ring_a.start()
    ring_z.left_in()
    rings_y[3].start()
    ring_z.right_in()
    rings_y[1].start()
    rings_y[0].both_in()
    ring_a.left_in()
    rings_x[3].start()
    ring_a.right_in()
    rings_x[1].start()
    rings_x[0].both_in()
    ring_z.far_in()
    rings_y[2].start()
    rings_y[3].both_in()
    rings_y[1].both_in()
    ring_a.far_in()
    rings_x[2].start()
    rings_y[0].far_in()
    pass_b(zs[0])
    rings_x[0].far_in()
    pass_a(ys[0])
    rings_x[3].both_in()
    rings_x[1].both_in()
    rings_y[2].both_in()
    rings_x[2].both_in()

    arrive(halo)
    for j in range(6):
        lanes = slice(128 * j, 128 * j + 128)
        rows_f[j, 8:264] = rows_in[:, lanes].astype(F32)
        rows_f[j, 0:8] = jnp.where(sq > 0, before[:, lanes].astype(F32)[8:16], 0.0)
        rows_f[j, 264:272] = jnp.where(sq < 7, after[:, lanes].astype(F32)[0:8], 0.0)
        for i in range(4):
            taps[i, :, lanes] = rows_f[j, pl.ds(7 + i, 128, stride=2)].astype(BF16)

    rings_y[3].far_in()
    pass_b(zs[3])
    rings_y[1].far_in()
    pass_b(zs[1])
    rings_x[3].far_in()
    pass_a(ys[3])
    rings_x[1].far_in()
    pass_a(ys[1])
    rings_y[2].far_in()
    pass_b(zs[2])
    rings_x[2].far_in()
    pass_a(ys[2])

    def transpose_tap(i):
        taps_t[i] = taps[i].T

    loop(4, transpose_tap)
    onehot_t[...] = onehot[...].T
    row = lax.broadcasted_iota(jnp.int32, (768, 512), 0)
    column = lax.broadcasted_iota(jnp.int32, (768, 512), 1)
    first_row = column // 16 * 24
    choose_x[...] = (first_row + lax.rem(column, 16) == row).astype(F32).astype(BF16)
    choose_y[...] = (first_row + 16 + lax.rem(column, 8) == row).astype(F32).astype(BF16)
    arrive(core[:-2])

    dna_full = do_g[:, :, :, 0:16].reshape(512, 768)
    out_full = do_g[:, :, :, 16:32].reshape(512, 768)
    d_attend = right_dot(upstream[...], out_full).astype(BF16)
    slope[...] = dot(onehot[...], dna_full)
    arrive(core[-2:])

    def one_tap(i):
        slope[...] += dot(taps[i], conv_g[i].reshape(768, 768))

    loop(4, one_tap)
    pre = slope[...]
    bend = jnp.tanh(math.sqrt(2.0 / math.pi) * (pre + 0.044715 * (pre * pre * pre)))
    share = 0.5 * (1.0 + bend)
    feature = (pre * share).astype(BF16).astype(F32)
    slope[...] = share + pre * (0.5 * (1.0 - bend * bend)) * (
        math.sqrt(2.0 / math.pi) * (1.0 + 3.0 * 0.044715 * (pre * pre))
    )
    scale = lax.rsqrt(jnp.mean(feature * feature, axis=1, keepdims=True) + epsilon)
    inverse[...] = scale
    unit[...] = feature * scale
    normed = unit[...].astype(BF16)
    wide_x[...] = dot(normed, choose_x[...]).astype(BF16)
    wide_y[...] = dot(normed, choose_y[...]).astype(BF16)
    side_of = lax.rem(lax.broadcasted_iota(jnp.int32, (128, 512), 1), 16) // 8
    for i in range(2):
        own_y = jnp.where(side_of == i, wide_y[...].astype(F32), 0.0).astype(BF16)
        projected = (dot(wide_x[...], qx_g[i].reshape(512, 768)) + dot(own_y, qy_g[...].reshape(512, 768))).astype(BF16)
        for piece in range(6):
            kind, head = divmod(6 * i + piece, 4)
            place = (2, 0, 1)[kind] * 128
            mine[head, :, place : place + 128] = projected[:, 128 * piece : 128 * piece + 128]
    for head in range(H):
        mine[head, :, 384:512] = d_attend[:, 128 * head : 128 * head + 128]

    kv, rest = pl.ds(0, 256), pl.ds(256, 256)
    kv_in, rest_in = [], {}
    for p in across:
        kv_in.append(send(mine.at[p["x"], :, kv], got_kv.at[x], device(p)))
    for p in partners:
        kv_in.append(send(mine.at[p["x"], :, kv], got.at[x, :, kv], device(p)))
    for k, p in zip((1, 2, 3), partners):
        rest_in[k] = send(mine.at[p["x"], :, rest], got.at[x, :, rest], device(p))
    got[x] = mine[x]
    wide_xt[...] = wide_x[...].T
    wide_yt[...] = wide_y[...].T
    d_kv[...] = jnp.zeros_like(d_kv)
    arrive(kv_in)
    keys = jnp.concatenate([got[:, :, 0:128].reshape(512, 128), got_kv[:, :, 0:128].reshape(512, 128)], axis=0)
    values = jnp.concatenate([got[:, :, 128:256].reshape(512, 128), got_kv[:, :, 128:256].reshape(512, 128)], axis=0)
    scaling = 1.0 / math.sqrt(128)
    home = []
    for k in (0, 1, 3, 2):
        if k:
            arrive([rest_in[k]])
        source = lax.rem(x + 4 - k, 4)
        queries = got[source, :, 256:384]
        upward = got[source, :, 384:512]
        scores = right_dot(queries, keys) * scaling
        powers = jnp.exp(scores - jnp.max(scores, axis=1, keepdims=True))
        probs = powers * (1.0 / jnp.sum(powers, axis=1, keepdims=True))
        probs_low = probs.astype(BF16)
        outgo[source, :, 0:128] = dot(probs_low, values).astype(BF16)
        d_probs = right_dot(upward, values)
        inner = jnp.sum(probs * d_probs, axis=1, keepdims=True)
        d_scores = (probs * (d_probs - inner) * scaling).astype(BF16)
        outgo[source, :, 128:256] = dot(d_scores, keys).astype(BF16)
        if k:
            block = pl.ds(0, 256)
            to = device(moved(at, x=4 - k))
            home.append(send(outgo.at[source, :, block], back.at[x, :, block], to))
        d_kv[:, 0:128] += row_dot(d_scores, queries)
        d_kv[:, 128:256] += row_dot(probs_low, upward)
    outgo_kv[...] = d_kv[512:1024].astype(BF16).reshape(4, 128, 256)
    for p in across:
        home.append(send(outgo_kv.at[p["x"]], back_kv.at[x], device(p)))
    outgo[:, :, 256:512] = d_kv[0:512].astype(BF16).reshape(4, 128, 256)
    for p in partners:
        block = pl.ds(256, 256)
        home.append(send(outgo.at[p["x"], :, block], back.at[x, :, block], device(p)))
    back[x] = outgo[x]
    arrive(home)
    for head in range(H):
        columns = slice(128 * head, 128 * head + 128)
        attended[:, columns] = back[head, :, 0:128]
        d_proj[:, columns] = back[head, :, 128:256]
        for kind in range(2):
            total = back[head, :, 256 + 128 * kind : 384 + 128 * kind].astype(F32) + back_kv[
                head, :, 128 * kind : 128 * kind + 128
            ].astype(F32)
            start = 512 * (kind + 1) + 128 * head
            d_proj[:, start : start + 128] = total.astype(BF16)

    d_halves = [d_proj[:, 0:768], d_proj[:, 768:1536]]
    for i in range(2):
        qx_p[i] = dot(wide_xt[...], d_halves[i]).astype(BF16).reshape(4, 4, 2, 16, 768)
    row_side = lax.rem(lax.broadcasted_iota(jnp.int32, (512, 768), 0), 16)
    both = [dot(wide_yt[...], d_half) for d_half in d_halves]
    qy_p[...] = jnp.where(row_side < 8, both[0], both[1]).astype(BF16).reshape(4, 4, 2, 16, 768)

    order = (2, 1, 3, 0)
    core_cx, core_cy, core_a, core_b = {}, {}, {}, {}
    for k in order:
        to_part, to_columns = corner(xs[k])
        core_cx[k] = send(
            qx_p.at[to_part, :, :, 1 - c, :, to_columns], qx_r.at[to_part, :, :, :, to_columns], sibling
        )
        core_cy[k] = send(qy_p.at[:, ys[k], 1 - c], qy_r.at[:, ys[k]], sibling)
    d_x = sum(right_dot(d_halves[i], qx_g[i].reshape(512, 768)) for i in range(2))
    both = [right_dot(d_half, qy_g[...].reshape(512, 768)) for d_half in d_halves]
    d_y = jnp.where(side_of == 0, both[0], both[1])

    def sum_cx(k):
        arrive([core_cx[k]])
        own_part, own_columns = corner(xs[k])

        def one(i):
            qx_p[own_part, i, :, c, :, own_columns] = add(
                qx_p, qx_p[own_part, i, :, c, :, own_columns], qx_r[own_part, i, :, :, own_columns]
            )

        loop(4, one)

    def sum_cy(k):
        arrive([core_cy[k]])
        qy_p[:, ys[k], c] = add(qy_p, qy_p[:, ys[k], c], qy_r[:, ys[k]])

    right_x, left_x = device(moved(at, x=1)), device(moved(at, x=3))
    right_y, left_y = device(moved(at, y=1)), device(moved(at, y=3))
    low, high = pl.ds(0, 2), pl.ds(2, 2)
    sum_cx(2)
    far_part, far_columns = corner(xs[2])
    far_cx = [
        send(qx_p.at[far_part, low, :, c, :, far_columns], fcx.at[0], right_x),
        send(qx_p.at[far_part, high, :, c, :, far_columns], fcx.at[1], left_x),
    ]
    sum_cy(2)
    far_cy = [
        send(qy_p.at[low, ys[2], c], fcy.at[0], right_y),
        send(qy_p.at[high, ys[2], c], fcy.at[1], left_y),
    ]
    d_normed = 0.0
    for terms, choose in ((d_x, choose_x), (d_y, choose_y)):
        d_high = terms.astype(BF16)
        d_low = (terms - d_high.astype(F32)).astype(BF16)
        d_normed += right_dot(d_high, choose[...]) + right_dot(d_low, choose[...])
    d_feature = upstream[...].astype(F32) + inverse[...] * (
        d_normed - unit[...] * jnp.mean(d_normed * unit[...], axis=1, keepdims=True)
    )
    d_pre = (d_feature * slope[...]).astype(BF16)

    def one_conv(i):
        conv_p[i] = dot(taps_t[i], d_pre).astype(BF16).reshape(4, 2, 96, 768)

    loop(4, one_conv)
    do_p[:, :, :, 0:16] = dot(onehot_t[...], d_pre).astype(BF16).reshape(4, 4, 2, 16, 768)
    do_p[:, :, :, 16:32] = row_dot(attended[...], upstream[...]).astype(BF16).reshape(4, 4, 2, 16, 768)
    for k in order:
        core_a[k] = [send(conv_p.at[:, :, 1 - c, rows16(xs[k])], conv_r.at[:, :, rows16(xs[k])], sibling)]
        core_b[k] = [
            send(conv_p.at[:, ys[k], 1 - c, tail], conv_r.at[:, ys[k], tail], sibling),
            send(do_p.at[:, ys[k], 1 - c], do_r.at[:, ys[k]], sibling),
        ]

    def sum_a(k):
        arrive(core_a[k])
        rows = rows16(xs[k])

        def one(i):
            conv_p[i, :, c, rows] = add(conv_p, conv_p[i, :, c, rows], conv_r[i, :, rows])

        loop(4, one)

    def sum_b(k):
        arrive(core_b[k])
        index = ys[k]

        def one(i):
            conv_p[i, index, c, 64:96] = add(conv_p, conv_p[i, index, c, 64:96], conv_r[i, index, 64:96])
            do_p[i, index, c] = add(do_p, do_p[i, index, c], do_r[i, index])

        loop(4, one)

    near_cx, near_cy = [], []
    for side, k in ((0, 1), (1, 3)):
        sum_cx(k)
        arrive([far_cx[side]])
        near_part, near_columns = corner(xs[k])

        def join_cx(i, side=side, near_part=near_part, near_columns=near_columns):
            block = qx_p[near_part, 2 * side + i, :, c, :, near_columns]
            qx_p[near_part, 2 * side + i, :, c, :, near_columns] = add(qx_p, block, fcx[side, i])

        loop(2, join_cx)
        to = (right_x, left_x)[side]
        near_cx.append(send(qx_p.at[near_part, :, :, c, :, near_columns], ncx.at[side], to))
        sum_cy(k)
        arrive([far_cy[side]])
        half = slice(2 * side, 2 * side + 2)
        qy_p[half, ys[k], c] = add(qy_p, qy_p[half, ys[k], c], fcy[side])
        to = (right_y, left_y)[side]
        near_cy.append(send(qy_p.at[:, ys[k], c], ncy.at[side], to))

    sum_a(2)
    far_a = [
        send(conv_p.at[low, :, c, rows16(xs[2])], fa.at[0], right_x),
        send(conv_p.at[high, :, c, rows16(xs[2])], fa.at[1], left_x),
    ]
    sum_b(2)
    far_b = []
    for side, heights in ((0, low), (1, high)):
        to = (right_y, left_y)[side]
        far_b.append(
            [
                send(conv_p.at[heights, ys[2], c, tail], fb.at[side, :, pl.ds(0, 32)], to),
                send(do_p.at[heights, ys[2], c], fb.at[side, :, pl.ds(32, 32)], to),
            ]
        )
    near_a, near_b = [], []
    for side, k in ((0, 1), (1, 3)):
        sum_a(k)
        sum_b(k)
        arrive([far_a[side]])

        def join_a(i, side=side, rows=rows16(xs[k])):
            block = conv_p[2 * side + i, :, c, rows]
            conv_p[2 * side + i, :, c, rows] = add(conv_p, block, fa[side, i])

        loop(2, join_a)
        to = (right_x, left_x)[side]
        near_a.append(send(conv_p.at[:, :, c, rows16(xs[k])], na.at[side], to))
        arrive(far_b[side])

        def join_b(i, side=side, index=ys[k]):
            i = 2 * side + i
            conv_p[i, index, c, 64:96] = add(conv_p, conv_p[i, index, c, 64:96], fb[side, i - 2 * side, 0:32])
            do_p[i, index, c] = add(do_p, do_p[i, index, c], fb[side, i - 2 * side, 32:64])

        loop(2, join_b)
        to = (right_y, left_y)[side]
        near_b += [
            send(conv_p.at[:, ys[k], c, tail], nb.at[side, :, pl.ds(0, 32)], to),
            send(do_p.at[:, ys[k], c], nb.at[side, :, pl.ds(32, 32)], to),
        ]

    sum_cx(0)
    arrive(near_cx)

    def first_cx(i):
        scx1[i] = add(scx1, qx_p[part, i, :, c, :, part_columns], ncx[0, i], ncx[1, i])

    loop(4, first_cx)
    cx2 = [send(scx1.at[:, ys[k]], rcx2.at[k - 1], device(moved(at, y=k))) for k in (1, 2, 3)]
    sum_cy(0)
    arrive(near_cy)
    scy1[...] = add(scy1, qy_p[:, y, c], ncy[0], ncy[1])
    cy2 = [send(scy1.at[zs[k]], rcy2.at[k - 1], device(moved(at, zh=k))) for k in (1, 2, 3)]
    sum_a(0)
    sum_b(0)

    def tap_grad(i):
        return right_dot(d_pre, conv_g[i].reshape(768, 768))

    rows_f[:, 256:272] = jnp.zeros((6, 16, 128), F32)
    for i in range(4):
        terms = tap_grad(i)
        for j in range(6):
            target = pl.ds(7 + i, 128, stride=2)
            block = terms[:, 128 * j : 128 * j + 128]
            rows_f[j, target] = block if i < 2 else rows_f[j, target] + block
    rim_out[0] = rows_f[:, 264:272]
    rim_out[1] = rows_f[:, 0:8]
    rims = [send(rim_out.at[0], rim_before, ahead), send(rim_out.at[1], rim_after, behind)]

    arrive(cx2)

    def second_cx(i):
        scx2[i] = add(scx2, scx1[i, y], rcx2[0, i], rcx2[1, i], rcx2[2, i])

    loop(4, second_cx)
    cx3 = [send(scx2.at[zs[k]], rcx3.at[k - 1], device(moved(at, zh=k))) for k in (1, 2, 3)]
    arrive(cy2)
    scy2[...] = add(scy2, scy1[zh], rcy2[0], rcy2[1], rcy2[2])
    cy3 = send(scy2, rcy3, near)

    arrive(near_a)

    def first_a(i):
        sa1[i] = add(sa1, conv_p[i, :, c, rows16(x)], na[0, i], na[1, i])

    loop(4, first_a)
    a2 = [send(sa1.at[:, ys[k]], ra2.at[k - 1], device(moved(at, y=k))) for k in (1, 2, 3)]
    arrive(near_b)

    def first_b(i):
        sb1[i, 0:32] = add(sb1, conv_p[i, y, c, 64:96], nb[0, i, 0:32], nb[1, i, 0:32])
        sb1[i, 32:64] = add(sb1, do_p[i, y, c], nb[0, i, 32:64], nb[1, i, 32:64])

    loop(4, first_b)
    b2 = [send(sb1.at[:, rows16(xs[k])], rb2.at[k - 1], device(moved(at, x=k))) for k in (1, 2, 3)]
    arrive(rims)
    rows_f[:, 8:9] += jnp.where(sq > 0, rim_before[:, 0:1], 0.0)
    rows_f[:, 263:264] += jnp.where(sq < 7, rim_after[:, 7:8], 0.0)
    for j in range(6):
        seq_o[:, 128 * j : 128 * j + 128] = rows_f[j, 8:264].astype(BF16)
    arrive(cx3)
    scx3[...] = add(scx3, scx2[zh], rcx3[0], rcx3[1], rcx3[2])
    cx4 = send(scx3, rcx4, near)
    arrive([cy3])
    scy3[...] = add(scy3, scy2[...], rcy3[...])
    cy4 = [send(scy3, rcy4.at[k - 1], device(moved(at, x=k))) for k in (1, 2, 3)]
    arrive(a2)

    def second_a(i):
        sa2[i] = add(sa2, sa1[i, y], ra2[0, i], ra2[1, i], ra2[2, i])

    loop(4, second_a)
    a3 = [send(sa2.at[zs[k]], ra3.at[k - 1], device(moved(at, zh=k))) for k in (1, 2, 3)]
    arrive(b2)

    def second_b(i):
        sb2[i] = add(sb2, sb1[i, rows16(x)], rb2[0, i], rb2[1, i], rb2[2, i])

    loop(4, second_b)
    b3 = [send(sb2.at[zs[k]], rb3.at[k - 1], device(moved(at, zh=k))) for k in (1, 2, 3)]
    arrive([cx4])
    final_x[x] = add(final_x, scx3[...], rcx4[...])
    spread = [send(final_x.at[x], final_x.at[x], device(moved(at, x=k))) for k in (1, 2, 3)]
    arrive(cy4)
    final_y[...] = add(final_y, scy3[...], rcy4[0], rcy4[1], rcy4[2])

    arrive(a3)
    sa3[...] = add(sa3, sa2[zh], ra3[0], ra3[1], ra3[2])
    a4 = send(sa3, ra4, near)
    arrive(b3)
    sb3[...] = add(sb3, sb2[zh], rb3[0], rb3[1], rb3[2])
    b4 = send(sb3, rb4, near)
    arrive([a4])
    final[x, 0] = add(final, sa3[...], ra4[...])
    arrive([b4])
    final[x, 1] = add(final, sb3[...], rb4[...])
    spread += [send(final.at[x], final.at[x], device(moved(at, x=k))) for k in (1, 2, 3)]
    arrive(spread)
    send.finish()


def finish_kernel(seq_i, final, final_x, final_y, seq_o, conv_o, dna_o, qkv_o, out_o):
    seq_o[0] = seq_i[...]
    for q in range(4):
        conv_o[16 * q : 16 * q + 16] = final[q, 0].astype(F32)
    conv_o[64:80] = final[0, 1].astype(F32)
    conv_o[80:96] = final[1, 1].astype(F32)
    dna_o[...] = final[2, 1].astype(F32)
    out_o[...] = final[3, 1].astype(F32)
    for q in range(4):
        qkv_o[0:16, 384 * q : 384 * q + 384] = final_x[q].astype(F32)
    last_rows = final_y[...].astype(F32)
    qkv_o[16:24, 0:768] = last_rows[0:8]
    qkv_o[16:24, 768:1536] = last_rows[8:16]


def layer(*operands):
    vmem = pl.BlockSpec(memory_space=pltpu.VMEM)
    low = [
        (4, 4, 2, 96, 768), (4, 4, 2, 32, 768), (2, 4, 4, 2, 16, 768), (4, 4, 2, 16, 768), (16, 768), (16, 768),
        (4, 128, 768), (4, 768, 128), (128, 512), (512, 128), (768, 512), (768, 512),
        (128, 512), (128, 512), (512, 128), (512, 128), (128, 1536), (128, 512),
        (4, 128, 512), (4, 128, 512), (4, 128, 256), (4, 128, 512), (4, 128, 256), (4, 128, 512), (4, 128, 256),
        (4, 4, 2, 96, 768), (4, 4, 2, 32, 768), (2, 4, 4, 2, 16, 768), (4, 4, 2, 16, 768),
        (4, 4, 96, 768), (4, 4, 32, 768), (2, 4, 4, 16, 768), (4, 4, 16, 768),
        (2, 2, 4, 16, 768), (2, 4, 4, 16, 768), (4, 4, 16, 768), (3, 4, 16, 768), (4, 16, 768), (3, 16, 768), (16, 768), (16, 768),
        (2, 2, 64, 768), (2, 4, 64, 768), (4, 64, 768), (3, 4, 16, 768), (4, 16, 768), (3, 16, 768), (16, 768), (16, 768),
        (2, 2, 4, 16, 384), (2, 4, 4, 16, 384), (4, 4, 16, 384), (3, 4, 16, 384), (4, 16, 384), (3, 16, 384), (16, 384), (16, 384),
        (2, 2, 16, 768), (2, 4, 16, 768), (4, 16, 768), (3, 16, 768), (16, 768), (16, 768), (16, 768), (3, 16, 768),
    ]
    wide = [(128, 768), (128, 768), (128, 1), (6, 272, 128), (1024, 256), (2, 6, 8, 128), (6, 8, 128), (6, 8, 128)]
    results = pl.pallas_call(
        layer_kernel,
        name="layer",
        out_shape=tuple(
            jax.ShapeDtypeStruct(shape, BF16)
            for shape in ((256, 768), (4, 2, 16, 768), (4, 16, 384), (16, 768))
        ),
        in_specs=[vmem] * 7,
        out_specs=(vmem,) * 4,
        scratch_shapes=[pltpu.VMEM(shape, BF16) for shape in low]
        + [pltpu.VMEM(shape, F32) for shape in wide]
        + [pltpu.SemaphoreType.DMA((250,)), pltpu.SemaphoreType.DMA((250,))],
        compiler_params=pltpu.CompilerParams(
            collective_id=1, has_side_effects=True, vmem_limit_bytes=60 * 2**20
        ),
    )(*operands)
    return pl.pallas_call(
        finish_kernel,
        name="finish",
        out_shape=(
            jax.ShapeDtypeStruct((1, 256, 768), BF16),
            jax.ShapeDtypeStruct((96, 768), F32),
            jax.ShapeDtypeStruct((16, 768), F32),
            jax.ShapeDtypeStruct((24, 1536), F32),
            jax.ShapeDtypeStruct((16, 768), F32),
        ),
        in_specs=[vmem] * 4,
        out_specs=(vmem,) * 5,
    )(*results)


def per_device(seq_in, bases, conv_weight, dna_weight, qkv_weight, out_weight, cotangent):
    return layer(
        conv_weight, dna_weight, qkv_weight, out_weight, seq_in[0], bases[0].reshape(128, BIN), cotangent[0]
    )


def solution(mesh):
    in_specs = (
        P("dp", "seq", None),
        P("dp", "seq"),
        P("dp", None),
        P("dp", None),
        P("dp", None),
        P("dp", None),
        P("dp", "seq", None),
    )
    out_specs = (P("dp", "seq", None), P("dp", None), P("dp", None), P("dp", None), P("dp", None))
    return jax.shard_map(
        per_device, mesh=mesh, in_specs=in_specs, out_specs=out_specs, check_vma=False
    )
```

```python
import math

import jax
import jax.numpy as jnp
from jax import lax
from jax.experimental import pallas as pl
from jax.experimental.pallas import tpu as pltpu
from jax.sharding import PartitionSpec as P

H = 4
BIN = 128
BF16 = jnp.bfloat16
F32 = jnp.float32
MESH = pl.DeviceIdType.MESH
epsilon = 1e-06

SIZES = {"zh": 4, "y": 4, "c": 2, "zl": 2, "x": 4}
PEERS = [(a, k) for a in ("zh", "y", "x") for k in (1, 2, 3)] + [("zl", 1), ("c", 1)]


def here():
    dp = lax.axis_index("dp")
    sq = lax.axis_index("seq")
    return {"zh": dp // 8, "y": lax.rem(dp // 2, 4), "c": lax.rem(dp, 2), "zl": sq // 4, "x": lax.rem(sq, 4)}


def moved(at, **steps):
    to = dict(at)
    for axis, step in steps.items():
        to[axis] = lax.rem(at[axis] + step, SIZES[axis])
    return to


def device(at):
    return (at["zh"] * 8 + at["y"] * 2 + at["c"], at["zl"] * 4 + at["x"])


class Sender:
    def __init__(self, send_sems, recv_sems):
        self.send_sems, self.recv_sems, self.sent, self.due, self.copies = send_sems, recv_sems, 0, 0, []

    def copy(self, src, dst, to, recv):
        copy = pltpu.make_async_remote_copy(
            src_ref=src,
            dst_ref=dst,
            send_sem=self.send_sems.at[self.sent],
            recv_sem=self.recv_sems.at[recv],
            device_id=to,
            device_id_type=MESH,
        )
        copy.start()
        self.sent += 1
        self.copies.append(copy)
        return copy

    def __call__(self, src, dst, to):
        self.due += 1
        return self.copy(src, dst, to, self.due - 1)

    def group(self, whole, copies):
        self.due += 1
        for src, dst, to in copies:
            self.copy(src, dst, to, self.due - 1)
        return pltpu.make_async_remote_copy(
            src_ref=whole,
            dst_ref=whole,
            send_sem=self.send_sems.at[0],
            recv_sem=self.recv_sems.at[self.due - 1],
            device_id=copies[0][2],
            device_id_type=MESH,
        )

    def finish(self):
        for copy in self.copies:
            copy.wait_send()
        self.sent, self.copies = 0, []


def arrive(copies):
    for copy in copies:
        copy.wait_recv()


def rows16(index, base=0):
    return pl.ds(pl.multiple_of(index * 16 + base, 16), 16)


def half_columns(index):
    return pl.ds(pl.multiple_of(index * 384, 128) if not isinstance(index, int) else index * 384, 384)


def right_dot(left, right):
    return lax.dot_general(left, right, (((1,), (1,)), ((), ())), preferred_element_type=F32)


def row_dot(left, right):
    return lax.dot_general(left, right, (((0,), (0,)), ((), ())), preferred_element_type=F32)


def dot(left, right):
    return jnp.dot(left, right, preferred_element_type=F32)


def add(target, *terms):
    total = terms[0].astype(F32)
    for term in terms[1:]:
        total += term.astype(F32)
    return total.astype(target.dtype)


def loop(n, body):
    def step(i, carry):
        body(i)
        return carry

    lax.fori_loop(0, n, step, 0)


class Ring:
    def __init__(self, send, at, axis, region):
        self.send, self.me, self.region = send, at[axis], region
        self.right, self.left = device(moved(at, **{axis: 1})), device(moved(at, **{axis: 3}))

    def at(self, step):
        return lax.rem(self.me + step, 4)

    def go(self, index, part, to):
        ref = self.region(index, part)
        return [self.send(ref, ref, to)]

    def start(self):
        self.from_left = self.go(self.me, None, self.right)
        self.from_right = self.go(self.me, None, self.left)

    def left_in(self):
        arrive(self.from_left)
        self.far_left = self.go(self.at(3), 0, self.right)

    def right_in(self):
        arrive(self.from_right)
        self.far_right = self.go(self.at(1), 1, self.left)

    def both_in(self):
        self.left_in()
        self.right_in()

    def far_in(self):
        arrive(self.far_left)
        arrive(self.far_right)


def layer_kernel(
    conv_s, dna_s, qkv_s, out_s, rows_in, letters, upstream,
    seq_o, final, final_x, final_y,
    ga, gb, before, after,
    taps, taps_t, onehot, onehot_t, choose_x, choose_y, wide_x, wide_y, wide_xt, wide_yt, d_proj, attended, attended_t,
    mine, got, got_kv, outgo, outgo_kv, back, back_kv, probs_s, scores_s,
    pa_s, pb_s, px_s, py_s, pa, pb, px, py, pa_r, pb_r, px_r, py_r,
    fa, na, sa1, ra2, sa2, ra3, sa3, ra4,
    fb, nb, sb1, rb2, sb2, rb3, sb3, rb4,
    fcx, ncx, scx1, rcx2, scx2, rcx3, scx3, rcx4,
    fcy, ncy, scy1, rcy2, scy2, rcy3, scy3, rcy4,
    slope, unit, inverse, rows_f, rim_out, rim_before, rim_after,
    send_sems, recv_sems,
):
    at = here()
    zh, y, c, zl, x = (at[a] for a in ("zh", "y", "c", "zl", "x"))
    sq = lax.axis_index("seq")
    dp = lax.axis_index("dp")
    behind, ahead = (dp, lax.rem(sq + 7, 8)), (dp, lax.rem(sq + 1, 8))
    sibling = device(moved(at, c=1))
    near = device(moved(at, zl=1))
    partners = [moved(at, x=k) for k in (1, 2, 3)]
    across = [moved(at, x=k, zl=1) for k in range(4)]
    everyone = [device(moved(at, **{a: k})) for a, k in PEERS] + [behind, ahead]
    everyone += [device(p) for p in across[1:]]
    barrier = pltpu.get_barrier_semaphore()
    for one in everyone:
        pl.semaphore_signal(barrier, inc=1, device_id=one, device_id_type=MESH)
    xs = [lax.rem(x + k, 4) for k in range(4)]
    ys = [lax.rem(y + k, 4) for k in range(4)]
    zs = [lax.rem(zh + k, 4) for k in range(4)]

    quarter = rows16(x)
    ga[zh, y, c, x, :, 0:768] = conv_s[quarter]
    ga[zh, y, c, x, :, 768:1152] = qkv_s[0:16, half_columns(x)]
    gb[zh, y, c, 0:32] = conv_s[64:96]
    gb[zh, y, c, 32:48] = dna_s[...]
    gb[zh, y, c, 48:64] = out_s[...]
    last_rows = [qkv_s[:, 768 * i : 768 * i + 768].astype(F32)[16:24] for i in range(2)]
    gb[zh, y, c, 64:80] = jnp.concatenate(last_rows, axis=0).astype(BF16)
    row = lax.broadcasted_iota(jnp.int32, (128, 512), 0)
    column = lax.broadcasted_iota(jnp.int32, (128, 512), 1)
    repeat = (column // 4 == row).astype(F32).astype(BF16)
    repeated = dot(letters[...].astype(F32).astype(BF16), repeat)
    onehot[...] = (repeated == lax.rem(column, 4).astype(F32)).astype(F32).astype(BF16)
    pl.semaphore_wait(barrier, len(everyone))

    send = Sender(send_sems, recv_sems)

    def ref_a(height, step, index, part=None):
        rows = pl.ds(0, 4) if part is None else pl.ds(2 * part, 2)
        return ga.at[rows if height is None else height, step, c, index]

    def ref_b(height, step, part=None):
        return gb.at[height, step, c] if part is None else gb.at[height, step, c, :, half_columns(part)]

    core = []

    def pass_on(ref):
        core.append(send(ref, ref, sibling))

    def pass_a(step):
        pass_on(ga.at[:, step, c])

    def pass_b(height):
        pass_on(gb.at[height, :, c])

    a1 = []
    for k in (1, 3, 2):
        a1.append(send(ref_a(zh, y, x), ref_a(zh, y, x), device(moved(at, zh=k))))
    halo = [
        send(rows_in.at[pl.ds(240, 16)], before, ahead),
        send(rows_in.at[pl.ds(0, 16)], after, behind),
    ]
    ring_z = Ring(send, at, "zh", lambda index, part: ref_b(index, y, part))
    rings_y = [Ring(send, at, "y", lambda index, part, v=zs[k]: ref_b(v, index, part)) for k in range(4)]
    rings_x = [Ring(send, at, "x", lambda index, part, v=ys[k]: ref_a(None, v, index, part)) for k in range(4)]
    ring_a = Ring(send, at, "y", lambda index, part: ref_a(None, index, x, part))
    ring_z.start()
    rings_y[0].start()
    arrive(a1)
    rings_x[0].start()
    ring_a.start()
    ring_z.left_in()
    rings_y[3].start()
    ring_z.right_in()
    rings_y[1].start()
    rings_y[0].both_in()
    ring_a.left_in()
    rings_x[3].start()
    ring_a.right_in()
    rings_x[1].start()
    rings_x[0].both_in()
    ring_z.far_in()
    rings_y[2].start()
    rings_y[3].both_in()
    rings_y[1].both_in()
    ring_a.far_in()
    rings_x[2].start()
    rings_y[0].far_in()
    pass_b(zs[0])
    rings_x[0].far_in()
    pass_a(ys[0])
    rings_x[3].both_in()
    rings_x[1].both_in()
    rings_y[2].both_in()
    rings_x[2].both_in()

    arrive(halo)
    for j in range(6):
        lanes = slice(128 * j, 128 * j + 128)
        rows_f[j, 8:264] = rows_in[:, lanes].astype(F32)
        rows_f[j, 0:8] = jnp.where(sq > 0, before[:, lanes].astype(F32)[8:16], 0.0)
        rows_f[j, 264:272] = jnp.where(sq < 7, after[:, lanes].astype(F32)[0:8], 0.0)
        for i in range(4):
            taps[i, :, lanes] = rows_f[j, pl.ds(7 + i, 128, stride=2)].astype(BF16)

    rings_y[3].far_in()
    pass_b(zs[3])
    rings_y[1].far_in()
    pass_b(zs[1])
    rings_x[3].far_in()
    pass_a(ys[3])
    rings_x[1].far_in()
    pass_a(ys[1])
    rings_y[2].far_in()
    pass_b(zs[2])
    rings_x[2].far_in()
    pass_a(ys[2])

    def transpose_tap(i):
        taps_t[i] = taps[i].T.reshape(4, 2, 96, 128)

    loop(4, transpose_tap)
    onehot_t[...] = onehot[...].T.reshape(4, 4, 2, 16, 128)
    row = lax.broadcasted_iota(jnp.int32, (768, 512), 0)
    column = lax.broadcasted_iota(jnp.int32, (768, 512), 1)
    first_row = column // 16 * 24
    choose_x[...] = (first_row + lax.rem(column, 16) == row).astype(F32).astype(BF16)
    choose_y[...] = (first_row + 16 + lax.rem(column, 8) == row).astype(F32).astype(BF16)
    arrive(core[:-1])

    def conv_full(i):
        first = ga[i, :, :, :, :, 0:768].reshape(4, 2, 64, 768)
        return jnp.concatenate([first, gb[i, :, :, 0:32]], axis=2).reshape(768, 768)

    def qx_full(i):
        return jnp.concatenate(
            [ga[:, :, :, 2 * i + j, :, 768:1152].reshape(512, 384) for j in range(2)], axis=1
        )

    def qy_full():
        return gb[:, :, :, 64:80].reshape(512, 768)

    dna_full = gb[:, :, :, 32:48].reshape(512, 768)
    out_full = gb[:, :, :, 48:64].reshape(512, 768)
    d_attend = right_dot(upstream[...], out_full).astype(BF16)
    slope[...] = dot(onehot[...], dna_full)
    arrive(core[-1:])

    def one_tap(i):
        slope[...] += dot(taps[i], conv_full(i))

    loop(4, one_tap)
    pre = slope[...]
    bend = jnp.tanh(math.sqrt(2.0 / math.pi) * (pre + 0.044715 * (pre * pre * pre)))
    share = 0.5 * (1.0 + bend)
    feature = (pre * share).astype(BF16).astype(F32)
    slope[...] = share + pre * (0.5 * (1.0 - bend * bend)) * (
        math.sqrt(2.0 / math.pi) * (1.0 + 3.0 * 0.044715 * (pre * pre))
    )
    scale = lax.rsqrt(jnp.mean(feature * feature, axis=1, keepdims=True) + epsilon)
    inverse[...] = scale
    unit[...] = feature * scale
    normed = unit[...].astype(BF16)
    wide_x[...] = dot(normed, choose_x[...]).astype(BF16)
    wide_y[...] = dot(normed, choose_y[...]).astype(BF16)
    side_of = lax.rem(lax.broadcasted_iota(jnp.int32, (128, 512), 1), 16) // 8
    for i in range(2):
        own_y = jnp.where(side_of == i, wide_y[...].astype(F32), 0.0).astype(BF16)
        projected = (dot(wide_x[...], qx_full(i)) + dot(own_y, qy_full())).astype(BF16)
        for piece in range(6):
            kind, head = divmod(6 * i + piece, 4)
            place = (2, 0, 1)[kind] * 128
            mine[head, :, place : place + 128] = projected[:, 128 * piece : 128 * piece + 128]
    for head in range(H):
        mine[head, :, 384:512] = d_attend[:, 128 * head : 128 * head + 128]

    kv, rest = pl.ds(0, 256), pl.ds(256, 256)
    kv_in, rest_in = {}, {}
    to_near = [(mine.at[x, :, kv], got_kv.at[x], near)]
    for k, p in zip((1, 2, 3), partners):
        kv_in[k] = send(mine.at[p["x"], :, kv], got.at[x, :, kv], device(p))
    for k, p in zip((1, 2, 3), partners):
        rest_in[k] = send(mine.at[p["x"], :, rest], got.at[x, :, rest], device(p))
    to_near += [(got.at[xs[3], :, kv], got_kv.at[xs[3]], near), (got.at[xs[1], :, kv], got_kv.at[xs[1]], near)]
    to_near += [(got.at[xs[2], :, kv], got_kv.at[xs[2]], near)]
    from_near = send.group(got_kv, to_near[:1])
    for k, copy in zip((1, 3, 2), to_near[1:]):
        arrive([kv_in[k]])
        send.copy(*copy, send.due - 1)
    got[x] = mine[x]
    wide_xt[...] = wide_x[...].T.reshape(4, 4, 2, 16, 128)
    wide_yt[...] = wide_y[...].T.reshape(4, 4, 2, 16, 128)
    arrive([from_near])
    keys = jnp.concatenate([got[:, :, 0:128].reshape(512, 128), got_kv[:, :, 0:128].reshape(512, 128)], axis=0)
    values = jnp.concatenate([got[:, :, 128:256].reshape(512, 128), got_kv[:, :, 128:256].reshape(512, 128)], axis=0)
    scaling = 1.0 / math.sqrt(128)
    home = []
    for k in (0, 1, 3, 2):
        if k:
            arrive([rest_in[k]])
        source = lax.rem(x + 4 - k, 4)
        queries = got[source, :, 256:384]
        upward = got[source, :, 384:512]
        scores = right_dot(queries, keys) * scaling
        powers = jnp.exp(scores - jnp.max(scores, axis=1, keepdims=True))
        probs = powers * (1.0 / jnp.sum(powers, axis=1, keepdims=True))
        probs_low = probs.astype(BF16)
        outgo[source, :, 0:128] = dot(probs_low, values).astype(BF16)
        d_probs = right_dot(upward, values)
        inner = jnp.sum(probs * d_probs, axis=1, keepdims=True)
        d_scores = (probs * (d_probs - inner) * scaling).astype(BF16)
        outgo[source, :, 128:256] = dot(d_scores, keys).astype(BF16)
        if k:
            block = pl.ds(0, 256)
            to = device(moved(at, x=4 - k))
            home.append(send(outgo.at[source, :, block], back.at[x, :, block], to))
        scores_s[source] = d_scores
        probs_s[source] = probs_low
    all_queries = got[:, :, 256:384].reshape(512, 128)
    all_upward = got[:, :, 384:512].reshape(512, 128)

    def d_pair(columns):
        d_keys = row_dot(all_queries, scores_s[:, :, columns].reshape(512, 512)).T
        d_values = row_dot(all_upward, probs_s[:, :, columns].reshape(512, 512)).T
        return jnp.concatenate([d_keys, d_values], axis=1).astype(BF16).reshape(4, 128, 256)

    outgo_kv[...] = d_pair(slice(512, 1024))
    from_across = send.group(back_kv, [(outgo_kv.at[p["x"]], back_kv.at[x], device(p)) for p in across])
    outgo[:, :, 256:512] = d_pair(slice(0, 512))
    for p in partners:
        block = pl.ds(256, 256)
        home.append(send(outgo.at[p["x"], :, block], back.at[x, :, block], device(p)))
    back[x] = outgo[x]
    arrive(home)
    arrive([from_across])
    send.finish()
    for head in range(H):
        columns = slice(128 * head, 128 * head + 128)
        attended[:, columns] = back[head, :, 0:128]
        d_proj[:, columns] = back[head, :, 128:256]
        for kind in range(2):
            total = back[head, :, 256 + 128 * kind : 384 + 128 * kind].astype(F32) + back_kv[
                head, :, 128 * kind : 128 * kind + 128
            ].astype(F32)
            start = 512 * (kind + 1) + 128 * head
            d_proj[:, start : start + 128] = total.astype(BF16)

    attended_t[...] = attended[...].T.reshape(4, 4, 2, 16, 128)
    d_halves = [d_proj[:, 0:768], d_proj[:, 768:1536]]
    row_side = lax.rem(lax.broadcasted_iota(jnp.int32, (256, 768), 0), 16)

    def qkv_grads(parity, to_x, to_y):
        left = wide_xt[:, :, parity].reshape(256, 128)
        for i in range(2):
            block = dot(left, d_halves[i]).astype(BF16)
            for j in range(2):
                to_x[2 * i + j] = block[:, 384 * j : 384 * j + 384].reshape(4, 4, 16, 384)
        left = wide_yt[:, :, parity].reshape(256, 128)
        both = [dot(left, d_half) for d_half in d_halves]
        to_y[...] = jnp.where(row_side < 8, both[0], both[1]).astype(BF16).reshape(4, 4, 16, 768)

    order = (2, 1, 3, 0)
    core_cx, core_cy, core_a, core_b = {}, {}, {}, {}
    qkv_grads(1 - c, px_s, py_s)
    for k in order:
        core_cx[k] = send(px_s.at[xs[k]], px_r.at[xs[k]], sibling)
        core_cy[k] = send(py_s.at[:, ys[k]], py_r.at[:, ys[k]], sibling)
    qkv_grads(c, px, py)
    d_x = sum(right_dot(d_halves[i], qx_full(i)) for i in range(2))
    both = [right_dot(d_half, qy_full()) for d_half in d_halves]
    d_y = jnp.where(side_of == 0, both[0], both[1])

    def sum_cx(k):
        arrive([core_cx[k]])
        px[xs[k]] = add(px, px[xs[k]], px_r[xs[k]])

    def sum_cy(k):
        arrive([core_cy[k]])
        py[:, ys[k]] = add(py, py[:, ys[k]], py_r[:, ys[k]])

    right_x, left_x = device(moved(at, x=1)), device(moved(at, x=3))
    right_y, left_y = device(moved(at, y=1)), device(moved(at, y=3))
    low, high = pl.ds(0, 2), pl.ds(2, 2)
    sides = ((0, 1, right_x, right_y), (1, 3, left_x, left_y))
    sum_cx(2)
    far_cx = [
        send(px.at[xs[2], heights], fcx.at[side], to) for side, heights, to in ((0, low, right_x), (1, high, left_x))
    ]
    sum_cy(2)
    far_cy = [
        send(py.at[heights, ys[2]], fcy.at[side], to) for side, heights, to in ((0, low, right_y), (1, high, left_y))
    ]
    d_normed = 0.0
    for terms, choose in ((d_x, choose_x), (d_y, choose_y)):
        d_high = terms.astype(BF16)
        d_low = (terms - d_high.astype(F32)).astype(BF16)
        d_normed += right_dot(d_high, choose[...]) + right_dot(d_low, choose[...])
    d_feature = upstream[...].astype(F32) + inverse[...] * (
        d_normed - unit[...] * jnp.mean(d_normed * unit[...], axis=1, keepdims=True)
    )
    d_pre = (d_feature * slope[...]).astype(BF16)

    def conv_grads(parity, to_a, to_b):
        def one(i):
            block = dot(taps_t[i, :, parity].reshape(384, 128), d_pre).astype(BF16).reshape(4, 96, 768)
            to_a[i] = block[:, 0:64]
            to_b[i, :, 0:32] = block[:, 64:96]

        loop(4, one)
        left = onehot_t[:, :, parity].reshape(256, 128)
        to_b[:, :, 32:48] = dot(left, d_pre).astype(BF16).reshape(4, 4, 16, 768)
        left = attended_t[:, :, parity].reshape(256, 128)
        to_b[:, :, 48:64] = dot(left, upstream[...]).astype(BF16).reshape(4, 4, 16, 768)

    conv_grads(1 - c, pa_s, pb_s)
    for k in order:
        core_a[k] = send(pa_s.at[:, :, rows16(xs[k])], pa_r.at[:, :, rows16(xs[k])], sibling)
        core_b[k] = send(pb_s.at[:, ys[k]], pb_r.at[:, ys[k]], sibling)
    conv_grads(c, pa, pb)

    def sum_a(k):
        arrive([core_a[k]])
        rows = rows16(xs[k])

        def one(i):
            pa[i, :, rows] = add(pa, pa[i, :, rows], pa_r[i, :, rows])

        loop(4, one)

    def sum_b(k):
        arrive([core_b[k]])

        def one(i):
            pb[i, ys[k]] = add(pb, pb[i, ys[k]], pb_r[i, ys[k]])

        loop(4, one)

    halves = [(h, pl.ds(384 * h, 384), slice(384 * h, 384 * h + 384)) for h in range(2)]
    far_a, far_b = {}, {}
    sum_a(2)
    sum_b(2)
    for h, columns, _ in halves:
        for side, heights, to_x, to_y in ((0, low, right_x, right_y), (1, high, left_x, left_y)):
            far_a[h, side] = send(pa.at[heights, :, rows16(xs[2]), columns], fa.at[h, side], to_x)
            far_b[h, side] = send(pb.at[heights, ys[2], :, columns], fb.at[h, side], to_y)
    near_cx, near_cy = [], []
    for side, k, to_x, to_y in sides:
        sum_cx(k)
        arrive([far_cx[side]])
        part = slice(2 * side, 2 * side + 2)
        px[xs[k], part] = add(px, px[xs[k], part], fcx[side])
        near_cx.append(send(px.at[xs[k]], ncx.at[side], to_x))
        sum_cy(k)
        arrive([far_cy[side]])
        py[part, ys[k]] = add(py, py[part, ys[k]], fcy[side])
        near_cy.append(send(py.at[:, ys[k]], ncy.at[side], to_y))
    for side, k, to_x, to_y in sides:
        sum_a(k)
        sum_b(k)
    near_a, near_b = {}, {}
    for h, columns, cols in halves:
        for side, k, to_x, to_y in sides:
            rows = rows16(xs[k])
            arrive([far_a[h, side]])

            def join_a(i, h=h, side=side, rows=rows, cols=cols):
                pa[2 * side + i, :, rows, cols] = add(pa, pa[2 * side + i, :, rows, cols], fa[h, side, i])

            loop(2, join_a)
            near_a[h, side] = send(pa.at[:, :, rows, columns], na.at[h, side], to_x)
            arrive([far_b[h, side]])

            def join_b(i, h=h, side=side, index=ys[k], cols=cols):
                pb[2 * side + i, index, :, cols] = add(pb, pb[2 * side + i, index, :, cols], fb[h, side, i])

            loop(2, join_b)
            near_b[h, side] = send(pb.at[:, ys[k], :, columns], nb.at[h, side], to_y)

    def three(axis, whole, source):
        return send.group(
            whole, [(source(k), whole.at[k - 1], device(moved(at, **{axis: k}))) for k in (1, 3, 2)]
        )

    sum_cx(0)
    arrive(near_cx)
    scx1[...] = add(scx1, px[x], ncx[0], ncx[1])
    cx2 = three("y", rcx2, lambda k: scx1.at[:, ys[k]])
    sum_cy(0)
    arrive(near_cy)
    scy1[...] = add(scy1, py[:, y], ncy[0], ncy[1])
    cy2 = three("zh", rcy2, lambda k: scy1.at[zs[k]])
    sum_a(0)
    sum_b(0)

    rows_f[:, 256:272] = jnp.zeros((6, 16, 128), F32)
    for i in range(4):
        terms = right_dot(d_pre, conv_full(i))
        for j in range(6):
            target = pl.ds(7 + i, 128, stride=2)
            block = terms[:, 128 * j : 128 * j + 128]
            rows_f[j, target] = block if i < 2 else rows_f[j, target] + block
    rim_out[0] = rows_f[:, 264:272]
    rim_out[1] = rows_f[:, 0:8]
    rims = [send(rim_out.at[0], rim_before, ahead), send(rim_out.at[1], rim_after, behind)]

    a2, b2, a3, b3, a4, b4 = {}, {}, {}, {}, {}, {}
    for h, columns, cols in halves:
        arrive([near_a[h, 0], near_a[h, 1]])

        def first_a(i, h=h, cols=cols):
            sa1[h, i] = add(sa1, pa[i, :, rows16(x), cols], na[h, 0, i], na[h, 1, i])

        loop(4, first_a)
        a2[h] = three("y", ra2.at[h], lambda k, h=h: sa1.at[h, :, ys[k]])
        arrive([near_b[h, 0], near_b[h, 1]])

        def first_b(i, h=h, cols=cols):
            sb1[h, i] = add(sb1, pb[i, y, :, cols], nb[h, 0, i], nb[h, 1, i])

        loop(4, first_b)
        b2[h] = three("x", rb2.at[h], lambda k, h=h: sb1.at[h, :, rows16(xs[k])])
        if h == 0:
            arrive([cx2])
            scx2[...] = add(scx2, scx1[:, y], rcx2[0], rcx2[1], rcx2[2])
            cx3 = three("zh", rcx3, lambda k: scx2.at[zs[k]])
            arrive([cy2])
            scy2[...] = add(scy2, scy1[zh], rcy2[0], rcy2[1], rcy2[2])
            cy3 = send(scy2, rcy3, near)
    arrive(rims)
    rows_f[:, 8:9] += jnp.where(sq > 0, rim_before[:, 0:1], 0.0)
    rows_f[:, 263:264] += jnp.where(sq < 7, rim_after[:, 7:8], 0.0)
    for j in range(6):
        seq_o[:, 128 * j : 128 * j + 128] = rows_f[j, 8:264].astype(BF16)
    for h in range(2):
        arrive([a2[h]])
        sa2[h] = add(sa2, sa1[h, :, y], ra2[h, 0], ra2[h, 1], ra2[h, 2])
        a3[h] = three("zh", ra3.at[h], lambda k, h=h: sa2.at[h, zs[k]])
        arrive([b2[h]])
        sb2[h] = add(sb2, sb1[h, :, rows16(x)], rb2[h, 0], rb2[h, 1], rb2[h, 2])
        b3[h] = three("zh", rb3.at[h], lambda k, h=h: sb2.at[h, zs[k]])
        if h == 0:
            arrive([cx3])
            scx3[...] = add(scx3, scx2[zh], rcx3[0], rcx3[1], rcx3[2])
            cx4 = send(scx3, rcx4, near)
            arrive([cy3])
            scy3[...] = add(scy3, scy2[...], rcy3[...])
            cy4 = three("x", rcy4, lambda k: scy3)

    for h in range(2):
        arrive([a3[h]])
        sa3[h] = add(sa3, sa2[h, zh], ra3[h, 0], ra3[h, 1], ra3[h, 2])
        a4[h] = send(sa3.at[h], ra4.at[h], near)
        arrive([b3[h]])
        sb3[h] = add(sb3, sb2[h, zh], rb3[h, 0], rb3[h, 1], rb3[h, 2])
        b4[h] = send(sb3.at[h], rb4.at[h], near)
        if h == 0:
            arrive([cx4])
            final_x[x] = add(final_x, scx3[...], rcx4[...])
            spread = [send(final_x.at[x], final_x.at[x], device(moved(at, x=k))) for k in (1, 2, 3)]
            arrive([cy4])
            final_y[...] = add(final_y, scy3[...], rcy4[0], rcy4[1], rcy4[2])
    for h in range(2):
        arrive([a4[h]])
        final[x, 0, h] = add(final, sa3[h], ra4[h])
        arrive([b4[h]])
        final[x, 1, h] = add(final, sb3[h], rb4[h])
    spread += [send(final.at[x], final.at[x], device(moved(at, x=k))) for k in (1, 2, 3)]
    arrive(spread)
    send.finish()


def finish_kernel(seq_i, final, final_x, final_y, seq_o, conv_o, dna_o, qkv_o, out_o):
    seq_o[0] = seq_i[...]
    for h in range(2):
        columns = slice(384 * h, 384 * h + 384)
        for q in range(4):
            conv_o[16 * q : 16 * q + 16, columns] = final[q, 0, h].astype(F32)
        conv_o[64:80, columns] = final[0, 1, h].astype(F32)
        conv_o[80:96, columns] = final[1, 1, h].astype(F32)
        dna_o[:, columns] = final[2, 1, h].astype(F32)
        out_o[:, columns] = final[3, 1, h].astype(F32)
    for q in range(4):
        qkv_o[0:16, 384 * q : 384 * q + 384] = final_x[q].astype(F32)
    last_rows = final_y[...].astype(F32)
    qkv_o[16:24, 0:768] = last_rows[0:8]
    qkv_o[16:24, 768:1536] = last_rows[8:16]


def layer(*operands):
    vmem = pl.BlockSpec(memory_space=pltpu.VMEM)
    low = [
        (4, 4, 2, 4, 16, 1152), (4, 4, 2, 80, 768), (16, 768), (16, 768),
        (4, 128, 768), (4, 4, 2, 96, 128), (128, 512), (4, 4, 2, 16, 128), (768, 512), (768, 512),
        (128, 512), (128, 512), (4, 4, 2, 16, 128), (4, 4, 2, 16, 128), (128, 1536), (128, 512), (4, 4, 2, 16, 128),
        (4, 128, 512), (4, 128, 512), (4, 128, 256), (4, 128, 512), (4, 128, 256), (4, 128, 512), (4, 128, 256),
        (4, 128, 1024), (4, 128, 1024),
    ] + 3 * [(4, 4, 64, 768), (4, 4, 64, 768), (4, 4, 4, 16, 384), (4, 4, 16, 768)] + [
        (2, 2, 2, 4, 16, 384), (2, 2, 4, 4, 16, 384), (2, 4, 4, 16, 384), (2, 3, 4, 16, 384),
        (2, 4, 16, 384), (2, 3, 16, 384), (2, 16, 384), (2, 16, 384),
        (2, 2, 2, 64, 384), (2, 2, 4, 64, 384), (2, 4, 64, 384), (2, 3, 4, 16, 384),
        (2, 4, 16, 384), (2, 3, 16, 384), (2, 16, 384), (2, 16, 384),
        (2, 2, 4, 16, 384), (2, 4, 4, 16, 384), (4, 4, 16, 384), (3, 4, 16, 384), (4, 16, 384), (3, 16, 384), (16, 384), (16, 384),
        (2, 2, 16, 768), (2, 4, 16, 768), (4, 16, 768), (3, 16, 768), (16, 768), (16, 768), (16, 768), (3, 16, 768),
    ]
    wide = [(128, 768), (128, 768), (128, 1), (6, 272, 128), (2, 6, 8, 128), (6, 8, 128), (6, 8, 128)]
    results = pl.pallas_call(
        layer_kernel,
        name="layer",
        out_shape=tuple(
            jax.ShapeDtypeStruct(shape, BF16)
            for shape in ((256, 768), (4, 2, 2, 16, 384), (4, 16, 384), (16, 768))
        ),
        in_specs=[vmem] * 7,
        out_specs=(vmem,) * 4,
        scratch_shapes=[pltpu.VMEM(shape, BF16) for shape in low]
        + [pltpu.VMEM(shape, F32) for shape in wide]
        + [pltpu.SemaphoreType.DMA((90,)), pltpu.SemaphoreType.DMA((133,))],
        compiler_params=pltpu.CompilerParams(
            collective_id=1, has_side_effects=True, vmem_limit_bytes=60 * 2**20
        ),
    )(*operands)
    return pl.pallas_call(
        finish_kernel,
        name="finish",
        out_shape=(
            jax.ShapeDtypeStruct((1, 256, 768), BF16),
            jax.ShapeDtypeStruct((96, 768), F32),
            jax.ShapeDtypeStruct((16, 768), F32),
            jax.ShapeDtypeStruct((24, 1536), F32),
            jax.ShapeDtypeStruct((16, 768), F32),
        ),
        in_specs=[vmem] * 4,
        out_specs=(vmem,) * 5,
    )(*results)


def per_device(seq_in, bases, conv_weight, dna_weight, qkv_weight, out_weight, cotangent):
    return layer(
        conv_weight, dna_weight, qkv_weight, out_weight, seq_in[0], bases[0].reshape(128, BIN), cotangent[0]
    )


def solution(mesh):
    in_specs = (
        P("dp", "seq", None),
        P("dp", "seq"),
        P("dp", None),
        P("dp", None),
        P("dp", None),
        P("dp", None),
        P("dp", "seq", None),
    )
    out_specs = (P("dp", "seq", None), P("dp", None), P("dp", None), P("dp", None), P("dp", None))
    return jax.shard_map(
        per_device, mesh=mesh, in_specs=in_specs, out_specs=out_specs, check_vma=False
    )
```

```python
import math

import jax
import jax.numpy as jnp
from jax import lax
from jax.experimental import pallas as pl
from jax.experimental.pallas import tpu as pltpu
from jax.sharding import PartitionSpec as P

H = 4
BIN = 128
BF16 = jnp.bfloat16
F32 = jnp.float32
MESH = pl.DeviceIdType.MESH
epsilon = 1e-06

SIZES = {"zh": 4, "y": 4, "c": 2, "zl": 2, "x": 4}
PEERS = [(a, k) for a in ("zh", "y", "x") for k in (1, 2, 3)] + [("zl", 1), ("c", 1)]


def here():
    dp = lax.axis_index("dp")
    sq = lax.axis_index("seq")
    return {"zh": dp // 8, "y": lax.rem(dp // 2, 4), "c": lax.rem(dp, 2), "zl": sq // 4, "x": lax.rem(sq, 4)}


def moved(at, **steps):
    to = dict(at)
    for axis, step in steps.items():
        to[axis] = lax.rem(at[axis] + step, SIZES[axis])
    return to


def device(at):
    return (at["zh"] * 8 + at["y"] * 2 + at["c"], at["zl"] * 4 + at["x"])


class Sender:
    def __init__(self, send_sems, recv_sems):
        self.send_sems, self.recv_sems, self.sent, self.due, self.copies = send_sems, recv_sems, 0, 0, []

    def copy(self, src, dst, to, recv):
        copy = pltpu.make_async_remote_copy(
            src_ref=src,
            dst_ref=dst,
            send_sem=self.send_sems.at[self.sent],
            recv_sem=self.recv_sems.at[recv],
            device_id=to,
            device_id_type=MESH,
        )
        copy.start()
        self.sent += 1
        self.copies.append(copy)
        return copy

    def __call__(self, src, dst, to):
        self.due += 1
        return self.copy(src, dst, to, self.due - 1)

    def group(self, whole, copies):
        self.due += 1
        for src, dst, to in copies:
            self.copy(src, dst, to, self.due - 1)
        return pltpu.make_async_remote_copy(
            src_ref=whole,
            dst_ref=whole,
            send_sem=self.send_sems.at[0],
            recv_sem=self.recv_sems.at[self.due - 1],
            device_id=copies[0][2],
            device_id_type=MESH,
        )

    def finish(self):
        for copy in self.copies:
            copy.wait_send()
        self.sent, self.copies = 0, []


def arrive(copies):
    for copy in copies:
        copy.wait_recv()


def rows16(index, base=0):
    return pl.ds(pl.multiple_of(index * 16 + base, 16), 16)


def half_columns(index):
    return pl.ds(pl.multiple_of(index * 384, 128) if not isinstance(index, int) else index * 384, 384)


def right_dot(left, right):
    return lax.dot_general(left, right, (((1,), (1,)), ((), ())), preferred_element_type=F32)


def row_dot(left, right):
    return lax.dot_general(left, right, (((0,), (0,)), ((), ())), preferred_element_type=F32)


def dot(left, right):
    return jnp.dot(left, right, preferred_element_type=F32)


def add(target, *terms):
    total = terms[0].astype(F32)
    for term in terms[1:]:
        total += term.astype(F32)
    return total.astype(target.dtype)


def loop(n, body):
    def step(i, carry):
        body(i)
        return carry

    lax.fori_loop(0, n, step, 0)


class Ring:
    def __init__(self, send, at, axis, region):
        self.send, self.me, self.region = send, at[axis], region
        self.right, self.left = device(moved(at, **{axis: 1})), device(moved(at, **{axis: 3}))

    def at(self, step):
        return lax.rem(self.me + step, 4)

    def go(self, index, part, to):
        ref = self.region(index, part)
        return [self.send(ref, ref, to)]

    def start(self):
        self.from_left = self.go(self.me, None, self.right)
        self.from_right = self.go(self.me, None, self.left)

    def left_in(self):
        arrive(self.from_left)
        self.far_left = self.go(self.at(3), 0, self.right)

    def right_in(self):
        arrive(self.from_right)
        self.far_right = self.go(self.at(1), 1, self.left)

    def both_in(self):
        self.left_in()
        self.right_in()

    def far_in(self):
        arrive(self.far_left)
        arrive(self.far_right)


def layer_kernel(
    conv_s, dna_s, qkv_s, out_s, rows_in, letters, upstream,
    seq_o, final, final_x, final_y,
    ga, gb, before, after,
    taps, taps_t, onehot, onehot_t, choose_x, choose_y, wide_x, wide_y, wide_xt, wide_yt, d_proj, attended, attended_t,
    mine, got, got_k, got_v, outgo, outgo_k, outgo_v, back, back_k, back_v, probs_s, scores_s,
    pa_s, pb_s, px_s, py_s, pa, pb, px, py, pa_r, pb_r, px_r, py_r,
    fa, na, sa1, ra2, sa2, ra3, sa3, ra4,
    fb, nb, sb1, rb2, sb2, rb3, sb3, rb4,
    fcx, ncx, scx1, rcx2, scx2, rcx3, scx3, rcx4,
    fcy, ncy, scy1, rcy2, scy2, rcy3, scy3, rcy4,
    slope, unit, inverse, rows_f, probs_f, rim_out, rim_before, rim_after,
    send_sems, recv_sems,
):
    at = here()
    zh, y, c, zl, x = (at[a] for a in ("zh", "y", "c", "zl", "x"))
    sq = lax.axis_index("seq")
    dp = lax.axis_index("dp")
    behind, ahead = (dp, lax.rem(sq + 7, 8)), (dp, lax.rem(sq + 1, 8))
    sibling = device(moved(at, c=1))
    near = device(moved(at, zl=1))
    across = [moved(at, x=k, zl=1) for k in range(4)]
    everyone = [device(moved(at, **{a: k})) for a, k in PEERS] + [behind, ahead]
    everyone += [device(p) for p in across[1:]]
    barrier = pltpu.get_barrier_semaphore()
    for one in everyone:
        pl.semaphore_signal(barrier, inc=1, device_id=one, device_id_type=MESH)
    xs = [lax.rem(x + k, 4) for k in range(4)]
    ys = [lax.rem(y + k, 4) for k in range(4)]
    zs = [lax.rem(zh + k, 4) for k in range(4)]

    quarter = rows16(x)
    ga[zh, y, c, x, :, 0:768] = conv_s[quarter]
    ga[zh, y, c, x, :, 768:1152] = qkv_s[0:16, half_columns(x)]
    gb[zh, y, c, 0:32] = conv_s[64:96]
    gb[zh, y, c, 32:48] = dna_s[...]
    gb[zh, y, c, 48:64] = out_s[...]
    last_rows = [qkv_s[:, 768 * i : 768 * i + 768].astype(F32)[16:24] for i in range(2)]
    gb[zh, y, c, 64:80] = jnp.concatenate(last_rows, axis=0).astype(BF16)
    pl.semaphore_wait(barrier, len(everyone))

    send = Sender(send_sems, recv_sems)

    def ref_a(height, step, index, part=None):
        rows = pl.ds(0, 4) if part is None else pl.ds(2 * part, 2)
        return ga.at[rows if height is None else height, step, c, index]

    def ref_b(height, step, part=None):
        return gb.at[height, step, c] if part is None else gb.at[height, step, c, :, half_columns(part)]

    core = []

    def pass_on(ref):
        core.append(send(ref, ref, sibling))

    def pass_a(step):
        pass_on(ga.at[:, step, c])

    def pass_b(height):
        pass_on(gb.at[height, :, c])

    a1 = []
    for k in (1, 3, 2):
        a1.append(send(ref_a(zh, y, x), ref_a(zh, y, x), device(moved(at, zh=k))))
    halo = [
        send(rows_in.at[pl.ds(240, 16)], before, ahead),
        send(rows_in.at[pl.ds(0, 16)], after, behind),
    ]
    ring_z = Ring(send, at, "zh", lambda index, part: ref_b(index, y, part))
    rings_y = [Ring(send, at, "y", lambda index, part, v=zs[k]: ref_b(v, index, part)) for k in range(4)]
    rings_x = [Ring(send, at, "x", lambda index, part, v=ys[k]: ref_a(None, v, index, part)) for k in range(4)]
    ring_a = Ring(send, at, "y", lambda index, part: ref_a(None, index, x, part))
    ring_z.start()
    rings_y[0].start()
    row = lax.broadcasted_iota(jnp.int32, (128, 512), 0)
    column = lax.broadcasted_iota(jnp.int32, (128, 512), 1)
    repeat = (column // 4 == row).astype(F32).astype(BF16)
    repeated = dot(letters[...].astype(F32).astype(BF16), repeat)
    onehot[...] = (repeated == lax.rem(column, 4).astype(F32)).astype(F32).astype(BF16)
    arrive(a1)
    ring_a.start()
    rings_x[0].start()
    ring_z.left_in()
    rings_y[3].start()
    ring_z.right_in()
    rings_y[0].both_in()
    ring_a.left_in()
    rings_x[3].start()
    ring_a.right_in()
    rings_x[1].start()
    rings_y[1].start()
    rings_x[0].both_in()
    ring_a.far_in()
    rings_x[2].start()
    ring_z.far_in()
    rings_y[2].start()
    rings_y[3].both_in()
    rings_x[3].both_in()
    rings_x[1].both_in()
    rings_y[1].both_in()
    rings_y[0].far_in()
    pass_b(zs[0])
    rings_x[0].far_in()
    pass_a(ys[0])
    rings_x[2].both_in()
    rings_y[2].both_in()

    arrive(halo)
    for j in range(6):
        lanes = slice(128 * j, 128 * j + 128)
        rows_f[j, 8:264] = rows_in[:, lanes].astype(F32)
        rows_f[j, 0:8] = jnp.where(sq > 0, before[:, lanes].astype(F32)[8:16], 0.0)
        rows_f[j, 264:272] = jnp.where(sq < 7, after[:, lanes].astype(F32)[0:8], 0.0)
        for i in range(4):
            taps[i, :, lanes] = rows_f[j, pl.ds(7 + i, 128, stride=2)].astype(BF16)

    rings_y[3].far_in()
    pass_b(zs[3])
    rings_y[1].far_in()
    pass_b(zs[1])
    rings_x[3].far_in()
    pass_a(ys[3])
    rings_x[1].far_in()
    pass_a(ys[1])
    rings_y[2].far_in()
    pass_b(zs[2])
    rings_x[2].far_in()
    pass_a(ys[2])

    def transpose_tap(i):
        taps_t[i] = taps[i].T.reshape(4, 2, 96, 128)

    loop(4, transpose_tap)
    onehot_t[...] = onehot[...].T.reshape(4, 4, 2, 16, 128)
    row = lax.broadcasted_iota(jnp.int32, (768, 512), 0)
    column = lax.broadcasted_iota(jnp.int32, (768, 512), 1)
    first_row = column // 16 * 24
    choose_x[...] = (first_row + lax.rem(column, 16) == row).astype(F32).astype(BF16)
    choose_y[...] = (first_row + 16 + lax.rem(column, 8) == row).astype(F32).astype(BF16)
    arrive(core[:-1])

    def conv_full(i):
        first = ga[i, :, :, :, :, 0:768].reshape(4, 2, 64, 768)
        return jnp.concatenate([first, gb[i, :, :, 0:32]], axis=2).reshape(768, 768)

    def qx_full(i):
        return jnp.concatenate(
            [ga[:, :, :, 2 * i + j, :, 768:1152].reshape(512, 384) for j in range(2)], axis=1
        )

    def qy_full():
        return gb[:, :, :, 64:80].reshape(512, 768)

    dna_full = gb[:, :, :, 32:48].reshape(512, 768)
    out_full = gb[:, :, :, 48:64].reshape(512, 768)
    d_attend = right_dot(upstream[...], out_full).astype(BF16)
    slope[...] = dot(onehot[...], dna_full)
    arrive(core[-1:])

    def one_tap(i):
        slope[...] += dot(taps[i], conv_full(i))

    loop(4, one_tap)
    pre = slope[...]
    bend = jnp.tanh(math.sqrt(2.0 / math.pi) * (pre + 0.044715 * (pre * pre * pre)))
    share = 0.5 * (1.0 + bend)
    feature = (pre * share).astype(BF16).astype(F32)
    slope[...] = share + pre * (0.5 * (1.0 - bend * bend)) * (
        math.sqrt(2.0 / math.pi) * (1.0 + 3.0 * 0.044715 * (pre * pre))
    )
    scale = lax.rsqrt(jnp.mean(feature * feature, axis=1, keepdims=True) + epsilon)
    inverse[...] = scale
    unit[...] = feature * scale
    normed = unit[...].astype(BF16)
    wide_x[...] = dot(normed, choose_x[...]).astype(BF16)
    wide_y[...] = dot(normed, choose_y[...]).astype(BF16)
    side_of = lax.rem(lax.broadcasted_iota(jnp.int32, (128, 512), 1), 16) // 8
    for i in range(2):
        own_y = jnp.where(side_of == i, wide_y[...].astype(F32), 0.0).astype(BF16)
        projected = (dot(wide_x[...], qx_full(i)) + dot(own_y, qy_full())).astype(BF16)
        for piece in range(6):
            kind, head = divmod(6 * i + piece, 4)
            place = (1, 0, 2)[kind] * 128
            mine[head, :, place : place + 128] = projected[:, 128 * piece : 128 * piece + 128]
    for head in range(H):
        mine[head, :, 384:512] = d_attend[:, 128 * head : 128 * head + 128]

    col_k, col_v, col_kq, col_vd = pl.ds(0, 128), pl.ds(256, 128), pl.ds(0, 256), pl.ds(256, 256)
    kq_in, vd_in = {}, {}
    from_near_k = send.group(got_k, [(mine.at[x, :, col_k], got_k.at[x], near)])
    near_k = send.due - 1
    for k in (1, 3, 2):
        kq_in[k] = send(mine.at[xs[k], :, col_kq], got.at[x, :, col_kq], device(moved(at, x=k)))
    for k in (1, 3, 2):
        vd_in[k] = send(mine.at[xs[k], :, col_vd], got.at[x, :, col_vd], device(moved(at, x=k)))
    sources = {k: lax.rem(x + 4 - k, 4) for k in (0, 1, 3, 2)}
    got[x] = mine[x]
    for k in (1, 3, 2):
        arrive([kq_in[k]])
        send.copy(got.at[sources[k], :, col_k], got_k.at[sources[k]], near, near_k)
    from_near_v = send.group(got_v, [(mine.at[x, :, col_v], got_v.at[x], near)])
    near_v = send.due - 1
    wide_xt[...] = wide_x[...].T.reshape(4, 4, 2, 16, 128)
    wide_yt[...] = wide_y[...].T.reshape(4, 4, 2, 16, 128)
    arrive([from_near_k])
    keys = jnp.concatenate([got[:, :, 0:128].reshape(512, 128), got_k[...].reshape(512, 128)], axis=0)
    scaling = 1.0 / math.sqrt(128)

    def soft(source):
        scores = right_dot(got[source, :, 128:256], keys) * scaling
        powers = jnp.exp(scores - jnp.max(scores, axis=1, keepdims=True))
        probs = powers * (1.0 / jnp.sum(powers, axis=1, keepdims=True))
        probs_f[source] = probs
        probs_s[source] = probs.astype(BF16)

    def pass_v(k):
        arrive([vd_in[k]])
        send.copy(got.at[sources[k], :, col_v], got_v.at[sources[k]], near, near_v)

    soft(sources[0])
    pass_v(1)
    pass_v(3)
    soft(sources[1])
    soft(sources[3])
    pass_v(2)
    soft(sources[2])
    home = []
    all_queries = got[:, :, 128:256].reshape(512, 128)
    all_upward = got[:, :, 384:512].reshape(512, 128)
    all_probs = probs_s[...].reshape(512, 1024)
    d_values = row_dot(all_upward, all_probs).T.astype(BF16).reshape(8, 128, 128)
    outgo_v[...] = d_values[4:8]
    home.append(send.group(back_v, [(outgo_v.at[p["x"]], back_v.at[x], device(p)) for p in across]))
    outgo[:, :, 384:512] = d_values[0:4]
    arrive([from_near_v])
    values = jnp.concatenate([got[:, :, 256:384].reshape(512, 128), got_v[...].reshape(512, 128)], axis=0)
    outgo[:, :, 0:128] = dot(all_probs, values).astype(BF16).reshape(4, 128, 128)
    for k in (1, 3, 2):
        block = pl.ds(0, 128)
        home.append(send(outgo.at[xs[k], :, block], back.at[x, :, block], device(moved(at, x=k))))

    def step(i, carry):
        probs = probs_f[i]
        d_probs = right_dot(got[i, :, 384:512], values)
        inner = jnp.sum(probs * d_probs, axis=1, keepdims=True)
        scores_s[i] = (probs * (d_probs - inner) * scaling).astype(BF16)
        return carry

    lax.fori_loop(0, 4, step, 0)

    def key_grads(columns):
        d_keys = row_dot(all_queries, scores_s[:, :, columns].reshape(512, 512)).T
        return d_keys.astype(BF16).reshape(4, 128, 128)

    outgo_k[...] = key_grads(slice(512, 1024))
    home.append(send.group(back_k, [(outgo_k.at[p["x"]], back_k.at[x], device(p)) for p in across]))
    outgo[:, :, 256:384] = key_grads(slice(0, 512))
    outgo[:, :, 128:256] = dot(scores_s[...].reshape(512, 1024), keys).astype(BF16).reshape(4, 128, 128)
    for k in (1, 3, 2):
        block = pl.ds(128, 384)
        home.append(send(outgo.at[xs[k], :, block], back.at[x, :, block], device(moved(at, x=k))))
    back[x] = outgo[x]
    arrive(home)
    send.finish()
    for head in range(H):
        columns = slice(128 * head, 128 * head + 128)
        attended[:, columns] = back[head, :, 0:128]
        d_proj[:, columns] = back[head, :, 128:256]
        for kind, other in ((1, back_k), (2, back_v)):
            total = back[head, :, 128 + 128 * kind : 256 + 128 * kind].astype(F32) + other[head].astype(F32)
            start = 512 * kind + 128 * head
            d_proj[:, start : start + 128] = total.astype(BF16)

    attended_t[...] = attended[...].T.reshape(4, 4, 2, 16, 128)
    d_halves = [d_proj[:, 0:768], d_proj[:, 768:1536]]
    row_side = lax.rem(lax.broadcasted_iota(jnp.int32, (256, 768), 0), 16)

    def qkv_grads(parity, to_x, to_y):
        left = wide_xt[:, :, parity].reshape(256, 128)
        for i in range(2):
            block = dot(left, d_halves[i]).astype(BF16)
            for j in range(2):
                to_x[2 * i + j] = block[:, 384 * j : 384 * j + 384].reshape(4, 4, 16, 384)
        left = wide_yt[:, :, parity].reshape(256, 128)
        both = [dot(left, d_half) for d_half in d_halves]
        to_y[...] = jnp.where(row_side < 8, both[0], both[1]).astype(BF16).reshape(4, 4, 16, 768)

    order = (2, 1, 3, 0)
    core_cx, core_cy, core_a, core_b = {}, {}, {}, {}
    qkv_grads(1 - c, px_s, py_s)
    for k in order:
        core_cx[k] = send(px_s.at[:, zs[k]], px_r.at[:, zs[k]], sibling)
        core_cy[k] = send(py_s.at[:, ys[k]], py_r.at[:, ys[k]], sibling)
    qkv_grads(c, px, py)
    d_x = sum(right_dot(d_halves[i], qx_full(i)) for i in range(2))
    both = [right_dot(d_half, qy_full()) for d_half in d_halves]
    d_y = jnp.where(side_of == 0, both[0], both[1])

    def sum_cx(k):
        arrive([core_cx[k]])
        px[:, zs[k]] = add(px, px[:, zs[k]], px_r[:, zs[k]])

    def sum_cy(k):
        arrive([core_cy[k]])
        py[:, ys[k]] = add(py, py[:, ys[k]], py_r[:, ys[k]])

    right_x, left_x = device(moved(at, x=1)), device(moved(at, x=3))
    right_y, left_y = device(moved(at, y=1)), device(moved(at, y=3))
    right_z, left_z = device(moved(at, zh=1)), device(moved(at, zh=3))
    low, high = pl.ds(0, 2), pl.ds(2, 2)
    sides = ((0, 1, right_x, right_y), (1, 3, left_x, left_y))
    sum_cx(2)
    far_cx = [
        send(px.at[quarters, zs[2]], fcx.at[side], to) for side, quarters, to in ((0, low, right_z), (1, high, left_z))
    ]
    sum_cy(2)
    far_cy = [
        send(py.at[heights, ys[2]], fcy.at[side], to) for side, heights, to in ((0, low, right_y), (1, high, left_y))
    ]
    d_normed = 0.0
    for terms, choose in ((d_x, choose_x), (d_y, choose_y)):
        d_high = terms.astype(BF16)
        d_low = (terms - d_high.astype(F32)).astype(BF16)
        d_normed += right_dot(d_high, choose[...]) + right_dot(d_low, choose[...])
    d_feature = upstream[...].astype(F32) + inverse[...] * (
        d_normed - unit[...] * jnp.mean(d_normed * unit[...], axis=1, keepdims=True)
    )
    d_pre = (d_feature * slope[...]).astype(BF16)

    def conv_grads(parity, to_a, to_b):
        def one(i):
            block = dot(taps_t[i, :, parity].reshape(384, 128), d_pre).astype(BF16).reshape(4, 96, 768)
            to_a[i] = block[:, 0:64]
            to_b[i, :, 0:32] = block[:, 64:96]

        loop(4, one)
        left = onehot_t[:, :, parity].reshape(256, 128)
        to_b[:, :, 32:48] = dot(left, d_pre).astype(BF16).reshape(4, 4, 16, 768)
        left = attended_t[:, :, parity].reshape(256, 128)
        to_b[:, :, 48:64] = dot(left, upstream[...]).astype(BF16).reshape(4, 4, 16, 768)

    conv_grads(1 - c, pa_s, pb_s)
    for k in order:
        core_a[k] = send(pa_s.at[:, :, rows16(xs[k])], pa_r.at[:, :, rows16(xs[k])], sibling)
        core_b[k] = send(pb_s.at[:, ys[k]], pb_r.at[:, ys[k]], sibling)
    conv_grads(c, pa, pb)

    def sum_a(k):
        arrive([core_a[k]])
        rows = rows16(xs[k])

        def one(i):
            pa[i, :, rows] = add(pa, pa[i, :, rows], pa_r[i, :, rows])

        loop(4, one)

    def sum_b(k):
        arrive([core_b[k]])

        def one(i):
            pb[i, ys[k]] = add(pb, pb[i, ys[k]], pb_r[i, ys[k]])

        loop(4, one)

    halves = [(h, pl.ds(384 * h, 384), slice(384 * h, 384 * h + 384)) for h in range(2)]
    far_a, far_b = {}, {}
    sum_a(2)
    sum_b(2)
    for h, columns, _ in halves:
        for side, heights, to_x, to_y in ((0, low, right_x, right_y), (1, high, left_x, left_y)):
            far_a[h, side] = send(pa.at[heights, :, rows16(xs[2]), columns], fa.at[h, side], to_x)
            far_b[h, side] = send(pb.at[heights, ys[2], :, columns], fb.at[h, side], to_y)
    near_cx, near_cy = [], []
    for side, k, to_x, to_y in sides:
        sum_cx(k)
        arrive([far_cx[side]])
        part = slice(2 * side, 2 * side + 2)
        px[part, zs[k]] = add(px, px[part, zs[k]], fcx[side])
        near_cx.append(send(px.at[:, zs[k]], ncx.at[side], (right_z, left_z)[side]))
        sum_cy(k)
        arrive([far_cy[side]])
        py[part, ys[k]] = add(py, py[part, ys[k]], fcy[side])
        near_cy.append(send(py.at[:, ys[k]], ncy.at[side], to_y))
    for side, k, to_x, to_y in sides:
        sum_a(k)
        sum_b(k)
    near_a, near_b = {}, {}
    for h, columns, cols in halves:
        for side, k, to_x, to_y in sides:
            rows = rows16(xs[k])
            arrive([far_a[h, side]])

            def join_a(i, h=h, side=side, rows=rows, cols=cols):
                pa[2 * side + i, :, rows, cols] = add(pa, pa[2 * side + i, :, rows, cols], fa[h, side, i])

            loop(2, join_a)
            near_a[h, side] = send(pa.at[:, :, rows, columns], na.at[h, side], to_x)
            arrive([far_b[h, side]])

            def join_b(i, h=h, side=side, index=ys[k], cols=cols):
                pb[2 * side + i, index, :, cols] = add(pb, pb[2 * side + i, index, :, cols], fb[h, side, i])

            loop(2, join_b)
            near_b[h, side] = send(pb.at[:, ys[k], :, columns], nb.at[h, side], to_y)

    def three(axis, whole, source):
        return send.group(
            whole, [(source(k), whole.at[k - 1], device(moved(at, **{axis: k}))) for k in (1, 3, 2)]
        )

    sum_cx(0)
    arrive(near_cx)
    scx1[...] = add(scx1, px[:, zh], ncx[0], ncx[1])
    cx2 = three("x", rcx2, lambda k: scx1.at[xs[k]])
    sum_cy(0)
    arrive(near_cy)
    scy1[...] = add(scy1, py[:, y], ncy[0], ncy[1])
    cy2 = three("zh", rcy2, lambda k: scy1.at[zs[k]])
    sum_a(0)
    sum_b(0)

    rows_f[:, 256:272] = jnp.zeros((6, 16, 128), F32)
    for i in range(4):
        terms = right_dot(d_pre, conv_full(i))
        for j in range(6):
            target = pl.ds(7 + i, 128, stride=2)
            block = terms[:, 128 * j : 128 * j + 128]
            rows_f[j, target] = block if i < 2 else rows_f[j, target] + block
    rim_out[0] = rows_f[:, 264:272]
    rim_out[1] = rows_f[:, 0:8]
    rims = [send(rim_out.at[0], rim_before, ahead), send(rim_out.at[1], rim_after, behind)]

    a2, b2, a3, b3, a4, b4 = {}, {}, {}, {}, {}, {}
    for h, columns, cols in halves:
        arrive([near_a[h, 0], near_a[h, 1]])

        def first_a(i, h=h, cols=cols):
            sa1[h, i] = add(sa1, pa[i, :, rows16(x), cols], na[h, 0, i], na[h, 1, i])

        loop(4, first_a)
        a2[h] = three("y", ra2.at[h], lambda k, h=h: sa1.at[h, :, ys[k]])
        arrive([near_b[h, 0], near_b[h, 1]])

        def first_b(i, h=h, cols=cols):
            sb1[h, i] = add(sb1, pb[i, y, :, cols], nb[h, 0, i], nb[h, 1, i])

        loop(4, first_b)
        b2[h] = three("x", rb2.at[h], lambda k, h=h: sb1.at[h, :, rows16(xs[k])])
        if h == 0:
            arrive([cx2])
            scx2[...] = add(scx2, scx1[x], rcx2[0], rcx2[1], rcx2[2])
            cx3 = three("y", rcx3, lambda k: scx2.at[ys[k]])
            arrive([cy2])
            scy2[...] = add(scy2, scy1[zh], rcy2[0], rcy2[1], rcy2[2])
            cy3 = send(scy2, rcy3, near)
    arrive(rims)
    rows_f[:, 8:9] += jnp.where(sq > 0, rim_before[:, 0:1], 0.0)
    rows_f[:, 263:264] += jnp.where(sq < 7, rim_after[:, 7:8], 0.0)
    for j in range(6):
        seq_o[:, 128 * j : 128 * j + 128] = rows_f[j, 8:264].astype(BF16)
    for h in range(2):
        arrive([a2[h]])
        sa2[h] = add(sa2, sa1[h, :, y], ra2[h, 0], ra2[h, 1], ra2[h, 2])
        a3[h] = three("zh", ra3.at[h], lambda k, h=h: sa2.at[h, zs[k]])
        arrive([b2[h]])
        sb2[h] = add(sb2, sb1[h, :, rows16(x)], rb2[h, 0], rb2[h, 1], rb2[h, 2])
        b3[h] = three("zh", rb3.at[h], lambda k, h=h: sb2.at[h, zs[k]])
        if h == 0:
            arrive([cx3])
            scx3[...] = add(scx3, scx2[y], rcx3[0], rcx3[1], rcx3[2])
            cx4 = send(scx3, rcx4, near)
            arrive([cy3])
            scy3[...] = add(scy3, scy2[...], rcy3[...])
            cy4 = three("x", rcy4, lambda k: scy3)

    for h in range(2):
        arrive([a3[h]])
        sa3[h] = add(sa3, sa2[h, zh], ra3[h, 0], ra3[h, 1], ra3[h, 2])
        a4[h] = send(sa3.at[h], ra4.at[h], near)
        arrive([b3[h]])
        sb3[h] = add(sb3, sb2[h, zh], rb3[h, 0], rb3[h, 1], rb3[h, 2])
        b4[h] = send(sb3.at[h], rb4.at[h], near)
        if h == 0:
            arrive([cx4])
            final_x[x] = add(final_x, scx3[...], rcx4[...])
            spread = [send(final_x.at[x], final_x.at[x], device(moved(at, x=k))) for k in (1, 2, 3)]
            arrive([cy4])
            final_y[...] = add(final_y, scy3[...], rcy4[0], rcy4[1], rcy4[2])
    for h in range(2):
        arrive([a4[h]])
        final[x, 0, h] = add(final, sa3[h], ra4[h])
        arrive([b4[h]])
        final[x, 1, h] = add(final, sb3[h], rb4[h])
    spread += [send(final.at[x], final.at[x], device(moved(at, x=k))) for k in (1, 2, 3)]
    arrive(spread)
    send.finish()


def finish_kernel(seq_i, final, final_x, final_y, seq_o, conv_o, dna_o, qkv_o, out_o):
    seq_o[0] = seq_i[...]
    for h in range(2):
        columns = slice(384 * h, 384 * h + 384)
        for q in range(4):
            conv_o[16 * q : 16 * q + 16, columns] = final[q, 0, h].astype(F32)
        conv_o[64:80, columns] = final[0, 1, h].astype(F32)
        conv_o[80:96, columns] = final[1, 1, h].astype(F32)
        dna_o[:, columns] = final[2, 1, h].astype(F32)
        out_o[:, columns] = final[3, 1, h].astype(F32)
    for q in range(4):
        qkv_o[0:16, 384 * q : 384 * q + 384] = final_x[q].astype(F32)
    last_rows = final_y[...].astype(F32)
    qkv_o[16:24, 0:768] = last_rows[0:8]
    qkv_o[16:24, 768:1536] = last_rows[8:16]


def layer(*operands):
    vmem = pl.BlockSpec(memory_space=pltpu.VMEM)
    low = [
        (4, 4, 2, 4, 16, 1152), (4, 4, 2, 80, 768), (16, 768), (16, 768),
        (4, 128, 768), (4, 4, 2, 96, 128), (128, 512), (4, 4, 2, 16, 128), (768, 512), (768, 512),
        (128, 512), (128, 512), (4, 4, 2, 16, 128), (4, 4, 2, 16, 128), (128, 1536), (128, 512), (4, 4, 2, 16, 128),
        (4, 128, 512),
        (4, 128, 512), (4, 128, 128), (4, 128, 128), (4, 128, 512), (4, 128, 128), (4, 128, 128),
        (4, 128, 512), (4, 128, 128), (4, 128, 128),
        (4, 128, 1024), (4, 128, 1024),
    ] + 3 * [(4, 4, 64, 768), (4, 4, 64, 768), (4, 4, 4, 16, 384), (4, 4, 16, 768)] + [
        (2, 2, 2, 4, 16, 384), (2, 2, 4, 4, 16, 384), (2, 4, 4, 16, 384), (2, 3, 4, 16, 384),
        (2, 4, 16, 384), (2, 3, 16, 384), (2, 16, 384), (2, 16, 384),
        (2, 2, 2, 64, 384), (2, 2, 4, 64, 384), (2, 4, 64, 384), (2, 3, 4, 16, 384),
        (2, 4, 16, 384), (2, 3, 16, 384), (2, 16, 384), (2, 16, 384),
        (2, 2, 4, 16, 384), (2, 4, 4, 16, 384), (4, 4, 16, 384), (3, 4, 16, 384), (4, 16, 384), (3, 16, 384), (16, 384), (16, 384),
        (2, 2, 16, 768), (2, 4, 16, 768), (4, 16, 768), (3, 16, 768), (16, 768), (16, 768), (16, 768), (3, 16, 768),
    ]
    wide = [(128, 768), (128, 768), (128, 1), (6, 272, 128), (4, 128, 1024), (2, 6, 8, 128), (6, 8, 128), (6, 8, 128)]
    results = pl.pallas_call(
        layer_kernel,
        name="layer",
        out_shape=tuple(
            jax.ShapeDtypeStruct(shape, BF16)
            for shape in ((256, 768), (4, 2, 2, 16, 384), (4, 16, 384), (16, 768))
        ),
        in_specs=[vmem] * 7,
        out_specs=(vmem,) * 4,
        scratch_shapes=[pltpu.VMEM(shape, BF16) for shape in low]
        + [pltpu.VMEM(shape, F32) for shape in wide]
        + [pltpu.SemaphoreType.DMA((90,)), pltpu.SemaphoreType.DMA((135,))],
        compiler_params=pltpu.CompilerParams(
            collective_id=1, has_side_effects=True, vmem_limit_bytes=60 * 2**20
        ),
    )(*operands)
    return pl.pallas_call(
        finish_kernel,
        name="finish",
        out_shape=(
            jax.ShapeDtypeStruct((1, 256, 768), BF16),
            jax.ShapeDtypeStruct((96, 768), F32),
            jax.ShapeDtypeStruct((16, 768), F32),
            jax.ShapeDtypeStruct((24, 1536), F32),
            jax.ShapeDtypeStruct((16, 768), F32),
        ),
        in_specs=[vmem] * 4,
        out_specs=(vmem,) * 5,
    )(*results)


def per_device(seq_in, bases, conv_weight, dna_weight, qkv_weight, out_weight, cotangent):
    return layer(
        conv_weight, dna_weight, qkv_weight, out_weight, seq_in[0], bases[0].reshape(128, BIN), cotangent[0]
    )


def solution(mesh):
    in_specs = (
        P("dp", "seq", None),
        P("dp", "seq"),
        P("dp", None),
        P("dp", None),
        P("dp", None),
        P("dp", None),
        P("dp", "seq", None),
    )
    out_specs = (P("dp", "seq", None), P("dp", None), P("dp", None), P("dp", None), P("dp", None))
    return jax.shard_map(
        per_device, mesh=mesh, in_specs=in_specs, out_specs=out_specs, check_vma=False
    )
```

```python
import math

import jax
import jax.numpy as jnp
from jax import lax
from jax.experimental import pallas as pl
from jax.experimental.pallas import tpu as pltpu
from jax.sharding import PartitionSpec as P

H = 4
BIN = 128
BF16 = jnp.bfloat16
F32 = jnp.float32
MESH = pl.DeviceIdType.MESH
epsilon = 1e-06

SIZES = {"zh": 4, "y": 4, "c": 2, "zl": 2, "x": 4}
PEERS = [(a, k) for a in ("zh", "y", "x") for k in (1, 2, 3)] + [("zl", 1), ("c", 1)]


def here():
    dp = lax.axis_index("dp")
    sq = lax.axis_index("seq")
    return {"zh": dp // 8, "y": lax.rem(dp // 2, 4), "c": lax.rem(dp, 2), "zl": sq // 4, "x": lax.rem(sq, 4)}


def moved(at, **steps):
    to = dict(at)
    for axis, step in steps.items():
        to[axis] = lax.rem(at[axis] + step, SIZES[axis])
    return to


def device(at):
    return (at["zh"] * 8 + at["y"] * 2 + at["c"], at["zl"] * 4 + at["x"])


class Sender:
    def __init__(self, send_sems, recv_sems):
        self.send_sems, self.recv_sems, self.sent, self.due, self.copies = send_sems, recv_sems, 0, 0, []

    def copy(self, src, dst, to, recv):
        copy = pltpu.make_async_remote_copy(
            src_ref=src,
            dst_ref=dst,
            send_sem=self.send_sems.at[self.sent],
            recv_sem=self.recv_sems.at[recv],
            device_id=to,
            device_id_type=MESH,
        )
        copy.start()
        self.sent += 1
        self.copies.append(copy)
        return copy

    def __call__(self, src, dst, to):
        self.due += 1
        return self.copy(src, dst, to, self.due - 1)

    def group(self, whole, copies):
        self.due += 1
        for src, dst, to in copies:
            self.copy(src, dst, to, self.due - 1)
        return pltpu.make_async_remote_copy(
            src_ref=whole,
            dst_ref=whole,
            send_sem=self.send_sems.at[0],
            recv_sem=self.recv_sems.at[self.due - 1],
            device_id=copies[0][2],
            device_id_type=MESH,
        )

    def finish(self):
        for copy in self.copies:
            copy.wait_send()
        self.sent, self.copies = 0, []


def arrive(copies):
    for copy in copies:
        copy.wait_recv()


def rows16(index, base=0):
    return pl.ds(pl.multiple_of(index * 16 + base, 16), 16)


def half_columns(index):
    return pl.ds(pl.multiple_of(index * 384, 128) if not isinstance(index, int) else index * 384, 384)


def right_dot(left, right):
    return lax.dot_general(left, right, (((1,), (1,)), ((), ())), preferred_element_type=F32)


def row_dot(left, right):
    return lax.dot_general(left, right, (((0,), (0,)), ((), ())), preferred_element_type=F32)


def dot(left, right):
    return jnp.dot(left, right, preferred_element_type=F32)


def add(target, *terms):
    total = terms[0].astype(F32)
    for term in terms[1:]:
        total += term.astype(F32)
    return total.astype(target.dtype)


def loop(n, body):
    def step(i, carry):
        body(i)
        return carry

    lax.fori_loop(0, n, step, 0)


class Ring:
    def __init__(self, send, at, axis, region):
        self.send, self.me, self.region = send, at[axis], region
        self.right, self.left = device(moved(at, **{axis: 1})), device(moved(at, **{axis: 3}))

    def at(self, step):
        return lax.rem(self.me + step, 4)

    def go(self, index, part, to):
        ref = self.region(index, part)
        return [self.send(ref, ref, to)]

    def start(self):
        self.from_left = self.go(self.me, None, self.right)
        self.from_right = self.go(self.me, None, self.left)

    def left_in(self):
        arrive(self.from_left)
        self.far_left = self.go(self.at(3), 0, self.right)

    def right_in(self):
        arrive(self.from_right)
        self.far_right = self.go(self.at(1), 1, self.left)

    def both_in(self):
        self.left_in()
        self.right_in()

    def far_in(self):
        arrive(self.far_left)
        arrive(self.far_right)


def layer_kernel(
    conv_s, dna_s, qkv_s, out_s, rows_in, letters, upstream,
    seq_o, final, final_x, final_y,
    ga, gb, before, after,
    taps, taps_t, onehot, onehot_t, choose_x, choose_y, wide_x, wide_y, wide_xt, wide_yt, d_proj, attended, attended_t,
    mine, got, got_k, got_v, outgo, outgo_k, outgo_v, back, back_k, back_v, probs_s, scores_s,
    pa_s, pb_s, px_s, py_s, pa, pb, px, py, pa_r, pb_r, px_r, py_r,
    fa, na, sa1, ra2, sa2, ra3, sa3, ra4,
    fb, nb, sb1, rb2, sb2, rb3, sb3, rb4,
    fcx, ncx, scx1, rcx2, scx2, rcx3, scx3, rcx4,
    fcy, ncy, scy1, rcy2, scy2, rcy3, scy3, rcy4,
    slope, unit, inverse, rows_f, probs_f, rim_out, rim_before, rim_after,
    send_sems, recv_sems,
):
    at = here()
    zh, y, c, zl, x = (at[a] for a in ("zh", "y", "c", "zl", "x"))
    sq = lax.axis_index("seq")
    dp = lax.axis_index("dp")
    behind, ahead = (dp, lax.rem(sq + 7, 8)), (dp, lax.rem(sq + 1, 8))
    sibling = device(moved(at, c=1))
    near = device(moved(at, zl=1))
    across = [moved(at, x=k, zl=1) for k in range(4)]
    everyone = [device(moved(at, **{a: k})) for a, k in PEERS] + [behind, ahead]
    everyone += [device(p) for p in across[1:]]
    barrier = pltpu.get_barrier_semaphore()
    for one in everyone:
        pl.semaphore_signal(barrier, inc=1, device_id=one, device_id_type=MESH)
    xs = [lax.rem(x + k, 4) for k in range(4)]
    ys = [lax.rem(y + k, 4) for k in range(4)]
    zs = [lax.rem(zh + k, 4) for k in range(4)]

    quarter = rows16(x)
    ga[zh, y, c, x, :, 0:768] = conv_s[quarter]
    ga[zh, y, c, x, :, 768:1152] = qkv_s[0:16, half_columns(x)]
    gb[zh, y, c, 0:32] = conv_s[64:96]
    gb[zh, y, c, 32:48] = dna_s[...]
    gb[zh, y, c, 48:64] = out_s[...]
    last_rows = [qkv_s[:, 768 * i : 768 * i + 768].astype(F32)[16:24] for i in range(2)]
    gb[zh, y, c, 64:80] = jnp.concatenate(last_rows, axis=0).astype(BF16)
    pl.semaphore_wait(barrier, len(everyone))

    send = Sender(send_sems, recv_sems)

    def ref_a(height, step, index, part=None):
        rows = pl.ds(0, 4) if part is None else pl.ds(2 * part, 2)
        return ga.at[rows if height is None else height, step, c, index]

    def ref_b(height, step, part=None):
        return gb.at[height, step, c] if part is None else gb.at[height, step, c, :, half_columns(part)]

    core = []

    def pass_on(ref):
        core.append(send(ref, ref, sibling))

    def pass_a(step):
        pass_on(ga.at[:, step, c])

    def pass_b(height):
        pass_on(gb.at[height, :, c])

    a1 = []
    for k in (2, 1, 3):
        a1.append(send(ref_a(zh, y, x), ref_a(zh, y, x), device(moved(at, zh=k))))
    halo = [
        send(rows_in.at[pl.ds(240, 16)], before, ahead),
        send(rows_in.at[pl.ds(0, 16)], after, behind),
    ]
    ring_z = Ring(send, at, "zh", lambda index, part: ref_b(index, y, part))
    rings_y = [Ring(send, at, "y", lambda index, part, v=zs[k]: ref_b(v, index, part)) for k in range(4)]
    rings_x = [Ring(send, at, "x", lambda index, part, v=ys[k]: ref_a(None, v, index, part)) for k in range(4)]
    ring_a = Ring(send, at, "y", lambda index, part: ref_a(None, index, x, part))
    ring_z.start()
    rings_y[0].start()
    row = lax.broadcasted_iota(jnp.int32, (128, 512), 0)
    column = lax.broadcasted_iota(jnp.int32, (128, 512), 1)
    repeat = (column // 4 == row).astype(F32).astype(BF16)
    repeated = dot(letters[...].astype(F32).astype(BF16), repeat)
    onehot[...] = (repeated == lax.rem(column, 4).astype(F32)).astype(F32).astype(BF16)
    arrive(a1)
    ring_a.start()
    rings_x[0].start()
    ring_z.left_in()
    rings_y[3].start()
    ring_z.right_in()
    rings_y[0].both_in()
    ring_a.left_in()
    rings_x[3].start()
    ring_a.right_in()
    rings_x[1].start()
    rings_y[1].start()
    rings_x[0].both_in()
    ring_a.far_in()
    rings_x[2].start()
    ring_z.far_in()
    rings_y[2].start()
    rings_y[3].both_in()
    rings_x[3].both_in()
    rings_x[1].both_in()
    rings_y[1].both_in()
    rings_y[0].far_in()
    pass_b(zs[0])
    rings_x[0].far_in()
    pass_a(ys[0])
    rings_x[2].both_in()
    rings_y[2].both_in()

    arrive(halo)
    for j in range(6):
        lanes = slice(128 * j, 128 * j + 128)
        rows_f[j, 8:264] = rows_in[:, lanes].astype(F32)
        rows_f[j, 0:8] = jnp.where(sq > 0, before[:, lanes].astype(F32)[8:16], 0.0)
        rows_f[j, 264:272] = jnp.where(sq < 7, after[:, lanes].astype(F32)[0:8], 0.0)
        for i in range(4):
            taps[i, :, lanes] = rows_f[j, pl.ds(7 + i, 128, stride=2)].astype(BF16)

    rings_y[3].far_in()
    pass_b(zs[3])
    rings_y[1].far_in()
    pass_b(zs[1])
    rings_x[3].far_in()
    pass_a(ys[3])
    rings_x[1].far_in()
    pass_a(ys[1])
    rings_y[2].far_in()
    pass_b(zs[2])
    rings_x[2].far_in()
    pass_a(ys[2])

    def transpose_tap(i):
        taps_t[i] = taps[i].T.reshape(4, 2, 96, 128)

    loop(4, transpose_tap)
    onehot_t[...] = onehot[...].T.reshape(4, 4, 2, 16, 128)
    row = lax.broadcasted_iota(jnp.int32, (768, 512), 0)
    column = lax.broadcasted_iota(jnp.int32, (768, 512), 1)
    first_row = column // 16 * 24
    choose_x[...] = (first_row + lax.rem(column, 16) == row).astype(F32).astype(BF16)
    choose_y[...] = (first_row + 16 + lax.rem(column, 8) == row).astype(F32).astype(BF16)
    arrive(core[:-1])

    def conv_full(i):
        first = ga[i, :, :, :, :, 0:768].reshape(4, 2, 64, 768)
        return jnp.concatenate([first, gb[i, :, :, 0:32]], axis=2).reshape(768, 768)

    def qx_full(i):
        return jnp.concatenate(
            [ga[:, :, :, 2 * i + j, :, 768:1152].reshape(512, 384) for j in range(2)], axis=1
        )

    def qy_full():
        return gb[:, :, :, 64:80].reshape(512, 768)

    dna_full = gb[:, :, :, 32:48].reshape(512, 768)
    out_full = gb[:, :, :, 48:64].reshape(512, 768)
    d_attend = right_dot(upstream[...], out_full).astype(BF16)
    slope[...] = dot(onehot[...], dna_full)
    arrive(core[-1:])

    def one_tap(i):
        slope[...] += dot(taps[i], conv_full(i))

    loop(4, one_tap)
    pre = slope[...]
    bend = jnp.tanh(math.sqrt(2.0 / math.pi) * (pre + 0.044715 * (pre * pre * pre)))
    share = 0.5 * (1.0 + bend)
    feature = (pre * share).astype(BF16).astype(F32)
    slope[...] = share + pre * (0.5 * (1.0 - bend * bend)) * (
        math.sqrt(2.0 / math.pi) * (1.0 + 3.0 * 0.044715 * (pre * pre))
    )
    scale = lax.rsqrt(jnp.mean(feature * feature, axis=1, keepdims=True) + epsilon)
    inverse[...] = scale
    unit[...] = feature * scale
    normed = unit[...].astype(BF16)
    wide_x[...] = dot(normed, choose_x[...]).astype(BF16)
    wide_y[...] = dot(normed, choose_y[...]).astype(BF16)
    side_of = lax.rem(lax.broadcasted_iota(jnp.int32, (128, 512), 1), 16) // 8
    for i in range(2):
        own_y = jnp.where(side_of == i, wide_y[...].astype(F32), 0.0).astype(BF16)
        projected = (dot(wide_x[...], qx_full(i)) + dot(own_y, qy_full())).astype(BF16)
        for piece in range(6):
            kind, head = divmod(6 * i + piece, 4)
            mine[head, (1, 0, 2)[kind]] = projected[:, 128 * piece : 128 * piece + 128]
    for head in range(H):
        mine[head, 3] = d_attend[:, 128 * head : 128 * head + 128]

    kq, vd = pl.ds(0, 2), pl.ds(2, 2)
    kq_in, vd_in = {}, {}
    from_near_k = send.group(got_k, [(mine.at[x, 0], got_k.at[x], near)])
    near_k = send.due - 1
    from_near_v = send.group(got_v, [(mine.at[x, 2], got_v.at[x], near)])
    near_v = send.due - 1
    for k in (1, 3, 2):
        kq_in[k] = send(mine.at[xs[k], kq], got.at[x, kq], device(moved(at, x=k)))
    for k in (1, 3, 2):
        vd_in[k] = send(mine.at[xs[k], vd], got.at[x, vd], device(moved(at, x=k)))
    sources = {k: lax.rem(x + 4 - k, 4) for k in (0, 1, 3, 2)}
    got[x] = mine[x]
    for k in (1, 3, 2):
        arrive([kq_in[k]])
        send.copy(got.at[sources[k], 0], got_k.at[sources[k]], near, near_k)
    wide_xt[...] = wide_x[...].T.reshape(4, 4, 2, 16, 128)
    wide_yt[...] = wide_y[...].T.reshape(4, 4, 2, 16, 128)
    arrive([from_near_k])
    keys = jnp.concatenate([got[:, 0].reshape(512, 128), got_k[...].reshape(512, 128)], axis=0)
    scaling = 1.0 / math.sqrt(128)

    def soft(source):
        scores = right_dot(got[source, 1], keys) * scaling
        powers = jnp.exp(scores - jnp.max(scores, axis=1, keepdims=True))
        probs = powers * (1.0 / jnp.sum(powers, axis=1, keepdims=True))
        probs_f[source] = probs
        probs_s[source] = probs.astype(BF16)

    def pass_v(k):
        arrive([vd_in[k]])
        send.copy(got.at[sources[k], 2], got_v.at[sources[k]], near, near_v)

    soft(sources[0])
    pass_v(1)
    pass_v(3)
    soft(sources[1])
    soft(sources[3])
    pass_v(2)
    soft(sources[2])
    home = []
    all_queries = got[:, 1].reshape(512, 128)
    all_upward = got[:, 3].reshape(512, 128)
    all_probs = probs_s[...].reshape(512, 1024)
    d_values = row_dot(all_upward, all_probs).T.astype(BF16).reshape(8, 128, 128)
    outgo_v[...] = d_values[4:8]
    home.append(send.group(back_v, [(outgo_v.at[p["x"]], back_v.at[x], device(p)) for p in across]))
    outgo[:, 1] = d_values[0:4]
    arrive([from_near_v])
    values = jnp.concatenate([got[:, 2].reshape(512, 128), got_v[...].reshape(512, 128)], axis=0)
    outgo[:, 0] = dot(all_probs, values).astype(BF16).reshape(4, 128, 128)
    for k in (1, 3, 2):
        block = pl.ds(0, 2)
        home.append(send(outgo.at[xs[k], block], back.at[x, block], device(moved(at, x=k))))
    for k in (1, 3, 2, 0):
        i = xs[k]
        probs = probs_f[i]
        d_probs = right_dot(got[i, 3], values)
        inner = jnp.sum(probs * d_probs, axis=1, keepdims=True)
        d_scores = (probs * (d_probs - inner) * scaling).astype(BF16)
        scores_s[i] = d_scores
        outgo[i, 2] = dot(d_scores, keys).astype(BF16)
        if k:
            home.append(send(outgo.at[i, 2], back.at[x, 2], device(moved(at, x=k))))

    def key_grads(columns):
        d_keys = row_dot(all_queries, scores_s[:, :, columns].reshape(512, 512)).T
        return d_keys.astype(BF16).reshape(4, 128, 128)

    outgo_k[...] = key_grads(slice(512, 1024))
    home.append(send.group(back_k, [(outgo_k.at[p["x"]], back_k.at[x], device(p)) for p in across]))
    outgo[:, 3] = key_grads(slice(0, 512))
    for k in (1, 3, 2):
        home.append(send(outgo.at[xs[k], 3], back.at[x, 3], device(moved(at, x=k))))
    back[x] = outgo[x]
    arrive(home)
    send.finish()
    for head in range(H):
        columns = slice(128 * head, 128 * head + 128)
        attended[:, columns] = back[head, 0]
        d_proj[:, columns] = back[head, 2]
        for start, place, other in ((512, 3, back_k), (1024, 1, back_v)):
            total = back[head, place].astype(F32) + other[head].astype(F32)
            d_proj[:, start + 128 * head : start + 128 * head + 128] = total.astype(BF16)

    attended_t[...] = attended[...].T.reshape(4, 4, 2, 16, 128)
    d_halves = [d_proj[:, 0:768], d_proj[:, 768:1536]]
    row_side = lax.rem(lax.broadcasted_iota(jnp.int32, (256, 768), 0), 16)

    def qkv_grads(parity, to_x, to_y):
        left = wide_xt[:, :, parity].reshape(256, 128)
        for i in range(2):
            block = dot(left, d_halves[i]).astype(BF16)
            for j in range(2):
                to_x[2 * i + j] = block[:, 384 * j : 384 * j + 384].reshape(4, 4, 16, 384)
        left = wide_yt[:, :, parity].reshape(256, 128)
        both = [dot(left, d_half) for d_half in d_halves]
        to_y[...] = jnp.where(row_side < 8, both[0], both[1]).astype(BF16).reshape(4, 4, 16, 768)

    order = (2, 1, 3, 0)
    core_cx, core_cy, core_a, core_b = {}, {}, {}, {}
    qkv_grads(1 - c, px_s, py_s)
    for k in order:
        core_cx[k] = send(px_s.at[:, zs[k]], px_r.at[:, zs[k]], sibling)
        core_cy[k] = send(py_s.at[:, ys[k]], py_r.at[:, ys[k]], sibling)
    qkv_grads(c, px, py)
    d_x = sum(right_dot(d_halves[i], qx_full(i)) for i in range(2))
    both = [right_dot(d_half, qy_full()) for d_half in d_halves]
    d_y = jnp.where(side_of == 0, both[0], both[1])

    def sum_cx(k):
        arrive([core_cx[k]])
        px[:, zs[k]] = add(px, px[:, zs[k]], px_r[:, zs[k]])

    def sum_cy(k):
        arrive([core_cy[k]])
        py[:, ys[k]] = add(py, py[:, ys[k]], py_r[:, ys[k]])

    right_x, left_x = device(moved(at, x=1)), device(moved(at, x=3))
    right_y, left_y = device(moved(at, y=1)), device(moved(at, y=3))
    right_z, left_z = device(moved(at, zh=1)), device(moved(at, zh=3))
    low, high = pl.ds(0, 2), pl.ds(2, 2)
    sides = ((0, 1, right_x, right_y), (1, 3, left_x, left_y))
    d_normed = 0.0
    for terms, choose in ((d_x, choose_x), (d_y, choose_y)):
        d_high = terms.astype(BF16)
        d_low = (terms - d_high.astype(F32)).astype(BF16)
        d_normed += right_dot(d_high, choose[...]) + right_dot(d_low, choose[...])
    d_feature = upstream[...].astype(F32) + inverse[...] * (
        d_normed - unit[...] * jnp.mean(d_normed * unit[...], axis=1, keepdims=True)
    )
    d_pre = (d_feature * slope[...]).astype(BF16)

    sum_cx(2)
    far_cx = [
        send(px.at[quarters, zs[2]], fcx.at[side], to) for side, quarters, to in ((0, low, right_z), (1, high, left_z))
    ]
    sum_cy(2)
    far_cy = [
        send(py.at[heights, ys[2]], fcy.at[side], to) for side, heights, to in ((0, low, right_y), (1, high, left_y))
    ]
    def conv_grads(parity, to_a, to_b):
        def one(i):
            block = dot(taps_t[i, :, parity].reshape(384, 128), d_pre).astype(BF16).reshape(4, 96, 768)
            to_a[i] = block[:, 0:64]
            to_b[i, :, 0:32] = block[:, 64:96]

        loop(4, one)
        left = onehot_t[:, :, parity].reshape(256, 128)
        to_b[:, :, 32:48] = dot(left, d_pre).astype(BF16).reshape(4, 4, 16, 768)
        left = attended_t[:, :, parity].reshape(256, 128)
        to_b[:, :, 48:64] = dot(left, upstream[...]).astype(BF16).reshape(4, 4, 16, 768)

    conv_grads(1 - c, pa_s, pb_s)
    for k in order:
        core_a[k] = send(pa_s.at[:, :, rows16(xs[k])], pa_r.at[:, :, rows16(xs[k])], sibling)
        core_b[k] = send(pb_s.at[:, ys[k]], pb_r.at[:, ys[k]], sibling)
    conv_grads(c, pa, pb)

    def sum_a(k):
        arrive([core_a[k]])
        rows = rows16(xs[k])

        def one(i):
            pa[i, :, rows] = add(pa, pa[i, :, rows], pa_r[i, :, rows])

        loop(4, one)

    def sum_b(k):
        arrive([core_b[k]])

        def one(i):
            pb[i, ys[k]] = add(pb, pb[i, ys[k]], pb_r[i, ys[k]])

        loop(4, one)

    halves = [(h, pl.ds(384 * h, 384), slice(384 * h, 384 * h + 384)) for h in range(2)]
    far_a, far_b = {}, {}
    sum_a(2)
    sum_b(2)
    for h, columns, _ in halves:
        for side, heights, to_x, to_y in ((0, low, right_x, right_y), (1, high, left_x, left_y)):
            far_a[h, side] = send(pa.at[heights, :, rows16(xs[2]), columns], fa.at[h, side], to_x)
            far_b[h, side] = send(pb.at[heights, ys[2], :, columns], fb.at[h, side], to_y)
    near_cx, near_cy = [], []
    for side, k, to_x, to_y in sides:
        sum_cx(k)
        arrive([far_cx[side]])
        part = slice(2 * side, 2 * side + 2)
        px[part, zs[k]] = add(px, px[part, zs[k]], fcx[side])
        near_cx.append(send(px.at[:, zs[k]], ncx.at[side], (right_z, left_z)[side]))
        sum_cy(k)
        arrive([far_cy[side]])
        py[part, ys[k]] = add(py, py[part, ys[k]], fcy[side])
        near_cy.append(send(py.at[:, ys[k]], ncy.at[side], to_y))
    for side, k, to_x, to_y in sides:
        sum_a(k)
        sum_b(k)
    near_a, near_b = {}, {}
    for h, columns, cols in halves:
        for side, k, to_x, to_y in sides:
            rows = rows16(xs[k])
            arrive([far_a[h, side]])

            def join_a(i, h=h, side=side, rows=rows, cols=cols):
                pa[2 * side + i, :, rows, cols] = add(pa, pa[2 * side + i, :, rows, cols], fa[h, side, i])

            loop(2, join_a)
            near_a[h, side] = send(pa.at[:, :, rows, columns], na.at[h, side], to_x)
            arrive([far_b[h, side]])

            def join_b(i, h=h, side=side, index=ys[k], cols=cols):
                pb[2 * side + i, index, :, cols] = add(pb, pb[2 * side + i, index, :, cols], fb[h, side, i])

            loop(2, join_b)
            near_b[h, side] = send(pb.at[:, ys[k], :, columns], nb.at[h, side], to_y)

    def three(axis, whole, source):
        return send.group(
            whole, [(source(k), whole.at[k - 1], device(moved(at, **{axis: k}))) for k in (1, 3, 2)]
        )

    sum_cx(0)
    arrive(near_cx)
    scx1[...] = add(scx1, px[:, zh], ncx[0], ncx[1])
    cx2 = three("x", rcx2, lambda k: scx1.at[xs[k]])
    sum_cy(0)
    arrive(near_cy)
    scy1[...] = add(scy1, py[:, y], ncy[0], ncy[1])
    cy2 = three("zh", rcy2, lambda k: scy1.at[zs[k]])
    sum_a(0)
    sum_b(0)

    rows_f[:, 256:272] = jnp.zeros((6, 16, 128), F32)
    for i in range(4):
        terms = right_dot(d_pre, conv_full(i))
        for j in range(6):
            target = pl.ds(7 + i, 128, stride=2)
            block = terms[:, 128 * j : 128 * j + 128]
            rows_f[j, target] = block if i < 2 else rows_f[j, target] + block
    rim_out[0] = rows_f[:, 264:272]
    rim_out[1] = rows_f[:, 0:8]
    rims = [send(rim_out.at[0], rim_before, ahead), send(rim_out.at[1], rim_after, behind)]

    a2, b2, a3, b3, a4, b4 = {}, {}, {}, {}, {}, {}
    for h, columns, cols in halves:
        arrive([near_a[h, 0], near_a[h, 1]])

        def first_a(i, h=h, cols=cols):
            sa1[h, i] = add(sa1, pa[i, :, rows16(x), cols], na[h, 0, i], na[h, 1, i])

        loop(4, first_a)
        a2[h] = three("y", ra2.at[h], lambda k, h=h: sa1.at[h, :, ys[k]])
        arrive([near_b[h, 0], near_b[h, 1]])

        def first_b(i, h=h, cols=cols):
            sb1[h, i] = add(sb1, pb[i, y, :, cols], nb[h, 0, i], nb[h, 1, i])

        loop(4, first_b)
        b2[h] = three("x", rb2.at[h], lambda k, h=h: sb1.at[h, :, rows16(xs[k])])
        if h == 0:
            arrive([cx2])
            scx2[...] = add(scx2, scx1[x], rcx2[0], rcx2[1], rcx2[2])
            cx3 = three("y", rcx3, lambda k: scx2.at[ys[k]])
            arrive([cy2])
            scy2[...] = add(scy2, scy1[zh], rcy2[0], rcy2[1], rcy2[2])
            cy3 = send(scy2, rcy3, near)
    arrive(rims)
    rows_f[:, 8:9] += jnp.where(sq > 0, rim_before[:, 0:1], 0.0)
    rows_f[:, 263:264] += jnp.where(sq < 7, rim_after[:, 7:8], 0.0)
    for j in range(6):
        seq_o[:, 128 * j : 128 * j + 128] = rows_f[j, 8:264].astype(BF16)
    for h in range(2):
        arrive([a2[h]])
        sa2[h] = add(sa2, sa1[h, :, y], ra2[h, 0], ra2[h, 1], ra2[h, 2])
        a3[h] = three("zh", ra3.at[h], lambda k, h=h: sa2.at[h, zs[k]])
        arrive([b2[h]])
        sb2[h] = add(sb2, sb1[h, :, rows16(x)], rb2[h, 0], rb2[h, 1], rb2[h, 2])
        b3[h] = three("zh", rb3.at[h], lambda k, h=h: sb2.at[h, zs[k]])
        if h == 0:
            arrive([cx3])
            scx3[...] = add(scx3, scx2[y], rcx3[0], rcx3[1], rcx3[2])
            cx4 = send(scx3, rcx4, near)
            arrive([cy3])
            scy3[...] = add(scy3, scy2[...], rcy3[...])
            cy4 = three("x", rcy4, lambda k: scy3)

    for h in range(2):
        arrive([a3[h]])
        sa3[h] = add(sa3, sa2[h, zh], ra3[h, 0], ra3[h, 1], ra3[h, 2])
        a4[h] = send(sa3.at[h], ra4.at[h], near)
        arrive([b3[h]])
        sb3[h] = add(sb3, sb2[h, zh], rb3[h, 0], rb3[h, 1], rb3[h, 2])
        b4[h] = send(sb3.at[h], rb4.at[h], near)
        if h == 0:
            arrive([cx4])
            final_x[x] = add(final_x, scx3[...], rcx4[...])
            spread = [send(final_x.at[x], final_x.at[x], device(moved(at, x=k))) for k in (1, 2, 3)]
            arrive([cy4])
            final_y[...] = add(final_y, scy3[...], rcy4[0], rcy4[1], rcy4[2])
    for h in range(2):
        arrive([a4[h]])
        final[x, 0, h] = add(final, sa3[h], ra4[h])
        arrive([b4[h]])
        final[x, 1, h] = add(final, sb3[h], rb4[h])
    spread += [send(final.at[x], final.at[x], device(moved(at, x=k))) for k in (1, 2, 3)]
    arrive(spread)
    send.finish()


def finish_kernel(seq_i, final, final_x, final_y, seq_o, conv_o, dna_o, qkv_o, out_o):
    seq_o[0] = seq_i[...]
    for h in range(2):
        columns = slice(384 * h, 384 * h + 384)
        for q in range(4):
            conv_o[16 * q : 16 * q + 16, columns] = final[q, 0, h].astype(F32)
        conv_o[64:80, columns] = final[0, 1, h].astype(F32)
        conv_o[80:96, columns] = final[1, 1, h].astype(F32)
        dna_o[:, columns] = final[2, 1, h].astype(F32)
        out_o[:, columns] = final[3, 1, h].astype(F32)
    for q in range(4):
        qkv_o[0:16, 384 * q : 384 * q + 384] = final_x[q].astype(F32)
    last_rows = final_y[...].astype(F32)
    qkv_o[16:24, 0:768] = last_rows[0:8]
    qkv_o[16:24, 768:1536] = last_rows[8:16]


def layer(*operands):
    vmem = pl.BlockSpec(memory_space=pltpu.VMEM)
    low = [
        (4, 4, 2, 4, 16, 1152), (4, 4, 2, 80, 768), (16, 768), (16, 768),
        (4, 128, 768), (4, 4, 2, 96, 128), (128, 512), (4, 4, 2, 16, 128), (768, 512), (768, 512),
        (128, 512), (128, 512), (4, 4, 2, 16, 128), (4, 4, 2, 16, 128), (128, 1536), (128, 512), (4, 4, 2, 16, 128),
        (4, 4, 128, 128), (4, 4, 128, 128), (4, 128, 128), (4, 128, 128), (4, 4, 128, 128), (4, 128, 128), (4, 128, 128),
        (4, 4, 128, 128), (4, 128, 128), (4, 128, 128),
        (4, 128, 1024), (4, 128, 1024),
    ] + 3 * [(4, 4, 64, 768), (4, 4, 64, 768), (4, 4, 4, 16, 384), (4, 4, 16, 768)] + [
        (2, 2, 2, 4, 16, 384), (2, 2, 4, 4, 16, 384), (2, 4, 4, 16, 384), (2, 3, 4, 16, 384),
        (2, 4, 16, 384), (2, 3, 16, 384), (2, 16, 384), (2, 16, 384),
        (2, 2, 2, 64, 384), (2, 2, 4, 64, 384), (2, 4, 64, 384), (2, 3, 4, 16, 384),
        (2, 4, 16, 384), (2, 3, 16, 384), (2, 16, 384), (2, 16, 384),
        (2, 2, 4, 16, 384), (2, 4, 4, 16, 384), (4, 4, 16, 384), (3, 4, 16, 384), (4, 16, 384), (3, 16, 384), (16, 384), (16, 384),
        (2, 2, 16, 768), (2, 4, 16, 768), (4, 16, 768), (3, 16, 768), (16, 768), (16, 768), (16, 768), (3, 16, 768),
    ]
    wide = [(128, 768), (128, 768), (128, 1), (6, 272, 128), (4, 128, 1024), (2, 6, 8, 128), (6, 8, 128), (6, 8, 128)]
    results = pl.pallas_call(
        layer_kernel,
        name="layer",
        out_shape=tuple(
            jax.ShapeDtypeStruct(shape, BF16)
            for shape in ((256, 768), (4, 2, 2, 16, 384), (4, 16, 384), (16, 768))
        ),
        in_specs=[vmem] * 7,
        out_specs=(vmem,) * 4,
        scratch_shapes=[pltpu.VMEM(shape, BF16) for shape in low]
        + [pltpu.VMEM(shape, F32) for shape in wide]
        + [pltpu.SemaphoreType.DMA((90,)), pltpu.SemaphoreType.DMA((138,))],
        compiler_params=pltpu.CompilerParams(
            collective_id=1, has_side_effects=True, vmem_limit_bytes=60 * 2**20
        ),
    )(*operands)
    return pl.pallas_call(
        finish_kernel,
        name="finish",
        out_shape=(
            jax.ShapeDtypeStruct((1, 256, 768), BF16),
            jax.ShapeDtypeStruct((96, 768), F32),
            jax.ShapeDtypeStruct((16, 768), F32),
            jax.ShapeDtypeStruct((24, 1536), F32),
            jax.ShapeDtypeStruct((16, 768), F32),
        ),
        in_specs=[vmem] * 4,
        out_specs=(vmem,) * 5,
    )(*results)


def per_device(seq_in, bases, conv_weight, dna_weight, qkv_weight, out_weight, cotangent):
    return layer(
        conv_weight, dna_weight, qkv_weight, out_weight, seq_in[0], bases[0].reshape(128, BIN), cotangent[0]
    )


def solution(mesh):
    in_specs = (
        P("dp", "seq", None),
        P("dp", "seq"),
        P("dp", None),
        P("dp", None),
        P("dp", None),
        P("dp", None),
        P("dp", "seq", None),
    )
    out_specs = (P("dp", "seq", None), P("dp", None), P("dp", None), P("dp", None), P("dp", None))
    return jax.shard_map(
        per_device, mesh=mesh, in_specs=in_specs, out_specs=out_specs, check_vma=False
    )
```

```python
import math

import jax
import jax.numpy as jnp
from jax import lax
from jax.experimental import pallas as pl
from jax.experimental.pallas import tpu as pltpu
from jax.sharding import PartitionSpec as P

H = 4
BIN = 128
BF16 = jnp.bfloat16
F32 = jnp.float32
MESH = pl.DeviceIdType.MESH
epsilon = 1e-06

SIZES = {"zh": 4, "y": 4, "c": 2, "zl": 2, "x": 4}
PEERS = [(a, k) for a in ("zh", "y", "x") for k in (1, 2, 3)] + [("zl", 1), ("c", 1)]


def here():
    dp = lax.axis_index("dp")
    sq = lax.axis_index("seq")
    return {"zh": dp // 8, "y": lax.rem(dp // 2, 4), "c": lax.rem(dp, 2), "zl": sq // 4, "x": lax.rem(sq, 4)}


def moved(at, **steps):
    to = dict(at)
    for axis, step in steps.items():
        to[axis] = lax.rem(at[axis] + step, SIZES[axis])
    return to


def device(at):
    return (at["zh"] * 8 + at["y"] * 2 + at["c"], at["zl"] * 4 + at["x"])


class Sender:
    def __init__(self, send_sems, recv_sems):
        self.send_sems, self.recv_sems, self.sent, self.due = send_sems, recv_sems, 0, 0
        self.free, self.copies = [], []

    def copy(self, src, dst, to, recv):
        if not self.free:
            self.free.append(self.sent)
            self.sent += 1
        place = self.free.pop(0)
        copy = pltpu.make_async_remote_copy(
            src_ref=src,
            dst_ref=dst,
            send_sem=self.send_sems.at[place],
            recv_sem=self.recv_sems.at[recv],
            device_id=to,
            device_id_type=MESH,
        )
        copy.start()
        self.copies.append((copy, place))
        return copy

    def __call__(self, src, dst, to):
        self.due += 1
        return self.copy(src, dst, to, self.due - 1)

    def group(self, whole, copies):
        self.due += 1
        for src, dst, to in copies:
            self.copy(src, dst, to, self.due - 1)
        return pltpu.make_async_remote_copy(
            src_ref=whole,
            dst_ref=whole,
            send_sem=self.send_sems.at[0],
            recv_sem=self.recv_sems.at[self.due - 1],
            device_id=copies[0][2],
            device_id_type=MESH,
        )

    def finish(self, oldest=None):
        done = self.copies[:oldest]
        for copy, place in done:
            copy.wait_send()
            self.free.append(place)
        self.copies = self.copies[len(done) :]


def arrive(copies):
    for copy in copies:
        copy.wait_recv()


def rows16(index, base=0):
    return pl.ds(pl.multiple_of(index * 16 + base, 16), 16)


def half_columns(index):
    return pl.ds(pl.multiple_of(index * 384, 128) if not isinstance(index, int) else index * 384, 384)


def right_dot(left, right):
    return lax.dot_general(left, right, (((1,), (1,)), ((), ())), preferred_element_type=F32)


def row_dot(left, right):
    return lax.dot_general(left, right, (((0,), (0,)), ((), ())), preferred_element_type=F32)


def dot(left, right):
    return jnp.dot(left, right, preferred_element_type=F32)


def add(target, *terms):
    total = terms[0].astype(F32)
    for term in terms[1:]:
        total += term.astype(F32)
    return total.astype(target.dtype)


def loop(n, body):
    def step(i, carry):
        body(i)
        return carry

    lax.fori_loop(0, n, step, 0)


class Ring:
    def __init__(self, send, at, axis, region):
        self.send, self.me, self.region = send, at[axis], region
        self.right, self.left = device(moved(at, **{axis: 1})), device(moved(at, **{axis: 3}))

    def at(self, step):
        return lax.rem(self.me + step, 4)

    def go(self, index, part, to):
        ref = self.region(index, part)
        return [self.send(ref, ref, to)]

    def start(self):
        self.from_left = self.go(self.me, None, self.right)
        self.from_right = self.go(self.me, None, self.left)

    def left_in(self):
        arrive(self.from_left)
        self.far_left = self.go(self.at(3), 0, self.right)

    def right_in(self):
        arrive(self.from_right)
        self.far_right = self.go(self.at(1), 1, self.left)

    def both_in(self):
        self.left_in()
        self.right_in()

    def far_in(self):
        arrive(self.far_left)
        arrive(self.far_right)


def layer_kernel(
    conv_s, dna_s, qkv_s, out_s, rows_in, letters, upstream,
    seq_o, final, final_x, final_y,
    ga, gb, before, after,
    taps, taps_t, onehot, onehot_t, choose_x, choose_y, wide_x, wide_y, wide_xt, wide_yt, d_proj, attended, attended_t,
    mine, got, got_k, got_v, outgo, outgo_k, outgo_v, back, back_k, back_v, probs_s, scores_s,
    pa_s, pb_s, px_s, py_s, pa, pb, px, py, pa_r, pb_r, px_r, py_r,
    fa, na, sa1, ra2, sa2, ra3, sa3, ra4,
    fb, nb, sb1, rb2, sb2, rb3, sb3, rb4,
    fcx, ncx, scx1, rcx2, scx2, rcx3, scx3, rcx4,
    fcy, ncy, scy1, rcy2, scy2, rcy3, scy3, rcy4,
    slope, unit, inverse, rows_f, probs_f, rim_out, rim_before, rim_after,
    send_sems, recv_sems,
):
    at = here()
    zh, y, c, zl, x = (at[a] for a in ("zh", "y", "c", "zl", "x"))
    sq = lax.axis_index("seq")
    dp = lax.axis_index("dp")
    behind, ahead = (dp, lax.rem(sq + 7, 8)), (dp, lax.rem(sq + 1, 8))
    sibling = device(moved(at, c=1))
    near = device(moved(at, zl=1))
    across = [moved(at, x=k, zl=1) for k in range(4)]
    everyone = [device(moved(at, **{a: k})) for a, k in PEERS] + [behind, ahead]
    everyone += [device(p) for p in across[1:]]
    barrier = pltpu.get_barrier_semaphore()
    for one in everyone:
        pl.semaphore_signal(barrier, inc=1, device_id=one, device_id_type=MESH)
    xs = [lax.rem(x + k, 4) for k in range(4)]
    ys = [lax.rem(y + k, 4) for k in range(4)]
    zs = [lax.rem(zh + k, 4) for k in range(4)]

    quarter = rows16(x)
    ga[zh, y, c, x, :, 0:768] = conv_s[quarter]
    ga[zh, y, c, x, :, 768:1152] = qkv_s[0:16, half_columns(x)]
    gb[zh, y, c, 0:32] = conv_s[64:96]
    gb[zh, y, c, 32:48] = dna_s[...]
    gb[zh, y, c, 48:64] = out_s[...]
    last_rows = [qkv_s[:, 768 * i : 768 * i + 768].astype(F32)[16:24] for i in range(2)]
    gb[zh, y, c, 64:80] = jnp.concatenate(last_rows, axis=0).astype(BF16)
    pl.semaphore_wait(barrier, len(everyone))

    send = Sender(send_sems, recv_sems)

    def ref_a(height, step, index, part=None):
        rows = pl.ds(0, 4) if part is None else pl.ds(2 * part, 2)
        return ga.at[rows if height is None else height, step, c, index]

    def ref_b(height, step, part=None):
        return gb.at[height, step, c] if part is None else gb.at[height, step, c, :, half_columns(part)]

    core = []

    def pass_on(ref):
        core.append(send(ref, ref, sibling))

    def pass_a(step):
        pass_on(ga.at[:, step, c])

    def pass_b(height):
        pass_on(gb.at[height, :, c])

    a1 = []
    for k in (2, 1, 3):
        a1.append(send(ref_a(zh, y, x), ref_a(zh, y, x), device(moved(at, zh=k))))
    halo = [
        send(rows_in.at[pl.ds(240, 16)], before, ahead),
        send(rows_in.at[pl.ds(0, 16)], after, behind),
    ]
    ring_z = Ring(send, at, "zh", lambda index, part: ref_b(index, y, part))
    rings_y = [Ring(send, at, "y", lambda index, part, v=zs[k]: ref_b(v, index, part)) for k in range(4)]
    rings_x = [Ring(send, at, "x", lambda index, part, v=ys[k]: ref_a(None, v, index, part)) for k in range(4)]
    ring_a = Ring(send, at, "y", lambda index, part: ref_a(None, index, x, part))
    ring_z.start()
    rings_y[0].start()
    row = lax.broadcasted_iota(jnp.int32, (128, 512), 0)
    column = lax.broadcasted_iota(jnp.int32, (128, 512), 1)
    repeat = (column // 4 == row).astype(F32).astype(BF16)
    repeated = dot(letters[...].astype(F32).astype(BF16), repeat)
    onehot[...] = (repeated == lax.rem(column, 4).astype(F32)).astype(F32).astype(BF16)
    arrive(a1)
    ring_a.start()
    rings_x[0].start()
    ring_z.left_in()
    rings_y[3].start()
    ring_z.right_in()
    rings_y[0].both_in()
    ring_a.left_in()
    rings_x[3].start()
    ring_a.right_in()
    rings_x[1].start()
    rings_y[1].start()
    rings_x[0].both_in()
    ring_a.far_in()
    rings_x[2].start()
    ring_z.far_in()
    rings_y[2].start()
    rings_y[3].both_in()
    rings_x[3].both_in()
    rings_x[1].both_in()
    rings_y[1].both_in()
    rings_y[0].far_in()
    pass_b(zs[0])
    rings_x[0].far_in()
    pass_a(ys[0])
    rings_x[2].both_in()
    rings_y[2].both_in()

    send.finish(24)
    arrive(halo)
    for j in range(6):
        lanes = slice(128 * j, 128 * j + 128)
        rows_f[j, 8:264] = rows_in[:, lanes].astype(F32)
        rows_f[j, 0:8] = jnp.where(sq > 0, before[:, lanes].astype(F32)[8:16], 0.0)
        rows_f[j, 264:272] = jnp.where(sq < 7, after[:, lanes].astype(F32)[0:8], 0.0)
        for i in range(4):
            taps[i, :, lanes] = rows_f[j, pl.ds(7 + i, 128, stride=2)].astype(BF16)

    rings_y[3].far_in()
    pass_b(zs[3])
    rings_y[1].far_in()
    pass_b(zs[1])
    rings_x[3].far_in()
    pass_a(ys[3])
    rings_x[1].far_in()
    pass_a(ys[1])
    rings_y[2].far_in()
    pass_b(zs[2])
    rings_x[2].far_in()
    pass_a(ys[2])

    def transpose_tap(i):
        taps_t[i] = taps[i].T.reshape(4, 2, 96, 128)

    loop(4, transpose_tap)
    onehot_t[...] = onehot[...].T.reshape(4, 4, 2, 16, 128)
    row = lax.broadcasted_iota(jnp.int32, (768, 512), 0)
    column = lax.broadcasted_iota(jnp.int32, (768, 512), 1)
    first_row = column // 16 * 24
    choose_x[...] = (first_row + lax.rem(column, 16) == row).astype(F32).astype(BF16)
    choose_y[...] = (first_row + 16 + lax.rem(column, 8) == row).astype(F32).astype(BF16)
    arrive(core[:-1])

    def conv_full(i):
        first = ga[i, :, :, :, :, 0:768].reshape(4, 2, 64, 768)
        return jnp.concatenate([first, gb[i, :, :, 0:32]], axis=2).reshape(768, 768)

    def qx_full(i):
        return jnp.concatenate(
            [ga[:, :, :, 2 * i + j, :, 768:1152].reshape(512, 384) for j in range(2)], axis=1
        )

    def qy_full():
        return gb[:, :, :, 64:80].reshape(512, 768)

    dna_full = gb[:, :, :, 32:48].reshape(512, 768)
    out_full = gb[:, :, :, 48:64].reshape(512, 768)
    d_attend = right_dot(upstream[...], out_full).astype(BF16)
    slope[...] = dot(onehot[...], dna_full)
    arrive(core[-1:])

    def one_tap(i):
        slope[...] += dot(taps[i], conv_full(i))

    loop(4, one_tap)
    pre = slope[...]
    bend = jnp.tanh(math.sqrt(2.0 / math.pi) * (pre + 0.044715 * (pre * pre * pre)))
    share = 0.5 * (1.0 + bend)
    feature = (pre * share).astype(BF16).astype(F32)
    slope[...] = share + pre * (0.5 * (1.0 - bend * bend)) * (
        math.sqrt(2.0 / math.pi) * (1.0 + 3.0 * 0.044715 * (pre * pre))
    )
    scale = lax.rsqrt(jnp.mean(feature * feature, axis=1, keepdims=True) + epsilon)
    inverse[...] = scale
    unit[...] = feature * scale
    normed = unit[...].astype(BF16)
    wide_x[...] = dot(normed, choose_x[...]).astype(BF16)
    wide_y[...] = dot(normed, choose_y[...]).astype(BF16)
    side_of = lax.rem(lax.broadcasted_iota(jnp.int32, (128, 512), 1), 16) // 8
    own_y = [jnp.where(side_of == i, wide_y[...].astype(F32), 0.0).astype(BF16) for i in range(2)]
    from_y = dot(jnp.concatenate(own_y, axis=0), qy_full())
    for i in range(2):
        projected = (dot(wide_x[...], qx_full(i)) + from_y[128 * i : 128 * i + 128]).astype(BF16)
        for piece in range(6):
            kind, head = divmod(6 * i + piece, 4)
            mine[head, (1, 0, 2)[kind]] = projected[:, 128 * piece : 128 * piece + 128]
    for head in range(H):
        mine[head, 3] = d_attend[:, 128 * head : 128 * head + 128]

    kq, vd = pl.ds(0, 2), pl.ds(2, 2)
    kq_in, vd_in = {}, {}
    from_near_k = send.group(got_k, [(mine.at[x, 0], got_k.at[x], near)])
    near_k = send.due - 1
    from_near_v = send.group(got_v, [(mine.at[x, 2], got_v.at[x], near)])
    near_v = send.due - 1
    for k in (1, 3, 2):
        kq_in[k] = send(mine.at[xs[k], kq], got.at[x, kq], device(moved(at, x=k)))
    for k in (1, 3, 2):
        vd_in[k] = send(mine.at[xs[k], vd], got.at[x, vd], device(moved(at, x=k)))
    sources = {k: lax.rem(x + 4 - k, 4) for k in (0, 1, 3, 2)}
    got[x] = mine[x]
    for k in (1, 3, 2):
        arrive([kq_in[k]])
        send.copy(got.at[sources[k], 0], got_k.at[sources[k]], near, near_k)
    wide_xt[...] = wide_x[...].T.reshape(4, 4, 2, 16, 128)
    wide_yt[...] = wide_y[...].T.reshape(4, 4, 2, 16, 128)
    arrive([from_near_k])
    keys = jnp.concatenate([got[:, 0].reshape(512, 128), got_k[...].reshape(512, 128)], axis=0)
    scaling = 1.0 / math.sqrt(128)

    pairs = (slice(0, 2), slice(2, 4))

    def soft(pair):
        scores = right_dot(got[pair, 1].reshape(256, 128), keys) * scaling
        powers = jnp.exp(scores - jnp.max(scores, axis=1, keepdims=True))
        probs = powers * (1.0 / jnp.sum(powers, axis=1, keepdims=True))
        probs_f[pair] = probs.reshape(2, 128, 1024)
        probs_s[pair] = probs.astype(BF16).reshape(2, 128, 1024)

    def pass_v(k):
        arrive([vd_in[k]])
        send.copy(got.at[sources[k], 2], got_v.at[sources[k]], near, near_v)

    soft(pairs[0])
    pass_v(1)
    pass_v(3)
    soft(pairs[1])
    pass_v(2)
    home = []
    all_queries = got[:, 1].reshape(512, 128)
    all_upward = got[:, 3].reshape(512, 128)
    all_probs = probs_s[...].reshape(512, 1024)
    d_values = row_dot(all_upward, all_probs).T.astype(BF16).reshape(8, 128, 128)
    outgo_v[...] = d_values[4:8]
    home.append(send.group(back_v, [(outgo_v.at[p["x"]], back_v.at[x], device(p)) for p in across]))
    outgo[:, 1] = d_values[0:4]
    arrive([from_near_v])
    values = jnp.concatenate([got[:, 2].reshape(512, 128), got_v[...].reshape(512, 128)], axis=0)
    outgo[:, 0] = dot(all_probs, values).astype(BF16).reshape(4, 128, 128)
    for k in (1, 3, 2):
        block = pl.ds(0, 2)
        home.append(send(outgo.at[xs[k], block], back.at[x, block], device(moved(at, x=k))))
    for pair in pairs:
        probs = probs_f[pair].reshape(256, 1024)
        d_probs = right_dot(got[pair, 3].reshape(256, 128), values)
        inner = jnp.sum(probs * d_probs, axis=1, keepdims=True)
        d_scores = (probs * (d_probs - inner) * scaling).astype(BF16)
        scores_s[pair] = d_scores.reshape(2, 128, 1024)
        outgo[pair, 2] = dot(d_scores, keys).astype(BF16).reshape(2, 128, 128)
    for k in (1, 3, 2):
        home.append(send(outgo.at[xs[k], 2], back.at[x, 2], device(moved(at, x=k))))

    def key_grads(columns):
        d_keys = row_dot(all_queries, scores_s[:, :, columns].reshape(512, 512)).T
        return d_keys.astype(BF16).reshape(4, 128, 128)

    outgo_k[...] = key_grads(slice(512, 1024))
    home.append(send.group(back_k, [(outgo_k.at[p["x"]], back_k.at[x], device(p)) for p in across]))
    outgo[:, 3] = key_grads(slice(0, 512))
    for k in (1, 3, 2):
        home.append(send(outgo.at[xs[k], 3], back.at[x, 3], device(moved(at, x=k))))
    back[x] = outgo[x]
    arrive(home)
    send.finish()
    for head in range(H):
        columns = slice(128 * head, 128 * head + 128)
        attended[:, columns] = back[head, 0]
        d_proj[:, columns] = back[head, 2]
        for start, place, other in ((512, 3, back_k), (1024, 1, back_v)):
            total = back[head, place].astype(F32) + other[head].astype(F32)
            d_proj[:, start + 128 * head : start + 128 * head + 128] = total.astype(BF16)

    attended_t[...] = attended[...].T.reshape(4, 4, 2, 16, 128)
    d_halves = [d_proj[:, 0:768], d_proj[:, 768:1536]]
    row_side = lax.rem(lax.broadcasted_iota(jnp.int32, (256, 768), 0), 16)

    def qkv_grads(parity, to_x, to_y):
        left = wide_xt[:, :, parity].reshape(256, 128)
        for i in range(2):
            block = dot(left, d_halves[i]).astype(BF16)
            for j in range(2):
                to_x[2 * i + j] = block[:, 384 * j : 384 * j + 384].reshape(4, 4, 16, 384)
        left = wide_yt[:, :, parity].reshape(256, 128)
        both = [dot(left, d_half) for d_half in d_halves]
        to_y[...] = jnp.where(row_side < 8, both[0], both[1]).astype(BF16).reshape(4, 4, 16, 768)

    order = (2, 1, 3, 0)
    core_cx, core_cy, core_a, core_b = {}, {}, {}, {}
    qkv_grads(1 - c, px_s, py_s)
    for k in order:
        core_cx[k] = send(px_s.at[:, zs[k]], px_r.at[:, zs[k]], sibling)
        core_cy[k] = send(py_s.at[:, ys[k]], py_r.at[:, ys[k]], sibling)
    qkv_grads(c, px, py)
    d_x = sum(right_dot(d_halves[i], qx_full(i)) for i in range(2))
    both = right_dot(jnp.concatenate(d_halves, axis=0), qy_full())
    d_y = jnp.where(side_of == 0, both[0:128], both[128:256])

    def sum_cx(k):
        arrive([core_cx[k]])
        px[:, zs[k]] = add(px, px[:, zs[k]], px_r[:, zs[k]])

    def sum_cy(k):
        arrive([core_cy[k]])
        py[:, ys[k]] = add(py, py[:, ys[k]], py_r[:, ys[k]])

    right_x, left_x = device(moved(at, x=1)), device(moved(at, x=3))
    right_y, left_y = device(moved(at, y=1)), device(moved(at, y=3))
    right_z, left_z = device(moved(at, zh=1)), device(moved(at, zh=3))
    low, high = pl.ds(0, 2), pl.ds(2, 2)
    sides = ((0, 1, right_x, right_y), (1, 3, left_x, left_y))
    d_normed = 0.0
    for terms, choose in ((d_x, choose_x), (d_y, choose_y)):
        d_high = terms.astype(BF16)
        d_low = (terms - d_high.astype(F32)).astype(BF16)
        both = right_dot(jnp.concatenate([d_high, d_low], axis=0), choose[...])
        d_normed += both[0:128] + both[128:256]
    d_feature = upstream[...].astype(F32) + inverse[...] * (
        d_normed - unit[...] * jnp.mean(d_normed * unit[...], axis=1, keepdims=True)
    )
    d_pre = (d_feature * slope[...]).astype(BF16)

    sum_cx(2)
    far_cx = [
        send(px.at[quarters, zs[2]], fcx.at[side], to) for side, quarters, to in ((0, low, right_z), (1, high, left_z))
    ]
    sum_cy(2)
    far_cy = [
        send(py.at[heights, ys[2]], fcy.at[side], to) for side, heights, to in ((0, low, right_y), (1, high, left_y))
    ]
    def conv_grads(parity, to_a, to_b):
        def one(i):
            block = dot(taps_t[i, :, parity].reshape(384, 128), d_pre).astype(BF16).reshape(4, 96, 768)
            to_a[i] = block[:, 0:64]
            to_b[i, :, 0:32] = block[:, 64:96]

        loop(4, one)
        left = onehot_t[:, :, parity].reshape(256, 128)
        to_b[:, :, 32:48] = dot(left, d_pre).astype(BF16).reshape(4, 4, 16, 768)
        left = attended_t[:, :, parity].reshape(256, 128)
        to_b[:, :, 48:64] = dot(left, upstream[...]).astype(BF16).reshape(4, 4, 16, 768)

    conv_grads(1 - c, pa_s, pb_s)
    for k in order:
        core_a[k] = send(pa_s.at[:, :, rows16(xs[k])], pa_r.at[:, :, rows16(xs[k])], sibling)
        core_b[k] = send(pb_s.at[:, ys[k]], pb_r.at[:, ys[k]], sibling)
    conv_grads(c, pa, pb)

    def sum_a(k):
        arrive([core_a[k]])
        rows = rows16(xs[k])

        def one(i):
            pa[i, :, rows] = add(pa, pa[i, :, rows], pa_r[i, :, rows])

        loop(4, one)

    def sum_b(k):
        arrive([core_b[k]])

        def one(i):
            pb[i, ys[k]] = add(pb, pb[i, ys[k]], pb_r[i, ys[k]])

        loop(4, one)

    halves = [(h, pl.ds(384 * h, 384), slice(384 * h, 384 * h + 384)) for h in range(2)]
    far_a, far_b = {}, {}
    sum_a(2)
    sum_b(2)
    for h, columns, _ in halves:
        for side, heights, to_x, to_y in ((0, low, right_x, right_y), (1, high, left_x, left_y)):
            far_a[h, side] = send(pa.at[heights, :, rows16(xs[2]), columns], fa.at[h, side], to_x)
            far_b[h, side] = send(pb.at[heights, ys[2], :, columns], fb.at[h, side], to_y)
    near_cx, near_cy = [], []
    for side, k, to_x, to_y in sides:
        sum_cx(k)
        arrive([far_cx[side]])
        part = slice(2 * side, 2 * side + 2)
        px[part, zs[k]] = add(px, px[part, zs[k]], fcx[side])
        near_cx.append(send(px.at[:, zs[k]], ncx.at[side], (right_z, left_z)[side]))
        sum_cy(k)
        arrive([far_cy[side]])
        py[part, ys[k]] = add(py, py[part, ys[k]], fcy[side])
        near_cy.append(send(py.at[:, ys[k]], ncy.at[side], to_y))
    for side, k, to_x, to_y in sides:
        sum_a(k)
        sum_b(k)
    near_a, near_b = {}, {}
    for h, columns, cols in halves:
        for side, k, to_x, to_y in sides:
            rows = rows16(xs[k])
            arrive([far_a[h, side]])

            def join_a(i, h=h, side=side, rows=rows, cols=cols):
                pa[2 * side + i, :, rows, cols] = add(pa, pa[2 * side + i, :, rows, cols], fa[h, side, i])

            loop(2, join_a)
            near_a[h, side] = send(pa.at[:, :, rows, columns], na.at[h, side], to_x)
            arrive([far_b[h, side]])

            def join_b(i, h=h, side=side, index=ys[k], cols=cols):
                pb[2 * side + i, index, :, cols] = add(pb, pb[2 * side + i, index, :, cols], fb[h, side, i])

            loop(2, join_b)
            near_b[h, side] = send(pb.at[:, ys[k], :, columns], nb.at[h, side], to_y)

    def three(axis, whole, source):
        return send.group(
            whole, [(source(k), whole.at[k - 1], device(moved(at, **{axis: k}))) for k in (1, 3, 2)]
        )

    sum_cx(0)
    arrive(near_cx)
    scx1[...] = add(scx1, px[:, zh], ncx[0], ncx[1])
    cx2 = three("x", rcx2, lambda k: scx1.at[xs[k]])
    sum_cy(0)
    arrive(near_cy)
    scy1[...] = add(scy1, py[:, y], ncy[0], ncy[1])
    cy2 = three("zh", rcy2, lambda k: scy1.at[zs[k]])
    sum_a(0)
    sum_b(0)

    send.finish(28)
    rows_f[:, 256:272] = jnp.zeros((6, 16, 128), F32)
    for i in range(4):
        terms = right_dot(d_pre, conv_full(i))
        for j in range(6):
            target = pl.ds(7 + i, 128, stride=2)
            block = terms[:, 128 * j : 128 * j + 128]
            rows_f[j, target] = block if i < 2 else rows_f[j, target] + block
    rim_out[0] = rows_f[:, 264:272]
    rim_out[1] = rows_f[:, 0:8]
    rims = [send(rim_out.at[0], rim_before, ahead), send(rim_out.at[1], rim_after, behind)]

    a2, b2, a3, b3, a4, b4 = {}, {}, {}, {}, {}, {}
    for h, columns, cols in halves:
        arrive([near_a[h, 0], near_a[h, 1]])

        def first_a(i, h=h, cols=cols):
            sa1[h, i] = add(sa1, pa[i, :, rows16(x), cols], na[h, 0, i], na[h, 1, i])

        loop(4, first_a)
        a2[h] = three("y", ra2.at[h], lambda k, h=h: sa1.at[h, :, ys[k]])
        arrive([near_b[h, 0], near_b[h, 1]])

        def first_b(i, h=h, cols=cols):
            sb1[h, i] = add(sb1, pb[i, y, :, cols], nb[h, 0, i], nb[h, 1, i])

        loop(4, first_b)
        b2[h] = three("x", rb2.at[h], lambda k, h=h: sb1.at[h, :, rows16(xs[k])])
        if h == 0:
            arrive([cx2])
            scx2[...] = add(scx2, scx1[x], rcx2[0], rcx2[1], rcx2[2])
            cx3 = three("y", rcx3, lambda k: scx2.at[ys[k]])
            arrive([cy2])
            scy2[...] = add(scy2, scy1[zh], rcy2[0], rcy2[1], rcy2[2])
            cy3 = send(scy2, rcy3, near)
    arrive(rims)
    rows_f[:, 8:9] += jnp.where(sq > 0, rim_before[:, 0:1], 0.0)
    rows_f[:, 263:264] += jnp.where(sq < 7, rim_after[:, 7:8], 0.0)
    for j in range(6):
        seq_o[:, 128 * j : 128 * j + 128] = rows_f[j, 8:264].astype(BF16)
    for h in range(2):
        arrive([a2[h]])
        sa2[h] = add(sa2, sa1[h, :, y], ra2[h, 0], ra2[h, 1], ra2[h, 2])
        a3[h] = three("zh", ra3.at[h], lambda k, h=h: sa2.at[h, zs[k]])
        arrive([b2[h]])
        sb2[h] = add(sb2, sb1[h, :, rows16(x)], rb2[h, 0], rb2[h, 1], rb2[h, 2])
        b3[h] = three("zh", rb3.at[h], lambda k, h=h: sb2.at[h, zs[k]])
        if h == 0:
            arrive([cx3])
            scx3[...] = add(scx3, scx2[y], rcx3[0], rcx3[1], rcx3[2])
            cx4 = send(scx3, rcx4, near)
            arrive([cy3])
            scy3[...] = add(scy3, scy2[...], rcy3[...])
            cy4 = three("x", rcy4, lambda k: scy3)

    send.finish(12)
    for h in range(2):
        arrive([a3[h]])
        sa3[h] = add(sa3, sa2[h, zh], ra3[h, 0], ra3[h, 1], ra3[h, 2])
        a4[h] = send(sa3.at[h], ra4.at[h], near)
        arrive([b3[h]])
        sb3[h] = add(sb3, sb2[h, zh], rb3[h, 0], rb3[h, 1], rb3[h, 2])
        b4[h] = send(sb3.at[h], rb4.at[h], near)
        if h == 0:
            arrive([cx4])
            final_x[x] = add(final_x, scx3[...], rcx4[...])
            spread = [send(final_x.at[x], final_x.at[x], device(moved(at, x=k))) for k in (1, 2, 3)]
            arrive([cy4])
            final_y[...] = add(final_y, scy3[...], rcy4[0], rcy4[1], rcy4[2])
    for h in range(2):
        arrive([a4[h]])
        final[x, 0, h] = add(final, sa3[h], ra4[h])
        arrive([b4[h]])
        final[x, 1, h] = add(final, sb3[h], rb4[h])
    spread += [send(final.at[x], final.at[x], device(moved(at, x=k))) for k in (1, 2, 3)]
    arrive(spread)
    send.finish()


def finish_kernel(seq_i, final, final_x, final_y, seq_o, conv_o, dna_o, qkv_o, out_o):
    seq_o[0] = seq_i[...]
    for h in range(2):
        columns = slice(384 * h, 384 * h + 384)
        for q in range(4):
            conv_o[16 * q : 16 * q + 16, columns] = final[q, 0, h].astype(F32)
        conv_o[64:80, columns] = final[0, 1, h].astype(F32)
        conv_o[80:96, columns] = final[1, 1, h].astype(F32)
        dna_o[:, columns] = final[2, 1, h].astype(F32)
        out_o[:, columns] = final[3, 1, h].astype(F32)
    for q in range(4):
        qkv_o[0:16, 384 * q : 384 * q + 384] = final_x[q].astype(F32)
    last_rows = final_y[...].astype(F32)
    qkv_o[16:24, 0:768] = last_rows[0:8]
    qkv_o[16:24, 768:1536] = last_rows[8:16]


def layer(*operands):
    vmem = pl.BlockSpec(memory_space=pltpu.VMEM)
    low = [
        (4, 4, 2, 4, 16, 1152), (4, 4, 2, 80, 768), (16, 768), (16, 768),
        (4, 128, 768), (4, 4, 2, 96, 128), (128, 512), (4, 4, 2, 16, 128), (768, 512), (768, 512),
        (128, 512), (128, 512), (4, 4, 2, 16, 128), (4, 4, 2, 16, 128), (128, 1536), (128, 512), (4, 4, 2, 16, 128),
        (4, 4, 128, 128), (4, 4, 128, 128), (4, 128, 128), (4, 128, 128), (4, 4, 128, 128), (4, 128, 128), (4, 128, 128),
        (4, 4, 128, 128), (4, 128, 128), (4, 128, 128),
        (4, 128, 1024), (4, 128, 1024),
    ] + 3 * [(4, 4, 64, 768), (4, 4, 64, 768), (4, 4, 4, 16, 384), (4, 4, 16, 768)] + [
        (2, 2, 2, 4, 16, 384), (2, 2, 4, 4, 16, 384), (2, 4, 4, 16, 384), (2, 3, 4, 16, 384),
        (2, 4, 16, 384), (2, 3, 16, 384), (2, 16, 384), (2, 16, 384),
        (2, 2, 2, 64, 384), (2, 2, 4, 64, 384), (2, 4, 64, 384), (2, 3, 4, 16, 384),
        (2, 4, 16, 384), (2, 3, 16, 384), (2, 16, 384), (2, 16, 384),
        (2, 2, 4, 16, 384), (2, 4, 4, 16, 384), (4, 4, 16, 384), (3, 4, 16, 384), (4, 16, 384), (3, 16, 384), (16, 384), (16, 384),
        (2, 2, 16, 768), (2, 4, 16, 768), (4, 16, 768), (3, 16, 768), (16, 768), (16, 768), (16, 768), (3, 16, 768),
    ]
    wide = [(128, 768), (128, 768), (128, 1), (6, 272, 128), (4, 128, 1024), (2, 6, 8, 128), (6, 8, 128), (6, 8, 128)]
    results = pl.pallas_call(
        layer_kernel,
        name="layer",
        out_shape=tuple(
            jax.ShapeDtypeStruct(shape, BF16)
            for shape in ((256, 768), (4, 2, 2, 16, 384), (4, 16, 384), (16, 768))
        ),
        in_specs=[vmem] * 7,
        out_specs=(vmem,) * 4,
        scratch_shapes=[pltpu.VMEM(shape, BF16) for shape in low]
        + [pltpu.VMEM(shape, F32) for shape in wide]
        + [pltpu.SemaphoreType.DMA((60,)), pltpu.SemaphoreType.DMA((138,))],
        compiler_params=pltpu.CompilerParams(
            collective_id=1, has_side_effects=True, vmem_limit_bytes=60 * 2**20
        ),
    )(*operands)
    return pl.pallas_call(
        finish_kernel,
        name="finish",
        out_shape=(
            jax.ShapeDtypeStruct((1, 256, 768), BF16),
            jax.ShapeDtypeStruct((96, 768), F32),
            jax.ShapeDtypeStruct((16, 768), F32),
            jax.ShapeDtypeStruct((24, 1536), F32),
            jax.ShapeDtypeStruct((16, 768), F32),
        ),
        in_specs=[vmem] * 4,
        out_specs=(vmem,) * 5,
    )(*results)


def per_device(seq_in, bases, conv_weight, dna_weight, qkv_weight, out_weight, cotangent):
    return layer(
        conv_weight, dna_weight, qkv_weight, out_weight, seq_in[0], bases[0].reshape(128, BIN), cotangent[0]
    )


def solution(mesh):
    in_specs = (
        P("dp", "seq", None),
        P("dp", "seq"),
        P("dp", None),
        P("dp", None),
        P("dp", None),
        P("dp", None),
        P("dp", "seq", None),
    )
    out_specs = (P("dp", "seq", None), P("dp", None), P("dp", None), P("dp", None), P("dp", None))
    return jax.shard_map(
        per_device, mesh=mesh, in_specs=in_specs, out_specs=out_specs, check_vma=False
    )
```

```python
import math

import jax
import jax.numpy as jnp
from jax import lax
from jax.experimental import pallas as pl
from jax.experimental.pallas import tpu as pltpu
from jax.sharding import PartitionSpec as P

H = 4
BIN = 128
BF16 = jnp.bfloat16
F32 = jnp.float32
MESH = pl.DeviceIdType.MESH
epsilon = 1e-06

SIZES = {"zh": 4, "y": 4, "c": 2, "zl": 2, "x": 4}
PEERS = [(a, k) for a in ("zh", "y", "x") for k in (1, 2, 3)] + [("zl", 1), ("c", 1)]


def here():
    dp = lax.axis_index("dp")
    sq = lax.axis_index("seq")
    return {"zh": dp // 8, "y": lax.rem(dp // 2, 4), "c": lax.rem(dp, 2), "zl": sq // 4, "x": lax.rem(sq, 4)}


def moved(at, **steps):
    to = dict(at)
    for axis, step in steps.items():
        to[axis] = lax.rem(at[axis] + step, SIZES[axis])
    return to


def device(at):
    return (at["zh"] * 8 + at["y"] * 2 + at["c"], at["zl"] * 4 + at["x"])


class Sender:
    def __init__(self, send_sems, recv_sems):
        self.send_sems, self.recv_sems, self.sent, self.due = send_sems, recv_sems, 0, 0
        self.free, self.copies = [], []

    def copy(self, src, dst, to, recv):
        if not self.free:
            self.free.append(self.sent)
            self.sent += 1
        place = self.free.pop(0)
        copy = pltpu.make_async_remote_copy(
            src_ref=src,
            dst_ref=dst,
            send_sem=self.send_sems.at[place],
            recv_sem=self.recv_sems.at[recv],
            device_id=to,
            device_id_type=MESH,
        )
        copy.start()
        self.copies.append((copy, place))
        return copy

    def __call__(self, src, dst, to):
        self.due += 1
        return self.copy(src, dst, to, self.due - 1)

    def group(self, whole, copies):
        self.due += 1
        for src, dst, to in copies:
            self.copy(src, dst, to, self.due - 1)
        return pltpu.make_async_remote_copy(
            src_ref=whole,
            dst_ref=whole,
            send_sem=self.send_sems.at[0],
            recv_sem=self.recv_sems.at[self.due - 1],
            device_id=copies[0][2],
            device_id_type=MESH,
        )

    def finish(self, oldest=None):
        done = self.copies[:oldest]
        for copy, place in done:
            copy.wait_send()
            self.free.append(place)
        self.copies = self.copies[len(done) :]


def arrive(copies):
    for copy in copies:
        copy.wait_recv()


def rows16(index, base=0):
    return pl.ds(pl.multiple_of(index * 16 + base, 16), 16)


def half_columns(index):
    return pl.ds(pl.multiple_of(index * 384, 128) if not isinstance(index, int) else index * 384, 384)


def right_dot(left, right):
    return lax.dot_general(left, right, (((1,), (1,)), ((), ())), preferred_element_type=F32)


def row_dot(left, right):
    return lax.dot_general(left, right, (((0,), (0,)), ((), ())), preferred_element_type=F32)


def dot(left, right):
    return jnp.dot(left, right, preferred_element_type=F32)


def add(target, *terms):
    total = terms[0].astype(F32)
    for term in terms[1:]:
        total += term.astype(F32)
    return total.astype(target.dtype)


def loop(n, body):
    def step(i, carry):
        body(i)
        return carry

    lax.fori_loop(0, n, step, 0)


class Ring:
    def __init__(self, send, at, axis, region):
        self.send, self.me, self.region = send, at[axis], region
        self.right, self.left = device(moved(at, **{axis: 1})), device(moved(at, **{axis: 3}))

    def at(self, step):
        return lax.rem(self.me + step, 4)

    def go(self, index, part, to):
        ref = self.region(index, part)
        return [self.send(ref, ref, to)]

    def start(self):
        self.from_left = self.go(self.me, None, self.right)
        self.from_right = self.go(self.me, None, self.left)

    def left_in(self):
        arrive(self.from_left)
        self.far_left = self.go(self.at(3), 0, self.right)

    def right_in(self):
        arrive(self.from_right)
        self.far_right = self.go(self.at(1), 1, self.left)

    def both_in(self):
        self.left_in()
        self.right_in()

    def far_in(self):
        arrive(self.far_left)
        arrive(self.far_right)


def layer_kernel(
    conv_s, dna_s, qkv_s, out_s, rows_in, letters, upstream,
    seq_o, final, final_x, final_y,
    ga, gb, before, after,
    taps, taps_t, onehot, onehot_t, choose_x, choose_y, wide_x, wide_y, wide_xt, wide_yt, d_proj, attended, attended_t,
    mine, got, got_k, got_v, outgo, outgo_k, outgo_v, back, back_k, back_v, probs_s, scores_s,
    pa_s, pb_s, px_s, py_s, pa, pb, px, py, pa_r, pb_r, px_r, py_r,
    fa, na, sa1, ra2, sa2, ra3, sa3, ra4,
    fb, nb, sb1, rb2, sb2, rb3, sb3, rb4,
    fcx, ncx, scx1, rcx2, scx2, rcx3, scx3, rcx4,
    fcy, ncy, scy1, rcy2, scy2, rcy3, scy3, rcy4,
    slope, unit, inverse, rows_f, probs_f, rim_out, rim_before, rim_after,
    send_sems, recv_sems,
):
    at = here()
    zh, y, c, zl, x = (at[a] for a in ("zh", "y", "c", "zl", "x"))
    sq = lax.axis_index("seq")
    dp = lax.axis_index("dp")
    behind, ahead = (dp, lax.rem(sq + 7, 8)), (dp, lax.rem(sq + 1, 8))
    sibling = device(moved(at, c=1))
    near = device(moved(at, zl=1))
    across = [moved(at, x=k, zl=1) for k in range(4)]
    everyone = [device(moved(at, **{a: k})) for a, k in PEERS] + [behind, ahead]
    everyone += [device(p) for p in across[1:]]
    barrier = pltpu.get_barrier_semaphore()
    for one in everyone:
        pl.semaphore_signal(barrier, inc=1, device_id=one, device_id_type=MESH)
    xs = [lax.rem(x + k, 4) for k in range(4)]
    ys = [lax.rem(y + k, 4) for k in range(4)]
    zs = [lax.rem(zh + k, 4) for k in range(4)]

    quarter = rows16(x)
    ga[zh, y, c, x, :, 0:768] = conv_s[quarter]
    ga[zh, y, c, x, :, 768:1152] = qkv_s[0:16, half_columns(x)]
    gb[zh, y, c, 0:32] = conv_s[64:96]
    gb[zh, y, c, 32:48] = dna_s[...]
    gb[zh, y, c, 48:64] = out_s[...]
    last_rows = [qkv_s[:, 768 * i : 768 * i + 768].astype(F32)[16:24] for i in range(2)]
    gb[zh, y, c, 64:80] = jnp.concatenate(last_rows, axis=0).astype(BF16)
    pl.semaphore_wait(barrier, len(everyone))

    send = Sender(send_sems, recv_sems)

    def ref_a(height, step, index, part=None):
        rows = pl.ds(0, 4) if part is None else pl.ds(2 * part, 2)
        return ga.at[rows if height is None else height, step, c, index]

    def ref_b(height, step, part=None):
        return gb.at[height, step, c] if part is None else gb.at[height, step, c, :, half_columns(part)]

    core = []

    def pass_on(ref):
        core.append(send(ref, ref, sibling))

    def pass_a(step):
        pass_on(ga.at[:, step, c])

    def pass_b(height):
        pass_on(gb.at[height, :, c])

    a1 = []
    for k in (2, 1, 3):
        a1.append(send(ref_a(zh, y, x), ref_a(zh, y, x), device(moved(at, zh=k))))
    halo = [
        send(rows_in.at[pl.ds(240, 16)], before, ahead),
        send(rows_in.at[pl.ds(0, 16)], after, behind),
    ]
    ring_z = Ring(send, at, "zh", lambda index, part: ref_b(index, y, part))
    rings_y = [Ring(send, at, "y", lambda index, part, v=zs[k]: ref_b(v, index, part)) for k in range(4)]
    rings_x = [Ring(send, at, "x", lambda index, part, v=ys[k]: ref_a(None, v, index, part)) for k in range(4)]
    ring_a = Ring(send, at, "y", lambda index, part: ref_a(None, index, x, part))
    ring_z.start()
    rings_y[0].start()
    row = lax.broadcasted_iota(jnp.int32, (128, 512), 0)
    column = lax.broadcasted_iota(jnp.int32, (128, 512), 1)
    repeat = (column // 4 == row).astype(F32).astype(BF16)
    repeated = dot(letters[...].astype(F32).astype(BF16), repeat)
    onehot[...] = (repeated == lax.rem(column, 4).astype(F32)).astype(F32).astype(BF16)
    arrive(a1)
    ring_a.start()
    rings_x[0].start()
    ring_z.left_in()
    rings_y[3].start()
    ring_z.right_in()
    rings_y[0].both_in()
    ring_a.left_in()
    rings_x[3].start()
    ring_a.right_in()
    rings_x[1].start()
    rings_y[1].start()
    rings_x[0].both_in()
    ring_a.far_in()
    rings_x[2].start()
    ring_z.far_in()
    rings_y[2].start()
    rings_y[3].both_in()
    rings_x[3].both_in()
    rings_x[1].both_in()
    rings_y[1].both_in()
    rings_y[0].far_in()
    pass_b(zs[0])
    rings_x[0].far_in()
    pass_a(ys[0])
    rings_x[2].both_in()
    rings_y[2].both_in()

    send.finish(24)
    arrive(halo)
    for j in range(6):
        lanes = slice(128 * j, 128 * j + 128)
        rows_f[j, 8:264] = rows_in[:, lanes].astype(F32)
        rows_f[j, 0:8] = jnp.where(sq > 0, before[:, lanes].astype(F32)[8:16], 0.0)
        rows_f[j, 264:272] = jnp.where(sq < 7, after[:, lanes].astype(F32)[0:8], 0.0)
        for i in range(4):
            taps[i, :, lanes] = rows_f[j, pl.ds(7 + i, 128, stride=2)].astype(BF16)

    rings_y[3].far_in()
    pass_b(zs[3])
    rings_y[1].far_in()
    pass_b(zs[1])
    rings_x[3].far_in()
    pass_a(ys[3])
    rings_x[1].far_in()
    pass_a(ys[1])
    rings_y[2].far_in()
    pass_b(zs[2])
    rings_x[2].far_in()
    pass_a(ys[2])

    def transpose_tap(i):
        taps_t[i] = taps[i].T.reshape(4, 2, 96, 128)

    loop(4, transpose_tap)
    onehot_t[...] = onehot[...].T.reshape(4, 4, 2, 16, 128)
    row = lax.broadcasted_iota(jnp.int32, (768, 512), 0)
    column = lax.broadcasted_iota(jnp.int32, (768, 512), 1)
    first_row = column // 16 * 24
    choose_x[...] = (first_row + lax.rem(column, 16) == row).astype(F32).astype(BF16)
    choose_y[...] = (first_row + 16 + lax.rem(column, 8) == row).astype(F32).astype(BF16)
    arrive(core[:-1])

    def conv_full(i):
        first = ga[i, :, :, :, :, 0:768].reshape(4, 2, 64, 768)
        return jnp.concatenate([first, gb[i, :, :, 0:32]], axis=2).reshape(768, 768)

    def qx_full(i):
        return jnp.concatenate(
            [ga[:, :, :, 2 * i + j, :, 768:1152].reshape(512, 384) for j in range(2)], axis=1
        )

    def qy_full():
        return gb[:, :, :, 64:80].reshape(512, 768)

    dna_full = gb[:, :, :, 32:48].reshape(512, 768)
    out_full = gb[:, :, :, 48:64].reshape(512, 768)
    d_attend = right_dot(upstream[...], out_full).astype(BF16)
    slope[...] = dot(onehot[...], dna_full)
    arrive(core[-1:])

    def one_tap(i):
        slope[...] += dot(taps[i], conv_full(i))

    loop(4, one_tap)
    pre = slope[...]
    bend = jnp.tanh(math.sqrt(2.0 / math.pi) * (pre + 0.044715 * (pre * pre * pre)))
    share = 0.5 * (1.0 + bend)
    feature = (pre * share).astype(BF16).astype(F32)
    slope[...] = share + pre * (0.5 * (1.0 - bend * bend)) * (
        math.sqrt(2.0 / math.pi) * (1.0 + 3.0 * 0.044715 * (pre * pre))
    )
    scale = lax.rsqrt(jnp.mean(feature * feature, axis=1, keepdims=True) + epsilon)
    inverse[...] = scale
    unit[...] = feature * scale
    normed = unit[...].astype(BF16)
    wide_x[...] = dot(normed, choose_x[...]).astype(BF16)
    wide_y[...] = dot(normed, choose_y[...]).astype(BF16)
    side_of = lax.rem(lax.broadcasted_iota(jnp.int32, (128, 512), 1), 16) // 8
    own_y = [jnp.where(side_of == i, wide_y[...].astype(F32), 0.0).astype(BF16) for i in range(2)]
    from_y = dot(jnp.concatenate(own_y, axis=0), qy_full())
    for i in range(2):
        projected = (dot(wide_x[...], qx_full(i)) + from_y[128 * i : 128 * i + 128]).astype(BF16)
        for piece in range(6):
            kind, head = divmod(6 * i + piece, 4)
            mine[head, (1, 0, 2)[kind]] = projected[:, 128 * piece : 128 * piece + 128]
    for head in range(H):
        mine[head, 3] = d_attend[:, 128 * head : 128 * head + 128]

    kq, vd = pl.ds(0, 2), pl.ds(2, 2)
    kq_in, vd_in = {}, {}
    from_near_k = send.group(got_k, [(mine.at[x, 0], got_k.at[x], near)])
    near_k = send.due - 1
    from_near_v = send.group(got_v, [(mine.at[x, 2], got_v.at[x], near)])
    near_v = send.due - 1
    for k in (1, 3, 2):
        kq_in[k] = send(mine.at[xs[k], kq], got.at[x, kq], device(moved(at, x=k)))
    for k in (1, 3, 2):
        vd_in[k] = send(mine.at[xs[k], vd], got.at[x, vd], device(moved(at, x=k)))
    sources = {k: lax.rem(x + 4 - k, 4) for k in (0, 1, 3, 2)}
    got[x] = mine[x]
    for k in (1, 3, 2):
        arrive([kq_in[k]])
        send.copy(got.at[sources[k], 0], got_k.at[sources[k]], near, near_k)
    wide_xt[...] = wide_x[...].T.reshape(4, 4, 2, 16, 128)
    wide_yt[...] = wide_y[...].T.reshape(4, 4, 2, 16, 128)
    arrive([from_near_k])
    keys = jnp.concatenate([got[:, 0].reshape(512, 128), got_k[...].reshape(512, 128)], axis=0)
    scaling = 1.0 / math.sqrt(128)

    pairs = (slice(0, 2), slice(2, 4))

    def soft(pair):
        scores = right_dot(got[pair, 1].reshape(256, 128), keys) * scaling
        powers = jnp.exp(scores - jnp.max(scores, axis=1, keepdims=True))
        probs = powers * (1.0 / jnp.sum(powers, axis=1, keepdims=True))
        probs_f[pair] = probs.reshape(2, 128, 1024)
        probs_s[pair] = probs.astype(BF16).reshape(2, 128, 1024)

    def pass_v(k):
        arrive([vd_in[k]])
        send.copy(got.at[sources[k], 2], got_v.at[sources[k]], near, near_v)

    soft(pairs[0])
    pass_v(1)
    pass_v(3)
    soft(pairs[1])
    pass_v(2)
    home_v, home_q, home_k = [], [], []
    all_queries = got[:, 1].reshape(512, 128)
    all_upward = got[:, 3].reshape(512, 128)
    all_probs = probs_s[...].reshape(512, 1024)
    d_values = row_dot(all_upward, all_probs).T.astype(BF16).reshape(8, 128, 128)
    outgo_v[...] = d_values[4:8]
    home_v.append(send.group(back_v, [(outgo_v.at[p["x"]], back_v.at[x], device(p)) for p in across]))
    outgo[:, 1] = d_values[0:4]
    arrive([from_near_v])
    values = jnp.concatenate([got[:, 2].reshape(512, 128), got_v[...].reshape(512, 128)], axis=0)
    outgo[:, 0] = dot(all_probs, values).astype(BF16).reshape(4, 128, 128)
    for k in (1, 3, 2):
        block = pl.ds(0, 2)
        home_v.append(send(outgo.at[xs[k], block], back.at[x, block], device(moved(at, x=k))))
    for pair in pairs:
        probs = probs_f[pair].reshape(256, 1024)
        d_probs = right_dot(got[pair, 3].reshape(256, 128), values)
        inner = jnp.sum(probs * d_probs, axis=1, keepdims=True)
        d_scores = (probs * (d_probs - inner) * scaling).astype(BF16)
        scores_s[pair] = d_scores.reshape(2, 128, 1024)
        outgo[pair, 2] = dot(d_scores, keys).astype(BF16).reshape(2, 128, 128)
    for k in (1, 3, 2):
        home_q.append(send(outgo.at[xs[k], 2], back.at[x, 2], device(moved(at, x=k))))

    def key_grads(columns):
        d_keys = row_dot(all_queries, scores_s[:, :, columns].reshape(512, 512)).T
        return d_keys.astype(BF16).reshape(4, 128, 128)

    outgo_k[...] = key_grads(slice(512, 1024))
    home_k.append(send.group(back_k, [(outgo_k.at[p["x"]], back_k.at[x], device(p)) for p in across]))
    outgo[:, 3] = key_grads(slice(0, 512))
    for k in (1, 3, 2):
        home_k.append(send(outgo.at[xs[k], 3], back.at[x, 3], device(moved(at, x=k))))
    back[x] = outgo[x]

    def columns_of(head, start=0):
        return slice(start + 128 * head, start + 128 * head + 128)

    arrive(home_v)
    for head in range(H):
        attended[:, columns_of(head)] = back[head, 0]
        total = back[head, 1].astype(F32) + back_v[head].astype(F32)
        d_proj[:, columns_of(head, 1024)] = total.astype(BF16)
    attended_t[...] = attended[...].T.reshape(4, 4, 2, 16, 128)
    for parity, to_b in ((1 - c, pb_s), (c, pb)):
        left = attended_t[:, :, parity].reshape(256, 128)
        to_b[:, :, 48:64] = dot(left, upstream[...]).astype(BF16).reshape(4, 4, 16, 768)
    arrive(home_q)
    for head in range(H):
        d_proj[:, columns_of(head)] = back[head, 2]

    def qkv_quarters(parity, to_x, quarters):
        left = wide_xt[:, :, parity].reshape(256, 128)
        for q in quarters:
            block = dot(left, d_proj[:, 384 * q : 384 * q + 384]).astype(BF16)
            to_x[q] = block.reshape(4, 4, 16, 384)

    qkv_quarters(1 - c, px_s, (0, 3))
    qkv_quarters(c, px, (0, 3))
    d_q, d_v = d_proj[:, 0:512], d_proj[:, 1024:1536]
    d_x = right_dot(d_q, qx_full(0)[:, 0:512]) + right_dot(d_v, qx_full(1)[:, 256:768])
    d_y0, d_y1 = right_dot(d_q, qy_full()[:, 0:512]), right_dot(d_v, qy_full()[:, 256:768])
    arrive(home_k)
    send.finish()
    for head in range(H):
        total = back[head, 3].astype(F32) + back_k[head].astype(F32)
        d_proj[:, columns_of(head, 512)] = total.astype(BF16)

    row_side = lax.rem(lax.broadcasted_iota(jnp.int32, (256, 768), 0), 16)

    def qkv_grads(parity, to_x, to_y):
        qkv_quarters(parity, to_x, (1, 2))
        left = wide_yt[:, :, parity].reshape(256, 128)
        both = [dot(left, d_proj[:, 768 * i : 768 * i + 768]) for i in range(2)]
        to_y[...] = jnp.where(row_side < 8, both[0], both[1]).astype(BF16).reshape(4, 4, 16, 768)

    order = (2, 1, 3, 0)
    core_cx, core_cy, core_a, core_b = {}, {}, {}, {}
    qkv_grads(1 - c, px_s, py_s)
    for k in order:
        core_cx[k] = send(px_s.at[:, zs[k]], px_r.at[:, zs[k]], sibling)
        core_cy[k] = send(py_s.at[:, ys[k]], py_r.at[:, ys[k]], sibling)
    qkv_grads(c, px, py)
    d_k0, d_k1 = d_proj[:, 512:768], d_proj[:, 768:1024]
    d_x += right_dot(d_k0, qx_full(0)[:, 512:768]) + right_dot(d_k1, qx_full(1)[:, 0:256])
    d_y0 += right_dot(d_k0, qy_full()[:, 512:768])
    d_y1 += right_dot(d_k1, qy_full()[:, 0:256])
    d_y = jnp.where(side_of == 0, d_y0, d_y1)

    def sum_cx(k):
        arrive([core_cx[k]])
        px[:, zs[k]] = add(px, px[:, zs[k]], px_r[:, zs[k]])

    def sum_cy(k):
        arrive([core_cy[k]])
        py[:, ys[k]] = add(py, py[:, ys[k]], py_r[:, ys[k]])

    right_x, left_x = device(moved(at, x=1)), device(moved(at, x=3))
    right_y, left_y = device(moved(at, y=1)), device(moved(at, y=3))
    right_z, left_z = device(moved(at, zh=1)), device(moved(at, zh=3))
    low, high = pl.ds(0, 2), pl.ds(2, 2)
    sides = ((0, 1, right_x, right_y), (1, 3, left_x, left_y))
    d_normed = 0.0
    for terms, choose in ((d_x, choose_x), (d_y, choose_y)):
        d_high = terms.astype(BF16)
        d_low = (terms - d_high.astype(F32)).astype(BF16)
        both = right_dot(jnp.concatenate([d_high, d_low], axis=0), choose[...])
        d_normed += both[0:128] + both[128:256]
    d_feature = upstream[...].astype(F32) + inverse[...] * (
        d_normed - unit[...] * jnp.mean(d_normed * unit[...], axis=1, keepdims=True)
    )
    d_pre = (d_feature * slope[...]).astype(BF16)

    sum_cx(2)
    far_cx = [
        send(px.at[quarters, zs[2]], fcx.at[side], to) for side, quarters, to in ((0, low, right_z), (1, high, left_z))
    ]
    sum_cy(2)
    far_cy = [
        send(py.at[heights, ys[2]], fcy.at[side], to) for side, heights, to in ((0, low, right_y), (1, high, left_y))
    ]
    def conv_grads(parity, to_a, to_b):
        def one(i):
            block = dot(taps_t[i, :, parity].reshape(384, 128), d_pre).astype(BF16).reshape(4, 96, 768)
            to_a[i] = block[:, 0:64]
            to_b[i, :, 0:32] = block[:, 64:96]

        loop(4, one)
        left = onehot_t[:, :, parity].reshape(256, 128)
        to_b[:, :, 32:48] = dot(left, d_pre).astype(BF16).reshape(4, 4, 16, 768)

    conv_grads(1 - c, pa_s, pb_s)
    for k in order:
        core_a[k] = send(pa_s.at[:, :, rows16(xs[k])], pa_r.at[:, :, rows16(xs[k])], sibling)
        core_b[k] = send(pb_s.at[:, ys[k]], pb_r.at[:, ys[k]], sibling)
    conv_grads(c, pa, pb)

    def sum_a(k):
        arrive([core_a[k]])
        rows = rows16(xs[k])

        def one(i):
            pa[i, :, rows] = add(pa, pa[i, :, rows], pa_r[i, :, rows])

        loop(4, one)

    def sum_b(k):
        arrive([core_b[k]])

        def one(i):
            pb[i, ys[k]] = add(pb, pb[i, ys[k]], pb_r[i, ys[k]])

        loop(4, one)

    halves = [(h, pl.ds(384 * h, 384), slice(384 * h, 384 * h + 384)) for h in range(2)]
    far_a, far_b = {}, {}
    sum_a(2)
    sum_b(2)
    for h, columns, _ in halves:
        for side, heights, to_x, to_y in ((0, low, right_x, right_y), (1, high, left_x, left_y)):
            far_a[h, side] = send(pa.at[heights, :, rows16(xs[2]), columns], fa.at[h, side], to_x)
            far_b[h, side] = send(pb.at[heights, ys[2], :, columns], fb.at[h, side], to_y)
    near_cx, near_cy = [], []
    for side, k, to_x, to_y in sides:
        sum_cx(k)
        arrive([far_cx[side]])
        part = slice(2 * side, 2 * side + 2)
        px[part, zs[k]] = add(px, px[part, zs[k]], fcx[side])
        near_cx.append(send(px.at[:, zs[k]], ncx.at[side], (right_z, left_z)[side]))
        sum_cy(k)
        arrive([far_cy[side]])
        py[part, ys[k]] = add(py, py[part, ys[k]], fcy[side])
        near_cy.append(send(py.at[:, ys[k]], ncy.at[side], to_y))
    for side, k, to_x, to_y in sides:
        sum_a(k)
        sum_b(k)
    near_a, near_b = {}, {}
    for h, columns, cols in halves:
        for side, k, to_x, to_y in sides:
            rows = rows16(xs[k])
            arrive([far_a[h, side]])

            def join_a(i, h=h, side=side, rows=rows, cols=cols):
                pa[2 * side + i, :, rows, cols] = add(pa, pa[2 * side + i, :, rows, cols], fa[h, side, i])

            loop(2, join_a)
            near_a[h, side] = send(pa.at[:, :, rows, columns], na.at[h, side], to_x)
            arrive([far_b[h, side]])

            def join_b(i, h=h, side=side, index=ys[k], cols=cols):
                pb[2 * side + i, index, :, cols] = add(pb, pb[2 * side + i, index, :, cols], fb[h, side, i])

            loop(2, join_b)
            near_b[h, side] = send(pb.at[:, ys[k], :, columns], nb.at[h, side], to_y)

    def three(axis, whole, source):
        return send.group(
            whole, [(source(k), whole.at[k - 1], device(moved(at, **{axis: k}))) for k in (1, 3, 2)]
        )

    sum_cx(0)
    arrive(near_cx)
    scx1[...] = add(scx1, px[:, zh], ncx[0], ncx[1])
    cx2 = three("x", rcx2, lambda k: scx1.at[xs[k]])
    sum_cy(0)
    arrive(near_cy)
    scy1[...] = add(scy1, py[:, y], ncy[0], ncy[1])
    cy2 = three("zh", rcy2, lambda k: scy1.at[zs[k]])
    sum_a(0)
    sum_b(0)

    send.finish(28)
    rows_f[:, 256:272] = jnp.zeros((6, 16, 128), F32)
    for i in range(4):
        terms = right_dot(d_pre, conv_full(i))
        for j in range(6):
            target = pl.ds(7 + i, 128, stride=2)
            block = terms[:, 128 * j : 128 * j + 128]
            rows_f[j, target] = block if i < 2 else rows_f[j, target] + block
    rim_out[0] = rows_f[:, 264:272]
    rim_out[1] = rows_f[:, 0:8]
    rims = [send(rim_out.at[0], rim_before, ahead), send(rim_out.at[1], rim_after, behind)]

    a2, b2, a3, b3, a4, b4 = {}, {}, {}, {}, {}, {}
    for h, columns, cols in halves:
        arrive([near_a[h, 0], near_a[h, 1]])

        def first_a(i, h=h, cols=cols):
            sa1[h, i] = add(sa1, pa[i, :, rows16(x), cols], na[h, 0, i], na[h, 1, i])

        loop(4, first_a)
        a2[h] = three("y", ra2.at[h], lambda k, h=h: sa1.at[h, :, ys[k]])
        arrive([near_b[h, 0], near_b[h, 1]])

        def first_b(i, h=h, cols=cols):
            sb1[h, i] = add(sb1, pb[i, y, :, cols], nb[h, 0, i], nb[h, 1, i])

        loop(4, first_b)
        b2[h] = three("x", rb2.at[h], lambda k, h=h: sb1.at[h, :, rows16(xs[k])])
        if h == 0:
            arrive([cx2])
            scx2[...] = add(scx2, scx1[x], rcx2[0], rcx2[1], rcx2[2])
            cx3 = three("y", rcx3, lambda k: scx2.at[ys[k]])
            arrive([cy2])
            scy2[...] = add(scy2, scy1[zh], rcy2[0], rcy2[1], rcy2[2])
            cy3 = send(scy2, rcy3, near)
    arrive(rims)
    rows_f[:, 8:9] += jnp.where(sq > 0, rim_before[:, 0:1], 0.0)
    rows_f[:, 263:264] += jnp.where(sq < 7, rim_after[:, 7:8], 0.0)
    for j in range(6):
        seq_o[:, 128 * j : 128 * j + 128] = rows_f[j, 8:264].astype(BF16)
    for h in range(2):
        arrive([a2[h]])
        sa2[h] = add(sa2, sa1[h, :, y], ra2[h, 0], ra2[h, 1], ra2[h, 2])
        a3[h] = three("zh", ra3.at[h], lambda k, h=h: sa2.at[h, zs[k]])
        arrive([b2[h]])
        sb2[h] = add(sb2, sb1[h, :, rows16(x)], rb2[h, 0], rb2[h, 1], rb2[h, 2])
        b3[h] = three("zh", rb3.at[h], lambda k, h=h: sb2.at[h, zs[k]])
        if h == 0:
            arrive([cx3])
            scx3[...] = add(scx3, scx2[y], rcx3[0], rcx3[1], rcx3[2])
            cx4 = send(scx3, rcx4, near)
            arrive([cy3])
            scy3[...] = add(scy3, scy2[...], rcy3[...])
            cy4 = three("x", rcy4, lambda k: scy3)

    send.finish(12)
    for h in range(2):
        arrive([a3[h]])
        sa3[h] = add(sa3, sa2[h, zh], ra3[h, 0], ra3[h, 1], ra3[h, 2])
        a4[h] = send(sa3.at[h], ra4.at[h], near)
        arrive([b3[h]])
        sb3[h] = add(sb3, sb2[h, zh], rb3[h, 0], rb3[h, 1], rb3[h, 2])
        b4[h] = send(sb3.at[h], rb4.at[h], near)
        if h == 0:
            arrive([cx4])
            final_x[x] = add(final_x, scx3[...], rcx4[...])
            spread = [send(final_x.at[x], final_x.at[x], device(moved(at, x=k))) for k in (1, 2, 3)]
            arrive([cy4])
            final_y[...] = add(final_y, scy3[...], rcy4[0], rcy4[1], rcy4[2])
    for h in range(2):
        arrive([a4[h]])
        final[x, 0, h] = add(final, sa3[h], ra4[h])
        arrive([b4[h]])
        final[x, 1, h] = add(final, sb3[h], rb4[h])
    spread += [send(final.at[x], final.at[x], device(moved(at, x=k))) for k in (1, 2, 3)]
    arrive(spread)
    send.finish()


def finish_kernel(seq_i, final, final_x, final_y, seq_o, conv_o, dna_o, qkv_o, out_o):
    seq_o[0] = seq_i[...]
    for h in range(2):
        columns = slice(384 * h, 384 * h + 384)
        for q in range(4):
            conv_o[16 * q : 16 * q + 16, columns] = final[q, 0, h].astype(F32)
        conv_o[64:80, columns] = final[0, 1, h].astype(F32)
        conv_o[80:96, columns] = final[1, 1, h].astype(F32)
        dna_o[:, columns] = final[2, 1, h].astype(F32)
        out_o[:, columns] = final[3, 1, h].astype(F32)
    for q in range(4):
        qkv_o[0:16, 384 * q : 384 * q + 384] = final_x[q].astype(F32)
    last_rows = final_y[...].astype(F32)
    qkv_o[16:24, 0:768] = last_rows[0:8]
    qkv_o[16:24, 768:1536] = last_rows[8:16]


def layer(*operands):
    vmem = pl.BlockSpec(memory_space=pltpu.VMEM)
    low = [
        (4, 4, 2, 4, 16, 1152), (4, 4, 2, 80, 768), (16, 768), (16, 768),
        (4, 128, 768), (4, 4, 2, 96, 128), (128, 512), (4, 4, 2, 16, 128), (768, 512), (768, 512),
        (128, 512), (128, 512), (4, 4, 2, 16, 128), (4, 4, 2, 16, 128), (128, 1536), (128, 512), (4, 4, 2, 16, 128),
        (4, 4, 128, 128), (4, 4, 128, 128), (4, 128, 128), (4, 128, 128), (4, 4, 128, 128), (4, 128, 128), (4, 128, 128),
        (4, 4, 128, 128), (4, 128, 128), (4, 128, 128),
        (4, 128, 1024), (4, 128, 1024),
    ] + 3 * [(4, 4, 64, 768), (4, 4, 64, 768), (4, 4, 4, 16, 384), (4, 4, 16, 768)] + [
        (2, 2, 2, 4, 16, 384), (2, 2, 4, 4, 16, 384), (2, 4, 4, 16, 384), (2, 3, 4, 16, 384),
        (2, 4, 16, 384), (2, 3, 16, 384), (2, 16, 384), (2, 16, 384),
        (2, 2, 2, 64, 384), (2, 2, 4, 64, 384), (2, 4, 64, 384), (2, 3, 4, 16, 384),
        (2, 4, 16, 384), (2, 3, 16, 384), (2, 16, 384), (2, 16, 384),
        (2, 2, 4, 16, 384), (2, 4, 4, 16, 384), (4, 4, 16, 384), (3, 4, 16, 384), (4, 16, 384), (3, 16, 384), (16, 384), (16, 384),
        (2, 2, 16, 768), (2, 4, 16, 768), (4, 16, 768), (3, 16, 768), (16, 768), (16, 768), (16, 768), (3, 16, 768),
    ]
    wide = [(128, 768), (128, 768), (128, 1), (6, 272, 128), (4, 128, 1024), (2, 6, 8, 128), (6, 8, 128), (6, 8, 128)]
    results = pl.pallas_call(
        layer_kernel,
        name="layer",
        out_shape=tuple(
            jax.ShapeDtypeStruct(shape, BF16)
            for shape in ((256, 768), (4, 2, 2, 16, 384), (4, 16, 384), (16, 768))
        ),
        in_specs=[vmem] * 7,
        out_specs=(vmem,) * 4,
        scratch_shapes=[pltpu.VMEM(shape, BF16) for shape in low]
        + [pltpu.VMEM(shape, F32) for shape in wide]
        + [pltpu.SemaphoreType.DMA((60,)), pltpu.SemaphoreType.DMA((138,))],
        compiler_params=pltpu.CompilerParams(
            collective_id=1, has_side_effects=True, vmem_limit_bytes=60 * 2**20
        ),
    )(*operands)
    return pl.pallas_call(
        finish_kernel,
        name="finish",
        out_shape=(
            jax.ShapeDtypeStruct((1, 256, 768), BF16),
            jax.ShapeDtypeStruct((96, 768), F32),
            jax.ShapeDtypeStruct((16, 768), F32),
            jax.ShapeDtypeStruct((24, 1536), F32),
            jax.ShapeDtypeStruct((16, 768), F32),
        ),
        in_specs=[vmem] * 4,
        out_specs=(vmem,) * 5,
    )(*results)


def per_device(seq_in, bases, conv_weight, dna_weight, qkv_weight, out_weight, cotangent):
    return layer(
        conv_weight, dna_weight, qkv_weight, out_weight, seq_in[0], bases[0].reshape(128, BIN), cotangent[0]
    )


def solution(mesh):
    in_specs = (
        P("dp", "seq", None),
        P("dp", "seq"),
        P("dp", None),
        P("dp", None),
        P("dp", None),
        P("dp", None),
        P("dp", "seq", None),
    )
    out_specs = (P("dp", "seq", None), P("dp", None), P("dp", None), P("dp", None), P("dp", None))
    return jax.shard_map(
        per_device, mesh=mesh, in_specs=in_specs, out_specs=out_specs, check_vma=False
    )
```

```python
import math

import jax
import jax.numpy as jnp
from jax import lax
from jax.experimental import pallas as pl
from jax.experimental.pallas import tpu as pltpu
from jax.sharding import PartitionSpec as P

H = 4
BIN = 128
BF16 = jnp.bfloat16
F32 = jnp.float32
MESH = pl.DeviceIdType.MESH
epsilon = 1e-06

SIZES = {"zh": 4, "y": 4, "c": 2, "zl": 2, "x": 4}
PEERS = [(a, k) for a in ("zh", "y", "x") for k in (1, 2, 3)] + [("zl", 1), ("c", 1)]


def here():
    dp = lax.axis_index("dp")
    sq = lax.axis_index("seq")
    return {"zh": dp // 8, "y": lax.rem(dp // 2, 4), "c": lax.rem(dp, 2), "zl": sq // 4, "x": lax.rem(sq, 4)}


def moved(at, **steps):
    to = dict(at)
    for axis, step in steps.items():
        to[axis] = lax.rem(at[axis] + step, SIZES[axis])
    return to


def device(at):
    return (at["zh"] * 8 + at["y"] * 2 + at["c"], at["zl"] * 4 + at["x"])


class Sender:
    def __init__(self, send_sems, recv_sems):
        self.send_sems, self.recv_sems, self.sent, self.due = send_sems, recv_sems, 0, 0
        self.free, self.copies = [], []

    def copy(self, src, dst, to, recv):
        if not self.free:
            self.free.append(self.sent)
            self.sent += 1
        place = self.free.pop(0)
        copy = pltpu.make_async_remote_copy(
            src_ref=src,
            dst_ref=dst,
            send_sem=self.send_sems.at[place],
            recv_sem=self.recv_sems.at[recv],
            device_id=to,
            device_id_type=MESH,
        )
        copy.start()
        self.copies.append((copy, place))
        return copy

    def __call__(self, src, dst, to):
        self.due += 1
        return self.copy(src, dst, to, self.due - 1)

    def group(self, whole, copies):
        self.due += 1
        for src, dst, to in copies:
            self.copy(src, dst, to, self.due - 1)
        return pltpu.make_async_remote_copy(
            src_ref=whole,
            dst_ref=whole,
            send_sem=self.send_sems.at[0],
            recv_sem=self.recv_sems.at[self.due - 1],
            device_id=copies[0][2],
            device_id_type=MESH,
        )

    def finish(self, oldest=None):
        done = self.copies[:oldest]
        for copy, place in done:
            copy.wait_send()
            self.free.append(place)
        self.copies = self.copies[len(done) :]


def arrive(copies):
    for copy in copies:
        copy.wait_recv()


def rows16(index, base=0):
    return pl.ds(pl.multiple_of(index * 16 + base, 16), 16)


def half_columns(index):
    return pl.ds(pl.multiple_of(index * 384, 128) if not isinstance(index, int) else index * 384, 384)


def right_dot(left, right):
    return lax.dot_general(left, right, (((1,), (1,)), ((), ())), preferred_element_type=F32)


def row_dot(left, right):
    return lax.dot_general(left, right, (((0,), (0,)), ((), ())), preferred_element_type=F32)


def dot(left, right):
    return jnp.dot(left, right, preferred_element_type=F32)


def add(target, *terms):
    total = terms[0].astype(F32)
    for term in terms[1:]:
        total += term.astype(F32)
    return total.astype(target.dtype)


def loop(n, body):
    def step(i, carry):
        body(i)
        return carry

    lax.fori_loop(0, n, step, 0)


class Ring:
    def __init__(self, send, at, axis, region):
        self.send, self.me, self.region = send, at[axis], region
        self.right, self.left = device(moved(at, **{axis: 1})), device(moved(at, **{axis: 3}))

    def at(self, step):
        return lax.rem(self.me + step, 4)

    def go(self, index, part, to):
        ref = self.region(index, part)
        return [self.send(ref, ref, to)]

    def start(self):
        self.from_left = self.go(self.me, None, self.right)
        self.from_right = self.go(self.me, None, self.left)

    def left_in(self):
        arrive(self.from_left)
        self.far_left = self.go(self.at(3), 0, self.right)

    def right_in(self):
        arrive(self.from_right)
        self.far_right = self.go(self.at(1), 1, self.left)

    def both_in(self):
        self.left_in()
        self.right_in()

    def far_in(self):
        arrive(self.far_left)
        arrive(self.far_right)


def layer_kernel(
    conv_s, dna_s, qkv_s, out_s, rows_in, letters, upstream,
    seq_o, final, final_x, final_y,
    ga, gb, before, after,
    taps, taps_y, taps_t, onehot, onehot_t, choose_x, choose_y, wide_x, wide_y, wide_xt, wide_yt, d_proj, attended, attended_t,
    mine, got, got_k, got_v, outgo, outgo_k, outgo_v, back, back_k, back_v, probs_s, scores_s,
    pa_s, pb_s, px_s, py_s, pa, pb, px, py, pa_r, pb_r, px_r, py_r,
    fa, na, sa1, ra2, sa2, ra3, sa3, ra4,
    fb, nb, sb1, rb2, sb2, rb3, sb3, rb4,
    fcx, ncx, scx1, rcx2, scx2, rcx3, scx3, rcx4,
    fcy, ncy, scy1, rcy2, scy2, rcy3, scy3, rcy4,
    slope, unit, inverse, rows_f, probs_f, rim_out, rim_before, rim_after,
    send_sems, recv_sems,
):
    at = here()
    zh, y, c, zl, x = (at[a] for a in ("zh", "y", "c", "zl", "x"))
    sq = lax.axis_index("seq")
    dp = lax.axis_index("dp")
    behind, ahead = (dp, lax.rem(sq + 7, 8)), (dp, lax.rem(sq + 1, 8))
    sibling = device(moved(at, c=1))
    near = device(moved(at, zl=1))
    across = [moved(at, x=k, zl=1) for k in range(4)]
    everyone = [device(moved(at, **{a: k})) for a, k in PEERS] + [behind, ahead]
    everyone += [device(p) for p in across[1:]]
    barrier = pltpu.get_barrier_semaphore()
    for one in everyone:
        pl.semaphore_signal(barrier, inc=1, device_id=one, device_id_type=MESH)
    xs = [lax.rem(x + k, 4) for k in range(4)]
    ys = [lax.rem(y + k, 4) for k in range(4)]
    zs = [lax.rem(zh + k, 4) for k in range(4)]

    quarter = rows16(x)
    ga[zh, y, c, x, :, 0:768] = conv_s[quarter]
    ga[zh, y, c, x, :, 768:1152] = qkv_s[0:16, half_columns(x)]
    gb[zh, y, c, 0:32] = conv_s[64:96]
    gb[zh, y, c, 32:48] = dna_s[...]
    gb[zh, y, c, 48:64] = out_s[...]
    last_rows = [qkv_s[:, 768 * i : 768 * i + 768].astype(F32)[16:24] for i in range(2)]
    gb[zh, y, c, 64:80] = jnp.concatenate(last_rows, axis=0).astype(BF16)
    pl.semaphore_wait(barrier, len(everyone))

    send = Sender(send_sems, recv_sems)

    def ref_a(height, step, index, part=None):
        rows = pl.ds(0, 4) if part is None else pl.ds(2 * part, 2)
        return ga.at[rows if height is None else height, step, c, index]

    def ref_b(height, step, part=None):
        return gb.at[height, step, c] if part is None else gb.at[height, step, c, :, half_columns(part)]

    core = []

    def pass_on(ref):
        core.append(send(ref, ref, sibling))

    def pass_a(step):
        pass_on(ga.at[:, step, c])

    def pass_b(height):
        pass_on(gb.at[height, :, c])

    a1 = []
    for k in (2, 1, 3):
        a1.append(send(ref_a(zh, y, x), ref_a(zh, y, x), device(moved(at, zh=k))))
    halo = [
        send(rows_in.at[pl.ds(240, 16)], before, ahead),
        send(rows_in.at[pl.ds(0, 16)], after, behind),
    ]
    ring_z = Ring(send, at, "zh", lambda index, part: ref_b(index, y, part))
    rings_y = [Ring(send, at, "y", lambda index, part, v=zs[k]: ref_b(v, index, part)) for k in range(4)]
    rings_x = [Ring(send, at, "x", lambda index, part, v=ys[k]: ref_a(None, v, index, part)) for k in range(4)]
    ring_a = Ring(send, at, "y", lambda index, part: ref_a(None, index, x, part))
    ring_z.start()
    rings_y[0].start()
    row = lax.broadcasted_iota(jnp.int32, (128, 512), 0)
    column = lax.broadcasted_iota(jnp.int32, (128, 512), 1)
    repeat = (column // 4 == row).astype(F32).astype(BF16)
    repeated = dot(letters[...].astype(F32).astype(BF16), repeat)
    onehot[...] = (repeated == lax.rem(column, 4).astype(F32)).astype(F32).astype(BF16)
    row = lax.broadcasted_iota(jnp.int32, (768, 512), 0)
    column = lax.broadcasted_iota(jnp.int32, (768, 512), 1)
    first_row = column // 16 * 24
    choose_x[...] = (first_row + lax.rem(column, 16) == row).astype(F32).astype(BF16)
    choose_y[...] = (first_row + 16 + lax.rem(column, 8) == row).astype(F32).astype(BF16)
    arrive(a1)
    ring_a.start()
    rings_x[0].start()
    ring_z.left_in()
    rings_y[3].start()
    ring_z.right_in()
    rings_y[0].both_in()
    ring_a.left_in()
    rings_x[3].start()
    ring_a.right_in()
    rings_x[1].start()
    rings_y[1].start()
    rings_x[0].both_in()
    ring_a.far_in()
    rings_x[2].start()
    ring_z.far_in()
    rings_y[2].start()
    rings_y[3].both_in()
    rings_x[3].both_in()
    rings_x[1].both_in()
    rings_y[1].both_in()
    rings_y[0].far_in()
    pass_b(zs[0])
    rings_x[0].far_in()
    pass_a(ys[0])
    rings_x[2].both_in()
    rings_y[2].both_in()

    send.finish(24)
    arrive(halo)
    for j in range(6):
        lanes = slice(128 * j, 128 * j + 128)
        rows_f[j, 8:264] = rows_in[:, lanes].astype(F32)
        rows_f[j, 0:8] = jnp.where(sq > 0, before[:, lanes].astype(F32)[8:16], 0.0)
        rows_f[j, 264:272] = jnp.where(sq < 7, after[:, lanes].astype(F32)[0:8], 0.0)
        for i in range(4):
            taps[i, :, lanes] = rows_f[j, pl.ds(7 + i, 128, stride=2)].astype(BF16)
    for i in range(4):
        whole = taps[i].astype(F32)
        moved_on = pltpu.roll(whole, 704, 1).astype(BF16)
        for k in range(4):
            start = 384 * (k // 2) + 128 * (k % 2)
            taps_y[k, i] = moved_on[:, start : start + 256] if k % 2 else taps[i, :, start : start + 256]

    rings_y[3].far_in()
    pass_b(zs[3])
    rings_y[1].far_in()
    pass_b(zs[1])
    rings_x[3].far_in()
    pass_a(ys[3])
    rings_x[1].far_in()
    pass_a(ys[1])
    rings_y[2].far_in()
    pass_b(zs[2])
    rings_x[2].far_in()
    pass_a(ys[2])

    arrive(core[:-1])

    def conv_full(i):
        first = ga[i, :, :, :, :, 0:768].reshape(4, 2, 64, 768)
        return jnp.concatenate([first, gb[i, :, :, 0:32]], axis=2).reshape(768, 768)

    def qx_full(i):
        return jnp.concatenate(
            [ga[:, :, :, 2 * i + j, :, 768:1152].reshape(512, 384) for j in range(2)], axis=1
        )

    def qy_full():
        return gb[:, :, :, 64:80].reshape(512, 768)

    dna_full = gb[:, :, :, 32:48].reshape(512, 768)
    out_full = gb[:, :, :, 48:64].reshape(512, 768)
    d_attend = right_dot(upstream[...], out_full).astype(BF16)
    slope[...] = dot(onehot[...], dna_full)

    def y_block(k):
        total = 0.0
        for i in range(4):
            first = ga[i, ys[k], :, :, :, 0:768].reshape(2, 64, 768)
            block = jnp.concatenate([first, gb[i, ys[k], :, 0:32]], axis=1).reshape(192, 768)
            block = jnp.concatenate([block, jnp.zeros((64, 768), BF16)], axis=0)
            total += dot(taps_y[ys[k], i], block)
        slope[...] += total

    for k in (0, 3, 1):
        y_block(k)
    arrive(core[-1:])
    y_block(2)
    pre = slope[...]
    bend = jnp.tanh(math.sqrt(2.0 / math.pi) * (pre + 0.044715 * (pre * pre * pre)))
    share = 0.5 * (1.0 + bend)
    feature = (pre * share).astype(BF16).astype(F32)
    slope[...] = share + pre * (0.5 * (1.0 - bend * bend)) * (
        math.sqrt(2.0 / math.pi) * (1.0 + 3.0 * 0.044715 * (pre * pre))
    )
    scale = lax.rsqrt(jnp.mean(feature * feature, axis=1, keepdims=True) + epsilon)
    inverse[...] = scale
    unit[...] = feature * scale
    normed = unit[...].astype(BF16)
    wide_x[...] = dot(normed, choose_x[...]).astype(BF16)
    wide_y[...] = dot(normed, choose_y[...]).astype(BF16)
    side_of = lax.rem(lax.broadcasted_iota(jnp.int32, (128, 512), 1), 16) // 8
    own_y = [jnp.where(side_of == i, wide_y[...].astype(F32), 0.0).astype(BF16) for i in range(2)]
    from_y = dot(jnp.concatenate(own_y, axis=0), qy_full())
    for i in range(2):
        projected = (dot(wide_x[...], qx_full(i)) + from_y[128 * i : 128 * i + 128]).astype(BF16)
        for piece in range(6):
            kind, head = divmod(6 * i + piece, 4)
            mine[head, (1, 0, 2)[kind]] = projected[:, 128 * piece : 128 * piece + 128]
    for head in range(H):
        mine[head, 3] = d_attend[:, 128 * head : 128 * head + 128]

    kq, vd = pl.ds(0, 2), pl.ds(2, 2)
    kq_in, vd_in = {}, {}
    from_near_k = send.group(got_k, [(mine.at[x, 0], got_k.at[x], near)])
    near_k = send.due - 1
    from_near_v = send.group(got_v, [(mine.at[x, 2], got_v.at[x], near)])
    near_v = send.due - 1
    for k in (1, 3, 2):
        kq_in[k] = send(mine.at[xs[k], kq], got.at[x, kq], device(moved(at, x=k)))
    for k in (1, 3, 2):
        vd_in[k] = send(mine.at[xs[k], vd], got.at[x, vd], device(moved(at, x=k)))
    sources = {k: lax.rem(x + 4 - k, 4) for k in (0, 1, 3, 2)}
    got[x] = mine[x]
    for k in (1, 3, 2):
        arrive([kq_in[k]])
        send.copy(got.at[sources[k], 0], got_k.at[sources[k]], near, near_k)
    def transpose_tap(i):
        taps_t[i] = taps[i].T.reshape(4, 2, 96, 128)

    loop(4, transpose_tap)
    onehot_t[...] = onehot[...].T.reshape(4, 4, 2, 16, 128)
    wide_xt[...] = wide_x[...].T.reshape(4, 4, 2, 16, 128)
    wide_yt[...] = wide_y[...].T.reshape(4, 4, 2, 16, 128)
    arrive([from_near_k])
    keys = jnp.concatenate([got[:, 0].reshape(512, 128), got_k[...].reshape(512, 128)], axis=0)
    scaling = 1.0 / math.sqrt(128)

    pairs = (slice(0, 2), slice(2, 4))

    def soft(pair):
        scores = right_dot(got[pair, 1].reshape(256, 128), keys) * scaling
        powers = jnp.exp(scores - jnp.max(scores, axis=1, keepdims=True))
        probs = powers * (1.0 / jnp.sum(powers, axis=1, keepdims=True))
        probs_f[pair] = probs.reshape(2, 128, 1024)
        probs_s[pair] = probs.astype(BF16).reshape(2, 128, 1024)

    def pass_v(k):
        arrive([vd_in[k]])
        send.copy(got.at[sources[k], 2], got_v.at[sources[k]], near, near_v)

    soft(pairs[0])
    pass_v(1)
    pass_v(3)
    soft(pairs[1])
    pass_v(2)
    home_v, home_q, home_k = [], [], []
    all_queries = got[:, 1].reshape(512, 128)
    all_upward = got[:, 3].reshape(512, 128)
    all_probs = probs_s[...].reshape(512, 1024)
    d_values = row_dot(all_upward, all_probs).T.astype(BF16).reshape(8, 128, 128)
    outgo_v[...] = d_values[4:8]
    home_v.append(send.group(back_v, [(outgo_v.at[p["x"]], back_v.at[x], device(p)) for p in across]))
    outgo[:, 1] = d_values[0:4]
    arrive([from_near_v])
    values = jnp.concatenate([got[:, 2].reshape(512, 128), got_v[...].reshape(512, 128)], axis=0)
    outgo[:, 0] = dot(all_probs, values).astype(BF16).reshape(4, 128, 128)
    for k in (1, 3, 2):
        block = pl.ds(0, 2)
        home_v.append(send(outgo.at[xs[k], block], back.at[x, block], device(moved(at, x=k))))
    for pair in pairs:
        probs = probs_f[pair].reshape(256, 1024)
        d_probs = right_dot(got[pair, 3].reshape(256, 128), values)
        inner = jnp.sum(probs * d_probs, axis=1, keepdims=True)
        d_scores = (probs * (d_probs - inner) * scaling).astype(BF16)
        scores_s[pair] = d_scores.reshape(2, 128, 1024)
        outgo[pair, 2] = dot(d_scores, keys).astype(BF16).reshape(2, 128, 128)
    for k in (1, 3, 2):
        home_q.append(send(outgo.at[xs[k], 2], back.at[x, 2], device(moved(at, x=k))))

    def key_grads(columns):
        d_keys = row_dot(all_queries, scores_s[:, :, columns].reshape(512, 512)).T
        return d_keys.astype(BF16).reshape(4, 128, 128)

    outgo_k[...] = key_grads(slice(512, 1024))
    home_k.append(send.group(back_k, [(outgo_k.at[p["x"]], back_k.at[x], device(p)) for p in across]))
    outgo[:, 3] = key_grads(slice(0, 512))
    for k in (1, 3, 2):
        home_k.append(send(outgo.at[xs[k], 3], back.at[x, 3], device(moved(at, x=k))))
    back[x] = outgo[x]

    def columns_of(head, start=0):
        return slice(start + 128 * head, start + 128 * head + 128)

    arrive(home_v)
    for head in range(H):
        attended[:, columns_of(head)] = back[head, 0]
        total = back[head, 1].astype(F32) + back_v[head].astype(F32)
        d_proj[:, columns_of(head, 1024)] = total.astype(BF16)
    attended_t[...] = attended[...].T.reshape(4, 4, 2, 16, 128)
    for parity, to_b in ((1 - c, pb_s), (c, pb)):
        left = attended_t[:, :, parity].reshape(256, 128)
        to_b[:, :, 48:64] = dot(left, upstream[...]).astype(BF16).reshape(4, 4, 16, 768)
    arrive(home_q)
    for head in range(H):
        d_proj[:, columns_of(head)] = back[head, 2]

    def qkv_quarters(parity, to_x, quarters):
        left = wide_xt[:, :, parity].reshape(256, 128)
        for q in quarters:
            block = dot(left, d_proj[:, 384 * q : 384 * q + 384]).astype(BF16)
            to_x[q] = block.reshape(4, 4, 16, 384)

    qkv_quarters(1 - c, px_s, (0, 3))
    qkv_quarters(c, px, (0, 3))
    d_q, d_v = d_proj[:, 0:512], d_proj[:, 1024:1536]
    d_x = right_dot(d_q, qx_full(0)[:, 0:512]) + right_dot(d_v, qx_full(1)[:, 256:768])
    d_y0, d_y1 = right_dot(d_q, qy_full()[:, 0:512]), right_dot(d_v, qy_full()[:, 256:768])
    arrive(home_k)
    send.finish()
    for head in range(H):
        total = back[head, 3].astype(F32) + back_k[head].astype(F32)
        d_proj[:, columns_of(head, 512)] = total.astype(BF16)

    row_side = lax.rem(lax.broadcasted_iota(jnp.int32, (256, 768), 0), 16)

    def qkv_grads(parity, to_x, to_y):
        qkv_quarters(parity, to_x, (1, 2))
        left = wide_yt[:, :, parity].reshape(256, 128)
        both = [dot(left, d_proj[:, 768 * i : 768 * i + 768]) for i in range(2)]
        to_y[...] = jnp.where(row_side < 8, both[0], both[1]).astype(BF16).reshape(4, 4, 16, 768)

    order = (2, 1, 3, 0)
    core_cx, core_cy, core_a, core_b = {}, {}, {}, {}
    qkv_grads(1 - c, px_s, py_s)
    for k in order:
        core_cx[k] = send(px_s.at[:, zs[k]], px_r.at[:, zs[k]], sibling)
        core_cy[k] = send(py_s.at[:, ys[k]], py_r.at[:, ys[k]], sibling)
    qkv_grads(c, px, py)
    d_k0, d_k1 = d_proj[:, 512:768], d_proj[:, 768:1024]
    d_x += right_dot(d_k0, qx_full(0)[:, 512:768]) + right_dot(d_k1, qx_full(1)[:, 0:256])
    d_y0 += right_dot(d_k0, qy_full()[:, 512:768])
    d_y1 += right_dot(d_k1, qy_full()[:, 0:256])
    d_y = jnp.where(side_of == 0, d_y0, d_y1)

    def sum_cx(k):
        arrive([core_cx[k]])
        px[:, zs[k]] = add(px, px[:, zs[k]], px_r[:, zs[k]])

    def sum_cy(k):
        arrive([core_cy[k]])
        py[:, ys[k]] = add(py, py[:, ys[k]], py_r[:, ys[k]])

    right_x, left_x = device(moved(at, x=1)), device(moved(at, x=3))
    right_y, left_y = device(moved(at, y=1)), device(moved(at, y=3))
    right_z, left_z = device(moved(at, zh=1)), device(moved(at, zh=3))
    low, high = pl.ds(0, 2), pl.ds(2, 2)
    sides = ((0, 1, right_x, right_y), (1, 3, left_x, left_y))
    d_normed = 0.0
    for terms, choose in ((d_x, choose_x), (d_y, choose_y)):
        d_high = terms.astype(BF16)
        d_low = (terms - d_high.astype(F32)).astype(BF16)
        both = right_dot(jnp.concatenate([d_high, d_low], axis=0), choose[...])
        d_normed += both[0:128] + both[128:256]
    d_feature = upstream[...].astype(F32) + inverse[...] * (
        d_normed - unit[...] * jnp.mean(d_normed * unit[...], axis=1, keepdims=True)
    )
    d_pre = (d_feature * slope[...]).astype(BF16)

    sum_cx(2)
    far_cx = [
        send(px.at[quarters, zs[2]], fcx.at[side], to) for side, quarters, to in ((0, low, right_z), (1, high, left_z))
    ]
    sum_cy(2)
    far_cy = [
        send(py.at[heights, ys[2]], fcy.at[side], to) for side, heights, to in ((0, low, right_y), (1, high, left_y))
    ]
    def conv_grads(parity, to_a, to_b):
        def one(i):
            block = dot(taps_t[i, :, parity].reshape(384, 128), d_pre).astype(BF16).reshape(4, 96, 768)
            to_a[i] = block[:, 0:64]
            to_b[i, :, 0:32] = block[:, 64:96]

        loop(4, one)
        left = onehot_t[:, :, parity].reshape(256, 128)
        to_b[:, :, 32:48] = dot(left, d_pre).astype(BF16).reshape(4, 4, 16, 768)

    conv_grads(1 - c, pa_s, pb_s)
    for k in order:
        core_a[k] = send(pa_s.at[:, :, rows16(xs[k])], pa_r.at[:, :, rows16(xs[k])], sibling)
        core_b[k] = send(pb_s.at[:, ys[k]], pb_r.at[:, ys[k]], sibling)
    conv_grads(c, pa, pb)

    def sum_a(k):
        arrive([core_a[k]])
        rows = rows16(xs[k])

        def one(i):
            pa[i, :, rows] = add(pa, pa[i, :, rows], pa_r[i, :, rows])

        loop(4, one)

    def sum_b(k):
        arrive([core_b[k]])

        def one(i):
            pb[i, ys[k]] = add(pb, pb[i, ys[k]], pb_r[i, ys[k]])

        loop(4, one)

    halves = [(h, pl.ds(384 * h, 384), slice(384 * h, 384 * h + 384)) for h in range(2)]
    far_a, far_b = {}, {}
    sum_a(2)
    sum_b(2)
    for h, columns, _ in halves:
        for side, heights, to_x, to_y in ((0, low, right_x, right_y), (1, high, left_x, left_y)):
            far_a[h, side] = send(pa.at[heights, :, rows16(xs[2]), columns], fa.at[h, side], to_x)
            far_b[h, side] = send(pb.at[heights, ys[2], :, columns], fb.at[h, side], to_y)
    near_cx, near_cy = [], []
    for side, k, to_x, to_y in sides:
        sum_cx(k)
        arrive([far_cx[side]])
        part = slice(2 * side, 2 * side + 2)
        px[part, zs[k]] = add(px, px[part, zs[k]], fcx[side])
        near_cx.append(send(px.at[:, zs[k]], ncx.at[side], (right_z, left_z)[side]))
        sum_cy(k)
        arrive([far_cy[side]])
        py[part, ys[k]] = add(py, py[part, ys[k]], fcy[side])
        near_cy.append(send(py.at[:, ys[k]], ncy.at[side], to_y))
    for side, k, to_x, to_y in sides:
        sum_a(k)
        sum_b(k)
    near_a, near_b = {}, {}
    for h, columns, cols in halves:
        for side, k, to_x, to_y in sides:
            rows = rows16(xs[k])
            arrive([far_a[h, side]])

            def join_a(i, h=h, side=side, rows=rows, cols=cols):
                pa[2 * side + i, :, rows, cols] = add(pa, pa[2 * side + i, :, rows, cols], fa[h, side, i])

            loop(2, join_a)
            near_a[h, side] = send(pa.at[:, :, rows, columns], na.at[h, side], to_x)
            arrive([far_b[h, side]])

            def join_b(i, h=h, side=side, index=ys[k], cols=cols):
                pb[2 * side + i, index, :, cols] = add(pb, pb[2 * side + i, index, :, cols], fb[h, side, i])

            loop(2, join_b)
            near_b[h, side] = send(pb.at[:, ys[k], :, columns], nb.at[h, side], to_y)

    def three(axis, whole, source):
        return send.group(
            whole, [(source(k), whole.at[k - 1], device(moved(at, **{axis: k}))) for k in (1, 3, 2)]
        )

    sum_cx(0)
    arrive(near_cx)
    scx1[...] = add(scx1, px[:, zh], ncx[0], ncx[1])
    cx2 = three("x", rcx2, lambda k: scx1.at[xs[k]])
    sum_cy(0)
    arrive(near_cy)
    scy1[...] = add(scy1, py[:, y], ncy[0], ncy[1])
    cy2 = three("zh", rcy2, lambda k: scy1.at[zs[k]])
    sum_a(0)
    sum_b(0)

    send.finish(28)
    rows_f[:, 256:272] = jnp.zeros((6, 16, 128), F32)
    for i in range(4):
        terms = right_dot(d_pre, conv_full(i))
        for j in range(6):
            target = pl.ds(7 + i, 128, stride=2)
            block = terms[:, 128 * j : 128 * j + 128]
            rows_f[j, target] = block if i < 2 else rows_f[j, target] + block
    rim_out[0] = rows_f[:, 264:272]
    rim_out[1] = rows_f[:, 0:8]
    rims = [send(rim_out.at[0], rim_before, ahead), send(rim_out.at[1], rim_after, behind)]

    a2, b2, a3, b3, a4, b4 = {}, {}, {}, {}, {}, {}
    for h, columns, cols in halves:
        arrive([near_a[h, 0], near_a[h, 1]])

        def first_a(i, h=h, cols=cols):
            sa1[h, i] = add(sa1, pa[i, :, rows16(x), cols], na[h, 0, i], na[h, 1, i])

        loop(4, first_a)
        a2[h] = three("y", ra2.at[h], lambda k, h=h: sa1.at[h, :, ys[k]])
        arrive([near_b[h, 0], near_b[h, 1]])

        def first_b(i, h=h, cols=cols):
            sb1[h, i] = add(sb1, pb[i, y, :, cols], nb[h, 0, i], nb[h, 1, i])

        loop(4, first_b)
        b2[h] = three("x", rb2.at[h], lambda k, h=h: sb1.at[h, :, rows16(xs[k])])
        if h == 0:
            arrive([cx2])
            scx2[...] = add(scx2, scx1[x], rcx2[0], rcx2[1], rcx2[2])
            cx3 = three("y", rcx3, lambda k: scx2.at[ys[k]])
            arrive([cy2])
            scy2[...] = add(scy2, scy1[zh], rcy2[0], rcy2[1], rcy2[2])
            cy3 = send(scy2, rcy3, near)
    arrive(rims)
    rows_f[:, 8:9] += jnp.where(sq > 0, rim_before[:, 0:1], 0.0)
    rows_f[:, 263:264] += jnp.where(sq < 7, rim_after[:, 7:8], 0.0)
    for j in range(6):
        seq_o[:, 128 * j : 128 * j + 128] = rows_f[j, 8:264].astype(BF16)
    for h in range(2):
        arrive([a2[h]])
        sa2[h] = add(sa2, sa1[h, :, y], ra2[h, 0], ra2[h, 1], ra2[h, 2])
        a3[h] = three("zh", ra3.at[h], lambda k, h=h: sa2.at[h, zs[k]])
        arrive([b2[h]])
        sb2[h] = add(sb2, sb1[h, :, rows16(x)], rb2[h, 0], rb2[h, 1], rb2[h, 2])
        b3[h] = three("zh", rb3.at[h], lambda k, h=h: sb2.at[h, zs[k]])
        if h == 0:
            arrive([cx3])
            scx3[...] = add(scx3, scx2[y], rcx3[0], rcx3[1], rcx3[2])
            cx4 = send(scx3, rcx4, near)
            arrive([cy3])
            scy3[...] = add(scy3, scy2[...], rcy3[...])
            cy4 = three("x", rcy4, lambda k: scy3)

    send.finish(12)
    for h in range(2):
        arrive([a3[h]])
        sa3[h] = add(sa3, sa2[h, zh], ra3[h, 0], ra3[h, 1], ra3[h, 2])
        a4[h] = send(sa3.at[h], ra4.at[h], near)
        arrive([b3[h]])
        sb3[h] = add(sb3, sb2[h, zh], rb3[h, 0], rb3[h, 1], rb3[h, 2])
        b4[h] = send(sb3.at[h], rb4.at[h], near)
        if h == 0:
            arrive([cx4])
            final_x[x] = add(final_x, scx3[...], rcx4[...])
            spread = [send(final_x.at[x], final_x.at[x], device(moved(at, x=k))) for k in (1, 2, 3)]
            arrive([cy4])
            final_y[...] = add(final_y, scy3[...], rcy4[0], rcy4[1], rcy4[2])
    for h in range(2):
        arrive([a4[h]])
        final[x, 0, h] = add(final, sa3[h], ra4[h])
        arrive([b4[h]])
        final[x, 1, h] = add(final, sb3[h], rb4[h])
    spread += [send(final.at[x], final.at[x], device(moved(at, x=k))) for k in (1, 2, 3)]
    arrive(spread)
    send.finish()


def finish_kernel(seq_i, final, final_x, final_y, seq_o, conv_o, dna_o, qkv_o, out_o):
    seq_o[0] = seq_i[...]
    for h in range(2):
        columns = slice(384 * h, 384 * h + 384)
        for q in range(4):
            conv_o[16 * q : 16 * q + 16, columns] = final[q, 0, h].astype(F32)
        conv_o[64:80, columns] = final[0, 1, h].astype(F32)
        conv_o[80:96, columns] = final[1, 1, h].astype(F32)
        dna_o[:, columns] = final[2, 1, h].astype(F32)
        out_o[:, columns] = final[3, 1, h].astype(F32)
    for q in range(4):
        qkv_o[0:16, 384 * q : 384 * q + 384] = final_x[q].astype(F32)
    last_rows = final_y[...].astype(F32)
    qkv_o[16:24, 0:768] = last_rows[0:8]
    qkv_o[16:24, 768:1536] = last_rows[8:16]


def layer(*operands):
    vmem = pl.BlockSpec(memory_space=pltpu.VMEM)
    low = [
        (4, 4, 2, 4, 16, 1152), (4, 4, 2, 80, 768), (16, 768), (16, 768),
        (4, 128, 768), (4, 4, 128, 256), (4, 4, 2, 96, 128), (128, 512), (4, 4, 2, 16, 128), (768, 512), (768, 512),
        (128, 512), (128, 512), (4, 4, 2, 16, 128), (4, 4, 2, 16, 128), (128, 1536), (128, 512), (4, 4, 2, 16, 128),
        (4, 4, 128, 128), (4, 4, 128, 128), (4, 128, 128), (4, 128, 128), (4, 4, 128, 128), (4, 128, 128), (4, 128, 128),
        (4, 4, 128, 128), (4, 128, 128), (4, 128, 128),
        (4, 128, 1024), (4, 128, 1024),
    ] + 3 * [(4, 4, 64, 768), (4, 4, 64, 768), (4, 4, 4, 16, 384), (4, 4, 16, 768)] + [
        (2, 2, 2, 4, 16, 384), (2, 2, 4, 4, 16, 384), (2, 4, 4, 16, 384), (2, 3, 4, 16, 384),
        (2, 4, 16, 384), (2, 3, 16, 384), (2, 16, 384), (2, 16, 384),
        (2, 2, 2, 64, 384), (2, 2, 4, 64, 384), (2, 4, 64, 384), (2, 3, 4, 16, 384),
        (2, 4, 16, 384), (2, 3, 16, 384), (2, 16, 384), (2, 16, 384),
        (2, 2, 4, 16, 384), (2, 4, 4, 16, 384), (4, 4, 16, 384), (3, 4, 16, 384), (4, 16, 384), (3, 16, 384), (16, 384), (16, 384),
        (2, 2, 16, 768), (2, 4, 16, 768), (4, 16, 768), (3, 16, 768), (16, 768), (16, 768), (16, 768), (3, 16, 768),
    ]
    wide = [(128, 768), (128, 768), (128, 1), (6, 272, 128), (4, 128, 1024), (2, 6, 8, 128), (6, 8, 128), (6, 8, 128)]
    results = pl.pallas_call(
        layer_kernel,
        name="layer",
        out_shape=tuple(
            jax.ShapeDtypeStruct(shape, BF16)
            for shape in ((256, 768), (4, 2, 2, 16, 384), (4, 16, 384), (16, 768))
        ),
        in_specs=[vmem] * 7,
        out_specs=(vmem,) * 4,
        scratch_shapes=[pltpu.VMEM(shape, BF16) for shape in low]
        + [pltpu.VMEM(shape, F32) for shape in wide]
        + [pltpu.SemaphoreType.DMA((60,)), pltpu.SemaphoreType.DMA((138,))],
        compiler_params=pltpu.CompilerParams(
            collective_id=1, has_side_effects=True, vmem_limit_bytes=60 * 2**20
        ),
    )(*operands)
    return pl.pallas_call(
        finish_kernel,
        name="finish",
        out_shape=(
            jax.ShapeDtypeStruct((1, 256, 768), BF16),
            jax.ShapeDtypeStruct((96, 768), F32),
            jax.ShapeDtypeStruct((16, 768), F32),
            jax.ShapeDtypeStruct((24, 1536), F32),
            jax.ShapeDtypeStruct((16, 768), F32),
        ),
        in_specs=[vmem] * 4,
        out_specs=(vmem,) * 5,
    )(*results)


def per_device(seq_in, bases, conv_weight, dna_weight, qkv_weight, out_weight, cotangent):
    return layer(
        conv_weight, dna_weight, qkv_weight, out_weight, seq_in[0], bases[0].reshape(128, BIN), cotangent[0]
    )


def solution(mesh):
    in_specs = (
        P("dp", "seq", None),
        P("dp", "seq"),
        P("dp", None),
        P("dp", None),
        P("dp", None),
        P("dp", None),
        P("dp", "seq", None),
    )
    out_specs = (P("dp", "seq", None), P("dp", None), P("dp", None), P("dp", None), P("dp", None))
    return jax.shard_map(
        per_device, mesh=mesh, in_specs=in_specs, out_specs=out_specs, check_vma=False
    )
```

```python
import math

import jax
import jax.numpy as jnp
from jax import lax
from jax.experimental import pallas as pl
from jax.experimental.pallas import tpu as pltpu
from jax.sharding import PartitionSpec as P

H = 4
BIN = 128
BF16 = jnp.bfloat16
F32 = jnp.float32
MESH = pl.DeviceIdType.MESH
epsilon = 1e-06

SIZES = {"zh": 4, "y": 4, "c": 2, "zl": 2, "x": 4}
PEERS = [(a, k) for a in ("zh", "y", "x") for k in (1, 2, 3)] + [("zl", 1), ("c", 1)]


def here():
    dp = lax.axis_index("dp")
    sq = lax.axis_index("seq")
    return {"zh": dp // 8, "y": lax.rem(dp // 2, 4), "c": lax.rem(dp, 2), "zl": sq // 4, "x": lax.rem(sq, 4)}


def moved(at, **steps):
    to = dict(at)
    for axis, step in steps.items():
        to[axis] = lax.rem(at[axis] + step, SIZES[axis])
    return to


def device(at):
    return (at["zh"] * 8 + at["y"] * 2 + at["c"], at["zl"] * 4 + at["x"])


class Sender:
    def __init__(self, send_sems, recv_sems):
        self.send_sems, self.recv_sems, self.sent, self.due = send_sems, recv_sems, 0, 0
        self.free, self.copies = [], []

    def copy(self, src, dst, to, recv):
        if not self.free:
            self.free.append(self.sent)
            self.sent += 1
        place = self.free.pop(0)
        copy = pltpu.make_async_remote_copy(
            src_ref=src,
            dst_ref=dst,
            send_sem=self.send_sems.at[place],
            recv_sem=self.recv_sems.at[recv],
            device_id=to,
            device_id_type=MESH,
        )
        copy.start()
        self.copies.append((copy, place))
        return copy

    def __call__(self, src, dst, to):
        self.due += 1
        return self.copy(src, dst, to, self.due - 1)

    def group(self, whole, copies):
        self.due += 1
        for src, dst, to in copies:
            self.copy(src, dst, to, self.due - 1)
        return pltpu.make_async_remote_copy(
            src_ref=whole,
            dst_ref=whole,
            send_sem=self.send_sems.at[0],
            recv_sem=self.recv_sems.at[self.due - 1],
            device_id=copies[0][2],
            device_id_type=MESH,
        )

    def finish(self, oldest=None):
        done = self.copies[:oldest]
        for copy, place in done:
            copy.wait_send()
            self.free.append(place)
        self.copies = self.copies[len(done) :]


def arrive(copies):
    for copy in copies:
        copy.wait_recv()


def rows16(index, base=0):
    return pl.ds(pl.multiple_of(index * 16 + base, 16), 16)


def half_columns(index):
    return pl.ds(pl.multiple_of(index * 384, 128) if not isinstance(index, int) else index * 384, 384)


def right_dot(left, right):
    return lax.dot_general(left, right, (((1,), (1,)), ((), ())), preferred_element_type=F32)


def row_dot(left, right):
    return lax.dot_general(left, right, (((0,), (0,)), ((), ())), preferred_element_type=F32)


def dot(left, right):
    return jnp.dot(left, right, preferred_element_type=F32)


def add(target, *terms):
    total = terms[0].astype(F32)
    for term in terms[1:]:
        total += term.astype(F32)
    return total.astype(target.dtype)


def loop(n, body):
    def step(i, carry):
        body(i)
        return carry

    lax.fori_loop(0, n, step, 0)


class Ring:
    def __init__(self, send, at, axis, region):
        self.send, self.me, self.region = send, at[axis], region
        self.right, self.left = device(moved(at, **{axis: 1})), device(moved(at, **{axis: 3}))

    def at(self, step):
        return lax.rem(self.me + step, 4)

    def go(self, index, part, to):
        ref = self.region(index, part)
        return [self.send(ref, ref, to)]

    def start(self):
        self.from_left = self.go(self.me, None, self.right)
        self.from_right = self.go(self.me, None, self.left)

    def left_in(self):
        arrive(self.from_left)
        self.far_left = self.go(self.at(3), 0, self.right)

    def right_in(self):
        arrive(self.from_right)
        self.far_right = self.go(self.at(1), 1, self.left)

    def both_in(self):
        self.left_in()
        self.right_in()

    def far_in(self):
        arrive(self.far_left)
        arrive(self.far_right)


def layer_kernel(
    conv_s, dna_s, qkv_s, out_s, rows_in, letters, upstream,
    seq_o, final, final_x, final_y,
    ga, gb, before, after,
    taps, taps_y, taps_t, onehot, onehot_t, choose_x, choose_y, wide_x, wide_y, wide_xt, wide_yt, d_proj, attended, attended_t,
    mine, got, got_k, got_v, outgo, outgo_k, outgo_v, back, back_k, back_v, probs_s, scores_s,
    pa_s, pb_s, px_s, py_s, pa, pb, px, py, pa_r, pb_r, px_r, py_r,
    fa, na, sa1, ra2, sa2, ra3, sa3, ra4,
    fb, nb, sb1, rb2, sb2, rb3, sb3, rb4,
    fcx, ncx, scx1, rcx2, scx2, rcx3, scx3, rcx4,
    fcy, ncy, scy1, rcy2, scy2, rcy3, scy3, rcy4,
    slope, unit, inverse, rows_f, probs_f, rim_out, rim_before, rim_after,
    send_sems, recv_sems,
):
    at = here()
    zh, y, c, zl, x = (at[a] for a in ("zh", "y", "c", "zl", "x"))
    sq = lax.axis_index("seq")
    dp = lax.axis_index("dp")
    behind, ahead = (dp, lax.rem(sq + 7, 8)), (dp, lax.rem(sq + 1, 8))
    sibling = device(moved(at, c=1))
    near = device(moved(at, zl=1))
    across = [moved(at, x=k, zl=1) for k in range(4)]
    everyone = [device(moved(at, **{a: k})) for a, k in PEERS] + [behind, ahead]
    everyone += [device(p) for p in across[1:]]
    barrier = pltpu.get_barrier_semaphore()
    for one in everyone:
        pl.semaphore_signal(barrier, inc=1, device_id=one, device_id_type=MESH)
    xs = [lax.rem(x + k, 4) for k in range(4)]
    ys = [lax.rem(y + k, 4) for k in range(4)]
    zs = [lax.rem(zh + k, 4) for k in range(4)]

    quarter = rows16(x)
    ga[zh, y, c, x, :, 0:768] = conv_s[quarter]
    ga[zh, y, c, x, :, 768:1152] = qkv_s[0:16, half_columns(x)]
    gb[zh, y, c, 0:32] = conv_s[64:96]
    gb[zh, y, c, 32:48] = dna_s[...]
    gb[zh, y, c, 48:64] = out_s[...]
    last_rows = [qkv_s[:, 768 * i : 768 * i + 768].astype(F32)[16:24] for i in range(2)]
    gb[zh, y, c, 64:80] = jnp.concatenate(last_rows, axis=0).astype(BF16)
    pl.semaphore_wait(barrier, len(everyone))

    send = Sender(send_sems, recv_sems)

    def ref_a(height, step, index, part=None):
        rows = pl.ds(0, 4) if part is None else pl.ds(2 * part, 2)
        return ga.at[rows if height is None else height, step, c, index]

    def ref_b(height, step, part=None):
        return gb.at[height, step, c] if part is None else gb.at[height, step, c, :, half_columns(part)]

    core = []

    def pass_on(ref):
        core.append(send(ref, ref, sibling))

    def pass_a(step):
        pass_on(ga.at[:, step, c])

    def pass_b(height):
        pass_on(gb.at[height, :, c])

    a1 = []
    for k in (2, 1, 3):
        a1.append(send(ref_a(zh, y, x), ref_a(zh, y, x), device(moved(at, zh=k))))
    halo = [
        send(rows_in.at[pl.ds(240, 16)], before, ahead),
        send(rows_in.at[pl.ds(0, 16)], after, behind),
    ]
    ring_z = Ring(send, at, "zh", lambda index, part: ref_b(index, y, part))
    rings_y = [Ring(send, at, "y", lambda index, part, v=zs[k]: ref_b(v, index, part)) for k in range(4)]
    rings_x = [Ring(send, at, "x", lambda index, part, v=ys[k]: ref_a(None, v, index, part)) for k in range(4)]
    ring_a = Ring(send, at, "y", lambda index, part: ref_a(None, index, x, part))
    ring_z.start()
    rings_y[0].start()
    row = lax.broadcasted_iota(jnp.int32, (128, 512), 0)
    column = lax.broadcasted_iota(jnp.int32, (128, 512), 1)
    repeat = (column // 4 == row).astype(F32).astype(BF16)
    repeated = dot(letters[...].astype(F32).astype(BF16), repeat)
    onehot[...] = (repeated == lax.rem(column, 4).astype(F32)).astype(F32).astype(BF16)
    row = lax.broadcasted_iota(jnp.int32, (768, 512), 0)
    column = lax.broadcasted_iota(jnp.int32, (768, 512), 1)
    first_row = column // 16 * 24
    choose_x[...] = (first_row + lax.rem(column, 16) == row).astype(F32).astype(BF16)
    choose_y[...] = (first_row + 16 + lax.rem(column, 8) == row).astype(F32).astype(BF16)
    arrive(a1)
    ring_a.start()
    rings_x[0].start()
    ring_z.left_in()
    rings_y[3].start()
    ring_z.right_in()
    rings_y[0].both_in()
    ring_a.left_in()
    rings_x[3].start()
    ring_a.right_in()
    rings_x[1].start()
    rings_y[1].start()
    rings_x[0].both_in()
    ring_a.far_in()
    rings_x[2].start()
    ring_z.far_in()
    rings_y[2].start()
    rings_y[3].both_in()
    rings_x[3].both_in()
    rings_x[1].both_in()
    rings_y[1].both_in()
    rings_y[0].far_in()
    pass_b(zs[0])
    rings_x[0].far_in()
    pass_a(ys[0])
    rings_x[2].both_in()
    rings_y[2].both_in()

    send.finish(24)
    arrive(halo)
    for j in range(6):
        lanes = slice(128 * j, 128 * j + 128)
        rows_f[j, 8:264] = rows_in[:, lanes].astype(F32)
        rows_f[j, 0:8] = jnp.where(sq > 0, before[:, lanes].astype(F32)[8:16], 0.0)
        rows_f[j, 264:272] = jnp.where(sq < 7, after[:, lanes].astype(F32)[0:8], 0.0)
        for i in range(4):
            taps[i, :, lanes] = rows_f[j, pl.ds(7 + i, 128, stride=2)].astype(BF16)
    for i in range(4):
        whole = taps[i].astype(F32)
        moved_on = pltpu.roll(whole, 704, 1).astype(BF16)
        for k in range(4):
            start = 384 * (k // 2) + 128 * (k % 2)
            taps_y[k, i] = moved_on[:, start : start + 256] if k % 2 else taps[i, :, start : start + 256]

    rings_y[3].far_in()
    pass_b(zs[3])
    rings_y[1].far_in()
    pass_b(zs[1])
    rings_x[3].far_in()
    pass_a(ys[3])
    rings_x[1].far_in()
    pass_a(ys[1])
    rings_y[2].far_in()
    pass_b(zs[2])
    rings_x[2].far_in()
    pass_a(ys[2])

    arrive(core[:-1])

    def conv_full(i):
        first = ga[i, :, :, :, :, 0:768].reshape(4, 2, 64, 768)
        return jnp.concatenate([first, gb[i, :, :, 0:32]], axis=2).reshape(768, 768)

    def qx_full(i):
        return jnp.concatenate(
            [ga[:, :, :, 2 * i + j, :, 768:1152].reshape(512, 384) for j in range(2)], axis=1
        )

    def qy_full():
        return gb[:, :, :, 64:80].reshape(512, 768)

    dna_full = gb[:, :, :, 32:48].reshape(512, 768)
    out_full = gb[:, :, :, 48:64].reshape(512, 768)
    d_attend = right_dot(upstream[...], out_full).astype(BF16)
    slope[...] = dot(onehot[...], dna_full)

    def y_block(k):
        total = 0.0
        for i in range(4):
            first = ga[i, ys[k], :, :, :, 0:768].reshape(2, 64, 768)
            block = jnp.concatenate([first, gb[i, ys[k], :, 0:32]], axis=1).reshape(192, 768)
            block = jnp.concatenate([block, jnp.zeros((64, 768), BF16)], axis=0)
            total += dot(taps_y[ys[k], i], block)
        slope[...] += total

    for k in (0, 3, 1):
        y_block(k)
    arrive(core[-1:])
    y_block(2)
    pre = slope[...]
    bend = jnp.tanh(math.sqrt(2.0 / math.pi) * (pre + 0.044715 * (pre * pre * pre)))
    share = 0.5 * (1.0 + bend)
    feature = (pre * share).astype(BF16).astype(F32)
    slope[...] = share + pre * (0.5 * (1.0 - bend * bend)) * (
        math.sqrt(2.0 / math.pi) * (1.0 + 3.0 * 0.044715 * (pre * pre))
    )
    scale = lax.rsqrt(jnp.mean(feature * feature, axis=1, keepdims=True) + epsilon)
    inverse[...] = scale
    unit[...] = feature * scale
    normed = unit[...].astype(BF16)
    wide_x[...] = dot(normed, choose_x[...]).astype(BF16)
    wide_y[...] = dot(normed, choose_y[...]).astype(BF16)
    side_of = lax.rem(lax.broadcasted_iota(jnp.int32, (128, 512), 1), 16) // 8
    own_y = [jnp.where(side_of == i, wide_y[...].astype(F32), 0.0).astype(BF16) for i in range(2)]
    from_y = dot(jnp.concatenate(own_y, axis=0), qy_full())
    for i in range(2):
        projected = (dot(wide_x[...], qx_full(i)) + from_y[128 * i : 128 * i + 128]).astype(BF16)
        for piece in range(6):
            kind, head = divmod(6 * i + piece, 4)
            mine[head, (1, 0, 2)[kind]] = projected[:, 128 * piece : 128 * piece + 128]
    for head in range(H):
        mine[head, 3] = d_attend[:, 128 * head : 128 * head + 128]

    kq, vd = pl.ds(0, 2), pl.ds(2, 2)
    kq_in, vd_in = {}, {}
    from_near_k = send.group(got_k, [(mine.at[x, 0], got_k.at[x], near)])
    near_k = send.due - 1
    from_near_v = send.group(got_v, [(mine.at[x, 2], got_v.at[x], near)])
    near_v = send.due - 1
    for k in (1, 3, 2):
        kq_in[k] = send(mine.at[xs[k], kq], got.at[x, kq], device(moved(at, x=k)))
    for k in (1, 3, 2):
        vd_in[k] = send(mine.at[xs[k], vd], got.at[x, vd], device(moved(at, x=k)))
    sources = {k: lax.rem(x + 4 - k, 4) for k in (0, 1, 3, 2)}
    got[x] = mine[x]
    for k in (1, 3, 2):
        arrive([kq_in[k]])
        send.copy(got.at[sources[k], 0], got_k.at[sources[k]], near, near_k)
    def transpose_tap(i):
        taps_t[i] = taps[i].T.reshape(4, 2, 96, 128)

    loop(4, transpose_tap)
    onehot_t[...] = onehot[...].T.reshape(4, 4, 2, 16, 128)
    wide_xt[...] = wide_x[...].T.reshape(4, 4, 2, 16, 128)
    wide_yt[...] = wide_y[...].T.reshape(4, 4, 2, 16, 128)
    arrive([from_near_k])
    keys = jnp.concatenate([got[:, 0].reshape(512, 128), got_k[...].reshape(512, 128)], axis=0)
    scaling = 1.0 / math.sqrt(128)

    pairs = (slice(0, 2), slice(2, 4))

    def soft(pair):
        scores = right_dot(got[pair, 1].reshape(256, 128), keys) * scaling
        powers = jnp.exp(scores - jnp.max(scores, axis=1, keepdims=True))
        probs = powers * (1.0 / jnp.sum(powers, axis=1, keepdims=True))
        probs_f[pair] = probs.reshape(2, 128, 1024)
        probs_s[pair] = probs.astype(BF16).reshape(2, 128, 1024)

    def pass_v(k):
        arrive([vd_in[k]])
        send.copy(got.at[sources[k], 2], got_v.at[sources[k]], near, near_v)

    soft(pairs[0])
    pass_v(1)
    pass_v(3)
    soft(pairs[1])
    pass_v(2)
    home_v, home_q, home_k = [], [], []
    all_queries = got[:, 1].reshape(512, 128)
    all_upward = got[:, 3].reshape(512, 128)
    all_probs = probs_s[...].reshape(512, 1024)
    d_values = row_dot(all_upward, all_probs).T.astype(BF16).reshape(8, 128, 128)
    outgo_v[...] = d_values[4:8]
    home_v.append(send.group(back_v, [(outgo_v.at[p["x"]], back_v.at[x], device(p)) for p in across]))
    outgo[:, 1] = d_values[0:4]
    arrive([from_near_v])
    values = jnp.concatenate([got[:, 2].reshape(512, 128), got_v[...].reshape(512, 128)], axis=0)
    outgo[:, 0] = dot(all_probs, values).astype(BF16).reshape(4, 128, 128)
    for k in (1, 3, 2):
        block = pl.ds(0, 2)
        home_v.append(send(outgo.at[xs[k], block], back.at[x, block], device(moved(at, x=k))))
    for pair in pairs:
        probs = probs_f[pair].reshape(256, 1024)
        d_probs = right_dot(got[pair, 3].reshape(256, 128), values)
        inner = jnp.sum(probs * d_probs, axis=1, keepdims=True)
        d_scores = (probs * (d_probs - inner) * scaling).astype(BF16)
        scores_s[pair] = d_scores.reshape(2, 128, 1024)
        outgo[pair, 2] = dot(d_scores, keys).astype(BF16).reshape(2, 128, 128)
    for k in (1, 3, 2):
        home_q.append(send(outgo.at[xs[k], 2], back.at[x, 2], device(moved(at, x=k))))

    def key_grads(columns):
        d_keys = row_dot(all_queries, scores_s[:, :, columns].reshape(512, 512)).T
        return d_keys.astype(BF16).reshape(4, 128, 128)

    outgo_k[...] = key_grads(slice(512, 1024))
    home_k.append(send.group(back_k, [(outgo_k.at[p["x"]], back_k.at[x], device(p)) for p in across]))
    outgo[:, 3] = key_grads(slice(0, 512))
    for k in (1, 3, 2):
        home_k.append(send(outgo.at[xs[k], 3], back.at[x, 3], device(moved(at, x=k))))
    back[x] = outgo[x]

    def columns_of(head, start=0):
        return slice(start + 128 * head, start + 128 * head + 128)

    arrive(home_v)
    for head in range(H):
        attended[:, columns_of(head)] = back[head, 0]
        total = back[head, 1].astype(F32) + back_v[head].astype(F32)
        d_proj[:, columns_of(head, 1024)] = total.astype(BF16)
    attended_t[...] = attended[...].T.reshape(4, 4, 2, 16, 128)
    for parity, to_b in ((1 - c, pb_s), (c, pb)):
        left = attended_t[:, :, parity].reshape(256, 128)
        to_b[:, :, 48:64] = dot(left, upstream[...]).astype(BF16).reshape(4, 4, 16, 768)
    arrive(home_q)
    for head in range(H):
        d_proj[:, columns_of(head)] = back[head, 2]

    def qkv_quarters(parity, to_x, quarters):
        left = wide_xt[:, :, parity].reshape(256, 128)
        for q in quarters:
            block = dot(left, d_proj[:, 384 * q : 384 * q + 384]).astype(BF16)
            to_x[q] = block.reshape(4, 4, 16, 384)

    qkv_quarters(1 - c, px_s, (0, 3))
    qkv_quarters(c, px, (0, 3))
    d_q, d_v = d_proj[:, 0:512], d_proj[:, 1024:1536]
    d_x = right_dot(d_q, qx_full(0)[:, 0:512]) + right_dot(d_v, qx_full(1)[:, 256:768])
    d_y0, d_y1 = right_dot(d_q, qy_full()[:, 0:512]), right_dot(d_v, qy_full()[:, 256:768])
    send.finish(-7)
    arrive(home_k)
    for head in range(H):
        total = back[head, 3].astype(F32) + back_k[head].astype(F32)
        d_proj[:, columns_of(head, 512)] = total.astype(BF16)

    row_side = lax.rem(lax.broadcasted_iota(jnp.int32, (256, 768), 0), 16)

    def qkv_grads(parity, to_x, to_y):
        qkv_quarters(parity, to_x, (1, 2))
        left = wide_yt[:, :, parity].reshape(256, 128)
        both = [dot(left, d_proj[:, 768 * i : 768 * i + 768]) for i in range(2)]
        to_y[...] = jnp.where(row_side < 8, both[0], both[1]).astype(BF16).reshape(4, 4, 16, 768)

    order = (2, 1, 3, 0)
    core_cx, core_cy, core_a, core_b = {}, {}, {}, {}
    qkv_grads(1 - c, px_s, py_s)
    for k in order:
        core_cx[k] = send(px_s.at[:, zs[k]], px_r.at[:, zs[k]], sibling)
        core_cy[k] = send(py_s.at[:, ys[k]], py_r.at[:, ys[k]], sibling)
    qkv_grads(c, px, py)
    d_k0, d_k1 = d_proj[:, 512:768], d_proj[:, 768:1024]
    d_x += right_dot(d_k0, qx_full(0)[:, 512:768]) + right_dot(d_k1, qx_full(1)[:, 0:256])
    d_y0 += right_dot(d_k0, qy_full()[:, 512:768])
    d_y1 += right_dot(d_k1, qy_full()[:, 0:256])
    d_y = jnp.where(side_of == 0, d_y0, d_y1)

    def sum_cx(k):
        arrive([core_cx[k]])
        px[:, zs[k]] = add(px, px[:, zs[k]], px_r[:, zs[k]])

    def sum_cy(k):
        arrive([core_cy[k]])
        py[:, ys[k]] = add(py, py[:, ys[k]], py_r[:, ys[k]])

    right_x, left_x = device(moved(at, x=1)), device(moved(at, x=3))
    right_y, left_y = device(moved(at, y=1)), device(moved(at, y=3))
    right_z, left_z = device(moved(at, zh=1)), device(moved(at, zh=3))
    low, high = pl.ds(0, 2), pl.ds(2, 2)
    sides = ((0, 1, right_x, right_y), (1, 3, left_x, left_y))
    d_normed = 0.0
    for terms, choose in ((d_x, choose_x), (d_y, choose_y)):
        d_high = terms.astype(BF16)
        d_low = (terms - d_high.astype(F32)).astype(BF16)
        both = right_dot(jnp.concatenate([d_high, d_low], axis=0), choose[...])
        d_normed += both[0:128] + both[128:256]
    d_feature = upstream[...].astype(F32) + inverse[...] * (
        d_normed - unit[...] * jnp.mean(d_normed * unit[...], axis=1, keepdims=True)
    )
    d_pre = (d_feature * slope[...]).astype(BF16)

    sum_cx(2)
    far_cx = [
        send(px.at[quarters, zs[2]], fcx.at[side], to) for side, quarters, to in ((0, low, right_z), (1, high, left_z))
    ]
    sum_cy(2)
    far_cy = [
        send(py.at[heights, ys[2]], fcy.at[side], to) for side, heights, to in ((0, low, right_y), (1, high, left_y))
    ]
    def conv_grads(parity, to_a, to_b):
        def one(i):
            block = dot(taps_t[i, :, parity].reshape(384, 128), d_pre).astype(BF16).reshape(4, 96, 768)
            to_a[i] = block[:, 0:64]
            to_b[i, :, 0:32] = block[:, 64:96]

        loop(4, one)
        left = onehot_t[:, :, parity].reshape(256, 128)
        to_b[:, :, 32:48] = dot(left, d_pre).astype(BF16).reshape(4, 4, 16, 768)

    conv_grads(1 - c, pa_s, pb_s)
    for k in order:
        core_a[k] = send(pa_s.at[:, :, rows16(xs[k])], pa_r.at[:, :, rows16(xs[k])], sibling)
        core_b[k] = send(pb_s.at[:, ys[k]], pb_r.at[:, ys[k]], sibling)
    conv_grads(c, pa, pb)

    def sum_a(k):
        arrive([core_a[k]])
        rows = rows16(xs[k])

        def one(i):
            pa[i, :, rows] = add(pa, pa[i, :, rows], pa_r[i, :, rows])

        loop(4, one)

    def sum_b(k):
        arrive([core_b[k]])

        def one(i):
            pb[i, ys[k]] = add(pb, pb[i, ys[k]], pb_r[i, ys[k]])

        loop(4, one)

    halves = [(h, pl.ds(384 * h, 384), slice(384 * h, 384 * h + 384)) for h in range(2)]
    far_a, far_b = {}, {}
    sum_a(2)
    sum_b(2)
    for h, columns, _ in halves:
        for side, heights, to_x, to_y in ((0, low, right_x, right_y), (1, high, left_x, left_y)):
            far_a[h, side] = send(pa.at[heights, :, rows16(xs[2]), columns], fa.at[h, side], to_x)
            far_b[h, side] = send(pb.at[heights, ys[2], :, columns], fb.at[h, side], to_y)
    near_cx, near_cy = [], []
    for side, k, to_x, to_y in sides:
        sum_cx(k)
        arrive([far_cx[side]])
        part = slice(2 * side, 2 * side + 2)
        px[part, zs[k]] = add(px, px[part, zs[k]], fcx[side])
        near_cx.append(send(px.at[:, zs[k]], ncx.at[side], (right_z, left_z)[side]))
        sum_cy(k)
        arrive([far_cy[side]])
        py[part, ys[k]] = add(py, py[part, ys[k]], fcy[side])
        near_cy.append(send(py.at[:, ys[k]], ncy.at[side], to_y))
    for side, k, to_x, to_y in sides:
        sum_a(k)
        sum_b(k)
    near_a, near_b = {}, {}
    for h, columns, cols in halves:
        for side, k, to_x, to_y in sides:
            rows = rows16(xs[k])
            arrive([far_a[h, side]])

            def join_a(i, h=h, side=side, rows=rows, cols=cols):
                pa[2 * side + i, :, rows, cols] = add(pa, pa[2 * side + i, :, rows, cols], fa[h, side, i])

            loop(2, join_a)
            near_a[h, side] = send(pa.at[:, :, rows, columns], na.at[h, side], to_x)
            arrive([far_b[h, side]])

            def join_b(i, h=h, side=side, index=ys[k], cols=cols):
                pb[2 * side + i, index, :, cols] = add(pb, pb[2 * side + i, index, :, cols], fb[h, side, i])

            loop(2, join_b)
            near_b[h, side] = send(pb.at[:, ys[k], :, columns], nb.at[h, side], to_y)

    def three(axis, whole, source):
        return send.group(
            whole, [(source(k), whole.at[k - 1], device(moved(at, **{axis: k}))) for k in (1, 3, 2)]
        )

    sum_cx(0)
    arrive(near_cx)
    scx1[...] = add(scx1, px[:, zh], ncx[0], ncx[1])
    cx2 = three("x", rcx2, lambda k: scx1.at[xs[k]])
    sum_cy(0)
    arrive(near_cy)
    scy1[...] = add(scy1, py[:, y], ncy[0], ncy[1])
    cy2 = three("zh", rcy2, lambda k: scy1.at[zs[k]])
    sum_a(0)
    sum_b(0)

    send.finish(28)
    rows_f[:, 256:272] = jnp.zeros((6, 16, 128), F32)
    for i in range(4):
        terms = right_dot(d_pre, conv_full(i))
        for j in range(6):
            target = pl.ds(7 + i, 128, stride=2)
            block = terms[:, 128 * j : 128 * j + 128]
            rows_f[j, target] = block if i < 2 else rows_f[j, target] + block
    rim_out[0] = rows_f[:, 264:272]
    rim_out[1] = rows_f[:, 0:8]
    rims = [send(rim_out.at[0], rim_before, ahead), send(rim_out.at[1], rim_after, behind)]

    a2, b2, a3, b3, a4, b4 = {}, {}, {}, {}, {}, {}
    for h, columns, cols in halves:
        arrive([near_a[h, 0], near_a[h, 1]])

        def first_a(i, h=h, cols=cols):
            sa1[h, i] = add(sa1, pa[i, :, rows16(x), cols], na[h, 0, i], na[h, 1, i])

        loop(4, first_a)
        a2[h] = three("y", ra2.at[h], lambda k, h=h: sa1.at[h, :, ys[k]])
        arrive([near_b[h, 0], near_b[h, 1]])

        def first_b(i, h=h, cols=cols):
            sb1[h, i] = add(sb1, pb[i, y, :, cols], nb[h, 0, i], nb[h, 1, i])

        loop(4, first_b)
        b2[h] = three("x", rb2.at[h], lambda k, h=h: sb1.at[h, :, rows16(xs[k])])
        if h == 0:
            arrive([cx2])
            scx2[...] = add(scx2, scx1[x], rcx2[0], rcx2[1], rcx2[2])
            cx3 = three("y", rcx3, lambda k: scx2.at[ys[k]])
            arrive([cy2])
            scy2[...] = add(scy2, scy1[zh], rcy2[0], rcy2[1], rcy2[2])
            cy3 = send(scy2, rcy3, near)
    arrive(rims)
    rows_f[:, 8:9] += jnp.where(sq > 0, rim_before[:, 0:1], 0.0)
    rows_f[:, 263:264] += jnp.where(sq < 7, rim_after[:, 7:8], 0.0)
    for j in range(6):
        seq_o[:, 128 * j : 128 * j + 128] = rows_f[j, 8:264].astype(BF16)
    for h in range(2):
        arrive([a2[h]])
        sa2[h] = add(sa2, sa1[h, :, y], ra2[h, 0], ra2[h, 1], ra2[h, 2])
        a3[h] = three("zh", ra3.at[h], lambda k, h=h: sa2.at[h, zs[k]])
        arrive([b2[h]])
        sb2[h] = add(sb2, sb1[h, :, rows16(x)], rb2[h, 0], rb2[h, 1], rb2[h, 2])
        b3[h] = three("zh", rb3.at[h], lambda k, h=h: sb2.at[h, zs[k]])
        if h == 0:
            arrive([cx3])
            scx3[...] = add(scx3, scx2[y], rcx3[0], rcx3[1], rcx3[2])
            cx4 = send(scx3, rcx4, near)
            arrive([cy3])
            scy3[...] = add(scy3, scy2[...], rcy3[...])
            cy4 = three("x", rcy4, lambda k: scy3)

    send.finish(12)
    for h in range(2):
        arrive([a3[h]])
        sa3[h] = add(sa3, sa2[h, zh], ra3[h, 0], ra3[h, 1], ra3[h, 2])
        a4[h] = send(sa3.at[h], ra4.at[h], near)
        arrive([b3[h]])
        sb3[h] = add(sb3, sb2[h, zh], rb3[h, 0], rb3[h, 1], rb3[h, 2])
        b4[h] = send(sb3.at[h], rb4.at[h], near)
        if h == 0:
            arrive([cx4])
            final_x[x] = add(final_x, scx3[...], rcx4[...])
            spread = [send(final_x.at[x], final_x.at[x], device(moved(at, x=k))) for k in (1, 2, 3)]
            arrive([cy4])
            final_y[...] = add(final_y, scy3[...], rcy4[0], rcy4[1], rcy4[2])
    for h in range(2):
        arrive([a4[h]])
        final[x, h, 0] = add(final, sa3[h], ra4[h])
        arrive([b4[h]])
        final[x, h, 1] = add(final, sb3[h], rb4[h])
        spread += [send(final.at[x, h], final.at[x, h], device(moved(at, x=k))) for k in (1, 3, 2)]
    send.finish(-6)
    arrive(spread)
    send.finish()


def finish_kernel(seq_i, final, final_x, final_y, seq_o, conv_o, dna_o, qkv_o, out_o):
    seq_o[0] = seq_i[...]
    for h in range(2):
        columns = slice(384 * h, 384 * h + 384)
        for q in range(4):
            conv_o[16 * q : 16 * q + 16, columns] = final[q, h, 0].astype(F32)
        conv_o[64:80, columns] = final[0, h, 1].astype(F32)
        conv_o[80:96, columns] = final[1, h, 1].astype(F32)
        dna_o[:, columns] = final[2, h, 1].astype(F32)
        out_o[:, columns] = final[3, h, 1].astype(F32)
    for q in range(4):
        qkv_o[0:16, 384 * q : 384 * q + 384] = final_x[q].astype(F32)
    last_rows = final_y[...].astype(F32)
    qkv_o[16:24, 0:768] = last_rows[0:8]
    qkv_o[16:24, 768:1536] = last_rows[8:16]


def layer(*operands):
    vmem = pl.BlockSpec(memory_space=pltpu.VMEM)
    low = [
        (4, 4, 2, 4, 16, 1152), (4, 4, 2, 80, 768), (16, 768), (16, 768),
        (4, 128, 768), (4, 4, 128, 256), (4, 4, 2, 96, 128), (128, 512), (4, 4, 2, 16, 128), (768, 512), (768, 512),
        (128, 512), (128, 512), (4, 4, 2, 16, 128), (4, 4, 2, 16, 128), (128, 1536), (128, 512), (4, 4, 2, 16, 128),
        (4, 4, 128, 128), (4, 4, 128, 128), (4, 128, 128), (4, 128, 128), (4, 4, 128, 128), (4, 128, 128), (4, 128, 128),
        (4, 4, 128, 128), (4, 128, 128), (4, 128, 128),
        (4, 128, 1024), (4, 128, 1024),
    ] + 3 * [(4, 4, 64, 768), (4, 4, 64, 768), (4, 4, 4, 16, 384), (4, 4, 16, 768)] + [
        (2, 2, 2, 4, 16, 384), (2, 2, 4, 4, 16, 384), (2, 4, 4, 16, 384), (2, 3, 4, 16, 384),
        (2, 4, 16, 384), (2, 3, 16, 384), (2, 16, 384), (2, 16, 384),
        (2, 2, 2, 64, 384), (2, 2, 4, 64, 384), (2, 4, 64, 384), (2, 3, 4, 16, 384),
        (2, 4, 16, 384), (2, 3, 16, 384), (2, 16, 384), (2, 16, 384),
        (2, 2, 4, 16, 384), (2, 4, 4, 16, 384), (4, 4, 16, 384), (3, 4, 16, 384), (4, 16, 384), (3, 16, 384), (16, 384), (16, 384),
        (2, 2, 16, 768), (2, 4, 16, 768), (4, 16, 768), (3, 16, 768), (16, 768), (16, 768), (16, 768), (3, 16, 768),
    ]
    wide = [(128, 768), (128, 768), (128, 1), (6, 272, 128), (4, 128, 1024), (2, 6, 8, 128), (6, 8, 128), (6, 8, 128)]
    results = pl.pallas_call(
        layer_kernel,
        name="layer",
        out_shape=tuple(
            jax.ShapeDtypeStruct(shape, BF16)
            for shape in ((256, 768), (4, 2, 2, 16, 384), (4, 16, 384), (16, 768))
        ),
        in_specs=[vmem] * 7,
        out_specs=(vmem,) * 4,
        scratch_shapes=[pltpu.VMEM(shape, BF16) for shape in low]
        + [pltpu.VMEM(shape, F32) for shape in wide]
        + [pltpu.SemaphoreType.DMA((60,)), pltpu.SemaphoreType.DMA((141,))],
        compiler_params=pltpu.CompilerParams(
            collective_id=1, has_side_effects=True, vmem_limit_bytes=60 * 2**20
        ),
    )(*operands)
    return pl.pallas_call(
        finish_kernel,
        name="finish",
        out_shape=(
            jax.ShapeDtypeStruct((1, 256, 768), BF16),
            jax.ShapeDtypeStruct((96, 768), F32),
            jax.ShapeDtypeStruct((16, 768), F32),
            jax.ShapeDtypeStruct((24, 1536), F32),
            jax.ShapeDtypeStruct((16, 768), F32),
        ),
        in_specs=[vmem] * 4,
        out_specs=(vmem,) * 5,
    )(*results)


def per_device(seq_in, bases, conv_weight, dna_weight, qkv_weight, out_weight, cotangent):
    return layer(
        conv_weight, dna_weight, qkv_weight, out_weight, seq_in[0], bases[0].reshape(128, BIN), cotangent[0]
    )


def solution(mesh):
    in_specs = (
        P("dp", "seq", None),
        P("dp", "seq"),
        P("dp", None),
        P("dp", None),
        P("dp", None),
        P("dp", None),
        P("dp", "seq", None),
    )
    out_specs = (P("dp", "seq", None), P("dp", None), P("dp", None), P("dp", None), P("dp", None))
    return jax.shard_map(
        per_device, mesh=mesh, in_specs=in_specs, out_specs=out_specs, check_vma=False
    )
```

```python
import math

import jax
import jax.numpy as jnp
from jax import lax
from jax.experimental import pallas as pl
from jax.experimental.pallas import tpu as pltpu
from jax.sharding import PartitionSpec as P

H = 4
BIN = 128
BF16 = jnp.bfloat16
F32 = jnp.float32
MESH = pl.DeviceIdType.MESH
epsilon = 1e-06

SIZES = {"zh": 4, "y": 4, "c": 2, "zl": 2, "x": 4}
PEERS = [(a, k) for a in ("zh", "y", "x") for k in (1, 2, 3)] + [("zl", 1), ("c", 1)]


def here():
    dp = lax.axis_index("dp")
    sq = lax.axis_index("seq")
    return {"zh": dp // 8, "y": lax.rem(dp // 2, 4), "c": lax.rem(dp, 2), "zl": sq // 4, "x": lax.rem(sq, 4)}


def moved(at, **steps):
    to = dict(at)
    for axis, step in steps.items():
        to[axis] = lax.rem(at[axis] + step, SIZES[axis])
    return to


def device(at):
    return (at["zh"] * 8 + at["y"] * 2 + at["c"], at["zl"] * 4 + at["x"])


class Sender:
    def __init__(self, send_sems, recv_sems):
        self.send_sems, self.recv_sems, self.sent, self.due = send_sems, recv_sems, 0, 0
        self.free, self.copies = [], []

    def copy(self, src, dst, to, recv):
        if not self.free:
            self.free.append(self.sent)
            self.sent += 1
        place = self.free.pop(0)
        copy = pltpu.make_async_remote_copy(
            src_ref=src,
            dst_ref=dst,
            send_sem=self.send_sems.at[place],
            recv_sem=self.recv_sems.at[recv],
            device_id=to,
            device_id_type=MESH,
        )
        copy.start()
        self.copies.append((copy, place))
        return copy

    def __call__(self, src, dst, to):
        self.due += 1
        return self.copy(src, dst, to, self.due - 1)

    def group(self, whole, copies):
        self.due += 1
        for src, dst, to in copies:
            self.copy(src, dst, to, self.due - 1)
        return pltpu.make_async_remote_copy(
            src_ref=whole,
            dst_ref=whole,
            send_sem=self.send_sems.at[0],
            recv_sem=self.recv_sems.at[self.due - 1],
            device_id=copies[0][2],
            device_id_type=MESH,
        )

    def finish(self, oldest=None):
        done = self.copies[:oldest]
        for copy, place in done:
            copy.wait_send()
            self.free.append(place)
        self.copies = self.copies[len(done) :]


def arrive(copies):
    for copy in copies:
        copy.wait_recv()


def rows16(index, base=0):
    return pl.ds(pl.multiple_of(index * 16 + base, 16), 16)


def half_columns(index):
    return pl.ds(pl.multiple_of(index * 384, 128) if not isinstance(index, int) else index * 384, 384)


def right_dot(left, right):
    return lax.dot_general(left, right, (((1,), (1,)), ((), ())), preferred_element_type=F32)


def row_dot(left, right):
    return lax.dot_general(left, right, (((0,), (0,)), ((), ())), preferred_element_type=F32)


def dot(left, right):
    return jnp.dot(left, right, preferred_element_type=F32)


def add(target, *terms):
    total = terms[0].astype(F32)
    for term in terms[1:]:
        total += term.astype(F32)
    return total.astype(target.dtype)


def loop(n, body):
    def step(i, carry):
        body(i)
        return carry

    lax.fori_loop(0, n, step, 0)


class Ring:
    def __init__(self, send, at, axis, region):
        self.send, self.me, self.region = send, at[axis], region
        self.right, self.left = device(moved(at, **{axis: 1})), device(moved(at, **{axis: 3}))

    def at(self, step):
        return lax.rem(self.me + step, 4)

    def go(self, index, part, to):
        ref = self.region(index, part)
        return [self.send(ref, ref, to)]

    def start(self):
        self.from_left = self.go(self.me, None, self.right)
        self.from_right = self.go(self.me, None, self.left)

    def left_in(self):
        arrive(self.from_left)
        self.far_left = self.go(self.at(3), 0, self.right)

    def right_in(self):
        arrive(self.from_right)
        self.far_right = self.go(self.at(1), 1, self.left)

    def both_in(self):
        self.left_in()
        self.right_in()

    def far_in(self):
        arrive(self.far_left)
        arrive(self.far_right)


def layer_kernel(
    conv_s, dna_s, qkv_s, out_s, rows_in, letters, upstream,
    seq_o, final, final_x, final_y,
    ga, gb, before, after,
    taps, taps_y, taps_t, onehot, onehot_t, choose_x, choose_y, wide_x, wide_y, wide_xt, wide_yt, d_proj, attended, attended_t,
    mine, got, got_k, got_v, outgo, outgo_k, outgo_v, back, back_k, back_v, probs_s, scores_s,
    pa_s, pb_s, px_s, py_s, pa, pb, px, py, pa_r, pb_r, px_r, py_r,
    fa, na, sa1, ra2, sa2, ra3, sa3, ra4,
    fb, nb, sb1, rb2, sb2, rb3, sb3, rb4,
    fcx, ncx, scx1, rcx2, scx2, rcx3, scx3, rcx4,
    fcy, ncy, scy1, rcy2, scy2, rcy3, scy3, rcy4,
    slope, unit, inverse, rows_f, probs_f, rim_out, rim_before, rim_after,
    send_sems, recv_sems,
):
    at = here()
    zh, y, c, zl, x = (at[a] for a in ("zh", "y", "c", "zl", "x"))
    sq = lax.axis_index("seq")
    dp = lax.axis_index("dp")
    behind, ahead = (dp, lax.rem(sq + 7, 8)), (dp, lax.rem(sq + 1, 8))
    sibling = device(moved(at, c=1))
    near = device(moved(at, zl=1))
    across = [moved(at, x=k, zl=1) for k in range(4)]
    everyone = [device(moved(at, **{a: k})) for a, k in PEERS] + [behind, ahead]
    everyone += [device(p) for p in across[1:]]
    barrier = pltpu.get_barrier_semaphore()
    for one in everyone:
        pl.semaphore_signal(barrier, inc=1, device_id=one, device_id_type=MESH)
    xs = [lax.rem(x + k, 4) for k in range(4)]
    ys = [lax.rem(y + k, 4) for k in range(4)]
    zs = [lax.rem(zh + k, 4) for k in range(4)]

    quarter = rows16(x)
    ga[zh, y, c, x, :, 0:768] = conv_s[quarter]
    ga[zh, y, c, x, :, 768:1152] = qkv_s[0:16, half_columns(x)]
    gb[zh, y, c, 0:32] = conv_s[64:96]
    gb[zh, y, c, 32:48] = dna_s[...]
    gb[zh, y, c, 48:64] = out_s[...]
    last_rows = [qkv_s[:, 768 * i : 768 * i + 768].astype(F32)[16:24] for i in range(2)]
    gb[zh, y, c, 64:80] = jnp.concatenate(last_rows, axis=0).astype(BF16)
    pl.semaphore_wait(barrier, len(everyone))

    send = Sender(send_sems, recv_sems)

    def ref_a(height, step, index, part=None):
        rows = pl.ds(0, 4) if part is None else pl.ds(2 * part, 2)
        return ga.at[rows if height is None else height, step, c, index]

    def ref_b(height, step, part=None):
        return gb.at[height, step, c] if part is None else gb.at[height, step, c, :, half_columns(part)]

    core = []

    def pass_on(ref):
        core.append(send(ref, ref, sibling))

    def pass_a(step):
        pass_on(ga.at[:, step, c])

    def pass_b(height):
        pass_on(gb.at[height, :, c])

    a1 = []
    for k in (2, 1, 3):
        a1.append(send(ref_a(zh, y, x), ref_a(zh, y, x), device(moved(at, zh=k))))
    halo = [
        send(rows_in.at[pl.ds(240, 16)], before, ahead),
        send(rows_in.at[pl.ds(0, 16)], after, behind),
    ]
    ring_z = Ring(send, at, "zh", lambda index, part: ref_b(index, y, part))
    rings_y = [Ring(send, at, "y", lambda index, part, v=zs[k]: ref_b(v, index, part)) for k in range(4)]
    rings_x = [Ring(send, at, "x", lambda index, part, v=ys[k]: ref_a(None, v, index, part)) for k in range(4)]
    ring_a = Ring(send, at, "y", lambda index, part: ref_a(None, index, x, part))
    ring_z.start()
    rings_y[0].start()
    row = lax.broadcasted_iota(jnp.int32, (128, 512), 0)
    column = lax.broadcasted_iota(jnp.int32, (128, 512), 1)
    repeat = (column // 4 == row).astype(F32).astype(BF16)
    repeated = dot(letters[...].astype(F32).astype(BF16), repeat)
    onehot[...] = (repeated == lax.rem(column, 4).astype(F32)).astype(F32).astype(BF16)
    row = lax.broadcasted_iota(jnp.int32, (768, 512), 0)
    column = lax.broadcasted_iota(jnp.int32, (768, 512), 1)
    first_row = column // 16 * 24
    choose_x[...] = (first_row + lax.rem(column, 16) == row).astype(F32).astype(BF16)
    choose_y[...] = (first_row + 16 + lax.rem(column, 8) == row).astype(F32).astype(BF16)
    arrive(a1)
    ring_a.start()
    rings_x[0].start()
    ring_z.left_in()
    rings_y[3].start()
    ring_z.right_in()
    rings_y[0].both_in()
    ring_a.left_in()
    rings_x[3].start()
    ring_a.right_in()
    rings_x[1].start()
    rings_y[1].start()
    rings_x[0].both_in()
    ring_a.far_in()
    rings_x[2].start()
    ring_z.far_in()
    rings_y[2].start()
    rings_y[3].both_in()
    rings_x[3].both_in()
    rings_x[1].both_in()
    rings_y[1].both_in()
    rings_y[0].far_in()
    pass_b(zs[0])
    rings_x[0].far_in()
    pass_a(ys[0])
    rings_x[2].both_in()
    rings_y[2].both_in()

    send.finish(24)
    arrive(halo)
    for j in range(6):
        lanes = slice(128 * j, 128 * j + 128)
        rows_f[j, 8:264] = rows_in[:, lanes].astype(F32)
        rows_f[j, 0:8] = jnp.where(sq > 0, before[:, lanes].astype(F32)[8:16], 0.0)
        rows_f[j, 264:272] = jnp.where(sq < 7, after[:, lanes].astype(F32)[0:8], 0.0)
        for i in range(4):
            taps[i, :, lanes] = rows_f[j, pl.ds(7 + i, 128, stride=2)].astype(BF16)
    for i in range(4):
        whole = taps[i].astype(F32)
        moved_on = pltpu.roll(whole, 704, 1).astype(BF16)
        for k in range(4):
            start = 384 * (k // 2) + 128 * (k % 2)
            taps_y[k, i] = moved_on[:, start : start + 256] if k % 2 else taps[i, :, start : start + 256]

    rings_y[3].far_in()
    pass_b(zs[3])
    rings_y[1].far_in()
    pass_b(zs[1])
    rings_x[3].far_in()
    pass_a(ys[3])
    rings_x[1].far_in()
    pass_a(ys[1])
    rings_y[2].far_in()
    pass_b(zs[2])
    rings_x[2].far_in()
    pass_a(ys[2])

    arrive(core[:-1])

    def conv_full(i):
        first = ga[i, :, :, :, :, 0:768].reshape(4, 2, 64, 768)
        return jnp.concatenate([first, gb[i, :, :, 0:32]], axis=2).reshape(768, 768)

    def qx_full(i):
        return jnp.concatenate(
            [ga[:, :, :, 2 * i + j, :, 768:1152].reshape(512, 384) for j in range(2)], axis=1
        )

    def qy_full():
        return gb[:, :, :, 64:80].reshape(512, 768)

    dna_full = gb[:, :, :, 32:48].reshape(512, 768)
    out_full = gb[:, :, :, 48:64].reshape(512, 768)
    d_attend = right_dot(upstream[...], out_full).astype(BF16)
    slope[...] = dot(onehot[...], dna_full)

    def y_block(k):
        total = 0.0
        for i in range(4):
            first = ga[i, ys[k], :, :, :, 0:768].reshape(2, 64, 768)
            block = jnp.concatenate([first, gb[i, ys[k], :, 0:32]], axis=1).reshape(192, 768)
            block = jnp.concatenate([block, jnp.zeros((64, 768), BF16)], axis=0)
            total += dot(taps_y[ys[k], i], block)
        slope[...] += total

    for k in (0, 3, 1):
        y_block(k)
    arrive(core[-1:])
    y_block(2)
    pre = slope[...]
    bend = jnp.tanh(math.sqrt(2.0 / math.pi) * (pre + 0.044715 * (pre * pre * pre)))
    share = 0.5 * (1.0 + bend)
    feature = (pre * share).astype(BF16).astype(F32)
    slope[...] = share + pre * (0.5 * (1.0 - bend * bend)) * (
        math.sqrt(2.0 / math.pi) * (1.0 + 3.0 * 0.044715 * (pre * pre))
    )
    scale = lax.rsqrt(jnp.mean(feature * feature, axis=1, keepdims=True) + epsilon)
    inverse[...] = scale
    unit[...] = feature * scale
    normed = unit[...].astype(BF16)
    wide_x[...] = dot(normed, choose_x[...]).astype(BF16)
    wide_y[...] = dot(normed, choose_y[...]).astype(BF16)
    side_of = lax.rem(lax.broadcasted_iota(jnp.int32, (128, 512), 1), 16) // 8
    own_y = [jnp.where(side_of == i, wide_y[...].astype(F32), 0.0).astype(BF16) for i in range(2)]
    from_y = dot(jnp.concatenate(own_y, axis=0), qy_full())
    for i in range(2):
        projected = (dot(wide_x[...], qx_full(i)) + from_y[128 * i : 128 * i + 128]).astype(BF16)
        for piece in range(6):
            kind, head = divmod(6 * i + piece, 4)
            mine[head, (1, 0, 2)[kind]] = projected[:, 128 * piece : 128 * piece + 128]
    for head in range(H):
        mine[head, 3] = d_attend[:, 128 * head : 128 * head + 128]

    kq, vd = pl.ds(0, 2), pl.ds(2, 2)
    kq_in, vd_in = {}, {}
    from_near_k = send.group(got_k, [(mine.at[x, 0], got_k.at[x], near)])
    near_k = send.due - 1
    from_near_v = send.group(got_v, [(mine.at[x, 2], got_v.at[x], near)])
    near_v = send.due - 1
    for k in (1, 3, 2):
        kq_in[k] = send(mine.at[xs[k], kq], got.at[x, kq], device(moved(at, x=k)))
    for k in (1, 3, 2):
        vd_in[k] = send(mine.at[xs[k], vd], got.at[x, vd], device(moved(at, x=k)))
    sources = {k: lax.rem(x + 4 - k, 4) for k in (0, 1, 3, 2)}
    got[x] = mine[x]
    for k in (1, 3, 2):
        arrive([kq_in[k]])
        send.copy(got.at[sources[k], 0], got_k.at[sources[k]], near, near_k)
    def transpose_tap(i):
        taps_t[i] = taps[i].T.reshape(4, 2, 96, 128)

    loop(4, transpose_tap)
    onehot_t[...] = onehot[...].T.reshape(4, 4, 2, 16, 128)
    wide_xt[...] = wide_x[...].T.reshape(4, 4, 2, 16, 128)
    wide_yt[...] = wide_y[...].T.reshape(4, 4, 2, 16, 128)
    arrive([from_near_k])
    keys = jnp.concatenate([got[:, 0].reshape(512, 128), got_k[...].reshape(512, 128)], axis=0)
    scaling = 1.0 / math.sqrt(128)

    pairs = (slice(0, 2), slice(2, 4))

    def soft(pair):
        scores = right_dot(got[pair, 1].reshape(256, 128), keys) * scaling
        powers = jnp.exp(scores - jnp.max(scores, axis=1, keepdims=True))
        probs = powers * (1.0 / jnp.sum(powers, axis=1, keepdims=True))
        probs_f[pair] = probs.reshape(2, 128, 1024)
        probs_s[pair] = probs.astype(BF16).reshape(2, 128, 1024)

    def pass_v(k):
        arrive([vd_in[k]])
        send.copy(got.at[sources[k], 2], got_v.at[sources[k]], near, near_v)

    soft(pairs[0])
    pass_v(1)
    pass_v(3)
    soft(pairs[1])
    pass_v(2)
    home_v, home_q, home_k = [], [], []
    all_queries = got[:, 1].reshape(512, 128)
    all_upward = got[:, 3].reshape(512, 128)
    all_probs = probs_s[...].reshape(512, 1024)
    d_values = row_dot(all_upward, all_probs).T.astype(BF16).reshape(8, 128, 128)
    outgo_v[...] = d_values[4:8]
    home_v.append(send.group(back_v, [(outgo_v.at[p["x"]], back_v.at[x], device(p)) for p in across]))
    outgo[:, 1] = d_values[0:4]
    arrive([from_near_v])
    values = jnp.concatenate([got[:, 2].reshape(512, 128), got_v[...].reshape(512, 128)], axis=0)
    outgo[:, 0] = dot(all_probs, values).astype(BF16).reshape(4, 128, 128)
    for k in (1, 3, 2):
        block = pl.ds(0, 2)
        home_v.append(send(outgo.at[xs[k], block], back.at[x, block], device(moved(at, x=k))))
    for pair in pairs:
        probs = probs_f[pair].reshape(256, 1024)
        d_probs = right_dot(got[pair, 3].reshape(256, 128), values)
        inner = jnp.sum(probs * d_probs, axis=1, keepdims=True)
        d_scores = (probs * (d_probs - inner) * scaling).astype(BF16)
        scores_s[pair] = d_scores.reshape(2, 128, 1024)
        outgo[pair, 2] = dot(d_scores, keys).astype(BF16).reshape(2, 128, 128)
    for k in (1, 3, 2):
        home_q.append(send(outgo.at[xs[k], 2], back.at[x, 2], device(moved(at, x=k))))

    def key_grads(columns):
        d_keys = row_dot(all_queries, scores_s[:, :, columns].reshape(512, 512)).T
        return d_keys.astype(BF16).reshape(4, 128, 128)

    outgo_k[...] = key_grads(slice(512, 1024))
    home_k.append(send.group(back_k, [(outgo_k.at[p["x"]], back_k.at[x], device(p)) for p in across]))
    outgo[:, 3] = key_grads(slice(0, 512))
    for k in (1, 3, 2):
        home_k.append(send(outgo.at[xs[k], 3], back.at[x, 3], device(moved(at, x=k))))
    back[x] = outgo[x]

    def columns_of(head, start=0):
        return slice(start + 128 * head, start + 128 * head + 128)

    arrive(home_v)
    for head in range(H):
        attended[:, columns_of(head)] = back[head, 0]
        total = back[head, 1].astype(F32) + back_v[head].astype(F32)
        d_proj[:, columns_of(head, 1024)] = total.astype(BF16)
    attended_t[...] = attended[...].T.reshape(4, 4, 2, 16, 128)
    for parity, to_b in ((1 - c, pb_s), (c, pb)):
        left = attended_t[:, :, parity].reshape(256, 128)
        to_b[:, :, 48:64] = dot(left, upstream[...]).astype(BF16).reshape(4, 4, 16, 768)
    arrive(home_q)
    for head in range(H):
        d_proj[:, columns_of(head)] = back[head, 2]

    def qkv_quarters(parity, to_x, quarters):
        left = wide_xt[:, :, parity].reshape(256, 128)
        for q in quarters:
            block = dot(left, d_proj[:, 384 * q : 384 * q + 384]).astype(BF16)
            to_x[q] = block.reshape(4, 4, 16, 384)

    qkv_quarters(1 - c, px_s, (0, 3))
    qkv_quarters(c, px, (0, 3))
    d_q, d_v = d_proj[:, 0:512], d_proj[:, 1024:1536]
    d_x = right_dot(d_q, qx_full(0)[:, 0:512]) + right_dot(d_v, qx_full(1)[:, 256:768])
    d_y0, d_y1 = right_dot(d_q, qy_full()[:, 0:512]), right_dot(d_v, qy_full()[:, 256:768])
    arrive(home_k)
    send.finish()
    for head in range(H):
        total = back[head, 3].astype(F32) + back_k[head].astype(F32)
        d_proj[:, columns_of(head, 512)] = total.astype(BF16)

    row_side = lax.rem(lax.broadcasted_iota(jnp.int32, (256, 768), 0), 16)

    def qkv_grads(parity, to_x, to_y):
        qkv_quarters(parity, to_x, (1, 2))
        left = wide_yt[:, :, parity].reshape(256, 128)
        both = [dot(left, d_proj[:, 768 * i : 768 * i + 768]) for i in range(2)]
        to_y[...] = jnp.where(row_side < 8, both[0], both[1]).astype(BF16).reshape(4, 4, 16, 768)

    order = (2, 1, 3, 0)
    core_cx, core_cy, core_a, core_b = {}, {}, {}, {}
    qkv_grads(1 - c, px_s, py_s)
    for k in order:
        core_cx[k] = send(px_s.at[:, zs[k]], px_r.at[:, zs[k]], sibling)
        core_cy[k] = send(py_s.at[:, ys[k]], py_r.at[:, ys[k]], sibling)
    qkv_grads(c, px, py)
    d_k0, d_k1 = d_proj[:, 512:768], d_proj[:, 768:1024]
    d_x += right_dot(d_k0, qx_full(0)[:, 512:768]) + right_dot(d_k1, qx_full(1)[:, 0:256])
    d_y0 += right_dot(d_k0, qy_full()[:, 512:768])
    d_y1 += right_dot(d_k1, qy_full()[:, 0:256])
    d_y = jnp.where(side_of == 0, d_y0, d_y1)

    def sum_cx(k):
        arrive([core_cx[k]])
        px[:, zs[k]] = add(px, px[:, zs[k]], px_r[:, zs[k]])

    def sum_cy(k):
        arrive([core_cy[k]])
        py[:, ys[k]] = add(py, py[:, ys[k]], py_r[:, ys[k]])

    right_x, left_x = device(moved(at, x=1)), device(moved(at, x=3))
    right_y, left_y = device(moved(at, y=1)), device(moved(at, y=3))
    right_z, left_z = device(moved(at, zh=1)), device(moved(at, zh=3))
    low, high = pl.ds(0, 2), pl.ds(2, 2)
    sides = ((0, 1, right_x, right_y), (1, 3, left_x, left_y))
    d_normed = 0.0
    for terms, choose in ((d_x, choose_x), (d_y, choose_y)):
        d_high = terms.astype(BF16)
        d_low = (terms - d_high.astype(F32)).astype(BF16)
        both = right_dot(jnp.concatenate([d_high, d_low], axis=0), choose[...])
        d_normed += both[0:128] + both[128:256]
    d_feature = upstream[...].astype(F32) + inverse[...] * (
        d_normed - unit[...] * jnp.mean(d_normed * unit[...], axis=1, keepdims=True)
    )
    d_pre = (d_feature * slope[...]).astype(BF16)

    sum_cx(2)
    far_cx = [
        send(px.at[quarters, zs[2]], fcx.at[side], to) for side, quarters, to in ((0, low, right_z), (1, high, left_z))
    ]
    sum_cy(2)
    far_cy = [
        send(py.at[heights, ys[2]], fcy.at[side], to) for side, heights, to in ((0, low, right_y), (1, high, left_y))
    ]
    def conv_grads(parity, to_a, to_b):
        def one(i):
            block = dot(taps_t[i, :, parity].reshape(384, 128), d_pre).astype(BF16).reshape(4, 96, 768)
            to_a[i] = block[:, 0:64]
            to_b[i, :, 0:32] = block[:, 64:96]

        loop(4, one)
        left = onehot_t[:, :, parity].reshape(256, 128)
        to_b[:, :, 32:48] = dot(left, d_pre).astype(BF16).reshape(4, 4, 16, 768)

    conv_grads(1 - c, pa_s, pb_s)
    for k in order:
        core_a[k] = send(pa_s.at[:, :, rows16(xs[k])], pa_r.at[:, :, rows16(xs[k])], sibling)
        core_b[k] = send(pb_s.at[:, ys[k]], pb_r.at[:, ys[k]], sibling)
    conv_grads(c, pa, pb)

    def sum_a(k):
        arrive([core_a[k]])
        rows = rows16(xs[k])

        def one(i):
            pa[i, :, rows] = add(pa, pa[i, :, rows], pa_r[i, :, rows])

        loop(4, one)

    def sum_b(k):
        arrive([core_b[k]])

        def one(i):
            pb[i, ys[k]] = add(pb, pb[i, ys[k]], pb_r[i, ys[k]])

        loop(4, one)

    halves = [(h, pl.ds(384 * h, 384), slice(384 * h, 384 * h + 384)) for h in range(2)]
    far_a, far_b = {}, {}
    sum_a(2)
    sum_b(2)
    for h, columns, _ in halves:
        for side, heights, to_x, to_y in ((0, low, right_x, right_y), (1, high, left_x, left_y)):
            far_a[h, side] = send(pa.at[heights, :, rows16(xs[2]), columns], fa.at[h, side], to_x)
            far_b[h, side] = send(pb.at[heights, ys[2], :, columns], fb.at[h, side], to_y)
    near_cx, near_cy = [], []
    for side, k, to_x, to_y in sides:
        sum_cx(k)
        arrive([far_cx[side]])
        part = slice(2 * side, 2 * side + 2)
        px[part, zs[k]] = add(px, px[part, zs[k]], fcx[side])
        near_cx.append(send(px.at[:, zs[k]], ncx.at[side], (right_z, left_z)[side]))
        sum_cy(k)
        arrive([far_cy[side]])
        py[part, ys[k]] = add(py, py[part, ys[k]], fcy[side])
        near_cy.append(send(py.at[:, ys[k]], ncy.at[side], to_y))
    for side, k, to_x, to_y in sides:
        sum_a(k)
        sum_b(k)
    near_a, near_b = {}, {}
    for h, columns, cols in halves:
        for side, k, to_x, to_y in sides:
            rows = rows16(xs[k])
            arrive([far_a[h, side]])

            def join_a(i, h=h, side=side, rows=rows, cols=cols):
                pa[2 * side + i, :, rows, cols] = add(pa, pa[2 * side + i, :, rows, cols], fa[h, side, i])

            loop(2, join_a)
            near_a[h, side] = send(pa.at[:, :, rows, columns], na.at[h, side], to_x)
            arrive([far_b[h, side]])

            def join_b(i, h=h, side=side, index=ys[k], cols=cols):
                pb[2 * side + i, index, :, cols] = add(pb, pb[2 * side + i, index, :, cols], fb[h, side, i])

            loop(2, join_b)
            near_b[h, side] = send(pb.at[:, ys[k], :, columns], nb.at[h, side], to_y)

    def three(axis, whole, source):
        return send.group(
            whole, [(source(k), whole.at[k - 1], device(moved(at, **{axis: k}))) for k in (2, 1, 3)]
        )

    sum_cx(0)
    arrive(near_cx)
    scx1[...] = add(scx1, px[:, zh], ncx[0], ncx[1])
    cx2 = three("x", rcx2, lambda k: scx1.at[xs[k]])
    sum_cy(0)
    arrive(near_cy)
    scy1[...] = add(scy1, py[:, y], ncy[0], ncy[1])
    cy2 = three("zh", rcy2, lambda k: scy1.at[zs[k]])
    sum_a(0)
    sum_b(0)

    send.finish(28)
    rows_f[:, 256:272] = jnp.zeros((6, 16, 128), F32)
    for i in range(4):
        terms = right_dot(d_pre, conv_full(i))
        for j in range(6):
            target = pl.ds(7 + i, 128, stride=2)
            block = terms[:, 128 * j : 128 * j + 128]
            rows_f[j, target] = block if i < 2 else rows_f[j, target] + block
    rim_out[0] = rows_f[:, 264:272]
    rim_out[1] = rows_f[:, 0:8]
    rims = [send(rim_out.at[0], rim_before, ahead), send(rim_out.at[1], rim_after, behind)]

    a2, b2, a3, b3, a4, b4 = {}, {}, {}, {}, {}, {}
    for h, columns, cols in halves:
        arrive([near_a[h, 0], near_a[h, 1]])

        def first_a(i, h=h, cols=cols):
            sa1[h, i] = add(sa1, pa[i, :, rows16(x), cols], na[h, 0, i], na[h, 1, i])

        loop(4, first_a)
        a2[h] = three("y", ra2.at[h], lambda k, h=h: sa1.at[h, :, ys[k]])
        arrive([near_b[h, 0], near_b[h, 1]])

        def first_b(i, h=h, cols=cols):
            sb1[h, i] = add(sb1, pb[i, y, :, cols], nb[h, 0, i], nb[h, 1, i])

        loop(4, first_b)
        b2[h] = three("x", rb2.at[h], lambda k, h=h: sb1.at[h, :, rows16(xs[k])])
        if h == 0:
            arrive([cx2])
            scx2[...] = add(scx2, scx1[x], rcx2[0], rcx2[1], rcx2[2])
            cx3 = three("y", rcx3, lambda k: scx2.at[ys[k]])
            arrive([cy2])
            scy2[...] = add(scy2, scy1[zh], rcy2[0], rcy2[1], rcy2[2])
            cy3 = send(scy2, rcy3, near)
    arrive(rims)
    rows_f[:, 8:9] += jnp.where(sq > 0, rim_before[:, 0:1], 0.0)
    rows_f[:, 263:264] += jnp.where(sq < 7, rim_after[:, 7:8], 0.0)
    for j in range(6):
        seq_o[:, 128 * j : 128 * j + 128] = rows_f[j, 8:264].astype(BF16)
    for h in range(2):
        arrive([a2[h]])
        sa2[h] = add(sa2, sa1[h, :, y], ra2[h, 0], ra2[h, 1], ra2[h, 2])
        a3[h] = three("zh", ra3.at[h], lambda k, h=h: sa2.at[h, zs[k]])
        arrive([b2[h]])
        sb2[h] = add(sb2, sb1[h, :, rows16(x)], rb2[h, 0], rb2[h, 1], rb2[h, 2])
        b3[h] = three("zh", rb3.at[h], lambda k, h=h: sb2.at[h, zs[k]])
        if h == 0:
            arrive([cx3])
            scx3[...] = add(scx3, scx2[y], rcx3[0], rcx3[1], rcx3[2])
            cx4 = send(scx3, rcx4, near)
            arrive([cy3])
            scy3[...] = add(scy3, scy2[...], rcy3[...])
            cy4 = three("x", rcy4, lambda k: scy3)

    send.finish(12)
    for h in range(2):
        arrive([a3[h]])
        sa3[h] = add(sa3, sa2[h, zh], ra3[h, 0], ra3[h, 1], ra3[h, 2])
        a4[h] = send(sa3.at[h], ra4.at[h], near)
        arrive([b3[h]])
        sb3[h] = add(sb3, sb2[h, zh], rb3[h, 0], rb3[h, 1], rb3[h, 2])
        b4[h] = send(sb3.at[h], rb4.at[h], near)
        if h == 0:
            arrive([cx4])
            final_x[x] = add(final_x, scx3[...], rcx4[...])
            spread = [send(final_x.at[x], final_x.at[x], device(moved(at, x=k))) for k in (1, 2, 3)]
            arrive([cy4])
            final_y[...] = add(final_y, scy3[...], rcy4[0], rcy4[1], rcy4[2])
    for h in range(2):
        arrive([a4[h]])
        final[x, 0, h] = add(final, sa3[h], ra4[h])
        arrive([b4[h]])
        final[x, 1, h] = add(final, sb3[h], rb4[h])
    spread += [send(final.at[x], final.at[x], device(moved(at, x=k))) for k in (1, 2, 3)]
    arrive(spread)
    send.finish()


def finish_kernel(seq_i, final, final_x, final_y, seq_o, conv_o, dna_o, qkv_o, out_o):
    seq_o[0] = seq_i[...]
    for h in range(2):
        columns = slice(384 * h, 384 * h + 384)
        for q in range(4):
            conv_o[16 * q : 16 * q + 16, columns] = final[q, 0, h].astype(F32)
        conv_o[64:80, columns] = final[0, 1, h].astype(F32)
        conv_o[80:96, columns] = final[1, 1, h].astype(F32)
        dna_o[:, columns] = final[2, 1, h].astype(F32)
        out_o[:, columns] = final[3, 1, h].astype(F32)
    for q in range(4):
        qkv_o[0:16, 384 * q : 384 * q + 384] = final_x[q].astype(F32)
    last_rows = final_y[...].astype(F32)
    qkv_o[16:24, 0:768] = last_rows[0:8]
    qkv_o[16:24, 768:1536] = last_rows[8:16]


def layer(*operands):
    vmem = pl.BlockSpec(memory_space=pltpu.VMEM)
    low = [
        (4, 4, 2, 4, 16, 1152), (4, 4, 2, 80, 768), (16, 768), (16, 768),
        (4, 128, 768), (4, 4, 128, 256), (4, 4, 2, 96, 128), (128, 512), (4, 4, 2, 16, 128), (768, 512), (768, 512),
        (128, 512), (128, 512), (4, 4, 2, 16, 128), (4, 4, 2, 16, 128), (128, 1536), (128, 512), (4, 4, 2, 16, 128),
        (4, 4, 128, 128), (4, 4, 128, 128), (4, 128, 128), (4, 128, 128), (4, 4, 128, 128), (4, 128, 128), (4, 128, 128),
        (4, 4, 128, 128), (4, 128, 128), (4, 128, 128),
        (4, 128, 1024), (4, 128, 1024),
    ] + 3 * [(4, 4, 64, 768), (4, 4, 64, 768), (4, 4, 4, 16, 384), (4, 4, 16, 768)] + [
        (2, 2, 2, 4, 16, 384), (2, 2, 4, 4, 16, 384), (2, 4, 4, 16, 384), (2, 3, 4, 16, 384),
        (2, 4, 16, 384), (2, 3, 16, 384), (2, 16, 384), (2, 16, 384),
        (2, 2, 2, 64, 384), (2, 2, 4, 64, 384), (2, 4, 64, 384), (2, 3, 4, 16, 384),
        (2, 4, 16, 384), (2, 3, 16, 384), (2, 16, 384), (2, 16, 384),
        (2, 2, 4, 16, 384), (2, 4, 4, 16, 384), (4, 4, 16, 384), (3, 4, 16, 384), (4, 16, 384), (3, 16, 384), (16, 384), (16, 384),
        (2, 2, 16, 768), (2, 4, 16, 768), (4, 16, 768), (3, 16, 768), (16, 768), (16, 768), (16, 768), (3, 16, 768),
    ]
    wide = [(128, 768), (128, 768), (128, 1), (6, 272, 128), (4, 128, 1024), (2, 6, 8, 128), (6, 8, 128), (6, 8, 128)]
    results = pl.pallas_call(
        layer_kernel,
        name="layer",
        out_shape=tuple(
            jax.ShapeDtypeStruct(shape, BF16)
            for shape in ((256, 768), (4, 2, 2, 16, 384), (4, 16, 384), (16, 768))
        ),
        in_specs=[vmem] * 7,
        out_specs=(vmem,) * 4,
        scratch_shapes=[pltpu.VMEM(shape, BF16) for shape in low]
        + [pltpu.VMEM(shape, F32) for shape in wide]
        + [pltpu.SemaphoreType.DMA((60,)), pltpu.SemaphoreType.DMA((138,))],
        compiler_params=pltpu.CompilerParams(
            collective_id=1, has_side_effects=True, vmem_limit_bytes=60 * 2**20
        ),
    )(*operands)
    return pl.pallas_call(
        finish_kernel,
        name="finish",
        out_shape=(
            jax.ShapeDtypeStruct((1, 256, 768), BF16),
            jax.ShapeDtypeStruct((96, 768), F32),
            jax.ShapeDtypeStruct((16, 768), F32),
            jax.ShapeDtypeStruct((24, 1536), F32),
            jax.ShapeDtypeStruct((16, 768), F32),
        ),
        in_specs=[vmem] * 4,
        out_specs=(vmem,) * 5,
    )(*results)


def per_device(seq_in, bases, conv_weight, dna_weight, qkv_weight, out_weight, cotangent):
    return layer(
        conv_weight, dna_weight, qkv_weight, out_weight, seq_in[0], bases[0].reshape(128, BIN), cotangent[0]
    )


def solution(mesh):
    in_specs = (
        P("dp", "seq", None),
        P("dp", "seq"),
        P("dp", None),
        P("dp", None),
        P("dp", None),
        P("dp", None),
        P("dp", "seq", None),
    )
    out_specs = (P("dp", "seq", None), P("dp", None), P("dp", None), P("dp", None), P("dp", None))
    return jax.shard_map(
        per_device, mesh=mesh, in_specs=in_specs, out_specs=out_specs, check_vma=False
    )
```
